32 devices in a mesh: lat: 4 (over z), lon: 8 (over y, x, core).
Axes of the slice: x: 2, y: 2, z: 4, core: 2. Of those that a mesh axis runs over, the one named last changes fastest.
Arguments:
- adjoint_field: float32 [128, 128, 2048], P(None, 'lat', 'lon'), may hold values from -6 to 6
- mixing_inverse: float32 [128, 128, 128], P('lat'), as said below
- cloud_top: int32 [128, 2048], P('lat', 'lon'), may hold values from 1 to 128
- conv_frac: float32 [128, 2048], P('lat', 'lon'), may hold values from 0.2 to 0.9
- thickness: float32 [128], replicated, may hold values from 0.3 to 3
- zonal_shift: int32 [128, 128], P(None, 'lat'), may hold values from 0 to 48
- zonal_frac: float32 [128, 128], P(None, 'lat'), may hold values from 0 to 1
- merid_courant: float32 [128, 128, 2048], P(None, 'lat', 'lon'), may hold values from 0.1 to 0.9
- obs_kernel: bfloat16 [16384, 128], P(('lat', 'lon')), may hold values from -6 to 6
- obs_depart: float32 [16384], P(('lat', 'lon')), may hold values from -6 to 6
- obs_dest: int32 [16384], P(('lat', 'lon')), may hold values from 0 to 31, as said below
- obs_col: int32 [16384], P(('lat', 'lon')), may hold values from 0 to 8191
- obs_count: int32 [32], P(('lat', 'lon')), may hold values from 16 to 512, as said below
Outputs:
- adjoint_out: float32 [128, 128, 2048], P(None, 'lat', 'lon')
The draws below stay inside these ranges and needn't reach their ends.
Inputs may be any that keep to these rules, and one draw needn't show every extreme that they name: `obs_dest`: live rows of each device are in non-decreasing order of destination, at most 16 of them to one destination; some destination receives exactly 16 live rows from every device. Rows past a device's count carry no sounding. `obs_count`: some device has all its rows live. `mixing_inverse`: entries are positive.
All inputs are finite; a program needn't handle non-finite values.
Results may differ from the reference program's by a relative error of at most 0.00095.
Values may be sent and summed in bfloat16 or wider, within the bound.
No kernel may reach another device: no remote copies, remote signals or barrier semaphores. Data moves between devices by JAX's collectives and lax.ppermute only.
A program may use at most 128 MiB of HBM per device.

```python
import math
import jax
import jax.numpy as jnp
from jax import lax

LEV = 128
RLAT = 32
CLON = 256
SHIFT_MAX = 48
CAP = 16
NLAT = 128
NLON = 2048
OBS_DEV = 512
OBS = 16384
N_LAT = 4
N_LON = 8


def route_tables(key):
    devices = N_LAT * N_LON
    base = jax.random.fold_in(key, 7)
    key_counts, key_hot, key_full = jax.random.split(base, 3)
    counts = jax.random.randint(key_counts, (devices, devices), 0, CAP + 1)
    hot_dest = jax.random.randint(key_hot, (), 0, devices)
    full_source = jax.random.randint(key_full, (), 0, devices)
    device_ids = jnp.arange(devices)
    counts = jnp.where(device_ids[None, :] == hot_dest, CAP, counts)
    counts = jnp.where(device_ids[:, None] == full_source, CAP, counts)
    group_ends = jnp.cumsum(counts, axis=1)
    live_total = group_ends[:, -1]
    row_ids = jnp.arange(OBS_DEV)
    dest_ids = jnp.sum((row_ids[None, :, None] >= group_ends[:, None, :]).astype(jnp.int32), axis=2)
    dest_ids = jnp.where(row_ids[None, :] < live_total[:, None], dest_ids, 0)
    return (dest_ids.reshape(-1).astype(jnp.int32), live_total.astype(jnp.int32))


def draw_obs_dest(key, part):
    dest_ids, live_total = route_tables(key)
    return dest_ids


def draw_obs_count(key, part):
    dest_ids, live_total = route_tables(key)
    return live_total


def draw_zonal_shift(key, part):
    key_values, key_place = jax.random.split(jax.random.fold_in(key, 11))
    shifts = jax.random.randint(key_values, (LEV, NLAT), 0, SHIFT_MAX + 1)
    place = jax.random.randint(key_place, (), 0, LEV * NLAT)
    flat_ids = jnp.arange(LEV * NLAT).reshape(LEV, NLAT)
    return jnp.where(flat_ids == place, SHIFT_MAX, shifts).astype(jnp.int32)


def draw_mixing_inverse(key, part):
    rough = jax.random.uniform(jax.random.fold_in(key, 13), (NLAT, LEV, LEV), jnp.float32, 0.5, 1.5)
    level_ids = jnp.arange(LEV)
    distance = jnp.abs(level_ids[:, None] - level_ids[None, :]).astype(jnp.float32)
    reach = 8.0
    weight = 0.3
    spread = weight * jnp.exp(-distance / reach)[None] * rough
    return jnp.where(distance[None] == 0.0, 0.6 + 0.4 * rough, spread).astype(jnp.float32)


def set_ends(result, own_key, smallest, high):
    shape = result.shape
    spot = [jax.random.randint(jax.random.fold_in(own_key, axis), (), 0, shape[axis]) for axis in range(len(shape))]
    result = result.at[tuple(spot)].set(smallest)
    longest = shape.index(max(shape))
    spot[longest] = (spot[longest] + 1) % shape[longest]
    return result.at[tuple(spot)].set(high)


def steps_of(own_key, dims, shards, least, top_value):
    gain, own = 1.0, jax.random.fold_in(own_key, 6)
    for position, parts in shards:
        steps = jnp.exp(jax.random.uniform(jax.random.fold_in(own, position), (parts,), jnp.float32, least / len(shards), top_value / len(shards)))
        gain = gain * jnp.repeat(steps, dims[position] // parts).reshape([-1 if axis == position else 1 for axis in range(len(dims))])
    return gain


def centred(key, dims, width, limit, pieces=(), kind=jnp.bfloat16):
    drawn = jax.random.normal(key, dims, jnp.float32) * width
    if len(pieces) > 0:
        drawn = steps_of(key, dims, pieces, -0.22, 0.18) * drawn
    return jnp.clip(drawn, min=-limit, max=limit).astype(kind)


def setup_inputs(seed: int = 0) -> dict:
    seeds = jax.random.split(jax.random.key(seed), 14)
    adjoint_field = centred(seeds[0], (LEV, NLAT, NLON), 1.0, 6.0, ((1, 4), (2, 8)), jnp.float32)
    mixing_inverse = draw_mixing_inverse(jax.random.fold_in(seeds[13], 71), 0)
    cloud_top = set_ends(jax.random.randint(seeds[2], (NLAT, NLON), 1, LEV + 1), jax.random.fold_in(seeds[2], 1), 1, LEV).astype(jnp.int32)
    conv_frac = jnp.clip(0.2 + 0.7 * jax.random.uniform(seeds[3], (NLAT, NLON), jnp.float32) ** steps_of(seeds[3], (NLAT, NLON), ((0, 4), (1, 8)), -0.2, 0.2), 0.2, 0.9)
    thickness = jnp.clip(jnp.exp(jax.random.uniform(seeds[4], (LEV,), jnp.float32, math.log(0.3), math.log(3.0))), 0.3, 3.0)
    zonal_shift = draw_zonal_shift(jax.random.fold_in(seeds[13], 71), 0)
    zonal_frac = jnp.clip(1.0 * jax.random.uniform(seeds[6], (LEV, NLAT), jnp.float32) ** steps_of(seeds[6], (LEV, NLAT), ((1, 4),), -0.2, 0.2), 0.0, 1.0)
    merid_courant = jnp.clip(0.1 + 0.79999997 * jax.random.uniform(seeds[7], (LEV, NLAT, NLON), jnp.float32) ** steps_of(seeds[7], (LEV, NLAT, NLON), ((1, 4), (2, 8)), -0.2, 0.2), 0.1, 0.9)
    obs_kernel = centred(seeds[8], (OBS, LEV), 1.0, 6.0, ((0, 32),))
    obs_depart = centred(seeds[9], (OBS,), 1.0, 6.0, ((0, 32),), jnp.float32)
    obs_dest = draw_obs_dest(jax.random.fold_in(seeds[13], 71), 0)
    obs_col = set_ends(jax.random.randint(seeds[11], (OBS,), 0, RLAT * CLON), jax.random.fold_in(seeds[11], 1), 0, (RLAT * CLON) - 1).astype(jnp.int32)
    obs_count = draw_obs_count(jax.random.fold_in(seeds[13], 71), 0)
    return dict(adjoint_field=adjoint_field, mixing_inverse=mixing_inverse, cloud_top=cloud_top, conv_frac=conv_frac, thickness=thickness, zonal_shift=zonal_shift, zonal_frac=zonal_frac, merid_courant=merid_courant, obs_kernel=obs_kernel, obs_depart=obs_depart, obs_dest=obs_dest, obs_col=obs_col, obs_count=obs_count)


def reference(adjoint_field, mixing_inverse, cloud_top, conv_frac, thickness, zonal_shift, zonal_frac, merid_courant, obs_kernel, obs_depart, obs_dest, obs_col, obs_count):
    row_ids = jnp.arange(OBS, dtype=jnp.int32)
    owner_ids = row_ids // OBS_DEV
    live_rows = (row_ids % OBS_DEV) < obs_count[owner_ids]
    contribution = jnp.where(live_rows[:, None], obs_kernel.astype(jnp.float32) * obs_depart[:, None], 0.0).astype(jnp.bfloat16)
    lat_index = obs_dest // N_LON
    lon_index = obs_dest % N_LON
    global_row = lat_index * RLAT + obs_col // CLON
    global_col = lon_index * CLON + obs_col % CLON
    cell_ids = (global_row * NLON + global_col).astype(jnp.int32)
    forcing = jax.ops.segment_sum(contribution.astype(jnp.float32), cell_ids, num_segments=NLAT * NLON)
    field_forced = adjoint_field + forcing.T.reshape(LEV, NLAT, NLON)
    field_mixed = jnp.einsum("rkj,jrc->krc", mixing_inverse, field_forced, precision=lax.Precision.HIGHEST)
    level_ids = jnp.arange(LEV, dtype=jnp.int32)[:, None, None]
    in_cloud = (level_ids < cloud_top[None, :, :]).astype(jnp.float32)
    layer_mass = thickness[:, None, None]
    cloud_total = jnp.sum(in_cloud * field_mixed, axis=0)
    cloud_mass = jnp.sum(in_cloud * layer_mass, axis=0)
    field_convected = field_mixed + conv_frac[None] * in_cloud * (layer_mass * (cloud_total / cloud_mass)[None] - field_mixed)
    col_ids = jnp.arange(NLON, dtype=jnp.int32)[None, None, :]
    first_index = (col_ids + zonal_shift[:, :, None]) % NLON
    second_index = (first_index + 1) % NLON
    first_cells = jnp.take_along_axis(field_convected, first_index, axis=2)
    second_cells = jnp.take_along_axis(field_convected, second_index, axis=2)
    fraction = zonal_frac[:, :, None]
    field_zonal = (1.0 - fraction) * first_cells + fraction * second_cells
    zero_row = jnp.zeros((LEV, 1, NLON), jnp.float32)
    next_field = jnp.concatenate([field_zonal[:, 1:], zero_row], axis=1)
    next_courant = jnp.concatenate([merid_courant[:, 1:], zero_row], axis=1)
    return (1.0 - merid_courant) * field_zonal + next_courant * next_field
```

```python
import functools

import jax
import jax.numpy as jnp
from jax import lax
from jax.experimental import pallas as pl
from jax.experimental.pallas import tpu as pltpu
from jax.sharding import PartitionSpec as P

F32, BF16, I32 = jnp.float32, jnp.bfloat16, jnp.int32
CAP = 16
SLOTS = 40
EDGE = 64
LANES = 128
GROUP = 32
CHUNK = 256
VMEM = 56 * 1024 * 1024


def iota(shape, dim):
    return lax.broadcasted_iota(I32, shape, dim)


def params(**kw):
    return pltpu.CompilerParams(vmem_limit_bytes=VMEM, **kw)


def dot(left, right):
    return jnp.dot(left, right, preferred_element_type=F32)


def dot_nt(left, right):
    return lax.dot_general(left, right, (((1,), (1,)), ((), ())), preferred_element_type=F32)


def halves(value):
    high = value.astype(BF16)
    return high, (value - high.astype(F32)).astype(BF16)


def thirds(value):
    high = value.astype(BF16)
    rest = value - high.astype(F32)
    mid = rest.astype(BF16)
    return [high, mid, (rest - mid.astype(F32)).astype(BF16)]


def as_column(line):
    return jnp.broadcast_to(line, (LANES, line.shape[1])).T


def convect(mixed, top, frac, layer_mass):
    inside = iota(mixed.shape, 0) < top
    total = jnp.sum(jnp.where(inside, mixed, 0.0), axis=0, keepdims=True)
    mass = jnp.sum(jnp.where(inside, layer_mass, 0.0), axis=0, keepdims=True)
    mean = total / jnp.where(mass > 0.0, mass, 1.0)
    return mixed + jnp.where(inside, frac * (layer_mass * mean - mixed), 0.0)


def prep_kernel(lon_count, count_ref, dest_ref, col_ref, depart_ref, obs_ref, out_ref):
    n = obs_ref.shape[0]
    rows = GROUP * SLOTS
    lane = iota((1, n), 1)
    live = lane < count_ref[0]
    dest = jnp.where(live, dest_ref[...], -1)
    cell = col_ref[...]
    cell_row = (cell // 256).astype(F32)
    cell_col = (cell % 256).astype(F32)
    contribution = (obs_ref[...].astype(F32) * as_column(depart_ref[...])).astype(BF16)
    local = iota((GROUP, n), 0)
    own_id = pl.program_id(0) * GROUP + local
    lon_id = own_id % lon_count
    east_id = jnp.where(lon_id == lon_count - 1, own_id - lon_id, own_id + 1)
    slots, places, left = [], [], []
    for ident, offset in ((own_id, 0), (east_id, CAP)):
        hit = dest == ident
        before = jnp.sum((live & (dest < ident)).astype(I32), axis=1, keepdims=True)
        place = lane - before
        slot = jnp.where(hit, local * SLOTS + offset + place + 1, 0)
        slots.append(jnp.sum(slot, axis=0, keepdims=True) - 1)
        places.append(jnp.sum(jnp.where(hit, place, 0), axis=0, keepdims=True))
        left.append(jnp.where(hit, cell_row, 0.0).astype(BF16))
        left.append(jnp.where(hit, cell_col, 0.0).astype(BF16))
    out_row = iota((rows, n), 0)
    pick = ((out_row == slots[0]) | (out_row == slots[1])).astype(F32).astype(BF16)
    spot = iota((LANES, n), 0)
    right = [
        (spot == 32 * kind + places[kind // 2]).astype(F32).astype(BF16) for kind in range(4)
    ]
    cells = dot_nt(jnp.concatenate(left, axis=1), jnp.concatenate(right, axis=1))
    spread = (iota((rows, GROUP), 0) == iota((rows, GROUP), 1) * SLOTS + 2 * CAP)
    spread = spread.astype(F32).astype(BF16)
    out_ref[...] = (dot(pick, contribution) + dot(spread, cells.astype(BF16))).astype(BF16)


def prepare(devices, lon_count, obs_count, obs_dest, obs_col, obs_depart, obs_kernel):
    n, levels = obs_kernel.shape
    steps = devices // GROUP
    whole = lambda shape: pl.BlockSpec(shape, lambda g: (0, 0))
    return pl.pallas_call(
        functools.partial(prep_kernel, lon_count),
        grid=(steps,),
        in_specs=[
            pl.BlockSpec(memory_space=pltpu.SMEM),
            whole((1, n)),
            whole((1, n)),
            whole((1, n)),
            whole((n, levels)),
        ],
        out_specs=pl.BlockSpec((GROUP * SLOTS, levels), lambda g: (g, 0)),
        out_shape=jax.ShapeDtypeStruct((devices * SLOTS, levels), BF16),
        compiler_params=params(),
        name="soundings_out",
    )(obs_count, obs_dest.reshape(1, n), obs_col.reshape(1, n), obs_depart.reshape(1, n), obs_kernel)


def pack_edge(block):
    parts = [block[:, 8 * q : 8 * q + 8, :] for q in range(4)]
    low = iota(parts[0].shape, 2) < EDGE
    pairs = [
        jnp.where(low, parts[2 * h], pltpu.roll(parts[2 * h + 1], EDGE, 2)) for h in range(2)
    ]
    return jnp.concatenate(pairs, axis=2)


def edge_kernel(field_ref, top_ref, frac_ref, out_ref):
    levels = field_ref.shape[0]
    out_ref[:levels] = pack_edge(field_ref[...])
    out_ref[levels : levels + 1] = pack_edge(top_ref[...].astype(F32)[None])
    out_ref[levels + 1 :] = pack_edge(frac_ref[...][None])


def edge(adjoint_field, cloud_top, conv_frac):
    levels, row_count, _ = adjoint_field.shape
    flat = pl.BlockSpec((row_count, LANES), lambda i: (0, 0))
    return pl.pallas_call(
        edge_kernel,
        grid=(1,),
        in_specs=[pl.BlockSpec((levels, row_count, LANES), lambda i: (0, 0, 0)), flat, flat],
        out_specs=pl.BlockSpec((levels + 2, 8, 4 * EDGE), lambda i: (0, 0, 0)),
        out_shape=jax.ShapeDtypeStruct((levels + 2, 8, 4 * EDGE), F32),
        compiler_params=params(),
        name="edge_columns",
    )(adjoint_field, cloud_top, conv_frac)


def level_rows(ref, row):
    levels = ref.shape[0]
    return ref.reshape(levels * 8, LANES)[pl.ds(row, levels, stride=8), :]


def mix_kernel(west_ref, east_ref, mixing_ref, top_ref, frac_ref, mass_ref, out_ref, wide_ref):
    levels = west_ref.shape[0]
    layer_mass = jnp.broadcast_to(mass_ref[...], (levels, 2 * LANES))
    for row in range(8):
        value = jnp.concatenate([level_rows(west_ref, row), level_rows(east_ref, row)], axis=1)
        high, low = halves(value)
        mix_high, mix_low = halves(mixing_ref[row])
        wide_ref[:levels, row * levels : (row + 1) * levels] = mix_high
        wide_ref[levels:, row * levels : (row + 1) * levels] = mix_low
        mixed = dot(
            jnp.concatenate([mix_high, mix_high, mix_low], axis=1),
            jnp.concatenate([high, low, high], axis=0),
        )
        out_ref[row] = convect(
            mixed, top_ref[row : row + 1, :], frac_ref[row : row + 1, :], layer_mass
        )


def mix(adjoint_field, mixing_inverse, cloud_top, conv_frac, layer_mass):
    levels, row_count, col_count = adjoint_field.shape
    blocks = row_count // 8
    half = lambda h: pl.BlockSpec((levels, 8, LANES), lambda b, h=h: (0, b, h))
    flat = pl.BlockSpec((8, col_count), lambda b: (b, 0))
    return pl.pallas_call(
        mix_kernel,
        grid=(blocks,),
        in_specs=[
            half(0),
            half(1),
            pl.BlockSpec((8, levels, levels), lambda b: (b, 0, 0)),
            flat,
            flat,
            pl.BlockSpec((levels, 1), lambda b: (0, 0)),
        ],
        out_specs=[
            pl.BlockSpec((8, levels, col_count), lambda b: (b, 0, 0)),
            pl.BlockSpec((2 * levels, 8 * levels), lambda b: (0, b)),
        ],
        out_shape=[
            jax.ShapeDtypeStruct((row_count, levels, col_count), F32),
            jax.ShapeDtypeStruct((2 * levels, row_count * levels), BF16),
        ],
        compiler_params=params(),
        cost_estimate=pl.CostEstimate(
            flops=2 * levels * levels * 3 * row_count * col_count,
            bytes_accessed=12 * levels * row_count * col_count,
            transcendentals=0,
        ),
        name="mix_own",
    )(adjoint_field, adjoint_field, mixing_inverse, cloud_top, conv_frac, layer_mass)


def mix_edge_kernel(edge_ref, edge_far_ref, lines_ref, wide_ref, mass_ref, out_ref):
    levels = mass_ref.shape[0]
    width = 2 * LANES
    layer_mass = jnp.broadcast_to(mass_ref[...], (levels, width))
    group = iota((levels, width), 1) // EDGE
    for row in range(8):
        value = jnp.concatenate([level_rows(edge_ref, row), level_rows(edge_far_ref, row)], axis=1)
        left, right = [], []
        for q in range(4):
            cols = slice((8 * q + row) * levels, (8 * q + row + 1) * levels)
            mix_high, mix_low = wide_ref[:levels, cols], wide_ref[levels:, cols]
            high, low = halves(jnp.where(group == q, value, 0.0))
            left += [mix_high, mix_high, mix_low]
            right += [high, low, high]
        mixed = dot(jnp.concatenate(left, axis=1), jnp.concatenate(right, axis=0))
        top = lines_ref[0, row : row + 1, :].astype(I32)
        out_ref[row] = convect(mixed, top, lines_ref[1, row : row + 1, :], layer_mass)


def mix_edge(edge_in, wide, layer_mass):
    levels = layer_mass.shape[0]
    half = lambda h: pl.BlockSpec((levels, 8, LANES), lambda i, h=h: (0, 0, h))
    return pl.pallas_call(
        mix_edge_kernel,
        grid=(1,),
        in_specs=[
            half(0),
            half(1),
            pl.BlockSpec((2, 8, 2 * LANES), lambda i: (levels // 2, 0, 0)),
            pl.BlockSpec(wide.shape, lambda i: (0, 0)),
            pl.BlockSpec((levels, 1), lambda i: (0, 0)),
        ],
        out_specs=pl.BlockSpec((8, levels, 2 * LANES), lambda i: (0, 0, 0)),
        out_shape=jax.ShapeDtypeStruct((8, levels, 2 * LANES), F32),
        compiler_params=params(),
        name="mix_edge",
    )(edge_in, edge_in, edge_in, wide, layer_mass)


def sounding_phase(
    got_ref, wide_ref, top_ref, frac_ref, lines_ref, mass_ref, edge_ref,
    columns, rows_scr, tops, fracs, stack, high_scr, low_scr, own_hot, edge_hot, edge_scr,
):
    devices = got_ref.shape[0]
    levels = mass_ref.shape[0]
    n = devices * CAP
    row_count = top_ref.shape[0]
    width = 2 * LANES
    got = got_ref[...].astype(F32)
    columns[:, :n] = got[:, :CAP].reshape(n, levels).T.astype(BF16)
    columns[:, n:] = got[:, CAP : 2 * CAP].reshape(n, levels).T.astype(BF16)
    info = got[:, 2 * CAP :].reshape(devices * 8, LANES).astype(BF16)
    first = (iota((devices, devices * 8), 1) == 8 * iota((devices, devices * 8), 0))
    info = dot(first.astype(F32).astype(BF16), info).astype(BF16)
    lines = []
    for kind in range(4):
        chosen = iota((LANES, n), 0) == iota((LANES, n), 1) % CAP + 32 * kind
        spread = dot(info, chosen.astype(F32).astype(BF16))
        mine = iota((devices, n), 0) == iota((devices, n), 1) // CAP
        lines.append(jnp.sum(jnp.where(mine, spread, 0.0), axis=0, keepdims=True))
    own_row, own_col, east_row, east_col = [line.astype(I32) for line in lines]
    near = east_col < EDGE
    packed_col = jnp.where(near, (east_row // 8) * EDGE + east_col, -1)
    packed_row = east_row % 8
    rows_scr[0:1, :n] = own_row
    rows_scr[0:1, n:] = east_row
    rows_scr[1:2, :n] = packed_row

    parts = [
        (own_col, own_row, top_ref[...].astype(F32), frac_ref[...], own_hot, row_count, 0),
        (packed_col, packed_row, lines_ref[0], lines_ref[1], edge_hot, 8, n),
    ]
    for col, row, top, frac, hot_ref, count, start in parts:
        hot_t = (iota((width, n), 0) == col).astype(F32).astype(BF16)
        table = jnp.concatenate([top.astype(BF16)] + thirds(frac), axis=0)
        found = dot(table, hot_t)
        here = iota((count, n), 0) == row
        found = [
            jnp.sum(jnp.where(here, found[i * count : (i + 1) * count], 0.0), axis=0, keepdims=True)
            for i in range(4)
        ]
        tops[0:1, start : start + n] = found[0].astype(I32)
        fracs[0:1, start : start + n] = (found[1] + found[2]) + found[3]
        col_t = as_column(col.astype(F32)).astype(I32)
        lane = iota((n, LANES), 1)
        for h in range(2):
            hot = (col_t == lane + h * LANES).astype(F32).astype(BF16)
            hot_ref[:n, h * LANES : (h + 1) * LANES] = hot
            hot_ref[n:, h * LANES : (h + 1) * LANES] = hot

    layer_mass = jnp.broadcast_to(mass_ref[...], (levels, CHUNK))

    def mix_chunk(index, carry):
        here = pl.ds(pl.multiple_of(index * CHUNK, CHUNK), CHUNK)
        value = columns[:, here]
        row = rows_scr[0:1, here]
        for r in range(row_count):
            stack[r * levels : (r + 1) * levels, :] = value * (row == r).astype(F32).astype(BF16)
        both = dot(wide_ref[...], stack[...])
        mixed = both[:levels] + both[levels:]
        high, low = halves(convect(mixed, tops[0:1, here], fracs[0:1, here], layer_mass))
        high_scr[:, here] = high
        low_scr[:, here] = low
        return carry

    lax.fori_loop(0, 2 * n // CHUNK, mix_chunk, 0)

    row = rows_scr[1:2, :n]
    for r in range(8):
        chosen = (row == r).astype(F32).astype(BF16)
        left = jnp.concatenate([high_scr[:, n:] * chosen, low_scr[:, n:] * chosen], axis=1)
        value = edge_ref[r] + dot(left, edge_hot[...])
        for h in range(2):
            part = value[:, h * LANES : (h + 1) * LANES]
            edge_scr[16 * h + r] = part
            edge_scr[16 * h + 8 + r] = pltpu.roll(part, EDGE, 1)


def shifted(tiles, shift, weight):
    lane = iota(tiles[0].shape, 1)
    sums = []
    for extra in range(2):
        place = lane + (shift + extra)
        inside = place < LANES
        place = place & (LANES - 1)
        moved = [jnp.take_along_axis(t, place, axis=1, mode="promise_in_bounds") for t in tiles]
        sums.append([jnp.where(inside, moved[h], moved[h + 1]) for h in range(2)])
    return [(1.0 - weight) * sums[0][h] + weight * sums[1][h] for h in range(2)]


def advect_kernel(
    got_ref, wide_ref, top_ref, frac_ref, lines_ref, mass_ref, edge_ref,
    field_ref, west_ref, east_ref, shift_ref, weight_ref,
    out_ref, first_ref,
    columns, rows_scr, tops, fracs, stack, high_scr, low_scr, own_hot, edge_hot, edge_scr,
    out_scr, prev, sem,
):
    step = pl.program_id(0)
    blocks = pl.num_programs(0)
    block = blocks - 1 - step
    levels = mass_ref.shape[0]
    n = got_ref.shape[0] * CAP

    @pl.when(step == 0)
    def _():
        sounding_phase(
            got_ref, wide_ref, top_ref, frac_ref, lines_ref, mass_ref, edge_ref,
            columns, rows_scr, tops, fracs, stack, high_scr, low_scr, own_hot, edge_hot, edge_scr,
        )
        prev[...] = jnp.zeros_like(prev)

    later = [prev[0], prev[1]]
    cell_row = rows_scr[0:1, :n]
    for r in reversed(range(8)):
        row = 8 * block + r
        chosen = (cell_row == row).astype(F32).astype(BF16)
        left = jnp.concatenate([high_scr[:, :n] * chosen, low_scr[:, :n] * chosen], axis=1)
        value = field_ref[r] + dot(left, own_hot[...])
        tiles = [value[:, :LANES], value[:, LANES:], edge_scr[row]]
        zonal = shifted(tiles, shift_ref[0, :, r : r + 1], weight_ref[0, :, r : r + 1])
        for h, courant_ref in enumerate((west_ref, east_ref)):
            courant = level_rows(courant_ref, r)
            place = out_scr.at[block, h].reshape(levels * 8, LANES)
            place[pl.ds(r, levels, stride=8), :] = (1.0 - courant) * zonal[h] + later[h]
            later[h] = courant * zonal[h]
    prev[0] = later[0]
    prev[1] = later[1]
    first_ref[:, :LANES] = later[0]
    first_ref[:, LANES:] = later[1]

    def copies(b):
        return [
            pltpu.make_async_copy(
                out_scr.at[b, h],
                out_ref.at[:, pl.ds(b * 8, 8), pl.ds(h * LANES, LANES)],
                sem.at[b, h],
            )
            for h in range(2)
        ]

    for b in range(4):

        @pl.when(block == b)
        def _():
            for copy in copies(b):
                copy.start()

    @pl.when(step == blocks - 1)
    def _():
        for b in range(4):
            for copy in copies(b):
                copy.wait()


def advect(got, wide, cloud_top, conv_frac, edge_in, layer_mass, edge_field, field, courant, shift, weight):
    row_count, levels, col_count = field.shape
    blocks = row_count // 8
    n = got.shape[0] * CAP
    width = 2 * LANES
    full = lambda array: pl.BlockSpec(array.shape, lambda s: (0,) * array.ndim)
    half = lambda h: pl.BlockSpec((levels, 8, LANES), lambda s, h=h: (0, blocks - 1 - s, h))
    per_block = lambda array: pl.BlockSpec((1,) + array.shape[1:], lambda s: (blocks - 1 - s, 0, 0))
    return pl.pallas_call(
        advect_kernel,
        grid=(blocks,),
        in_specs=[
            full(got),
            full(wide),
            full(cloud_top),
            full(conv_frac),
            pl.BlockSpec((2, 8, width), lambda s: (levels // 2, 0, 0)),
            full(layer_mass),
            full(edge_field),
            pl.BlockSpec((8, levels, col_count), lambda s: (blocks - 1 - s, 0, 0)),
            half(0),
            half(1),
            per_block(shift),
            per_block(weight),
        ],
        out_specs=[
            pl.BlockSpec(memory_space=pl.ANY),
            pl.BlockSpec((levels, col_count), lambda s: (0, 0)),
        ],
        out_shape=[
            jax.ShapeDtypeStruct((levels, row_count, col_count), F32),
            jax.ShapeDtypeStruct((levels, col_count), F32),
        ],
        scratch_shapes=[
            pltpu.VMEM((levels, 2 * n), BF16),
            pltpu.VMEM((8, 2 * n), I32),
            pltpu.VMEM((8, 2 * n), I32),
            pltpu.VMEM((8, 2 * n), F32),
            pltpu.VMEM((row_count * levels, CHUNK), BF16),
            pltpu.VMEM((levels, 2 * n), BF16),
            pltpu.VMEM((levels, 2 * n), BF16),
            pltpu.VMEM((2 * n, width), BF16),
            pltpu.VMEM((2 * n, width), BF16),
            pltpu.VMEM((row_count, levels, LANES), F32),
            pltpu.VMEM((blocks, 2, levels, 8, LANES), F32),
            pltpu.VMEM((2, levels, LANES), F32),
            pltpu.SemaphoreType.DMA((blocks, 2)),
        ],
        compiler_params=params(),
        name="advect",
    )(got, wide, cloud_top, conv_frac, edge_in, layer_mass, edge_field, field, courant, courant, shift, weight)


def close_kernel(out_ref, north_ref, result_ref):
    levels = out_ref.shape[0]
    result_ref[...] = out_ref[...]
    result_ref.reshape(levels * 8, LANES)[pl.ds(7, levels, stride=8), :] = (
        level_rows(out_ref, 7) + north_ref[...]
    )


def close(out, north):
    levels, row_count, col_count = out.shape
    spec = pl.BlockSpec((levels, 8, LANES), lambda h: (0, row_count // 8 - 1, h))
    return pl.pallas_call(
        close_kernel,
        grid=(col_count // LANES,),
        in_specs=[spec, pl.BlockSpec((levels, LANES), lambda h: (0, h))],
        out_specs=spec,
        out_shape=jax.ShapeDtypeStruct(out.shape, F32),
        input_output_aliases={0: 0},
        compiler_params=params(),
        name="close_last_row",
    )(out, north)


def shards(
    adjoint_field,
    mixing_inverse,
    cloud_top,
    conv_frac,
    thickness,
    zonal_shift,
    zonal_frac,
    merid_courant,
    obs_kernel,
    obs_depart,
    obs_dest,
    obs_col,
    obs_count,
):
    levels, row_count, col_count = adjoint_field.shape
    lat_count, lon_count = lax.axis_size("lat"), lax.axis_size("lon")
    devices = lat_count * lon_count
    sent = prepare(devices, lon_count, obs_count, obs_dest, obs_col, obs_depart, obs_kernel)
    got = lax.all_to_all(
        sent.reshape(devices, SLOTS, levels), ("lat", "lon"), split_axis=0, concat_axis=0, tiled=True
    )
    westward = [((i + 1) % lon_count, i) for i in range(lon_count)]
    edge_in = lax.ppermute(edge(adjoint_field, cloud_top, conv_frac), "lon", westward)
    layer_mass = thickness.reshape(levels, 1)
    field, wide = mix(adjoint_field, mixing_inverse, cloud_top, conv_frac, layer_mass)
    edge_field = mix_edge(edge_in, wide, layer_mass)
    by_block = lambda array: array.reshape(levels, row_count // 8, 8).transpose(1, 0, 2)
    out, first = advect(
        got, wide, cloud_top, conv_frac, edge_in, layer_mass, edge_field, field, merid_courant,
        by_block(zonal_shift), by_block(zonal_frac),
    )
    southward = [(i + 1, i) for i in range(lat_count - 1)]
    return close(out, lax.ppermute(first, "lat", southward))


def solution(mesh):
    in_specs = (
        P(None, "lat", "lon"),
        P("lat", None, None),
        P("lat", "lon"),
        P("lat", "lon"),
        P(),
        P(None, "lat"),
        P(None, "lat"),
        P(None, "lat", "lon"),
        P(("lat", "lon"), None),
        P(("lat", "lon")),
        P(("lat", "lon")),
        P(("lat", "lon")),
        P(("lat", "lon")),
    )
    out_specs = P(None, "lat", "lon")
    return jax.shard_map(shards, mesh=mesh, in_specs=in_specs, out_specs=out_specs, check_vma=False)
```

```python
import functools

import jax
import jax.numpy as jnp
from jax import lax
from jax.experimental import pallas as pl
from jax.experimental.pallas import tpu as pltpu
from jax.sharding import PartitionSpec as P

F32, BF16, I32 = jnp.float32, jnp.bfloat16, jnp.int32
CAP = 16
SLOTS = 40
EDGE = 64
LANES = 128
GROUP = 32
CHUNK = 256
MIB = 1024 * 1024


def iota(shape, dim):
    return lax.broadcasted_iota(I32, shape, dim)


def params(mib):
    return pltpu.CompilerParams(vmem_limit_bytes=mib * MIB)


def dot(left, right):
    return jnp.dot(left, right, preferred_element_type=F32)


def dot_nt(left, right):
    return lax.dot_general(left, right, (((1,), (1,)), ((), ())), preferred_element_type=F32)


def halves(value):
    high = value.astype(BF16)
    return high, (value - high.astype(F32)).astype(BF16)


def thirds(value):
    high = value.astype(BF16)
    rest = value - high.astype(F32)
    mid = rest.astype(BF16)
    return [high, mid, (rest - mid.astype(F32)).astype(BF16)]


def as_column(line):
    return jnp.broadcast_to(line, (LANES, line.shape[1])).T


def as_wide_column(line):
    column = as_column(line)
    return jnp.concatenate([column, column], axis=1)


def convect(mixed, top, frac, layer_mass):
    inside = iota(mixed.shape, 0) < top
    total = jnp.sum(jnp.where(inside, mixed, 0.0), axis=0, keepdims=True)
    mass = jnp.sum(jnp.where(inside, layer_mass, 0.0), axis=0, keepdims=True)
    mean = total / jnp.where(mass > 0.0, mass, 1.0)
    return mixed + jnp.where(inside, frac * (layer_mass * mean - mixed), 0.0)


def prep_kernel(lon_count, count_ref, dest_ref, col_ref, depart_ref, obs_ref, out_ref):
    n = obs_ref.shape[0]
    rows = GROUP * SLOTS
    lane = iota((1, n), 1)
    live = lane < count_ref[0]
    dest = jnp.where(live, dest_ref[...], -1)
    cell = col_ref[...]
    cell_row = (cell // 256).astype(F32)
    cell_col = (cell % 256).astype(F32)
    contribution = (obs_ref[...].astype(F32) * as_column(depart_ref[...])).astype(BF16)
    local = iota((GROUP, n), 0)
    own_id = pl.program_id(0) * GROUP + local
    lon_id = own_id % lon_count
    east_id = jnp.where(lon_id == lon_count - 1, own_id - lon_id, own_id + 1)
    slots, places, left = [], [], []
    for ident, offset in ((own_id, 0), (east_id, CAP)):
        hit = dest == ident
        before = jnp.sum((live & (dest < ident)).astype(I32), axis=1, keepdims=True)
        place = lane - before
        slot = jnp.where(hit, local * SLOTS + offset + place + 1, 0)
        slots.append(jnp.sum(slot, axis=0, keepdims=True) - 1)
        places.append(jnp.sum(jnp.where(hit, place, 0), axis=0, keepdims=True))
        left.append(jnp.where(hit, cell_row, 0.0).astype(BF16))
        left.append(jnp.where(hit, cell_col, 0.0).astype(BF16))
    out_row = iota((rows, n), 0)
    pick = ((out_row == slots[0]) | (out_row == slots[1])).astype(F32).astype(BF16)
    spot = iota((LANES, n), 0)
    right = [
        (spot == 32 * kind + places[kind // 2]).astype(F32).astype(BF16) for kind in range(4)
    ]
    cells = dot_nt(jnp.concatenate(left, axis=1), jnp.concatenate(right, axis=1))
    spread = (iota((rows, GROUP), 0) == iota((rows, GROUP), 1) * SLOTS + 2 * CAP)
    spread = spread.astype(F32).astype(BF16)
    out_ref[...] = (dot(pick, contribution) + dot(spread, cells.astype(BF16))).astype(BF16)


def prepare(devices, lon_count, obs_count, obs_dest, obs_col, obs_depart, obs_kernel):
    n, levels = obs_kernel.shape
    steps = devices // GROUP
    whole = lambda shape: pl.BlockSpec(shape, lambda g: (0, 0))
    return pl.pallas_call(
        functools.partial(prep_kernel, lon_count),
        grid=(steps,),
        in_specs=[
            pl.BlockSpec(memory_space=pltpu.SMEM),
            whole((1, n)),
            whole((1, n)),
            whole((1, n)),
            whole((n, levels)),
        ],
        out_specs=pl.BlockSpec((GROUP * SLOTS, levels), lambda g: (g, 0)),
        out_shape=jax.ShapeDtypeStruct((devices * SLOTS, levels), BF16),
        compiler_params=params(16 + devices // 4),
        name="soundings_out",
    )(obs_count, obs_dest.reshape(1, n), obs_col.reshape(1, n), obs_depart.reshape(1, n), obs_kernel)


def pack_edge(block):
    parts = [block[:, 8 * q : 8 * q + 8, :] for q in range(4)]
    low = iota(parts[0].shape, 2) < EDGE
    pairs = [
        jnp.where(low, parts[2 * h], pltpu.roll(parts[2 * h + 1], EDGE, 2)) for h in range(2)
    ]
    return jnp.concatenate(pairs, axis=2)


def edge_kernel(field_ref, top_ref, frac_ref, out_ref):
    last = pl.num_programs(0) - 1

    @pl.when(pl.program_id(0) < last)
    def _():
        out_ref[...] = pack_edge(field_ref[...])

    @pl.when(pl.program_id(0) == last)
    def _():
        out_ref[0:1] = pack_edge(top_ref[...].astype(F32)[None])
        out_ref[1:2] = pack_edge(frac_ref[...][None])


def edge(adjoint_field, cloud_top, conv_frac):
    levels, row_count, _ = adjoint_field.shape
    steps = 8
    flat = pl.BlockSpec((row_count, LANES), lambda i: (0, 0))
    return pl.pallas_call(
        edge_kernel,
        grid=(steps + 1,),
        in_specs=[
            pl.BlockSpec((levels // steps, row_count, LANES), lambda i: (jnp.minimum(i, steps - 1), 0, 0)),
            flat,
            flat,
        ],
        out_specs=pl.BlockSpec((levels // steps, 8, 4 * EDGE), lambda i: (i, 0, 0)),
        out_shape=jax.ShapeDtypeStruct((levels + 2, 8, 4 * EDGE), F32),
        compiler_params=params(16),
        name="edge_columns",
    )(adjoint_field, cloud_top, conv_frac)


def level_rows(ref, row):
    levels = ref.shape[0]
    return ref.reshape(levels * 8, LANES)[pl.ds(row, levels, stride=8), :]


def mix_kernel(west_ref, east_ref, mixing_ref, top_ref, frac_ref, mass_ref, out_ref, wide_ref):
    levels = west_ref.shape[0]
    layer_mass = as_wide_column(mass_ref[...])
    for row in range(8):
        value = jnp.concatenate([level_rows(west_ref, row), level_rows(east_ref, row)], axis=1)
        high, low = halves(value)
        mix_high, mix_low = halves(mixing_ref[row])
        wide_ref[:levels, row * levels : (row + 1) * levels] = mix_high
        wide_ref[levels:, row * levels : (row + 1) * levels] = mix_low
        four = jnp.concatenate([mix_high, mix_low], axis=0)
        both = dot(jnp.concatenate([four, four], axis=1), jnp.concatenate([high, low], axis=0))
        mixed = both[:levels] + both[levels:]
        out_ref[row] = convect(
            mixed, top_ref[row : row + 1, :], frac_ref[row : row + 1, :], layer_mass
        )


def mix(adjoint_field, mixing_inverse, cloud_top, conv_frac, layer_mass):
    levels, row_count, col_count = adjoint_field.shape
    blocks = row_count // 8
    half = lambda h: pl.BlockSpec((levels, 8, LANES), lambda b, h=h: (0, b, h))
    flat = pl.BlockSpec((8, col_count), lambda b: (b, 0))
    return pl.pallas_call(
        mix_kernel,
        grid=(blocks,),
        in_specs=[
            half(0),
            half(1),
            pl.BlockSpec((8, levels, levels), lambda b: (b, 0, 0)),
            flat,
            flat,
            pl.BlockSpec((1, levels), lambda b: (0, 0)),
        ],
        out_specs=[
            pl.BlockSpec((8, levels, col_count), lambda b: (b, 0, 0)),
            pl.BlockSpec((2 * levels, 8 * levels), lambda b: (0, b)),
        ],
        out_shape=[
            jax.ShapeDtypeStruct((row_count, levels, col_count), F32),
            jax.ShapeDtypeStruct((2 * levels, row_count * levels), BF16),
        ],
        compiler_params=params(20),
        cost_estimate=pl.CostEstimate(
            flops=2 * levels * levels * 3 * row_count * col_count,
            bytes_accessed=12 * levels * row_count * col_count,
            transcendentals=0,
        ),
        name="mix_own",
    )(adjoint_field, adjoint_field, mixing_inverse, cloud_top, conv_frac, layer_mass)


def mix_edge_kernel(edge_ref, edge_far_ref, lines_ref, wide_ref, mass_ref, out_ref):
    levels = mass_ref.shape[1]
    width = 2 * LANES
    layer_mass = as_wide_column(mass_ref[...])
    group = iota((levels, width), 1) // EDGE
    for row in range(8):
        value = jnp.concatenate([level_rows(edge_ref, row), level_rows(edge_far_ref, row)], axis=1)
        left, right = [], []
        for q in range(4):
            cols = slice((8 * q + row) * levels, (8 * q + row + 1) * levels)
            high, low = halves(jnp.where(group == q, value, 0.0))
            left += [wide_ref[:, cols], wide_ref[:, cols]]
            right += [high, low]
        both = dot(jnp.concatenate(left, axis=1), jnp.concatenate(right, axis=0))
        mixed = both[:levels] + both[levels:]
        top = lines_ref[0, row : row + 1, :].astype(I32)
        out_ref[row] = convect(mixed, top, lines_ref[1, row : row + 1, :], layer_mass)


def mix_edge(edge_in, wide, layer_mass):
    levels = layer_mass.shape[1]
    half = lambda h: pl.BlockSpec((levels, 8, LANES), lambda i, h=h: (0, 0, h))
    return pl.pallas_call(
        mix_edge_kernel,
        grid=(1,),
        in_specs=[
            half(0),
            half(1),
            pl.BlockSpec((2, 8, 2 * LANES), lambda i: (levels // 2, 0, 0)),
            pl.BlockSpec(wide.shape, lambda i: (0, 0)),
            pl.BlockSpec((1, levels), lambda i: (0, 0)),
        ],
        out_specs=pl.BlockSpec((8, levels, 2 * LANES), lambda i: (0, 0, 0)),
        out_shape=jax.ShapeDtypeStruct((8, levels, 2 * LANES), F32),
        compiler_params=params(20),
        name="mix_edge",
    )(edge_in, edge_in, edge_in, wide, layer_mass)


def sounding_phase(
    got_ref, wide_ref, top_ref, frac_ref, lines_ref, mass_ref, edge_ref,
    columns, rows_scr, tops, fracs, stack, high_scr, low_scr, own_hot, edge_hot, edge_scr, wide_stack, forced,
):
    devices = got_ref.shape[0]
    levels = mass_ref.shape[1]
    n = devices * CAP
    row_count = top_ref.shape[0]
    width = 2 * LANES
    got = got_ref[...].astype(F32)
    columns[:, :n] = got[:, :CAP].reshape(n, levels).T.astype(BF16)
    columns[:, n:] = got[:, CAP : 2 * CAP].reshape(n, levels).T.astype(BF16)
    info = got[:, 2 * CAP :].reshape(devices * 8, LANES).astype(BF16)
    first = (iota((devices, devices * 8), 1) == 8 * iota((devices, devices * 8), 0))
    info = dot(first.astype(F32).astype(BF16), info).astype(BF16)
    lines = []
    for kind in range(4):
        chosen = iota((LANES, n), 0) == iota((LANES, n), 1) % CAP + 32 * kind
        spread = dot(info, chosen.astype(F32).astype(BF16))
        mine = iota((devices, n), 0) == iota((devices, n), 1) // CAP
        lines.append(jnp.sum(jnp.where(mine, spread, 0.0), axis=0, keepdims=True))
    own_row, own_col, east_row, east_col = [line.astype(I32) for line in lines]
    near = east_col < EDGE
    packed_col = jnp.where(near, (east_row // 8) * EDGE + east_col, -1)
    packed_row = east_row % 8
    rows_scr[0:1, :n] = own_row
    rows_scr[0:1, n:] = east_row
    rows_scr[1:2, :n] = packed_row

    parts = [
        (own_col, own_row, top_ref[...].astype(F32), frac_ref[...], own_hot, row_count, 0),
        (packed_col, packed_row, lines_ref[0], lines_ref[1], edge_hot, 8, n),
    ]
    for col, row, top, frac, hot_ref, count, start in parts:
        hot_t = (iota((width, n), 0) == col).astype(F32).astype(BF16)
        table = jnp.concatenate([top.astype(BF16)] + thirds(frac), axis=0)
        found = dot(table, hot_t)
        here = iota((count, n), 0) == row
        found = [
            jnp.sum(jnp.where(here, found[i * count : (i + 1) * count], 0.0), axis=0, keepdims=True)
            for i in range(4)
        ]
        tops[0:1, start : start + n] = found[0].astype(I32)
        fracs[0:1, start : start + n] = (found[1] + found[2]) + found[3]
        col_t = as_column(col.astype(F32)).astype(I32)
        lane = iota((n, LANES), 1)
        for h in range(2):
            hot = (col_t == lane + h * LANES).astype(F32).astype(BF16)
            hot_ref[:n, h * LANES : (h + 1) * LANES] = hot
            hot_ref[n:, h * LANES : (h + 1) * LANES] = hot

    layer_mass = as_wide_column(mass_ref[...])

    def mix_chunk(index, carry):
        here = pl.ds(pl.multiple_of(index * CHUNK, CHUNK), CHUNK)
        value = columns[:, here]
        row = rows_scr[0:1, here]
        for r in range(row_count):
            stack[r * levels : (r + 1) * levels, :] = value * (row == r).astype(F32).astype(BF16)
        both = dot(wide_ref[...], stack[...])
        mixed = both[:levels] + both[levels:]
        high, low = halves(convect(mixed, tops[0:1, here], fracs[0:1, here], layer_mass))
        high_scr[:, here] = high
        low_scr[:, here] = low
        return carry

    lax.fori_loop(0, 2 * n // CHUNK, mix_chunk, 0)

    row = rows_scr[1:2, :n]
    for r in range(8):
        chosen = (row == r).astype(F32).astype(BF16)
        here = slice(r * levels, (r + 1) * levels)
        wide_stack[here, :n] = high_scr[:, n:] * chosen
        wide_stack[here, n:] = low_scr[:, n:] * chosen
    forced[...] = dot(wide_stack[...], edge_hot[...])
    for r in range(8):
        value = edge_ref[r] + forced[r * levels : (r + 1) * levels, :]
        for h in range(2):
            part = value[:, h * LANES : (h + 1) * LANES]
            edge_scr[16 * h + r] = part
            edge_scr[16 * h + 8 + r] = pltpu.roll(part, EDGE, 1)


def columns_of(lines):
    return jnp.concatenate([lines] * (LANES // 8), axis=0).T


def shifted(tiles, shift, weight):
    lane = iota(tiles[0].shape, 1)
    sums = []
    for extra in range(2):
        place = lane + (shift + extra)
        inside = place < LANES
        place = place & (LANES - 1)
        moved = [jnp.take_along_axis(t, place, axis=1, mode="promise_in_bounds") for t in tiles]
        sums.append([jnp.where(inside, moved[h], moved[h + 1]) for h in range(2)])
    return [(1.0 - weight) * sums[0][h] + weight * sums[1][h] for h in range(2)]


def advect_kernel(
    got_ref, wide_ref, top_ref, frac_ref, lines_ref, mass_ref, edge_ref,
    field_ref, west_ref, east_ref, shift_ref, weight_ref,
    out_ref, first_ref,
    columns, rows_scr, tops, fracs, stack, high_scr, low_scr, own_hot, edge_hot, edge_scr, wide_stack, forced,
    out_scr, prev, sem,
):
    step = pl.program_id(0)
    blocks = pl.num_programs(0)
    block = blocks - 1 - step
    levels = mass_ref.shape[1]
    n = got_ref.shape[0] * CAP

    @pl.when(step == 0)
    def _():
        sounding_phase(
            got_ref, wide_ref, top_ref, frac_ref, lines_ref, mass_ref, edge_ref,
            columns, rows_scr, tops, fracs, stack, high_scr, low_scr, own_hot, edge_hot, edge_scr, wide_stack, forced,
        )
        prev[...] = jnp.zeros_like(prev)

    later = [prev[0], prev[1]]
    cell_row = rows_scr[0:1, :n]
    for r in range(8):
        chosen = (cell_row == 8 * block + r).astype(F32).astype(BF16)
        here = slice(r * levels, (r + 1) * levels)
        wide_stack[here, :n] = high_scr[:, :n] * chosen
        wide_stack[here, n:] = low_scr[:, :n] * chosen
    forced[...] = dot(wide_stack[...], own_hot[...])
    shifts = columns_of(shift_ref[...].astype(F32)).astype(I32)
    weights = columns_of(weight_ref[...])
    for r in reversed(range(8)):
        row = 8 * block + r
        value = field_ref[r] + forced[r * levels : (r + 1) * levels, :]
        tiles = [value[:, :LANES], value[:, LANES:], edge_scr[row]]
        zonal = shifted(tiles, shifts[:, r : r + 1], weights[:, r : r + 1])
        for h, courant_ref in enumerate((west_ref, east_ref)):
            courant = level_rows(courant_ref, r)
            place = out_scr.at[block, h].reshape(levels * 8, LANES)
            place[pl.ds(r, levels, stride=8), :] = (1.0 - courant) * zonal[h] + later[h]
            later[h] = courant * zonal[h]
    prev[0] = later[0]
    prev[1] = later[1]
    first_ref[:, :LANES] = later[0]
    first_ref[:, LANES:] = later[1]

    def copies(b):
        return [
            pltpu.make_async_copy(
                out_scr.at[b, h],
                out_ref.at[:, pl.ds(b * 8, 8), pl.ds(h * LANES, LANES)],
                sem.at[b, h],
            )
            for h in range(2)
        ]

    for b in range(4):

        @pl.when(block == b)
        def _():
            for copy in copies(b):
                copy.start()

    @pl.when(step == blocks - 1)
    def _():
        for b in range(4):
            for copy in copies(b):
                copy.wait()


def advect(got, wide, cloud_top, conv_frac, edge_in, layer_mass, edge_field, field, courant, shift, weight):
    row_count, levels, col_count = field.shape
    blocks = row_count // 8
    n = got.shape[0] * CAP
    width = 2 * LANES
    full = lambda array: pl.BlockSpec(array.shape, lambda s: (0,) * array.ndim)
    half = lambda h: pl.BlockSpec((levels, 8, LANES), lambda s, h=h: (0, blocks - 1 - s, h))
    lines = pl.BlockSpec((8, levels), lambda s: (blocks - 1 - s, 0))
    return pl.pallas_call(
        advect_kernel,
        grid=(blocks,),
        in_specs=[
            full(got),
            full(wide),
            full(cloud_top),
            full(conv_frac),
            pl.BlockSpec((2, 8, width), lambda s: (levels // 2, 0, 0)),
            full(layer_mass),
            full(edge_field),
            pl.BlockSpec((8, levels, col_count), lambda s: (blocks - 1 - s, 0, 0)),
            half(0),
            half(1),
            lines,
            lines,
        ],
        out_specs=[
            pl.BlockSpec(memory_space=pl.ANY),
            pl.BlockSpec((levels, col_count), lambda s: (0, 0)),
        ],
        out_shape=[
            jax.ShapeDtypeStruct((levels, row_count, col_count), F32),
            jax.ShapeDtypeStruct((levels, col_count), F32),
        ],
        scratch_shapes=[
            pltpu.VMEM((levels, 2 * n), BF16),
            pltpu.VMEM((8, 2 * n), I32),
            pltpu.VMEM((8, 2 * n), I32),
            pltpu.VMEM((8, 2 * n), F32),
            pltpu.VMEM((row_count * levels, CHUNK), BF16),
            pltpu.VMEM((levels, 2 * n), BF16),
            pltpu.VMEM((levels, 2 * n), BF16),
            pltpu.VMEM((2 * n, width), BF16),
            pltpu.VMEM((2 * n, width), BF16),
            pltpu.VMEM((row_count, levels, LANES), F32),
            pltpu.VMEM((8 * levels, 2 * n), BF16),
            pltpu.VMEM((8 * levels, width), F32),
            pltpu.VMEM((blocks, 2, levels, 8, LANES), F32),
            pltpu.VMEM((2, levels, LANES), F32),
            pltpu.SemaphoreType.DMA((blocks, 2)),
        ],
        compiler_params=params(20 + n // 64),
        name="advect",
    )(got, wide, cloud_top, conv_frac, edge_in, layer_mass, edge_field, field, courant, courant, shift, weight)


def close_kernel(out_ref, north_ref, result_ref):
    levels = out_ref.shape[0]
    result_ref[...] = out_ref[...]
    result_ref.reshape(levels * 8, LANES)[pl.ds(7, levels, stride=8), :] = (
        level_rows(out_ref, 7) + north_ref[...]
    )


def close(out, north):
    levels, row_count, col_count = out.shape
    spec = pl.BlockSpec((levels, 8, LANES), lambda h: (0, row_count // 8 - 1, h))
    return pl.pallas_call(
        close_kernel,
        grid=(col_count // LANES,),
        in_specs=[spec, pl.BlockSpec((levels, LANES), lambda h: (0, h))],
        out_specs=spec,
        out_shape=jax.ShapeDtypeStruct(out.shape, F32),
        input_output_aliases={0: 0},
        compiler_params=params(16),
        name="close_last_row",
    )(out, north)


def shards(
    adjoint_field,
    mixing_inverse,
    cloud_top,
    conv_frac,
    thickness,
    zonal_shift,
    zonal_frac,
    merid_courant,
    obs_kernel,
    obs_depart,
    obs_dest,
    obs_col,
    obs_count,
):
    levels, row_count, col_count = adjoint_field.shape
    lat_count, lon_count = lax.axis_size("lat"), lax.axis_size("lon")
    devices = lat_count * lon_count
    sent = prepare(devices, lon_count, obs_count, obs_dest, obs_col, obs_depart, obs_kernel)
    got = lax.all_to_all(
        sent.reshape(devices, SLOTS, levels), ("lat", "lon"), split_axis=0, concat_axis=0, tiled=True
    )
    westward = [((i + 1) % lon_count, i) for i in range(lon_count)]
    edge_in = lax.ppermute(edge(adjoint_field, cloud_top, conv_frac), "lon", westward)
    layer_mass = thickness.reshape(1, levels)
    field, wide = mix(adjoint_field, mixing_inverse, cloud_top, conv_frac, layer_mass)
    edge_field = mix_edge(edge_in, wide, layer_mass)
    out, first = advect(
        got, wide, cloud_top, conv_frac, edge_in, layer_mass, edge_field, field, merid_courant,
        zonal_shift.T, zonal_frac.T,
    )
    southward = [(i + 1, i) for i in range(lat_count - 1)]
    return close(out, lax.ppermute(first, "lat", southward))


def solution(mesh):
    in_specs = (
        P(None, "lat", "lon"),
        P("lat", None, None),
        P("lat", "lon"),
        P("lat", "lon"),
        P(),
        P(None, "lat"),
        P(None, "lat"),
        P(None, "lat", "lon"),
        P(("lat", "lon"), None),
        P(("lat", "lon")),
        P(("lat", "lon")),
        P(("lat", "lon")),
        P(("lat", "lon")),
    )
    out_specs = P(None, "lat", "lon")
    return jax.shard_map(shards, mesh=mesh, in_specs=in_specs, out_specs=out_specs, check_vma=False)
```

```python
import functools

import jax
import jax.numpy as jnp
from jax import lax
from jax.experimental import pallas as pl
from jax.experimental.pallas import tpu as pltpu
from jax.sharding import PartitionSpec as P

F32, BF16, I32 = jnp.float32, jnp.bfloat16, jnp.int32
CAP = 16
SLOTS = 40
EDGE = 64
LANES = 128
GROUP = 32
CHUNK = 256
MIB = 1024 * 1024


def iota(shape, dim):
    return lax.broadcasted_iota(I32, shape, dim)


def params(mib):
    return pltpu.CompilerParams(vmem_limit_bytes=mib * MIB)


def in_hbm(array):
    return pltpu.with_memory_space_constraint(array, pltpu.HBM)


def dot(left, right):
    return jnp.dot(left, right, preferred_element_type=F32)


def dot_nt(left, right):
    return lax.dot_general(left, right, (((1,), (1,)), ((), ())), preferred_element_type=F32)


def halves(value):
    high = value.astype(BF16)
    return high, (value - high.astype(F32)).astype(BF16)


def thirds(value):
    high = value.astype(BF16)
    rest = value - high.astype(F32)
    mid = rest.astype(BF16)
    return [high, mid, (rest - mid.astype(F32)).astype(BF16)]


def as_column(line):
    return jnp.broadcast_to(line, (LANES, line.shape[1])).T


def as_wide_column(line):
    column = as_column(line)
    return jnp.concatenate([column, column], axis=1)


def convect(mixed, top, frac, layer_mass):
    inside = iota(mixed.shape, 0) < top
    total = jnp.sum(jnp.where(inside, mixed, 0.0), axis=0, keepdims=True)
    mass = jnp.sum(jnp.where(inside, layer_mass, 0.0), axis=0, keepdims=True)
    mean = total / jnp.where(mass > 0.0, mass, 1.0)
    return mixed + jnp.where(inside, frac * (layer_mass * mean - mixed), 0.0)


def prep_kernel(lon_count, count_ref, dest_ref, col_ref, depart_ref, obs_ref, out_ref):
    n = obs_ref.shape[0]
    rows = GROUP * SLOTS
    lane = iota((1, n), 1)
    live = lane < count_ref[0]
    dest = jnp.where(live, dest_ref[...], -1)
    cell = col_ref[...]
    cell_row = (cell // 256).astype(F32)
    cell_col = (cell % 256).astype(F32)
    contribution = (obs_ref[...].astype(F32) * as_column(depart_ref[...])).astype(BF16)
    local = iota((GROUP, n), 0)
    own_id = pl.program_id(0) * GROUP + local
    lon_id = own_id % lon_count
    east_id = jnp.where(lon_id == lon_count - 1, own_id - lon_id, own_id + 1)
    slots, places, left = [], [], []
    for ident, offset in ((own_id, 0), (east_id, CAP)):
        hit = dest == ident
        before = jnp.sum((live & (dest < ident)).astype(I32), axis=1, keepdims=True)
        place = lane - before
        slot = jnp.where(hit, local * SLOTS + offset + place + 1, 0)
        slots.append(jnp.sum(slot, axis=0, keepdims=True) - 1)
        places.append(jnp.sum(jnp.where(hit, place, 0), axis=0, keepdims=True))
        left.append(jnp.where(hit, cell_row, 0.0).astype(BF16))
        left.append(jnp.where(hit, cell_col, 0.0).astype(BF16))
    out_row = iota((rows, n), 0)
    pick = ((out_row == slots[0]) | (out_row == slots[1])).astype(F32).astype(BF16)
    spot = iota((LANES, n), 0)
    right = [
        (spot == 32 * kind + places[kind // 2]).astype(F32).astype(BF16) for kind in range(4)
    ]
    cells = dot_nt(jnp.concatenate(left, axis=1), jnp.concatenate(right, axis=1))
    spread = (iota((rows, GROUP), 0) == iota((rows, GROUP), 1) * SLOTS + 2 * CAP)
    spread = spread.astype(F32).astype(BF16)
    out_ref[...] = (dot(pick, contribution) + dot(spread, cells.astype(BF16))).astype(BF16)


def prepare(devices, lon_count, obs_count, obs_dest, obs_col, obs_depart, obs_kernel):
    n, levels = obs_kernel.shape
    steps = devices // GROUP
    whole = lambda shape: pl.BlockSpec(shape, lambda g: (0, 0))
    return pl.pallas_call(
        functools.partial(prep_kernel, lon_count),
        grid=(steps,),
        in_specs=[
            pl.BlockSpec(memory_space=pltpu.SMEM),
            whole((1, n)),
            whole((1, n)),
            whole((1, n)),
            whole((n, levels)),
        ],
        out_specs=pl.BlockSpec((GROUP * SLOTS, levels), lambda g: (g, 0)),
        out_shape=jax.ShapeDtypeStruct((devices * SLOTS, levels), BF16),
        compiler_params=params(16 + devices // 4),
        name="soundings_out",
    )(obs_count, obs_dest.reshape(1, n), obs_col.reshape(1, n), obs_depart.reshape(1, n), obs_kernel)


def pack_edge(block):
    parts = [block[:, 8 * q : 8 * q + 8, :] for q in range(4)]
    low = iota(parts[0].shape, 2) < EDGE
    pairs = [
        jnp.where(low, parts[2 * h], pltpu.roll(parts[2 * h + 1], EDGE, 2)) for h in range(2)
    ]
    return jnp.concatenate(pairs, axis=2)


def edge_kernel(field_ref, top_ref, frac_ref, out_ref):
    last = pl.num_programs(0) - 1

    @pl.when(pl.program_id(0) < last)
    def _():
        out_ref[...] = pack_edge(field_ref[...])

    @pl.when(pl.program_id(0) == last)
    def _():
        out_ref[0:1] = pack_edge(top_ref[...].astype(F32)[None])
        out_ref[1:2] = pack_edge(frac_ref[...][None])


def edge(adjoint_field, cloud_top, conv_frac):
    levels, row_count, _ = adjoint_field.shape
    steps = 8
    flat = pl.BlockSpec((row_count, LANES), lambda i: (0, 0))
    return pl.pallas_call(
        edge_kernel,
        grid=(steps + 1,),
        in_specs=[
            pl.BlockSpec((levels // steps, row_count, LANES), lambda i: (jnp.minimum(i, steps - 1), 0, 0)),
            flat,
            flat,
        ],
        out_specs=pl.BlockSpec((levels // steps, 8, 4 * EDGE), lambda i: (i, 0, 0)),
        out_shape=jax.ShapeDtypeStruct((levels + 2, 8, 4 * EDGE), F32),
        compiler_params=params(16),
        name="edge_columns",
    )(adjoint_field, cloud_top, conv_frac)


def level_rows(ref, row):
    levels = ref.shape[0]
    return ref.reshape(levels * 8, LANES)[pl.ds(row, levels, stride=8), :]


def mix_kernel(west_ref, east_ref, mixing_ref, top_ref, frac_ref, mass_ref, out_ref, wide_ref):
    levels = west_ref.shape[0]
    layer_mass = as_wide_column(mass_ref[...])
    for row in range(8):
        value = jnp.concatenate([level_rows(west_ref, row), level_rows(east_ref, row)], axis=1)
        high, low = halves(value)
        mix_high, mix_low = halves(mixing_ref[row])
        wide_ref[:levels, row * levels : (row + 1) * levels] = mix_high
        wide_ref[levels:, row * levels : (row + 1) * levels] = mix_low
        four = jnp.concatenate([mix_high, mix_low], axis=0)
        both = dot(jnp.concatenate([four, four], axis=1), jnp.concatenate([high, low], axis=0))
        mixed = both[:levels] + both[levels:]
        out_ref[row] = convect(
            mixed, top_ref[row : row + 1, :], frac_ref[row : row + 1, :], layer_mass
        )


def mix(adjoint_field, mixing_inverse, cloud_top, conv_frac, layer_mass):
    levels, row_count, col_count = adjoint_field.shape
    blocks = row_count // 8
    half = lambda h: pl.BlockSpec((levels, 8, LANES), lambda b, h=h: (0, b, h))
    flat = pl.BlockSpec((8, col_count), lambda b: (b, 0))
    return pl.pallas_call(
        mix_kernel,
        grid=(blocks,),
        in_specs=[
            half(0),
            half(1),
            pl.BlockSpec((8, levels, levels), lambda b: (b, 0, 0)),
            flat,
            flat,
            pl.BlockSpec((1, levels), lambda b: (0, 0)),
        ],
        out_specs=[
            pl.BlockSpec((8, levels, col_count), lambda b: (b, 0, 0)),
            pl.BlockSpec((2 * levels, 8 * levels), lambda b: (0, b)),
        ],
        out_shape=[
            jax.ShapeDtypeStruct((row_count, levels, col_count), F32),
            jax.ShapeDtypeStruct((2 * levels, row_count * levels), BF16),
        ],
        compiler_params=params(20),
        cost_estimate=pl.CostEstimate(
            flops=2 * levels * levels * 3 * row_count * col_count,
            bytes_accessed=12 * levels * row_count * col_count,
            transcendentals=0,
        ),
        name="mix_own",
    )(adjoint_field, adjoint_field, mixing_inverse, cloud_top, conv_frac, layer_mass)


def mix_edge_kernel(edge_ref, edge_far_ref, lines_ref, wide_ref, mass_ref, out_ref):
    levels = mass_ref.shape[1]
    width = 2 * LANES
    layer_mass = as_wide_column(mass_ref[...])
    group = iota((levels, width), 1) // EDGE
    for row in range(8):
        value = jnp.concatenate([level_rows(edge_ref, row), level_rows(edge_far_ref, row)], axis=1)
        left, right = [], []
        for q in range(4):
            cols = slice((8 * q + row) * levels, (8 * q + row + 1) * levels)
            high, low = halves(jnp.where(group == q, value, 0.0))
            left += [wide_ref[:, cols], wide_ref[:, cols]]
            right += [high, low]
        both = dot(jnp.concatenate(left, axis=1), jnp.concatenate(right, axis=0))
        mixed = both[:levels] + both[levels:]
        top = lines_ref[0, row : row + 1, :].astype(I32)
        out_ref[row] = convect(mixed, top, lines_ref[1, row : row + 1, :], layer_mass)


def mix_edge(edge_in, wide, layer_mass):
    levels = layer_mass.shape[1]
    half = lambda h: pl.BlockSpec((levels, 8, LANES), lambda i, h=h: (0, 0, h))
    return pl.pallas_call(
        mix_edge_kernel,
        grid=(1,),
        in_specs=[
            half(0),
            half(1),
            pl.BlockSpec((2, 8, 2 * LANES), lambda i: (levels // 2, 0, 0)),
            pl.BlockSpec(wide.shape, lambda i: (0, 0)),
            pl.BlockSpec((1, levels), lambda i: (0, 0)),
        ],
        out_specs=pl.BlockSpec((8, levels, 2 * LANES), lambda i: (0, 0, 0)),
        out_shape=jax.ShapeDtypeStruct((8, levels, 2 * LANES), F32),
        compiler_params=params(20),
        name="mix_edge",
    )(edge_in, edge_in, edge_in, wide, layer_mass)


def sounding_phase(
    got_ref, wide_ref, top_ref, frac_ref, lines_ref, mass_ref, edge_ref,
    columns, rows_scr, tops, fracs, stack, high_scr, low_scr, own_hot, edge_hot, edge_scr, wide_stack, forced,
):
    devices = got_ref.shape[0]
    levels = mass_ref.shape[1]
    n = devices * CAP
    row_count = top_ref.shape[0]
    width = 2 * LANES
    got = got_ref[...].astype(F32)
    columns[:, :n] = got[:, :CAP].reshape(n, levels).T.astype(BF16)
    columns[:, n:] = got[:, CAP : 2 * CAP].reshape(n, levels).T.astype(BF16)
    info = got[:, 2 * CAP :].reshape(devices * 8, LANES).astype(BF16)
    first = (iota((devices, devices * 8), 1) == 8 * iota((devices, devices * 8), 0))
    info = dot(first.astype(F32).astype(BF16), info).astype(BF16)
    lines = []
    for kind in range(4):
        chosen = iota((LANES, n), 0) == iota((LANES, n), 1) % CAP + 32 * kind
        spread = dot(info, chosen.astype(F32).astype(BF16))
        mine = iota((devices, n), 0) == iota((devices, n), 1) // CAP
        lines.append(jnp.sum(jnp.where(mine, spread, 0.0), axis=0, keepdims=True))
    own_row, own_col, east_row, east_col = [line.astype(I32) for line in lines]
    near = east_col < EDGE
    packed_col = jnp.where(near, (east_row // 8) * EDGE + east_col, -1)
    packed_row = east_row % 8
    rows_scr[0:1, :n] = own_row
    rows_scr[0:1, n:] = east_row
    rows_scr[1:2, :n] = packed_row

    parts = [
        (own_col, own_row, top_ref[...].astype(F32), frac_ref[...], own_hot, row_count, 0),
        (packed_col, packed_row, lines_ref[0], lines_ref[1], edge_hot, 8, n),
    ]
    for col, row, top, frac, hot_ref, count, start in parts:
        hot_t = (iota((width, n), 0) == col).astype(F32).astype(BF16)
        table = jnp.concatenate([top.astype(BF16)] + thirds(frac), axis=0)
        found = dot(table, hot_t)
        here = iota((count, n), 0) == row
        found = [
            jnp.sum(jnp.where(here, found[i * count : (i + 1) * count], 0.0), axis=0, keepdims=True)
            for i in range(4)
        ]
        tops[0:1, start : start + n] = found[0].astype(I32)
        fracs[0:1, start : start + n] = (found[1] + found[2]) + found[3]
        col_t = as_column(col.astype(F32)).astype(I32)
        lane = iota((n, LANES), 1)
        for h in range(2):
            hot = (col_t == lane + h * LANES).astype(F32).astype(BF16)
            hot_ref[:n, h * LANES : (h + 1) * LANES] = hot
            hot_ref[n:, h * LANES : (h + 1) * LANES] = hot

    layer_mass = as_wide_column(mass_ref[...])

    def mix_chunk(index, carry):
        here = pl.ds(pl.multiple_of(index * CHUNK, CHUNK), CHUNK)
        value = columns[:, here]
        row = rows_scr[0:1, here]
        for r in range(row_count):
            stack[r * levels : (r + 1) * levels, :] = value * (row == r).astype(F32).astype(BF16)
        both = dot(wide_ref[...], stack[...])
        mixed = both[:levels] + both[levels:]
        high, low = halves(convect(mixed, tops[0:1, here], fracs[0:1, here], layer_mass))
        high_scr[:, here] = high
        low_scr[:, here] = low
        return carry

    lax.fori_loop(0, 2 * n // CHUNK, mix_chunk, 0)

    row = rows_scr[1:2, :n]
    for r in range(8):
        chosen = (row == r).astype(F32).astype(BF16)
        here = slice(r * levels, (r + 1) * levels)
        wide_stack[here, :n] = high_scr[:, n:] * chosen
        wide_stack[here, n:] = low_scr[:, n:] * chosen
    forced[...] = dot(wide_stack[...], edge_hot[...])
    for r in range(8):
        value = edge_ref[r] + forced[r * levels : (r + 1) * levels, :]
        for h in range(2):
            part = value[:, h * LANES : (h + 1) * LANES]
            edge_scr[16 * h + r] = part
            edge_scr[16 * h + 8 + r] = pltpu.roll(part, EDGE, 1)


def columns_of(lines):
    return jnp.concatenate([lines] * (LANES // 8), axis=0).T


def shifted(tiles, shift, weight):
    lane = iota(tiles[0].shape, 1)
    sums = []
    for extra in range(2):
        place = lane + (shift + extra)
        inside = place < LANES
        place = place & (LANES - 1)
        moved = [jnp.take_along_axis(t, place, axis=1, mode="promise_in_bounds") for t in tiles]
        sums.append([jnp.where(inside, moved[h], moved[h + 1]) for h in range(2)])
    return [(1.0 - weight) * sums[0][h] + weight * sums[1][h] for h in range(2)]


def first_row_kernel(
    got_ref, wide_ref, top_ref, frac_ref, lines_ref, mass_ref, edge_ref,
    field_ref, west_ref, east_ref, shift_ref, weight_ref,
    rows_ref, high_ref, low_ref, own_hot, edge_out, first_ref,
    columns, tops, fracs, stack, edge_hot, wide_stack, forced,
):
    levels = mass_ref.shape[1]
    n = got_ref.shape[0] * CAP
    sounding_phase(
        got_ref, wide_ref, top_ref, frac_ref, lines_ref, mass_ref, edge_ref,
        columns, rows_ref, tops, fracs, stack, high_ref, low_ref, own_hot, edge_hot, edge_out,
        wide_stack, forced,
    )
    chosen = (rows_ref[0:1, :n] == 0).astype(F32).astype(BF16)
    left = jnp.concatenate([high_ref[:, :n] * chosen, low_ref[:, :n] * chosen], axis=1)
    value = field_ref[0] + dot(left, own_hot[...])
    shift = as_column(shift_ref[0:1, :].astype(F32)).astype(I32)
    weight = as_column(weight_ref[0:1, :])
    zonal = shifted([value[:, :LANES], value[:, LANES:], edge_out[0]], shift, weight)
    first_ref[:, :LANES] = level_rows(west_ref, 0) * zonal[0]
    first_ref[:, LANES:] = level_rows(east_ref, 0) * zonal[1]


IN_VMEM = pl.BlockSpec(memory_space=pltpu.VMEM)


def first_row(got, wide, cloud_top, conv_frac, edge_in, layer_mass, edge_field, field, courant, shift, weight):
    row_count, levels, col_count = field.shape
    n = got.shape[0] * CAP
    width = 2 * LANES
    full = lambda array: pl.BlockSpec(array.shape, lambda s: (0,) * array.ndim)
    half = lambda h: pl.BlockSpec((levels, 8, LANES), lambda s, h=h: (0, 0, h))
    lines = pl.BlockSpec((8, levels), lambda s: (0, 0))
    return pl.pallas_call(
        first_row_kernel,
        grid=(1,),
        in_specs=[
            IN_VMEM,
            IN_VMEM,
            full(cloud_top),
            full(conv_frac),
            pl.BlockSpec((2, 8, width), lambda s: (levels // 2, 0, 0)),
            full(layer_mass),
            IN_VMEM,
            pl.BlockSpec((1, levels, col_count), lambda s: (0, 0, 0)),
            half(0),
            half(1),
            lines,
            lines,
        ],
        out_specs=[IN_VMEM] * 6,
        out_shape=[
            jax.ShapeDtypeStruct((8, 2 * n), I32),
            jax.ShapeDtypeStruct((levels, 2 * n), BF16),
            jax.ShapeDtypeStruct((levels, 2 * n), BF16),
            jax.ShapeDtypeStruct((2 * n, width), BF16),
            jax.ShapeDtypeStruct((row_count, levels, LANES), F32),
            jax.ShapeDtypeStruct((levels, col_count), F32),
        ],
        scratch_shapes=[
            pltpu.VMEM((levels, 2 * n), BF16),
            pltpu.VMEM((8, 2 * n), I32),
            pltpu.VMEM((8, 2 * n), F32),
            pltpu.VMEM((row_count * levels, CHUNK), BF16),
            pltpu.VMEM((2 * n, width), BF16),
            pltpu.VMEM((8 * levels, 2 * n), BF16),
            pltpu.VMEM((8 * levels, width), F32),
        ],
        compiler_params=params(16 + n // 128),
        name="mix_soundings",
    )(got, wide, cloud_top, conv_frac, edge_in, layer_mass, edge_field, field, courant, courant, shift, weight)


def advect_kernel(
    rows_ref, high_ref, low_ref, own_hot, edge_ref, field_ref,
    west_ref, east_ref, shift_ref, weight_ref,
    out_ref,
    wide_stack, forced, out_scr, prev, sem,
):
    step = pl.program_id(0)
    blocks = pl.num_programs(0)
    block = blocks - 1 - step
    levels = high_ref.shape[0]
    n = high_ref.shape[1] // 2

    @pl.when(step == 0)
    def _():
        prev[...] = jnp.zeros_like(prev)

    later = [prev[0], prev[1]]
    cell_row = rows_ref[0:1, :n]
    for r in range(8):
        chosen = (cell_row == 8 * block + r).astype(F32).astype(BF16)
        here = slice(r * levels, (r + 1) * levels)
        wide_stack[here, :n] = high_ref[:, :n] * chosen
        wide_stack[here, n:] = low_ref[:, :n] * chosen
    forced[...] = dot(wide_stack[...], own_hot[...])
    shifts = columns_of(shift_ref[...].astype(F32)).astype(I32)
    weights = columns_of(weight_ref[...])
    for r in reversed(range(8)):
        row = 8 * block + r
        value = field_ref[row] + forced[r * levels : (r + 1) * levels, :]
        tiles = [value[:, :LANES], value[:, LANES:], edge_ref[row]]
        zonal = shifted(tiles, shifts[:, r : r + 1], weights[:, r : r + 1])
        for h, courant_ref in enumerate((west_ref, east_ref)):
            courant = level_rows(courant_ref, r)
            place = out_scr.at[block, h].reshape(levels * 8, LANES)
            place[pl.ds(r, levels, stride=8), :] = (1.0 - courant) * zonal[h] + later[h]
            later[h] = courant * zonal[h]
    prev[0] = later[0]
    prev[1] = later[1]

    def copies(b):
        return [
            pltpu.make_async_copy(
                out_scr.at[b, h],
                out_ref.at[:, pl.ds(b * 8, 8), pl.ds(h * LANES, LANES)],
                sem.at[b, h],
            )
            for h in range(2)
        ]

    for b in range(out_scr.shape[0]):

        @pl.when(block == b)
        def _():
            for copy in copies(b):
                copy.start()

    @pl.when(step == blocks - 1)
    def _():
        for b in range(out_scr.shape[0]):
            for copy in copies(b):
                copy.wait()


def advect(rows, high, low, own_hot, edge_field, field, courant, shift, weight):
    row_count, levels, col_count = field.shape
    blocks = row_count // 8
    n = rows.shape[1] // 2
    half = lambda h: pl.BlockSpec((levels, 8, LANES), lambda s, h=h: (0, blocks - 1 - s, h))
    lines = pl.BlockSpec((8, levels), lambda s: (blocks - 1 - s, 0))
    return pl.pallas_call(
        advect_kernel,
        grid=(blocks,),
        in_specs=[IN_VMEM] * 6 + [half(0), half(1), lines, lines],
        out_specs=pl.BlockSpec(memory_space=pl.ANY),
        out_shape=jax.ShapeDtypeStruct((levels, row_count, col_count), F32),
        scratch_shapes=[
            pltpu.VMEM((8 * levels, 2 * n), BF16),
            pltpu.VMEM((8 * levels, 2 * LANES), F32),
            pltpu.VMEM((blocks, 2, levels, 8, LANES), F32),
            pltpu.VMEM((2, levels, LANES), F32),
            pltpu.SemaphoreType.DMA((blocks, 2)),
        ],
        compiler_params=params(16 + n // 128),
        cost_estimate=pl.CostEstimate(
            flops=4 * levels * row_count * n * col_count,
            bytes_accessed=12 * levels * row_count * col_count,
            transcendentals=0,
        ),
        name="advect",
    )(rows, high, low, own_hot, edge_field, field, courant, courant, shift, weight)


def close_kernel(out_ref, north_ref, result_ref):
    levels = out_ref.shape[0]
    result_ref[...] = out_ref[...]
    result_ref.reshape(levels * 8, LANES)[pl.ds(7, levels, stride=8), :] = (
        level_rows(out_ref, 7) + north_ref[...]
    )


def close(out, north):
    levels, row_count, col_count = out.shape
    spec = pl.BlockSpec((levels, 8, LANES), lambda h: (0, row_count // 8 - 1, h))
    return pl.pallas_call(
        close_kernel,
        grid=(col_count // LANES,),
        in_specs=[spec, pl.BlockSpec((levels, LANES), lambda h: (0, h))],
        out_specs=spec,
        out_shape=jax.ShapeDtypeStruct(out.shape, F32),
        input_output_aliases={0: 0},
        compiler_params=params(16),
        name="close_last_row",
    )(out, north)


def shards(
    adjoint_field,
    mixing_inverse,
    cloud_top,
    conv_frac,
    thickness,
    zonal_shift,
    zonal_frac,
    merid_courant,
    obs_kernel,
    obs_depart,
    obs_dest,
    obs_col,
    obs_count,
):
    adjoint_field, mixing_inverse, cloud_top, conv_frac, merid_courant, obs_kernel = [
        in_hbm(array)
        for array in (
            adjoint_field, mixing_inverse, cloud_top, conv_frac, merid_courant, obs_kernel
        )
    ]
    levels, row_count, col_count = adjoint_field.shape
    lat_count, lon_count = lax.axis_size("lat"), lax.axis_size("lon")
    devices = lat_count * lon_count
    sent = prepare(devices, lon_count, obs_count, obs_dest, obs_col, obs_depart, obs_kernel)
    got = lax.all_to_all(
        sent.reshape(devices, SLOTS, levels), ("lat", "lon"), split_axis=0, concat_axis=0, tiled=True
    )
    westward = [((i + 1) % lon_count, i) for i in range(lon_count)]
    edge_in = lax.ppermute(edge(adjoint_field, cloud_top, conv_frac), "lon", westward)
    layer_mass = thickness.reshape(1, levels)
    field, wide = mix(adjoint_field, mixing_inverse, cloud_top, conv_frac, layer_mass)
    edge_field = mix_edge(edge_in, wide, layer_mass)
    shift, weight = in_hbm(zonal_shift.T), in_hbm(zonal_frac.T)
    rows, high, low, own_hot, edge_total, first = first_row(
        got, wide, cloud_top, conv_frac, edge_in, layer_mass, edge_field, field, merid_courant,
        shift, weight,
    )
    southward = [(i + 1, i) for i in range(lat_count - 1)]
    north = lax.ppermute(first, "lat", southward)
    out = advect(rows, high, low, own_hot, edge_total, field, merid_courant, shift, weight)
    return close(out, north)


def solution(mesh):
    in_specs = (
        P(None, "lat", "lon"),
        P("lat", None, None),
        P("lat", "lon"),
        P("lat", "lon"),
        P(),
        P(None, "lat"),
        P(None, "lat"),
        P(None, "lat", "lon"),
        P(("lat", "lon"), None),
        P(("lat", "lon")),
        P(("lat", "lon")),
        P(("lat", "lon")),
        P(("lat", "lon")),
    )
    out_specs = P(None, "lat", "lon")
    return jax.shard_map(shards, mesh=mesh, in_specs=in_specs, out_specs=out_specs, check_vma=False)
```

```python
import functools

import jax
import jax.numpy as jnp
from jax import lax
from jax.experimental import pallas as pl
from jax.experimental.pallas import tpu as pltpu
from jax.sharding import PartitionSpec as P

F32, BF16, I32 = jnp.float32, jnp.bfloat16, jnp.int32
CAP = 16
SLOTS = 40
EDGE = 64
LANES = 128
GROUP = 32
CHUNK = 256
MIB = 1024 * 1024


IN_VMEM = pl.BlockSpec(memory_space=pltpu.VMEM)


def iota(shape, dim):
    return lax.broadcasted_iota(I32, shape, dim)


def params(mib):
    return pltpu.CompilerParams(vmem_limit_bytes=mib * MIB)


def in_hbm(array):
    return pltpu.with_memory_space_constraint(array, pltpu.HBM)


def dot(left, right):
    return jnp.dot(left, right, preferred_element_type=F32)


def dot_nt(left, right):
    return lax.dot_general(left, right, (((1,), (1,)), ((), ())), preferred_element_type=F32)


def halves(value):
    high = value.astype(BF16)
    return high, (value - high.astype(F32)).astype(BF16)


def thirds(value):
    high = value.astype(BF16)
    rest = value - high.astype(F32)
    mid = rest.astype(BF16)
    return [high, mid, (rest - mid.astype(F32)).astype(BF16)]


def as_column(line):
    return jnp.broadcast_to(line, (LANES, line.shape[1])).T


def as_wide_column(line):
    column = as_column(line)
    return jnp.concatenate([column, column], axis=1)


def convect(mixed, top, frac, layer_mass):
    inside = iota(mixed.shape, 0) < top
    total = jnp.sum(jnp.where(inside, mixed, 0.0), axis=0, keepdims=True)
    mass = jnp.sum(jnp.where(inside, layer_mass, 0.0), axis=0, keepdims=True)
    mean = total / jnp.where(mass > 0.0, mass, 1.0)
    return mixed + jnp.where(inside, frac * (layer_mass * mean - mixed), 0.0)


def prep_kernel(lon_count, count_ref, dest_ref, col_ref, depart_ref, obs_ref, out_ref):
    n = obs_ref.shape[0]
    rows = GROUP * SLOTS
    lane = iota((1, n), 1)
    live = lane < count_ref[0]
    dest = jnp.where(live, dest_ref[...], -1)
    cell = col_ref[...]
    cell_row = (cell // 256).astype(F32)
    cell_col = (cell % 256).astype(F32)
    contribution = (obs_ref[...].astype(F32) * as_column(depart_ref[...])).astype(BF16)
    local = iota((GROUP, n), 0)
    own_id = pl.program_id(0) * GROUP + local
    lon_id = own_id % lon_count
    east_id = jnp.where(lon_id == lon_count - 1, own_id - lon_id, own_id + 1)
    slots, places, left = [], [], []
    for ident, offset in ((own_id, 0), (east_id, CAP)):
        hit = dest == ident
        before = jnp.sum((live & (dest < ident)).astype(I32), axis=1, keepdims=True)
        place = lane - before
        slot = jnp.where(hit, local * SLOTS + offset + place + 1, 0)
        slots.append(jnp.sum(slot, axis=0, keepdims=True) - 1)
        places.append(jnp.sum(jnp.where(hit, place, 0), axis=0, keepdims=True))
        left.append(jnp.where(hit, cell_row, 0.0).astype(BF16))
        left.append(jnp.where(hit, cell_col, 0.0).astype(BF16))
    out_row = iota((rows, n), 0)
    pick = ((out_row == slots[0]) | (out_row == slots[1])).astype(F32).astype(BF16)
    spot = iota((LANES, n), 0)
    right = [
        (spot == 32 * kind + places[kind // 2]).astype(F32).astype(BF16) for kind in range(4)
    ]
    cells = dot_nt(jnp.concatenate(left, axis=1), jnp.concatenate(right, axis=1))
    spread = (iota((rows, GROUP), 0) == iota((rows, GROUP), 1) * SLOTS + 2 * CAP)
    spread = spread.astype(F32).astype(BF16)
    out_ref[...] = (dot(pick, contribution) + dot(spread, cells.astype(BF16))).astype(BF16)


def prepare(devices, lon_count, obs_count, obs_dest, obs_col, obs_depart, obs_kernel):
    n, levels = obs_kernel.shape
    steps = devices // GROUP
    whole = lambda shape: pl.BlockSpec(shape, lambda g: (0, 0))
    return pl.pallas_call(
        functools.partial(prep_kernel, lon_count),
        grid=(steps,),
        in_specs=[
            pl.BlockSpec(memory_space=pltpu.SMEM),
            whole((1, n)),
            whole((1, n)),
            whole((1, n)),
            whole((n, levels)),
        ],
        out_specs=pl.BlockSpec((GROUP * SLOTS, levels), lambda g: (g, 0)),
        out_shape=jax.ShapeDtypeStruct((devices * SLOTS, levels), BF16),
        compiler_params=params(16 + devices // 4),
        name="soundings_out",
    )(obs_count, obs_dest.reshape(1, n), obs_col.reshape(1, n), obs_depart.reshape(1, n), obs_kernel)


def pack_edge(block):
    parts = [block[:, 8 * q : 8 * q + 8, :] for q in range(4)]
    low = iota(parts[0].shape, 2) < EDGE
    pairs = [
        jnp.where(low, parts[2 * h], pltpu.roll(parts[2 * h + 1], EDGE, 2)) for h in range(2)
    ]
    return jnp.concatenate(pairs, axis=2)


def edge_kernel(field_ref, top_ref, frac_ref, out_ref):
    count = field_ref.shape[0]
    out_ref[:count] = pack_edge(field_ref[...])

    @pl.when(pl.program_id(0) == 0)
    def _():
        out_ref[count:] = pack_edge(top_ref[...].astype(F32)[None])

    @pl.when(pl.program_id(0) == 1)
    def _():
        out_ref[count:] = pack_edge(frac_ref[...][None])


def edge(adjoint_field, cloud_top, conv_frac):
    levels, row_count, _ = adjoint_field.shape
    count = levels // 2
    flat = pl.BlockSpec((row_count, LANES), lambda i: (0, 0))
    return pl.pallas_call(
        edge_kernel,
        grid=(2,),
        in_specs=[
            pl.BlockSpec((count, row_count, LANES), lambda i: (i, 0, 0)),
            flat,
            flat,
        ],
        out_specs=pl.BlockSpec((count + 1, 8, 4 * EDGE), lambda i: (i, 0, 0)),
        out_shape=pltpu.VMEM((levels + 2, 8, 4 * EDGE), F32),
        compiler_params=params(16),
        name="edge_columns",
    )(adjoint_field, cloud_top, conv_frac)


def level_rows(ref, row, first=0, count=None):
    levels = ref.shape[0]
    count = levels if count is None else count
    return ref.reshape(levels * 8, LANES)[pl.ds(8 * first + row, count, stride=8), :]


def mix_kernel(west_ref, east_ref, mixing_ref, top_ref, frac_ref, mass_ref, out_ref, wide_ref):
    levels = west_ref.shape[0]
    layer_mass = as_wide_column(mass_ref[...])
    for row in range(8):
        value = jnp.concatenate([level_rows(west_ref, row), level_rows(east_ref, row)], axis=1)
        high, low = halves(value)
        mix_high, mix_low = halves(mixing_ref[row])
        wide_ref[:levels, row * levels : (row + 1) * levels] = mix_high
        wide_ref[levels:, row * levels : (row + 1) * levels] = mix_low
        four = jnp.concatenate([mix_high, mix_low], axis=0)
        both = dot(jnp.concatenate([four, four], axis=1), jnp.concatenate([high, low], axis=0))
        mixed = both[:levels] + both[levels:]
        out_ref[row] = convect(
            mixed, top_ref[row : row + 1, :], frac_ref[row : row + 1, :], layer_mass
        )


def mix(adjoint_field, mixing_inverse, cloud_top, conv_frac, layer_mass):
    levels, row_count, col_count = adjoint_field.shape
    blocks = row_count // 8
    half = lambda h: pl.BlockSpec((levels, 8, LANES), lambda b, h=h: (0, b, h))
    flat = pl.BlockSpec((8, col_count), lambda b: (b, 0))
    return pl.pallas_call(
        mix_kernel,
        grid=(blocks,),
        in_specs=[
            half(0),
            half(1),
            pl.BlockSpec((8, levels, levels), lambda b: (b, 0, 0)),
            flat,
            flat,
            pl.BlockSpec((1, levels), lambda b: (0, 0)),
        ],
        out_specs=[
            pl.BlockSpec((8, levels, col_count), lambda b: (b, 0, 0)),
            pl.BlockSpec((2 * levels, 8 * levels), lambda b: (0, b)),
        ],
        out_shape=[
            pltpu.VMEM((row_count, levels, col_count), F32),
            pltpu.VMEM((2 * levels, row_count * levels), BF16),
        ],
        compiler_params=params(20),
        cost_estimate=pl.CostEstimate(
            flops=2 * levels * levels * 3 * row_count * col_count,
            bytes_accessed=12 * levels * row_count * col_count,
            transcendentals=0,
        ),
        name="mix_own",
    )(adjoint_field, adjoint_field, mixing_inverse, cloud_top, conv_frac, layer_mass)


def mix_edge_kernel(edge_ref, edge_far_ref, lines_ref, wide_ref, mass_ref, out_ref):
    levels = mass_ref.shape[1]
    width = 2 * LANES
    half = levels // 2
    layer_mass = as_wide_column(mass_ref[...])
    group = iota((levels, width), 1) // EDGE
    for row in range(8):
        halves_of = [
            jnp.concatenate(
                [level_rows(ref, row, 0, half), level_rows(ref, row, half + 1, half)], axis=0
            )
            for ref in (edge_ref, edge_far_ref)
        ]
        value = jnp.concatenate(halves_of, axis=1)
        left, right = [], []
        for q in range(4):
            cols = slice((8 * q + row) * levels, (8 * q + row + 1) * levels)
            high, low = halves(jnp.where(group == q, value, 0.0))
            left += [wide_ref[:, cols], wide_ref[:, cols]]
            right += [high, low]
        both = dot(jnp.concatenate(left, axis=1), jnp.concatenate(right, axis=0))
        mixed = both[:levels] + both[levels:]
        top = lines_ref[half, row : row + 1, :].astype(I32)
        frac = lines_ref[levels + 1, row : row + 1, :]
        out_ref[row] = convect(mixed, top, frac, layer_mass)


def mix_edge(edge_in, wide, layer_mass):
    levels = layer_mass.shape[1]
    half = lambda h: pl.BlockSpec((levels + 2, 8, LANES), lambda i, h=h: (0, 0, h))
    return pl.pallas_call(
        mix_edge_kernel,
        grid=(1,),
        in_specs=[
            half(0),
            half(1),
            IN_VMEM,
            IN_VMEM,
            pl.BlockSpec((1, levels), lambda i: (0, 0)),
        ],
        out_specs=pl.BlockSpec((8, levels, 2 * LANES), lambda i: (0, 0, 0)),
        out_shape=pltpu.VMEM((8, levels, 2 * LANES), F32),
        compiler_params=params(20),
        name="mix_edge",
    )(edge_in, edge_in, edge_in, wide, layer_mass)


def sounding_phase(
    got_ref, wide_ref, top_ref, frac_ref, lines_ref, mass_ref, edge_ref,
    columns, rows_scr, tops, fracs, stack, high_scr, low_scr, own_hot, edge_hot, edge_scr, wide_stack, forced,
):
    devices = got_ref.shape[0]
    levels = mass_ref.shape[1]
    n = devices * CAP
    row_count = top_ref.shape[0]
    width = 2 * LANES
    got = got_ref[...].astype(F32)
    columns[:, :n] = got[:, :CAP].reshape(n, levels).T.astype(BF16)
    columns[:, n:] = got[:, CAP : 2 * CAP].reshape(n, levels).T.astype(BF16)
    info = got[:, 2 * CAP :].reshape(devices * 8, LANES).astype(BF16)
    first = (iota((devices, devices * 8), 1) == 8 * iota((devices, devices * 8), 0))
    info = dot(first.astype(F32).astype(BF16), info).astype(BF16)
    lines = []
    for kind in range(4):
        chosen = iota((LANES, n), 0) == iota((LANES, n), 1) % CAP + 32 * kind
        spread = dot(info, chosen.astype(F32).astype(BF16))
        mine = iota((devices, n), 0) == iota((devices, n), 1) // CAP
        lines.append(jnp.sum(jnp.where(mine, spread, 0.0), axis=0, keepdims=True))
    own_row, own_col, east_row, east_col = [line.astype(I32) for line in lines]
    near = east_col < EDGE
    packed_col = jnp.where(near, (east_row // 8) * EDGE + east_col, -1)
    packed_row = east_row % 8
    rows_scr[0:1, :n] = own_row
    rows_scr[0:1, n:] = east_row
    rows_scr[1:2, :n] = packed_row

    parts = [
        (own_col, own_row, top_ref[...].astype(F32), frac_ref[...], own_hot, row_count, 0),
        (packed_col, packed_row, lines_ref[levels // 2], lines_ref[levels + 1], edge_hot, 8, n),
    ]
    for col, row, top, frac, hot_ref, count, start in parts:
        hot_t = (iota((width, n), 0) == col).astype(F32).astype(BF16)
        table = jnp.concatenate([top.astype(BF16)] + thirds(frac), axis=0)
        found = dot(table, hot_t)
        here = iota((count, n), 0) == row
        found = [
            jnp.sum(jnp.where(here, found[i * count : (i + 1) * count], 0.0), axis=0, keepdims=True)
            for i in range(4)
        ]
        tops[0:1, start : start + n] = found[0].astype(I32)
        fracs[0:1, start : start + n] = (found[1] + found[2]) + found[3]
        col_t = as_column(col.astype(F32)).astype(I32)
        lane = iota((n, LANES), 1)
        for h in range(2):
            hot = (col_t == lane + h * LANES).astype(F32).astype(BF16)
            hot_ref[:n, h * LANES : (h + 1) * LANES] = hot
            hot_ref[n:, h * LANES : (h + 1) * LANES] = hot

    layer_mass = as_wide_column(mass_ref[...])

    def mix_chunk(index, carry):
        here = pl.ds(pl.multiple_of(index * CHUNK, CHUNK), CHUNK)
        value = columns[:, here]
        row = rows_scr[0:1, here]
        for r in range(row_count):
            stack[r * levels : (r + 1) * levels, :] = value * (row == r).astype(F32).astype(BF16)
        both = dot(wide_ref[...], stack[...])
        mixed = both[:levels] + both[levels:]
        high, low = halves(convect(mixed, tops[0:1, here], fracs[0:1, here], layer_mass))
        high_scr[:, here] = high
        low_scr[:, here] = low
        return carry

    lax.fori_loop(0, 2 * n // CHUNK, mix_chunk, 0)

    row = rows_scr[1:2, :n]
    for r in range(8):
        chosen = (row == r).astype(F32).astype(BF16)
        here = slice(r * levels, (r + 1) * levels)
        wide_stack[here, :n] = high_scr[:, n:] * chosen
        wide_stack[here, n:] = low_scr[:, n:] * chosen
    forced[...] = dot(wide_stack[...], edge_hot[...])
    for r in range(8):
        value = edge_ref[r] + forced[r * levels : (r + 1) * levels, :]
        for h in range(2):
            part = value[:, h * LANES : (h + 1) * LANES]
            edge_scr[16 * h + r] = part
            edge_scr[16 * h + 8 + r] = pltpu.roll(part, EDGE, 1)


def columns_of(lines):
    return jnp.concatenate([lines] * (LANES // 8), axis=0).T


def shifted(tiles, shift, weight):
    shape = tiles[0].shape
    lane = iota(shape, 1)
    shift = jnp.broadcast_to(shift, shape)

    def moved(steps):
        turned = [pltpu.roll(tile, LANES - steps, 1) for tile in tiles]
        stays = lane < LANES - steps
        return [jnp.where(stays, turned[h], turned[h + 1]) for h in range(2)] + [turned[2]]

    for bit in (32, 16, 8, 4, 2, 1):
        chosen = (shift & bit) != 0
        tiles = [jnp.where(chosen, new, old) for new, old in zip(moved(bit), tiles)]
    return [(1.0 - weight) * tiles[h] + weight * new for h, new in enumerate(moved(1)[:2])]


def first_row_kernel(
    got_ref, wide_ref, top_ref, frac_ref, lines_ref, mass_ref, edge_ref,
    field_ref, west_ref, east_ref, shift_ref, weight_ref,
    rows_ref, high_ref, low_ref, own_hot, edge_out, first_ref,
    columns, tops, fracs, stack, edge_hot, wide_stack, forced,
):
    levels = mass_ref.shape[1]
    n = got_ref.shape[0] * CAP
    sounding_phase(
        got_ref, wide_ref, top_ref, frac_ref, lines_ref, mass_ref, edge_ref,
        columns, rows_ref, tops, fracs, stack, high_ref, low_ref, own_hot, edge_hot, edge_out,
        wide_stack, forced,
    )
    chosen = (rows_ref[0:1, :n] == 0).astype(F32).astype(BF16)
    left = jnp.concatenate([high_ref[:, :n] * chosen, low_ref[:, :n] * chosen], axis=1)
    value = field_ref[0] + dot(left, own_hot[...])
    shift = as_column(shift_ref[0:1, :].astype(F32)).astype(I32)
    weight = as_column(weight_ref[0:1, :])
    zonal = shifted([value[:, :LANES], value[:, LANES:], edge_out[0]], shift, weight)
    first_ref[:, :LANES] = level_rows(west_ref, 0) * zonal[0]
    first_ref[:, LANES:] = level_rows(east_ref, 0) * zonal[1]


def first_row(got, wide, cloud_top, conv_frac, edge_in, layer_mass, edge_field, field, courant, shift, weight):
    row_count, levels, col_count = field.shape
    n = got.shape[0] * CAP
    width = 2 * LANES
    full = lambda array: pl.BlockSpec(array.shape, lambda s: (0,) * array.ndim)
    half = lambda h: pl.BlockSpec((levels, 8, LANES), lambda s, h=h: (0, 0, h))
    lines = pl.BlockSpec((8, levels), lambda s: (0, 0))
    return pl.pallas_call(
        first_row_kernel,
        grid=(1,),
        in_specs=[
            IN_VMEM,
            IN_VMEM,
            full(cloud_top),
            full(conv_frac),
            IN_VMEM,
            full(layer_mass),
            IN_VMEM,
            pl.BlockSpec((1, levels, col_count), lambda s: (0, 0, 0)),
            half(0),
            half(1),
            lines,
            lines,
        ],
        out_specs=[IN_VMEM] * 6,
        out_shape=[
            jax.ShapeDtypeStruct((8, 2 * n), I32),
            jax.ShapeDtypeStruct((levels, 2 * n), BF16),
            jax.ShapeDtypeStruct((levels, 2 * n), BF16),
            jax.ShapeDtypeStruct((2 * n, width), BF16),
            jax.ShapeDtypeStruct((row_count, levels, LANES), F32),
            jax.ShapeDtypeStruct((levels, col_count), F32),
        ],
        scratch_shapes=[
            pltpu.VMEM((levels, 2 * n), BF16),
            pltpu.VMEM((8, 2 * n), I32),
            pltpu.VMEM((8, 2 * n), F32),
            pltpu.VMEM((row_count * levels, CHUNK), BF16),
            pltpu.VMEM((2 * n, width), BF16),
            pltpu.VMEM((8 * levels, 2 * n), BF16),
            pltpu.VMEM((8 * levels, width), F32),
        ],
        compiler_params=params(16 + n // 128),
        name="mix_soundings",
    )(got, wide, cloud_top, conv_frac, edge_in, layer_mass, edge_field, field, courant, courant, shift, weight)


def advect_kernel(
    rows_ref, high_ref, low_ref, own_hot, edge_ref, field_ref,
    west_ref, east_ref, shift_ref, weight_ref,
    out_ref,
    wide_stack, forced, out_scr, prev, sem,
):
    step = pl.program_id(0)
    blocks = pl.num_programs(0)
    block = blocks - 1 - step
    levels = high_ref.shape[0]
    n = high_ref.shape[1] // 2

    @pl.when(step == 0)
    def _():
        prev[...] = jnp.zeros_like(prev)

    later = [prev[0], prev[1]]
    cell_row = rows_ref[0:1, :n]
    for r in range(8):
        chosen = (cell_row == 8 * block + r).astype(F32).astype(BF16)
        here = slice(r * levels, (r + 1) * levels)
        wide_stack[here, :n] = high_ref[:, :n] * chosen
        wide_stack[here, n:] = low_ref[:, :n] * chosen
    forced[...] = dot(wide_stack[...], own_hot[...])
    shifts = columns_of(shift_ref[...].astype(F32)).astype(I32)
    weights = columns_of(weight_ref[...])
    for r in reversed(range(8)):
        row = 8 * block + r
        value = field_ref[row] + forced[r * levels : (r + 1) * levels, :]
        tiles = [value[:, :LANES], value[:, LANES:], edge_ref[row]]
        zonal = shifted(tiles, shifts[:, r : r + 1], weights[:, r : r + 1])
        for h, courant_ref in enumerate((west_ref, east_ref)):
            courant = level_rows(courant_ref, r)
            place = out_scr.at[block, h].reshape(levels * 8, LANES)
            place[pl.ds(r, levels, stride=8), :] = (1.0 - courant) * zonal[h] + later[h]
            later[h] = courant * zonal[h]
    prev[0] = later[0]
    prev[1] = later[1]

    def copies(b):
        return [
            pltpu.make_async_copy(
                out_scr.at[b, h],
                out_ref.at[:, pl.ds(b * 8, 8), pl.ds(h * LANES, LANES)],
                sem.at[b, h],
            )
            for h in range(2)
        ]

    for b in range(out_scr.shape[0]):

        @pl.when(block == b)
        def _():
            for copy in copies(b):
                copy.start()

    @pl.when(step == blocks - 1)
    def _():
        for b in range(out_scr.shape[0]):
            for copy in copies(b):
                copy.wait()


def advect(rows, high, low, own_hot, edge_field, field, courant, shift, weight):
    row_count, levels, col_count = field.shape
    blocks = row_count // 8
    n = rows.shape[1] // 2
    half = lambda h: pl.BlockSpec((levels, 8, LANES), lambda s, h=h: (0, blocks - 1 - s, h))
    lines = pl.BlockSpec((8, levels), lambda s: (blocks - 1 - s, 0))
    return pl.pallas_call(
        advect_kernel,
        grid=(blocks,),
        in_specs=[IN_VMEM] * 6 + [half(0), half(1), lines, lines],
        out_specs=pl.BlockSpec(memory_space=pl.ANY),
        out_shape=jax.ShapeDtypeStruct((levels, row_count, col_count), F32),
        scratch_shapes=[
            pltpu.VMEM((8 * levels, 2 * n), BF16),
            pltpu.VMEM((8 * levels, 2 * LANES), F32),
            pltpu.VMEM((blocks, 2, levels, 8, LANES), F32),
            pltpu.VMEM((2, levels, LANES), F32),
            pltpu.SemaphoreType.DMA((blocks, 2)),
        ],
        compiler_params=params(16 + n // 128),
        cost_estimate=pl.CostEstimate(
            flops=4 * levels * row_count * n * col_count,
            bytes_accessed=12 * levels * row_count * col_count,
            transcendentals=0,
        ),
        name="advect",
    )(rows, high, low, own_hot, edge_field, field, courant, courant, shift, weight)


def close_kernel(out_ref, north_ref, result_ref):
    levels = out_ref.shape[0]
    result_ref[...] = out_ref[...]
    result_ref.reshape(levels * 8, LANES)[pl.ds(7, levels, stride=8), :] = (
        level_rows(out_ref, 7) + north_ref[...]
    )


def close(out, north):
    levels, row_count, col_count = out.shape
    spec = pl.BlockSpec((levels, 8, LANES), lambda h: (0, row_count // 8 - 1, h))
    return pl.pallas_call(
        close_kernel,
        grid=(col_count // LANES,),
        in_specs=[spec, pl.BlockSpec((levels, LANES), lambda h: (0, h))],
        out_specs=spec,
        out_shape=jax.ShapeDtypeStruct(out.shape, F32),
        input_output_aliases={0: 0},
        compiler_params=params(16),
        name="close_last_row",
    )(out, north)


def shards(
    adjoint_field,
    mixing_inverse,
    cloud_top,
    conv_frac,
    thickness,
    zonal_shift,
    zonal_frac,
    merid_courant,
    obs_kernel,
    obs_depart,
    obs_dest,
    obs_col,
    obs_count,
):
    adjoint_field, mixing_inverse, cloud_top, conv_frac, merid_courant, obs_kernel = [
        in_hbm(array)
        for array in (
            adjoint_field, mixing_inverse, cloud_top, conv_frac, merid_courant, obs_kernel
        )
    ]
    levels, row_count, col_count = adjoint_field.shape
    lat_count, lon_count = lax.axis_size("lat"), lax.axis_size("lon")
    devices = lat_count * lon_count
    sent = prepare(devices, lon_count, obs_count, obs_dest, obs_col, obs_depart, obs_kernel)
    sent, edge_source = lax.optimization_barrier((sent, adjoint_field))
    got = lax.all_to_all(
        sent.reshape(devices, SLOTS, levels), ("lat", "lon"), split_axis=0, concat_axis=0, tiled=True
    )
    westward = [((i + 1) % lon_count, i) for i in range(lon_count)]
    edge_in = lax.ppermute(edge(in_hbm(edge_source), cloud_top, conv_frac), "lon", westward)
    layer_mass = thickness.reshape(1, levels)
    field, wide = mix(adjoint_field, mixing_inverse, cloud_top, conv_frac, layer_mass)
    edge_field = mix_edge(edge_in, wide, layer_mass)
    shift, weight = in_hbm(zonal_shift.T), in_hbm(zonal_frac.T)
    rows, high, low, own_hot, edge_total, first = first_row(
        got, wide, cloud_top, conv_frac, edge_in, layer_mass, edge_field, field, merid_courant,
        shift, weight,
    )
    southward = [(i + 1, i) for i in range(lat_count - 1)]
    north = lax.ppermute(first, "lat", southward)
    out = advect(rows, high, low, own_hot, edge_total, field, merid_courant, shift, weight)
    return close(out, north)


def solution(mesh):
    in_specs = (
        P(None, "lat", "lon"),
        P("lat", None, None),
        P("lat", "lon"),
        P("lat", "lon"),
        P(),
        P(None, "lat"),
        P(None, "lat"),
        P(None, "lat", "lon"),
        P(("lat", "lon"), None),
        P(("lat", "lon")),
        P(("lat", "lon")),
        P(("lat", "lon")),
        P(("lat", "lon")),
    )
    out_specs = P(None, "lat", "lon")
    return jax.shard_map(shards, mesh=mesh, in_specs=in_specs, out_specs=out_specs, check_vma=False)
```

```python
import functools

import jax
import jax.numpy as jnp
from jax import lax
from jax.experimental import pallas as pl
from jax.experimental.pallas import tpu as pltpu
from jax.sharding import PartitionSpec as P

F32, BF16, I32 = jnp.float32, jnp.bfloat16, jnp.int32
CAP = 16
SLOTS = 40
EDGE = 64
LANES = 128
GROUP = 32
CHUNK = 256
MIB = 1024 * 1024


IN_VMEM = pl.BlockSpec(memory_space=pltpu.VMEM)


def iota(shape, dim):
    return lax.broadcasted_iota(I32, shape, dim)


def params(mib):
    return pltpu.CompilerParams(vmem_limit_bytes=mib * MIB)


def in_hbm(array):
    return pltpu.with_memory_space_constraint(array, pltpu.HBM)


def in_vmem(array):
    return pltpu.with_memory_space_constraint(array, pltpu.VMEM)


def dot(left, right):
    return jnp.dot(left, right, preferred_element_type=F32)


def dot_nt(left, right):
    return lax.dot_general(left, right, (((1,), (1,)), ((), ())), preferred_element_type=F32)


def halves(value):
    high = value.astype(BF16)
    return high, (value - high.astype(F32)).astype(BF16)


def thirds(value):
    high = value.astype(BF16)
    rest = value - high.astype(F32)
    mid = rest.astype(BF16)
    return [high, mid, (rest - mid.astype(F32)).astype(BF16)]


def as_column(line):
    return jnp.broadcast_to(line, (LANES, line.shape[1])).T


def as_wide_column(line):
    column = as_column(line)
    return jnp.concatenate([column, column], axis=1)


def convect(mixed, top, frac, layer_mass):
    inside = iota(mixed.shape, 0) < top
    total = jnp.sum(jnp.where(inside, mixed, 0.0), axis=0, keepdims=True)
    mass = jnp.sum(jnp.where(inside, layer_mass, 0.0), axis=0, keepdims=True)
    mean = total / jnp.where(mass > 0.0, mass, 1.0)
    return mixed + jnp.where(inside, frac * (layer_mass * mean - mixed), 0.0)


def prep_kernel(lon_count, count_ref, dest_ref, col_ref, depart_ref, obs_ref, out_ref):
    n = obs_ref.shape[0]
    rows = GROUP * SLOTS
    lane = iota((1, n), 1)
    live = lane < count_ref[0]
    dest = jnp.where(live, dest_ref[...], -1)
    cell = col_ref[...]
    cell_row = (cell // 256).astype(F32)
    cell_col = (cell % 256).astype(F32)
    contribution = (obs_ref[...].astype(F32) * as_column(depart_ref[...])).astype(BF16)
    local = iota((GROUP, n), 0)
    own_id = pl.program_id(0) * GROUP + local
    lon_id = own_id % lon_count
    east_id = jnp.where(lon_id == lon_count - 1, own_id - lon_id, own_id + 1)
    slots, places, left = [], [], []
    for ident, offset in ((own_id, 0), (east_id, CAP)):
        hit = dest == ident
        before = jnp.sum((live & (dest < ident)).astype(I32), axis=1, keepdims=True)
        place = lane - before
        slot = jnp.where(hit, local * SLOTS + offset + place + 1, 0)
        slots.append(jnp.sum(slot, axis=0, keepdims=True) - 1)
        places.append(jnp.sum(jnp.where(hit, place, 0), axis=0, keepdims=True))
        left.append(jnp.where(hit, cell_row, 0.0).astype(BF16))
        left.append(jnp.where(hit, cell_col, 0.0).astype(BF16))
    out_row = iota((rows, n), 0)
    pick = ((out_row == slots[0]) | (out_row == slots[1])).astype(F32).astype(BF16)
    spot = iota((LANES, n), 0)
    right = [
        (spot == 32 * kind + places[kind // 2]).astype(F32).astype(BF16) for kind in range(4)
    ]
    cells = dot_nt(jnp.concatenate(left, axis=1), jnp.concatenate(right, axis=1))
    spread = (iota((rows, GROUP), 0) == iota((rows, GROUP), 1) * SLOTS + 2 * CAP)
    spread = spread.astype(F32).astype(BF16)
    out_ref[...] = (dot(pick, contribution) + dot(spread, cells.astype(BF16))).astype(BF16)


def prepare(devices, lon_count, obs_count, obs_dest, obs_col, obs_depart, obs_kernel):
    n, levels = obs_kernel.shape
    steps = devices // GROUP
    whole = lambda shape: pl.BlockSpec(shape, lambda g: (0, 0))
    return pl.pallas_call(
        functools.partial(prep_kernel, lon_count),
        grid=(steps,),
        in_specs=[
            pl.BlockSpec(memory_space=pltpu.SMEM),
            whole((1, n)),
            whole((1, n)),
            whole((1, n)),
            whole((n, levels)),
        ],
        out_specs=pl.BlockSpec((GROUP * SLOTS, levels), lambda g: (g, 0)),
        out_shape=jax.ShapeDtypeStruct((devices * SLOTS, levels), BF16),
        compiler_params=params(16 + devices // 4),
        name="soundings_out",
    )(
        obs_count,
        in_hbm(obs_dest.reshape(1, n)),
        in_hbm(obs_col.reshape(1, n)),
        in_hbm(obs_depart.reshape(1, n)),
        obs_kernel,
    )


def pack_edge(block):
    parts = [block[:, 8 * q : 8 * q + 8, :] for q in range(4)]
    low = iota(parts[0].shape, 2) < EDGE
    pairs = [
        jnp.where(low, parts[2 * h], pltpu.roll(parts[2 * h + 1], EDGE, 2)) for h in range(2)
    ]
    return jnp.concatenate(pairs, axis=2)


def edge_kernel(field_ref, top_ref, frac_ref, out_ref):
    count = field_ref.shape[0]
    out_ref[:count] = pack_edge(field_ref[...])

    @pl.when(pl.program_id(0) == 0)
    def _():
        out_ref[count:] = pack_edge(top_ref[...].astype(F32)[None])

    @pl.when(pl.program_id(0) == 1)
    def _():
        out_ref[count:] = pack_edge(frac_ref[...][None])


def edge(adjoint_field, cloud_top, conv_frac):
    levels, row_count, _ = adjoint_field.shape
    count = levels // 2
    flat = pl.BlockSpec((row_count, LANES), lambda i: (0, 0))
    return pl.pallas_call(
        edge_kernel,
        grid=(2,),
        in_specs=[
            pl.BlockSpec((count, row_count, LANES), lambda i: (i, 0, 0)),
            flat,
            flat,
        ],
        out_specs=pl.BlockSpec((count + 1, 8, 4 * EDGE), lambda i: (i, 0, 0)),
        out_shape=pltpu.VMEM((levels + 2, 8, 4 * EDGE), F32),
        compiler_params=params(16),
        name="edge_columns",
    )(adjoint_field, cloud_top, conv_frac)


def level_rows(ref, row, first=0, count=None):
    levels = ref.shape[0]
    count = levels if count is None else count
    return ref.reshape(levels * 8, LANES)[pl.ds(8 * first + row, count, stride=8), :]


def put_columns(ref, row, value):
    count = ref.shape[0]
    flat = ref.reshape(count * 8, LANES)
    for h in range(count // LANES):
        part = value[:, h * LANES : (h + 1) * LANES].T
        flat[pl.ds(h * LANES * 8 + row, LANES, stride=8), :] = part


def mix_kernel(west_ref, east_ref, mixing_ref, top_ref, frac_ref, mass_ref, out_ref, wide_ref):
    levels = west_ref.shape[0]
    block = pl.program_id(0)
    layer_mass = as_wide_column(mass_ref[...])
    for row in range(8):
        value = jnp.concatenate([level_rows(west_ref, row), level_rows(east_ref, row)], axis=1)
        high, low = halves(value)
        mix_high, mix_low = halves(mixing_ref[row])
        here = pl.ds(pl.multiple_of((8 * block + row) * levels, levels), levels)
        wide_ref[:levels, here] = mix_high
        wide_ref[levels:, here] = mix_low
        four = jnp.concatenate([mix_high, mix_low], axis=0)
        both = dot(jnp.concatenate([four, four], axis=1), jnp.concatenate([high, low], axis=0))
        mixed = both[:levels] + both[levels:]
        done = convect(mixed, top_ref[row : row + 1, :], frac_ref[row : row + 1, :], layer_mass)
        put_columns(out_ref.at[block], row, done)


def mix(adjoint_field, mixing_inverse, cloud_top, conv_frac, layer_mass):
    levels, row_count, col_count = adjoint_field.shape
    blocks = row_count // 8
    half = lambda h: pl.BlockSpec((levels, 8, LANES), lambda b, h=h: (0, b, h))
    flat = pl.BlockSpec((8, col_count), lambda b: (b, 0))
    return pl.pallas_call(
        mix_kernel,
        grid=(blocks,),
        in_specs=[
            half(0),
            half(1),
            pl.BlockSpec((8, levels, levels), lambda b: (b, 0, 0)),
            flat,
            flat,
            pl.BlockSpec((1, levels), lambda b: (0, 0)),
        ],
        out_specs=[IN_VMEM, IN_VMEM],
        out_shape=[
            pltpu.VMEM((blocks, col_count, 8, levels), F32),
            pltpu.VMEM((2 * levels, row_count * levels), BF16),
        ],
        compiler_params=params(20),
        cost_estimate=pl.CostEstimate(
            flops=2 * levels * levels * 3 * row_count * col_count,
            bytes_accessed=12 * levels * row_count * col_count,
            transcendentals=0,
        ),
        name="mix_own",
    )(adjoint_field, adjoint_field, mixing_inverse, cloud_top, conv_frac, layer_mass)


def mix_edge_kernel(edge_ref, edge_far_ref, lines_ref, wide_ref, mass_ref, out_ref):
    levels = mass_ref.shape[1]
    width = 2 * LANES
    half = levels // 2
    layer_mass = as_wide_column(mass_ref[...])
    group = iota((levels, width), 1) // EDGE
    for row in range(8):
        halves_of = [
            jnp.concatenate(
                [level_rows(ref, row, 0, half), level_rows(ref, row, half + 1, half)], axis=0
            )
            for ref in (edge_ref, edge_far_ref)
        ]
        value = jnp.concatenate(halves_of, axis=1)
        left, right = [], []
        for q in range(4):
            cols = slice((8 * q + row) * levels, (8 * q + row + 1) * levels)
            high, low = halves(jnp.where(group == q, value, 0.0))
            left += [wide_ref[:, cols], wide_ref[:, cols]]
            right += [high, low]
        both = dot(jnp.concatenate(left, axis=1), jnp.concatenate(right, axis=0))
        mixed = both[:levels] + both[levels:]
        top = lines_ref[half, row : row + 1, :].astype(I32)
        frac = lines_ref[levels + 1, row : row + 1, :]
        put_columns(out_ref, row, convect(mixed, top, frac, layer_mass))


def mix_edge(edge_in, wide, layer_mass):
    levels = layer_mass.shape[1]
    half = lambda h: pl.BlockSpec((levels + 2, 8, LANES), lambda i, h=h: (0, 0, h))
    return pl.pallas_call(
        mix_edge_kernel,
        grid=(1,),
        in_specs=[
            half(0),
            half(1),
            IN_VMEM,
            IN_VMEM,
            pl.BlockSpec((1, levels), lambda i: (0, 0)),
        ],
        out_specs=IN_VMEM,
        out_shape=pltpu.VMEM((2 * LANES, 8, levels), F32),
        compiler_params=params(20),
        name="mix_edge",
    )(edge_in, edge_in, edge_in, wide, layer_mass)


def expand(hot, high_ref, low_ref, rows, numbers):
    right = []
    for number in numbers:
        chosen = (rows == number).astype(F32).astype(BF16)
        right.append(jnp.concatenate([high_ref[...] * chosen, low_ref[...] * chosen], axis=0))
    return dot(hot, jnp.concatenate(right, axis=1))


def soundings_kernel(
    got_ref, wide_ref, top_ref, frac_ref, lines_ref, mass_ref, edge_ref,
    field_ref, west_ref, east_ref, shift_ref, weight_ref,
    rows_ref, high_ref, low_ref, hot_ref, edge_out, first_ref,
    columns, lines_scr, tops, fracs, stack, edge_high, edge_low, edge_hot,
):
    devices = got_ref.shape[0]
    levels = mass_ref.shape[1]
    n = devices * CAP
    row_count = top_ref.shape[0]
    width = 2 * LANES
    got = got_ref[...].astype(F32)
    columns[:, :n] = got[:, :CAP].reshape(n, levels).T.astype(BF16)
    columns[:, n:] = got[:, CAP : 2 * CAP].reshape(n, levels).T.astype(BF16)
    info = got[:, 2 * CAP :].reshape(devices * 8, LANES).astype(BF16)
    first = (iota((devices, devices * 8), 1) == 8 * iota((devices, devices * 8), 0))
    info = dot(first.astype(F32).astype(BF16), info).astype(BF16)
    lines = []
    for kind in range(4):
        chosen = iota((LANES, n), 0) == iota((LANES, n), 1) % CAP + 32 * kind
        spread = dot(info, chosen.astype(F32).astype(BF16))
        mine = iota((devices, n), 0) == iota((devices, n), 1) // CAP
        lines.append(jnp.sum(jnp.where(mine, spread, 0.0), axis=0, keepdims=True))
    own_row, own_col, east_row, east_col = [line.astype(I32) for line in lines]
    near = east_col < EDGE
    packed_col = jnp.where(near, (east_row // 8) * EDGE + east_col, -1)
    packed_row = east_row % 8
    lines_scr[0:1, :n] = own_row
    lines_scr[0:1, n:] = east_row
    rows_ref[...] = as_column(own_row.astype(F32)).astype(I32)

    parts = [
        (own_col, own_row, top_ref[...].astype(F32), frac_ref[...], hot_ref, row_count, 0),
        (packed_col, packed_row, lines_ref[levels // 2], lines_ref[levels + 1], edge_hot, 8, n),
    ]
    for col, row, top, frac, hot_out, count, start in parts:
        hot = (iota((width, n), 0) == col).astype(F32).astype(BF16)
        hot_out[:, :n] = hot
        hot_out[:, n:] = hot
        table = jnp.concatenate([top.astype(BF16)] + thirds(frac), axis=0)
        found = dot(table, hot)
        here = iota((count, n), 0) == row
        found = [
            jnp.sum(jnp.where(here, found[i * count : (i + 1) * count], 0.0), axis=0, keepdims=True)
            for i in range(4)
        ]
        tops[0:1, start : start + n] = found[0].astype(I32)
        fracs[0:1, start : start + n] = (found[1] + found[2]) + found[3]

    layer_mass = as_wide_column(mass_ref[...])

    def mix_chunk(high_out, low_out, start, index, carry):
        here = pl.ds(pl.multiple_of(start + index * CHUNK, CHUNK), CHUNK)
        value = columns[:, here]
        row = lines_scr[0:1, here]
        for r in range(row_count):
            stack[r * levels : (r + 1) * levels, :] = value * (row == r).astype(F32).astype(BF16)
        both = dot(wide_ref[...], stack[...])
        mixed = both[:levels] + both[levels:]
        done = convect(mixed, tops[0:1, here], fracs[0:1, here], layer_mass)
        turned = jnp.concatenate([done[:, h * LANES : (h + 1) * LANES].T for h in range(2)], axis=0)
        high, low = halves(turned)
        place = pl.ds(pl.multiple_of(index * CHUNK, CHUNK), CHUNK)
        high_out[place, :] = high
        low_out[place, :] = low
        return carry

    chunks = n // CHUNK
    lax.fori_loop(0, chunks, functools.partial(mix_chunk, high_ref, low_ref, 0), 0)
    lax.fori_loop(0, chunks, functools.partial(mix_chunk, edge_high, edge_low, n), 0)

    rows = as_column(packed_row.astype(F32)).astype(I32)
    flat = edge_out.reshape(width * 8, LANES)
    flat_in = edge_ref.reshape(width * 8, LANES)
    for pair in range(4):
        both = expand(edge_hot[...], edge_high, edge_low, rows, (2 * pair, 2 * pair + 1))
        for i in range(2):
            here = pl.ds(2 * pair + i, width, stride=8)
            flat[here, :] = flat_in[here, :] + both[:, i * LANES : (i + 1) * LANES]

    forced = expand(hot_ref[...], high_ref, low_ref, rows_ref[...], (0,))
    own = field_ref.at[0].reshape(width * 8, LANES)[pl.ds(0, width, stride=8), :] + forced
    value = jnp.concatenate([own, flat[pl.ds(0, EDGE, stride=8), :]], axis=0)
    shift = shift_ref[0:1, :]
    weight = weight_ref[0:1, :]
    for bit in (32, 16, 8, 4, 2, 1):
        value = jnp.where((shift & bit) != 0, value[bit:], value[:-bit])
    zonal = (1.0 - weight) * value[:width] + weight * value[1 : width + 1]
    for h, courant_ref in enumerate((west_ref, east_ref)):
        here = slice(h * LANES, (h + 1) * LANES)
        first_ref[:, here] = level_rows(courant_ref, 0) * zonal[here].T


def mix_soundings(got, wide, cloud_top, conv_frac, edge_in, layer_mass, edge_field, field, courant, shift, weight):
    levels = layer_mass.shape[1]
    row_count, col_count = cloud_top.shape
    n = got.shape[0] * CAP
    width = 2 * LANES
    full = lambda array: pl.BlockSpec(array.shape, lambda s: (0,) * array.ndim)
    half = lambda h: pl.BlockSpec((levels, 8, LANES), lambda s, h=h: (0, 0, h))
    lines = pl.BlockSpec((8, levels), lambda s: (0, 0))
    return pl.pallas_call(
        soundings_kernel,
        grid=(1,),
        in_specs=[
            IN_VMEM,
            IN_VMEM,
            full(cloud_top),
            full(conv_frac),
            IN_VMEM,
            full(layer_mass),
            IN_VMEM,
            IN_VMEM,
            half(0),
            half(1),
            lines,
            lines,
        ],
        out_specs=[IN_VMEM] * 6,
        out_shape=[
            pltpu.VMEM((n, LANES), I32),
            pltpu.VMEM((n, levels), BF16),
            pltpu.VMEM((n, levels), BF16),
            pltpu.VMEM((width, 2 * n), BF16),
            pltpu.VMEM((width, 8, levels), F32),
            jax.ShapeDtypeStruct((levels, col_count), F32),
        ],
        scratch_shapes=[
            pltpu.VMEM((levels, 2 * n), BF16),
            pltpu.VMEM((8, 2 * n), I32),
            pltpu.VMEM((8, 2 * n), I32),
            pltpu.VMEM((8, 2 * n), F32),
            pltpu.VMEM((row_count * levels, CHUNK), BF16),
            pltpu.VMEM((n, levels), BF16),
            pltpu.VMEM((n, levels), BF16),
            pltpu.VMEM((width, 2 * n), BF16),
        ],
        compiler_params=params(16 + n // 128),
        name="mix_soundings",
    )(got, wide, cloud_top, conv_frac, edge_in, layer_mass, edge_field, field, courant, courant, shift, weight)


def advect_kernel(
    rows_ref, high_ref, low_ref, hot_ref, edge_ref, field_ref,
    west_ref, east_ref, shift_ref, weight_ref,
    out_ref,
    forced, coarse, out_scr, prev, sem,
):
    step = pl.program_id(0)
    blocks = pl.num_programs(0)
    block = blocks - 1 - step
    levels = high_ref.shape[1]
    width = 2 * LANES

    @pl.when(step == 0)
    def _():
        prev[...] = jnp.zeros_like(prev)

    flat = forced.reshape(width * 8, LANES)
    rows = rows_ref[...]
    for pair in range(4):
        numbers = [8 * block + 2 * pair + i for i in range(2)]
        both = expand(hot_ref[...], high_ref, low_ref, rows, numbers)
        for i in range(2):
            flat[pl.ds(2 * pair + i, width, stride=8), :] = both[:, i * LANES : (i + 1) * LANES]

    shift = shift_ref[...]
    weight = weight_ref[...]
    chosen = {bit: (shift & bit) != 0 for bit in (32, 16, 8, 4, 2, 1)}

    def choose(tiles, bit, step):
        return [
            jnp.where(chosen[bit], new, old) for old, new in zip(tiles[:-step], tiles[step:])
        ]

    def by_eights(start, carry):
        tiles = [field_ref[block, start + 8 * i] + forced[start + 8 * i] for i in range(32)]
        tiles += [edge_ref[EDGE * block + start + 8 * i] for i in range(8)]
        for bit in (32, 16, 8):
            tiles = choose(tiles, bit, bit // 8)
        for i, tile in enumerate(tiles):
            coarse[start + 8 * i] = tile
        return carry

    lax.fori_loop(0, 8, by_eights, 0)

    def by_ones(chunk, carry):
        start = chunk * 32
        tiles = [coarse[start + i] for i in range(40)]
        for bit in (4, 2, 1):
            tiles = choose(tiles, bit, bit)
        for i in range(32):
            forced[start + i] = (1.0 - weight) * tiles[i] + weight * tiles[i + 1]
        return carry

    lax.fori_loop(0, width // 32, by_ones, 0)

    later = [prev[0], prev[1]]
    for r in reversed(range(8)):
        for h, courant_ref in enumerate((west_ref, east_ref)):
            zonal = flat[pl.ds(h * LANES * 8 + r, LANES, stride=8), :].T
            courant = level_rows(courant_ref, r)
            place = out_scr.at[block, h].reshape(levels * 8, LANES)
            place[pl.ds(r, levels, stride=8), :] = (1.0 - courant) * zonal + later[h]
            later[h] = courant * zonal
    prev[0] = later[0]
    prev[1] = later[1]

    def copies(b):
        return [
            pltpu.make_async_copy(
                out_scr.at[b, h],
                out_ref.at[:, pl.ds(b * 8, 8), pl.ds(h * LANES, LANES)],
                sem.at[b, h],
            )
            for h in range(2)
        ]

    for b in range(out_scr.shape[0]):

        @pl.when(block == b)
        def _():
            for copy in copies(b):
                copy.start()

    @pl.when(step == blocks - 1)
    def _():
        for b in range(out_scr.shape[0]):
            for copy in copies(b):
                copy.wait()


def advect(rows, high, low, hot, edge_total, field, courant, shift, weight):
    blocks, col_count, _, levels = field.shape
    n = rows.shape[0]
    half = lambda h: pl.BlockSpec((levels, 8, LANES), lambda s, h=h: (0, blocks - 1 - s, h))
    lines = pl.BlockSpec((8, levels), lambda s: (blocks - 1 - s, 0))
    return pl.pallas_call(
        advect_kernel,
        grid=(blocks,),
        in_specs=[IN_VMEM] * 6 + [half(0), half(1), lines, lines],
        out_specs=pl.BlockSpec(memory_space=pl.ANY),
        out_shape=jax.ShapeDtypeStruct(courant.shape, F32),
        scratch_shapes=[
            pltpu.VMEM((col_count, 8, levels), F32),
            pltpu.VMEM((col_count + 8, 8, levels), F32),
            pltpu.VMEM((blocks, 2, levels, 8, LANES), F32),
            pltpu.VMEM((2, levels, LANES), F32),
            pltpu.SemaphoreType.DMA((blocks, 2)),
        ],
        compiler_params=params(20 + n // 128),
        cost_estimate=pl.CostEstimate(
            flops=4 * levels * 8 * blocks * n * col_count,
            bytes_accessed=12 * levels * 8 * blocks * col_count,
            transcendentals=0,
        ),
        name="advect",
    )(rows, high, low, hot, edge_total, field, courant, courant, shift, weight)


def close_kernel(out_ref, north_ref, result_ref):
    levels = out_ref.shape[0]
    result_ref[...] = out_ref[...]
    result_ref.reshape(levels * 8, LANES)[pl.ds(7, levels, stride=8), :] = (
        level_rows(out_ref, 7) + north_ref[...]
    )


def close(out, north):
    levels, row_count, col_count = out.shape
    spec = pl.BlockSpec((levels, 8, LANES), lambda h: (0, row_count // 8 - 1, h))
    return pl.pallas_call(
        close_kernel,
        grid=(col_count // LANES,),
        in_specs=[spec, pl.BlockSpec((levels, LANES), lambda h: (0, h))],
        out_specs=spec,
        out_shape=jax.ShapeDtypeStruct(out.shape, F32),
        input_output_aliases={0: 0},
        compiler_params=params(16),
        name="close_last_row",
    )(out, north)


def shards(
    adjoint_field,
    mixing_inverse,
    cloud_top,
    conv_frac,
    thickness,
    zonal_shift,
    zonal_frac,
    merid_courant,
    obs_kernel,
    obs_depart,
    obs_dest,
    obs_col,
    obs_count,
):
    adjoint_field, mixing_inverse, cloud_top, conv_frac, merid_courant, obs_kernel = [
        in_hbm(array)
        for array in (
            adjoint_field, mixing_inverse, cloud_top, conv_frac, merid_courant, obs_kernel
        )
    ]
    levels, row_count, col_count = adjoint_field.shape
    lat_count, lon_count = lax.axis_size("lat"), lax.axis_size("lon")
    devices = lat_count * lon_count
    sent = prepare(devices, lon_count, obs_count, obs_dest, obs_col, obs_depart, obs_kernel)
    sent, edge_source = lax.optimization_barrier((sent, adjoint_field))
    got = lax.all_to_all(
        sent.reshape(devices, SLOTS, levels), ("lat", "lon"), split_axis=0, concat_axis=0, tiled=True
    )
    westward = [((i + 1) % lon_count, i) for i in range(lon_count)]
    edge_in = lax.ppermute(edge(in_hbm(edge_source), cloud_top, conv_frac), "lon", westward)
    layer_mass = in_hbm(thickness.reshape(1, levels))
    field, wide = mix(adjoint_field, mixing_inverse, cloud_top, conv_frac, layer_mass)
    field, wide, edge_in = in_vmem(field), in_vmem(wide), in_vmem(edge_in)
    edge_field = in_vmem(mix_edge(edge_in, wide, layer_mass))
    shift, weight = in_hbm(zonal_shift.T), in_hbm(zonal_frac.T)
    *parts, first = mix_soundings(
        got, wide, cloud_top, conv_frac, edge_in, layer_mass, edge_field, field, merid_courant,
        shift, weight,
    )
    southward = [(i + 1, i) for i in range(lat_count - 1)]
    north = lax.ppermute(first, "lat", southward)
    out = advect(*[in_vmem(part) for part in parts], field, merid_courant, shift, weight)
    return close(out, north)


def solution(mesh):
    in_specs = (
        P(None, "lat", "lon"),
        P("lat", None, None),
        P("lat", "lon"),
        P("lat", "lon"),
        P(),
        P(None, "lat"),
        P(None, "lat"),
        P(None, "lat", "lon"),
        P(("lat", "lon"), None),
        P(("lat", "lon")),
        P(("lat", "lon")),
        P(("lat", "lon")),
        P(("lat", "lon")),
    )
    out_specs = P(None, "lat", "lon")
    return jax.shard_map(shards, mesh=mesh, in_specs=in_specs, out_specs=out_specs, check_vma=False)
```

```python
import functools

import jax
import jax.numpy as jnp
from jax import lax
from jax.experimental import pallas as pl
from jax.experimental.pallas import tpu as pltpu
from jax.sharding import PartitionSpec as P

F32, BF16, I32 = jnp.float32, jnp.bfloat16, jnp.int32
CAP = 16
SLOTS = 40
EDGE = 64
LANES = 128
GROUP = 32
EDGE_LINES = 4
SCALE = 4096.0
CHUNK = 256
MIB = 1024 * 1024


IN_VMEM = pl.BlockSpec(memory_space=pltpu.VMEM)


def iota(shape, dim):
    return lax.broadcasted_iota(I32, shape, dim)


def params(mib):
    return pltpu.CompilerParams(vmem_limit_bytes=mib * MIB)


def in_hbm(array):
    return pltpu.with_memory_space_constraint(array, pltpu.HBM)


def in_vmem(array):
    return pltpu.with_memory_space_constraint(array, pltpu.VMEM)


def dot(left, right):
    return jnp.dot(left, right, preferred_element_type=F32)


def dot_nt(left, right):
    return lax.dot_general(left, right, (((1,), (1,)), ((), ())), preferred_element_type=F32)


def halves(value):
    high = value.astype(BF16)
    return high, (value - high.astype(F32)).astype(BF16)


def thirds(value):
    high = value.astype(BF16)
    rest = value - high.astype(F32)
    mid = rest.astype(BF16)
    return [high, mid, (rest - mid.astype(F32)).astype(BF16)]


def as_column(line):
    return jnp.broadcast_to(line, (LANES, line.shape[1])).T


def as_wide_column(line):
    column = as_column(line)
    return jnp.concatenate([column, column], axis=1)


def convect(mixed, top, frac, layer_mass):
    inside = iota(mixed.shape, 0) < top
    total = jnp.sum(jnp.where(inside, mixed, 0.0), axis=0, keepdims=True)
    mass = jnp.sum(jnp.where(inside, layer_mass, 0.0), axis=0, keepdims=True)
    mean = total / jnp.where(mass > 0.0, mass, 1.0)
    return mixed + jnp.where(inside, frac * (layer_mass * mean - mixed), 0.0)


def prep_kernel(lon_count, count_ref, dest_ref, col_ref, depart_ref, obs_ref, out_ref):
    n = obs_ref.shape[0]
    rows = GROUP * SLOTS
    lane = iota((1, n), 1)
    live = lane < count_ref[0]
    dest = jnp.where(live, dest_ref[...], -1)
    cell = col_ref[...]
    cell_row = (cell // 256).astype(F32)
    cell_col = (cell % 256).astype(F32)
    contribution = (obs_ref[...].astype(F32) * as_column(depart_ref[...])).astype(BF16)
    local = iota((GROUP, n), 0)
    own_id = pl.program_id(0) * GROUP + local
    lon_id = own_id % lon_count
    east_id = jnp.where(lon_id == lon_count - 1, own_id - lon_id, own_id + 1)
    slots, places, left = [], [], []
    for ident, offset in ((own_id, 0), (east_id, CAP)):
        hit = dest == ident
        before = jnp.sum((live & (dest < ident)).astype(I32), axis=1, keepdims=True)
        place = lane - before
        slot = jnp.where(hit, local * SLOTS + offset + place + 1, 0)
        slots.append(jnp.sum(slot, axis=0, keepdims=True) - 1)
        places.append(jnp.sum(jnp.where(hit, place, 0), axis=0, keepdims=True))
        left.append(jnp.where(hit, cell_row, 0.0).astype(BF16))
        left.append(jnp.where(hit, cell_col, 0.0).astype(BF16))
    out_row = iota((rows, n), 0)
    pick = ((out_row == slots[0]) | (out_row == slots[1])).astype(F32).astype(BF16)
    spot = iota((LANES, n), 0)
    right = [
        (spot == 32 * kind + places[kind // 2]).astype(F32).astype(BF16) for kind in range(4)
    ]
    cells = dot_nt(jnp.concatenate(left, axis=1), jnp.concatenate(right, axis=1))
    spread = (iota((rows, GROUP), 0) == iota((rows, GROUP), 1) * SLOTS + 2 * CAP)
    spread = spread.astype(F32).astype(BF16)
    out_ref[...] = (dot(pick, contribution) + dot(spread, cells.astype(BF16))).astype(BF16)


def prepare(devices, lon_count, obs_count, obs_dest, obs_col, obs_depart, obs_kernel):
    n, levels = obs_kernel.shape
    steps = devices // GROUP
    whole = lambda shape: pl.BlockSpec(shape, lambda g: (0, 0))
    return pl.pallas_call(
        functools.partial(prep_kernel, lon_count),
        grid=(steps,),
        in_specs=[
            pl.BlockSpec(memory_space=pltpu.SMEM),
            whole((1, n)),
            whole((1, n)),
            whole((1, n)),
            whole((n, levels)),
        ],
        out_specs=pl.BlockSpec((GROUP * SLOTS, levels), lambda g: (g, 0)),
        out_shape=jax.ShapeDtypeStruct((devices * SLOTS, levels), BF16),
        compiler_params=params(16 + devices // 4),
        name="soundings_out",
    )(
        obs_count,
        in_hbm(obs_dest.reshape(1, n)),
        in_hbm(obs_col.reshape(1, n)),
        in_hbm(obs_depart.reshape(1, n)),
        obs_kernel,
    )


def level_rows(ref, row, count=None):
    levels = ref.shape[0]
    count = levels if count is None else count
    return ref.reshape(levels * 8, LANES)[pl.ds(row, count, stride=8), :]


def put_edge(edge_ref, block, parts):
    here = pl.ds(pl.multiple_of(block // 2 * LANES, LANES), LANES)

    @pl.when(block % 2 == 0)
    def _():
        for place, part in parts:
            edge_ref[place, :, here] = part

    @pl.when(block % 2 == 1)
    def _():
        for place, part in parts:
            low = iota(part.shape, 2) < EDGE
            edge_ref[place, :, here] = jnp.where(
                low, edge_ref[place, :, here], pltpu.roll(part, EDGE, 2)
            )


def put_columns(ref, row, value):
    count = ref.shape[0]
    flat = ref.reshape(count * 8, LANES)
    for h in range(count // LANES):
        part = value[:, h * LANES : (h + 1) * LANES].T
        flat[pl.ds(h * LANES * 8 + row, LANES, stride=8), :] = part


def mix_kernel(
    west_ref, east_ref, mixing_ref, top_ref, frac_ref, mass_ref,
    out_ref, wide_ref, edge_ref, row_ref,
):
    levels = west_ref.shape[0]
    block = pl.program_id(0)
    pieces = thirds(frac_ref[:, :LANES])
    lines = [top_ref[:, :LANES].astype(F32)] + [piece.astype(F32) for piece in pieces]
    lines[2:] = [line * SCALE for line in lines[2:]]
    places = [(slice(levels + i, levels + i + 1), line[None]) for i, line in enumerate(lines)]
    put_edge(edge_ref, block, [(slice(0, levels), west_ref[...] * SCALE)] + places)
    layer_mass = as_wide_column(mass_ref[...])
    for row in range(8):
        value = jnp.concatenate([level_rows(west_ref, row), level_rows(east_ref, row)], axis=1)
        high, low = halves(value)
        mix_high, mix_low = halves(mixing_ref[row])
        here = pl.ds(pl.multiple_of((8 * block + row) * levels, levels), levels)
        wide_ref[:levels, here] = mix_high
        wide_ref[levels:, here] = mix_low
        four = jnp.concatenate([mix_high, mix_low], axis=0)
        both = dot(jnp.concatenate([four, four], axis=1), jnp.concatenate([high, low], axis=0))
        mixed = both[:levels] + both[levels:]
        done = convect(mixed, top_ref[row : row + 1, :], frac_ref[row : row + 1, :], layer_mass)
        put_columns(out_ref.at[0], row, done)

    @pl.when(block == 0)
    def _():
        flat = out_ref.at[0].reshape(row_ref.shape[0] * 8, LANES)
        row_ref[...] = flat[pl.ds(0, row_ref.shape[0], stride=8), :]


def mix(adjoint_field, mixing_inverse, cloud_top, conv_frac, layer_mass):
    levels, row_count, col_count = adjoint_field.shape
    blocks = row_count // 8
    half = lambda h: pl.BlockSpec((levels, 8, LANES), lambda b, h=h: (0, b, h))
    flat = pl.BlockSpec((8, col_count), lambda b: (b, 0))
    return pl.pallas_call(
        mix_kernel,
        grid=(blocks,),
        in_specs=[
            half(0),
            half(1),
            pl.BlockSpec((8, levels, levels), lambda b: (b, 0, 0)),
            flat,
            flat,
            pl.BlockSpec((1, levels), lambda b: (0, 0)),
        ],
        out_specs=[
            pl.BlockSpec((1, col_count, 8, levels), lambda b: (b, 0, 0, 0)),
            IN_VMEM,
            IN_VMEM,
            IN_VMEM,
        ],
        out_shape=[
            pltpu.HBM((blocks, col_count, 8, levels), F32),
            pltpu.VMEM((2 * levels, row_count * levels), BF16),
            pltpu.VMEM((levels + EDGE_LINES, 8, 4 * EDGE), F32),
            pltpu.VMEM((col_count, levels), F32),
        ],
        compiler_params=params(20),
        cost_estimate=pl.CostEstimate(
            flops=2 * levels * levels * 3 * row_count * col_count,
            bytes_accessed=12 * levels * row_count * col_count,
            transcendentals=0,
        ),
        name="mix_own",
    )(adjoint_field, adjoint_field, mixing_inverse, cloud_top, conv_frac, layer_mass)


def mix_edge_kernel(edge_ref, edge_far_ref, lines_ref, wide_ref, mass_ref, out_ref):
    levels = mass_ref.shape[1]
    width = 2 * LANES
    layer_mass = as_wide_column(mass_ref[...])
    group = iota((levels, width), 1) // EDGE
    for row in range(8):
        value = jnp.concatenate(
            [level_rows(ref, row, levels) for ref in (edge_ref, edge_far_ref)], axis=1
        ) * (1.0 / SCALE)
        left, right = [], []
        for q in range(4):
            cols = slice((8 * q + row) * levels, (8 * q + row + 1) * levels)
            high, low = halves(jnp.where(group == q, value, 0.0))
            left += [wide_ref[:, cols], wide_ref[:, cols]]
            right += [high, low]
        both = dot(jnp.concatenate(left, axis=1), jnp.concatenate(right, axis=0))
        mixed = both[:levels] + both[levels:]
        top, frac = edge_lines(lines_ref, levels)
        done = convect(mixed, top[row : row + 1].astype(I32), frac[row : row + 1], layer_mass)
        put_columns(out_ref, row, done)


def edge_lines(ref, levels):
    top, high, mid, low = [ref[levels + i] for i in range(EDGE_LINES)]
    return top, high + (mid + low) * (1.0 / SCALE)


def mix_edge(edge_in, wide, layer_mass):
    levels = layer_mass.shape[1]
    half = lambda h: pl.BlockSpec((levels + EDGE_LINES, 8, LANES), lambda i, h=h: (0, 0, h))
    return pl.pallas_call(
        mix_edge_kernel,
        grid=(1,),
        in_specs=[
            half(0),
            half(1),
            IN_VMEM,
            IN_VMEM,
            pl.BlockSpec((1, levels), lambda i: (0, 0)),
        ],
        out_specs=IN_VMEM,
        out_shape=pltpu.VMEM((2 * LANES, 8, levels), F32),
        compiler_params=params(20),
        name="mix_edge",
    )(edge_in, edge_in, edge_in, wide, layer_mass)


def expand(hot, high_ref, low_ref, rows, numbers):
    right = []
    for number in numbers:
        chosen = (rows == number).astype(F32).astype(BF16)
        right.append(jnp.concatenate([high_ref[...] * chosen, low_ref[...] * chosen], axis=0))
    return dot(hot, jnp.concatenate(right, axis=1))


def soundings_kernel(
    got_ref, wide_ref, top_ref, frac_ref, lines_ref, mass_ref, edge_ref,
    row_ref, west_ref, east_ref, shift_ref, weight_ref,
    rows_ref, high_ref, low_ref, hot_ref, edge_out, first_ref,
    columns, lines_scr, tops, fracs, stack, edge_high, edge_low, edge_hot,
):
    devices = got_ref.shape[0]
    levels = mass_ref.shape[1]
    n = devices * CAP
    row_count = top_ref.shape[0]
    width = 2 * LANES
    got = got_ref[...].astype(F32)
    columns[:, :n] = got[:, :CAP].reshape(n, levels).T.astype(BF16)
    columns[:, n:] = got[:, CAP : 2 * CAP].reshape(n, levels).T.astype(BF16)
    info = got[:, 2 * CAP :].reshape(devices * 8, LANES).astype(BF16)
    first = (iota((devices, devices * 8), 1) == 8 * iota((devices, devices * 8), 0))
    info = dot(first.astype(F32).astype(BF16), info).astype(BF16)
    lines = []
    for kind in range(4):
        chosen = iota((LANES, n), 0) == iota((LANES, n), 1) % CAP + 32 * kind
        spread = dot(info, chosen.astype(F32).astype(BF16))
        mine = iota((devices, n), 0) == iota((devices, n), 1) // CAP
        lines.append(jnp.sum(jnp.where(mine, spread, 0.0), axis=0, keepdims=True))
    own_row, own_col, east_row, east_col = [line.astype(I32) for line in lines]
    near = east_col < EDGE
    packed_col = jnp.where(near, (east_row // 8) * EDGE + east_col, -1)
    packed_row = east_row % 8
    lines_scr[0:1, :n] = own_row
    lines_scr[0:1, n:] = east_row
    rows_ref[...] = as_column(own_row.astype(F32)).astype(I32)

    parts = [
        (own_col, own_row, top_ref[...].astype(F32), frac_ref[...], hot_ref, row_count, 0),
        (packed_col, packed_row, *edge_lines(lines_ref, levels), edge_hot, 8, n),
    ]
    for col, row, top, frac, hot_out, count, start in parts:
        hot = (iota((width, n), 0) == col).astype(F32).astype(BF16)
        hot_out[:, :n] = hot
        hot_out[:, n:] = hot
        table = jnp.concatenate([top.astype(BF16)] + thirds(frac), axis=0)
        found = dot(table, hot)
        here = iota((count, n), 0) == row
        found = [
            jnp.sum(jnp.where(here, found[i * count : (i + 1) * count], 0.0), axis=0, keepdims=True)
            for i in range(4)
        ]
        tops[0:1, start : start + n] = found[0].astype(I32)
        fracs[0:1, start : start + n] = (found[1] + found[2]) + found[3]

    layer_mass = as_wide_column(mass_ref[...])

    def mix_chunk(high_out, low_out, start, index, carry):
        here = pl.ds(pl.multiple_of(start + index * CHUNK, CHUNK), CHUNK)
        value = columns[:, here]
        row = lines_scr[0:1, here]
        for r in range(row_count):
            stack[r * levels : (r + 1) * levels, :] = value * (row == r).astype(F32).astype(BF16)
        both = dot(wide_ref[...], stack[...])
        mixed = both[:levels] + both[levels:]
        done = convect(mixed, tops[0:1, here], fracs[0:1, here], layer_mass)
        turned = jnp.concatenate([done[:, h * LANES : (h + 1) * LANES].T for h in range(2)], axis=0)
        high, low = halves(turned)
        place = pl.ds(pl.multiple_of(index * CHUNK, CHUNK), CHUNK)
        high_out[place, :] = high
        low_out[place, :] = low
        return carry

    chunks = n // CHUNK
    lax.fori_loop(0, chunks, functools.partial(mix_chunk, high_ref, low_ref, 0), 0)
    lax.fori_loop(0, chunks, functools.partial(mix_chunk, edge_high, edge_low, n), 0)

    rows = as_column(packed_row.astype(F32)).astype(I32)
    flat = edge_out.reshape(width * 8, LANES)
    flat_in = edge_ref.reshape(width * 8, LANES)
    for pair in range(4):
        both = expand(edge_hot[...], edge_high, edge_low, rows, (2 * pair, 2 * pair + 1))
        for i in range(2):
            here = pl.ds(2 * pair + i, width, stride=8)
            flat[here, :] = flat_in[here, :] + both[:, i * LANES : (i + 1) * LANES]

    forced = expand(hot_ref[...], high_ref, low_ref, rows_ref[...], (0,))
    value = jnp.concatenate([row_ref[...] + forced, flat[pl.ds(0, EDGE, stride=8), :]], axis=0)
    shift = shift_ref[0:1, :]
    weight = weight_ref[0:1, :]
    for bit in (32, 16, 8, 4, 2, 1):
        value = jnp.where((shift & bit) != 0, value[bit:], value[:-bit])
    zonal = (1.0 - weight) * value[:width] + weight * value[1 : width + 1]
    for h, courant_ref in enumerate((west_ref, east_ref)):
        here = slice(h * LANES, (h + 1) * LANES)
        first_ref[:, here] = level_rows(courant_ref, 0) * zonal[here].T


def mix_soundings(got, wide, cloud_top, conv_frac, edge_in, layer_mass, edge_field, row, courant, shift, weight):
    levels = layer_mass.shape[1]
    row_count, col_count = cloud_top.shape
    n = got.shape[0] * CAP
    width = 2 * LANES
    full = lambda array: pl.BlockSpec(array.shape, lambda s: (0,) * array.ndim)
    half = lambda h: pl.BlockSpec((levels, 8, LANES), lambda s, h=h: (0, 0, h))
    lines = pl.BlockSpec((8, levels), lambda s: (0, 0))
    return pl.pallas_call(
        soundings_kernel,
        grid=(1,),
        in_specs=[
            IN_VMEM,
            IN_VMEM,
            full(cloud_top),
            full(conv_frac),
            IN_VMEM,
            full(layer_mass),
            IN_VMEM,
            IN_VMEM,
            half(0),
            half(1),
            lines,
            lines,
        ],
        out_specs=[IN_VMEM] * 6,
        out_shape=[
            pltpu.VMEM((n, LANES), I32),
            pltpu.VMEM((n, levels), BF16),
            pltpu.VMEM((n, levels), BF16),
            pltpu.VMEM((width, 2 * n), BF16),
            pltpu.VMEM((width, 8, levels), F32),
            jax.ShapeDtypeStruct((levels, col_count), F32),
        ],
        scratch_shapes=[
            pltpu.VMEM((levels, 2 * n), BF16),
            pltpu.VMEM((8, 2 * n), I32),
            pltpu.VMEM((8, 2 * n), I32),
            pltpu.VMEM((8, 2 * n), F32),
            pltpu.VMEM((row_count * levels, CHUNK), BF16),
            pltpu.VMEM((n, levels), BF16),
            pltpu.VMEM((n, levels), BF16),
            pltpu.VMEM((width, 2 * n), BF16),
        ],
        compiler_params=params(16 + n // 128),
        name="mix_soundings",
    )(got, wide, cloud_top, conv_frac, edge_in, layer_mass, edge_field, row, courant, courant, shift, weight)


def advect_kernel(
    rows_ref, high_ref, low_ref, hot_ref, edge_ref, field_ref,
    west_ref, east_ref, shift_ref, weight_ref,
    out_ref, last_ref,
    forced, coarse, out_scr, prev, sem,
):
    step = pl.program_id(0)
    blocks = pl.num_programs(0)
    block = blocks - 1 - step
    levels = high_ref.shape[1]
    width = 2 * LANES

    @pl.when(step == 0)
    def _():
        prev[...] = jnp.zeros_like(prev)

    flat = forced.reshape(width * 8, LANES)
    rows = rows_ref[...]
    for pair in range(4):
        numbers = [8 * block + 2 * pair + i for i in range(2)]
        both = expand(hot_ref[...], high_ref, low_ref, rows, numbers)
        for i in range(2):
            flat[pl.ds(2 * pair + i, width, stride=8), :] = both[:, i * LANES : (i + 1) * LANES]

    shift = shift_ref[...]
    weight = weight_ref[...]
    chosen = {bit: (shift & bit) != 0 for bit in (32, 16, 8, 4, 2, 1)}

    def choose(tiles, bit, step):
        return [
            jnp.where(chosen[bit], new, old) for old, new in zip(tiles[:-step], tiles[step:])
        ]

    def by_eights(start, carry):
        tiles = [field_ref[0, start + 8 * i] + forced[start + 8 * i] for i in range(32)]
        tiles += [edge_ref[EDGE * block + start + 8 * i] for i in range(8)]
        for bit in (32, 16, 8):
            tiles = choose(tiles, bit, bit // 8)
        for i, tile in enumerate(tiles):
            coarse[start + 8 * i] = tile
        return carry

    lax.fori_loop(0, 8, by_eights, 0)

    def by_ones(chunk, carry):
        start = chunk * 32
        tiles = [coarse[start + i] for i in range(40)]
        for bit in (4, 2, 1):
            tiles = choose(tiles, bit, bit)
        for i in range(32):
            forced[start + i] = (1.0 - weight) * tiles[i] + weight * tiles[i + 1]
        return carry

    lax.fori_loop(0, width // 32, by_ones, 0)

    later = [prev[0], prev[1]]
    for r in reversed(range(8)):
        for h, courant_ref in enumerate((west_ref, east_ref)):
            zonal = flat[pl.ds(h * LANES * 8 + r, LANES, stride=8), :].T
            courant = level_rows(courant_ref, r)
            place = out_scr.at[block, h].reshape(levels * 8, LANES)
            value = (1.0 - courant) * zonal + later[h]
            place[pl.ds(r, levels, stride=8), :] = value
            if r == 7:

                @pl.when(step == 0)
                def _():
                    last_ref[:, h * LANES : (h + 1) * LANES] = value

            later[h] = courant * zonal
    prev[0] = later[0]
    prev[1] = later[1]

    def copies(b):
        return [
            pltpu.make_async_copy(
                out_scr.at[b, h],
                out_ref.at[:, pl.ds(b * 8, 8), pl.ds(h * LANES, LANES)],
                sem.at[b, h],
            )
            for h in range(2)
        ]

    for b in range(out_scr.shape[0]):

        @pl.when(block == b)
        def _():
            for copy in copies(b):
                copy.start()

    @pl.when(step == blocks - 1)
    def _():
        for b in range(out_scr.shape[0]):
            for copy in copies(b):
                copy.wait()


def advect(rows, high, low, hot, edge_total, field, courant, shift, weight):
    blocks, col_count, _, levels = field.shape
    n = rows.shape[0]
    half = lambda h: pl.BlockSpec((levels, 8, LANES), lambda s, h=h: (0, blocks - 1 - s, h))
    lines = pl.BlockSpec((8, levels), lambda s: (blocks - 1 - s, 0))
    return pl.pallas_call(
        advect_kernel,
        grid=(blocks,),
        in_specs=[IN_VMEM] * 5
        + [
            pl.BlockSpec((1, col_count, 8, levels), lambda s: (blocks - 1 - s, 0, 0, 0)),
            half(0),
            half(1),
            lines,
            lines,
        ],
        out_specs=[pl.BlockSpec(memory_space=pl.ANY), IN_VMEM],
        out_shape=[
            jax.ShapeDtypeStruct(courant.shape, F32),
            pltpu.VMEM((levels, col_count), F32),
        ],
        scratch_shapes=[
            pltpu.VMEM((col_count, 8, levels), F32),
            pltpu.VMEM((col_count + 8, 8, levels), F32),
            pltpu.VMEM((blocks, 2, levels, 8, LANES), F32),
            pltpu.VMEM((2, levels, LANES), F32),
            pltpu.SemaphoreType.DMA((blocks, 2)),
        ],
        compiler_params=params(20 + n // 128),
        cost_estimate=pl.CostEstimate(
            flops=4 * levels * 8 * blocks * n * col_count,
            bytes_accessed=12 * levels * 8 * blocks * col_count,
            transcendentals=0,
        ),
        name="advect",
    )(rows, high, low, hot, edge_total, field, courant, courant, shift, weight)


def close_kernel(last_ref, north_ref, _, out_ref, row, sem):
    row[...] = last_ref[...] + north_ref[...]
    copy = pltpu.make_async_copy(row, out_ref.at[:, out_ref.shape[1] - 1, :], sem)
    copy.start()
    copy.wait()


def close(out, last, north):
    in_place = pl.BlockSpec(memory_space=pl.ANY)
    return pl.pallas_call(
        close_kernel,
        in_specs=[IN_VMEM, IN_VMEM, in_place],
        out_specs=in_place,
        out_shape=jax.ShapeDtypeStruct(out.shape, F32),
        scratch_shapes=[pltpu.VMEM(last.shape, F32), pltpu.SemaphoreType.DMA],
        input_output_aliases={2: 0},
        compiler_params=params(4),
        name="close_last_row",
    )(last, north, out)


def shards(
    adjoint_field,
    mixing_inverse,
    cloud_top,
    conv_frac,
    thickness,
    zonal_shift,
    zonal_frac,
    merid_courant,
    obs_kernel,
    obs_depart,
    obs_dest,
    obs_col,
    obs_count,
):
    adjoint_field, mixing_inverse, cloud_top, conv_frac, merid_courant, obs_kernel = [
        in_hbm(array)
        for array in (
            adjoint_field, mixing_inverse, cloud_top, conv_frac, merid_courant, obs_kernel
        )
    ]
    levels, row_count, col_count = adjoint_field.shape
    lat_count, lon_count = lax.axis_size("lat"), lax.axis_size("lon")
    devices = lat_count * lon_count
    sent = prepare(devices, lon_count, obs_count, obs_dest, obs_col, obs_depart, obs_kernel)
    sent, field_after = lax.optimization_barrier((sent, adjoint_field))
    got = lax.all_to_all(
        sent.reshape(devices, SLOTS, levels), ("lat", "lon"), split_axis=0, concat_axis=0, tiled=True
    )
    westward = [((i + 1) % lon_count, i) for i in range(lon_count)]
    layer_mass = in_hbm(thickness.reshape(1, levels))
    field, wide, edge, row = mix(
        in_hbm(field_after), mixing_inverse, cloud_top, conv_frac, layer_mass
    )
    edge_in = lax.ppermute(edge.astype(jnp.float16), "lon", westward).astype(F32)
    field, wide, edge_in, row = in_hbm(field), in_vmem(wide), in_vmem(edge_in), in_vmem(row)
    edge_field = in_vmem(mix_edge(edge_in, wide, layer_mass))
    shift, weight = in_hbm(zonal_shift.T), in_hbm(zonal_frac.T)
    *parts, first = mix_soundings(
        got, wide, cloud_top, conv_frac, edge_in, layer_mass, edge_field, row, merid_courant,
        shift, weight,
    )
    southward = [(i + 1, i) for i in range(lat_count - 1)]
    north = lax.ppermute(first, "lat", southward)
    out, last = advect(*[in_vmem(part) for part in parts], field, merid_courant, shift, weight)
    return close(out, last, north)


def solution(mesh):
    in_specs = (
        P(None, "lat", "lon"),
        P("lat", None, None),
        P("lat", "lon"),
        P("lat", "lon"),
        P(),
        P(None, "lat"),
        P(None, "lat"),
        P(None, "lat", "lon"),
        P(("lat", "lon"), None),
        P(("lat", "lon")),
        P(("lat", "lon")),
        P(("lat", "lon")),
        P(("lat", "lon")),
    )
    out_specs = P(None, "lat", "lon")
    return jax.shard_map(shards, mesh=mesh, in_specs=in_specs, out_specs=out_specs, check_vma=False)
```

```python
import functools

import jax
import jax.numpy as jnp
from jax import lax
from jax.experimental import pallas as pl
from jax.experimental.pallas import tpu as pltpu
from jax.sharding import PartitionSpec as P

F32, BF16, I32 = jnp.float32, jnp.bfloat16, jnp.int32
CAP = 16
SLOTS = 40
EDGE = 64
LANES = 128
GROUP = 32
EDGE_LINES = 4
SCALE = 4096.0
WINDOW = 32
REACH = 4 * LANES // 2 + EDGE
MIB = 1024 * 1024


IN_VMEM = pl.BlockSpec(memory_space=pltpu.VMEM)


def iota(shape, dim):
    return lax.broadcasted_iota(I32, shape, dim)


def params(mib):
    return pltpu.CompilerParams(vmem_limit_bytes=mib * MIB)


def in_hbm(array):
    return pltpu.with_memory_space_constraint(array, pltpu.HBM)


def in_vmem(array):
    return pltpu.with_memory_space_constraint(array, pltpu.VMEM)


def dot(left, right):
    return jnp.dot(left, right, preferred_element_type=F32)


def dot_nt(left, right):
    return lax.dot_general(left, right, (((1,), (1,)), ((), ())), preferred_element_type=F32)


def halves(value):
    high = value.astype(BF16)
    return high, (value - high.astype(F32)).astype(BF16)


def thirds(value):
    high = value.astype(BF16)
    rest = value - high.astype(F32)
    mid = rest.astype(BF16)
    return [high, mid, (rest - mid.astype(F32)).astype(BF16)]


def as_column(line):
    return jnp.broadcast_to(line, (LANES, line.shape[1])).T


def as_wide_column(line):
    column = as_column(line)
    return jnp.concatenate([column, column], axis=1)


def convect(mixed, top, frac, layer_mass):
    inside = iota(mixed.shape, 0) < top
    total = jnp.sum(jnp.where(inside, mixed, 0.0), axis=0, keepdims=True)
    mass = jnp.sum(jnp.where(inside, layer_mass, 0.0), axis=0, keepdims=True)
    mean = total / jnp.where(mass > 0.0, mass, 1.0)
    return mixed + jnp.where(inside, frac * (layer_mass * mean - mixed), 0.0)


def prep_kernel(lon_count, count_ref, dest_ref, col_ref, depart_ref, obs_ref, out_ref):
    n = obs_ref.shape[0]
    rows = GROUP * SLOTS
    lane = iota((1, n), 1)
    live = lane < count_ref[0]
    dest = jnp.where(live, dest_ref[...], -1)
    cell = col_ref[...]
    cell_row = (cell // 256 + 1).astype(F32)
    cell_col = (cell % 256).astype(F32)
    contribution = (obs_ref[...].astype(F32) * as_column(depart_ref[...])).astype(BF16)
    local = iota((GROUP, n), 0)
    own_id = pl.program_id(0) * GROUP + local
    lon_id = own_id % lon_count
    east_id = jnp.where(lon_id == lon_count - 1, own_id - lon_id, own_id + 1)
    slots, places, left = [], [], []
    for ident, offset in ((own_id, 0), (east_id, CAP)):
        hit = dest == ident
        before = jnp.sum((live & (dest < ident)).astype(I32), axis=1, keepdims=True)
        place = lane - before
        slot = jnp.where(hit, local * SLOTS + offset + place + 1, 0)
        slots.append(jnp.sum(slot, axis=0, keepdims=True) - 1)
        places.append(jnp.sum(jnp.where(hit, place, 0), axis=0, keepdims=True))
        left.append(jnp.where(hit, cell_row, 0.0).astype(BF16))
        left.append(jnp.where(hit, cell_col, 0.0).astype(BF16))
    out_row = iota((rows, n), 0)
    pick = ((out_row == slots[0]) | (out_row == slots[1])).astype(F32).astype(BF16)
    spot = iota((LANES, n), 0)
    right = [
        (spot == 32 * kind + places[kind // 2]).astype(F32).astype(BF16) for kind in range(4)
    ]
    cells = dot_nt(jnp.concatenate(left, axis=1), jnp.concatenate(right, axis=1))
    spread = (iota((rows, GROUP), 0) == iota((rows, GROUP), 1) * SLOTS + 2 * CAP)
    spread = spread.astype(F32).astype(BF16)
    out_ref[...] = (dot(pick, contribution) + dot(spread, cells.astype(BF16))).astype(BF16)


def prepare(devices, lon_count, obs_count, obs_dest, obs_col, obs_depart, obs_kernel):
    n, levels = obs_kernel.shape
    steps = devices // GROUP
    whole = lambda shape: pl.BlockSpec(shape, lambda g: (0, 0))
    return pl.pallas_call(
        functools.partial(prep_kernel, lon_count),
        grid=(steps,),
        in_specs=[
            pl.BlockSpec(memory_space=pltpu.SMEM),
            whole((1, n)),
            whole((1, n)),
            whole((1, n)),
            whole((n, levels)),
        ],
        out_specs=pl.BlockSpec((GROUP * SLOTS, levels), lambda g: (g, 0)),
        out_shape=jax.ShapeDtypeStruct((devices * SLOTS, levels), BF16),
        compiler_params=params(16 + devices // 4),
        name="soundings_out",
    )(
        obs_count,
        in_hbm(obs_dest.reshape(1, n)),
        in_hbm(obs_col.reshape(1, n)),
        in_hbm(obs_depart.reshape(1, n)),
        obs_kernel,
    )


def level_rows(ref, row, count=None):
    levels = ref.shape[0]
    count = levels if count is None else count
    return ref.reshape(levels * 8, LANES)[pl.ds(row, count, stride=8), :]


def put_edge(edge_ref, block, parts):
    here = pl.ds(pl.multiple_of(block // 2 * LANES, LANES), LANES)

    @pl.when(block % 2 == 0)
    def _():
        for place, part in parts:
            edge_ref[place, :, here] = part

    @pl.when(block % 2 == 1)
    def _():
        for place, part in parts:
            low = iota(part.shape, 2) < EDGE
            edge_ref[place, :, here] = jnp.where(
                low, edge_ref[place, :, here], pltpu.roll(part, EDGE, 2)
            )


def put_columns(ref, row, value):
    count = ref.shape[0]
    flat = ref.reshape(count * 8, LANES)
    for h in range(count // LANES):
        part = value[:, h * LANES : (h + 1) * LANES].T
        flat[pl.ds(h * LANES * 8 + row, LANES, stride=8), :] = part


def mix_rows(field_refs, mixing_ref, top, frac, layer_mass, block, out_ref, wide_ref):
    levels = mixing_ref.shape[1]
    for row in range(8):
        value = jnp.concatenate([level_rows(ref, row) for ref in field_refs], axis=1)
        high, low = halves(value)
        mix_high, mix_low = halves(mixing_ref[row])
        here = pl.ds(pl.multiple_of((8 * block + row) * levels, levels), levels)
        wide_ref[:levels, here] = mix_high
        wide_ref[levels:, here] = mix_low
        four = jnp.concatenate([mix_high, mix_low], axis=0)
        both = dot(jnp.concatenate([four, four], axis=1), jnp.concatenate([high, low], axis=0))
        mixed = both[:levels] + both[levels:]
        done = convect(mixed, top[row : row + 1, :], frac[row : row + 1, :], layer_mass)
        put_columns(out_ref.at[0], row, done)


def mix_first_kernel(
    west_ref, east_ref, far_ref, mixing_ref, top_ref, frac_ref, mass_ref,
    out_ref, wide_ref, edge_ref, row_ref,
):
    levels = west_ref.shape[0]
    block = pl.program_id(0)
    for number, source in ((block, west_ref), (block + pl.num_programs(0), far_ref)):
        rows = pl.ds(pl.multiple_of(8 * number, 8), 8)
        pieces = thirds(frac_ref[rows, :LANES])
        lines = [top_ref[rows, :LANES].astype(F32)] + [piece.astype(F32) for piece in pieces]
        lines[2:] = [line * SCALE for line in lines[2:]]
        places = [(slice(levels + i, levels + i + 1), line[None]) for i, line in enumerate(lines)]
        put_edge(edge_ref, number, [(slice(0, levels), source[...] * SCALE)] + places)
    rows = pl.ds(pl.multiple_of(8 * block, 8), 8)
    layer_mass = as_wide_column(mass_ref[...])
    mix_rows(
        (west_ref, east_ref), mixing_ref, top_ref[rows, :], frac_ref[rows, :], layer_mass, block,
        out_ref, wide_ref,
    )

    @pl.when(block == 0)
    def _():
        flat = out_ref.at[0].reshape(row_ref.shape[0] * 8, LANES)
        row_ref[...] = flat[pl.ds(0, row_ref.shape[0], stride=8), :]


def mix_second_kernel(
    west_ref, east_ref, mixing_ref, top_ref, frac_ref, mass_ref, _, __, out_ref, wide_ref
):
    layer_mass = as_wide_column(mass_ref[...])
    block = pl.program_id(0) + pl.num_programs(0)
    mix_rows(
        (west_ref, east_ref), mixing_ref, top_ref[...], frac_ref[...], layer_mass, block,
        out_ref, wide_ref,
    )


def mix(adjoint_field, mixing_inverse, cloud_top, conv_frac, layer_mass):
    levels, row_count, col_count = adjoint_field.shape
    blocks = row_count // 8
    steps = blocks // 2
    half = lambda h, skip: pl.BlockSpec((levels, 8, LANES), lambda b: (0, b + skip, h))
    mixing = lambda skip: pl.BlockSpec((8, levels, levels), lambda b: (b + skip, 0, 0))
    mass = pl.BlockSpec((1, levels), lambda b: (0, 0))
    whole = pl.BlockSpec((row_count, col_count), lambda b: (0, 0))
    flat = pl.BlockSpec((8, col_count), lambda b: (b + steps, 0))
    mixed = lambda skip: pl.BlockSpec((1, col_count, 8, levels), lambda b: (b + skip, 0, 0, 0))
    results = [
        pltpu.HBM((blocks, col_count, 8, levels), F32),
        pltpu.VMEM((2 * levels, row_count * levels), BF16),
    ]
    cost = pl.CostEstimate(
        flops=levels * levels * 4 * row_count * col_count,
        bytes_accessed=6 * levels * row_count * col_count,
        transcendentals=0,
    )
    field, wide, edge, row = pl.pallas_call(
        mix_first_kernel,
        grid=(steps,),
        in_specs=[half(0, 0), half(1, 0), half(0, steps), mixing(0), whole, whole, mass],
        out_specs=[mixed(0), IN_VMEM, IN_VMEM, IN_VMEM],
        out_shape=results
        + [
            pltpu.VMEM((levels + EDGE_LINES, 8, 4 * EDGE), F32),
            pltpu.VMEM((col_count, levels), F32),
        ],
        compiler_params=params(20),
        cost_estimate=cost,
        name="mix_first",
    )(adjoint_field, adjoint_field, adjoint_field, mixing_inverse, cloud_top, conv_frac, layer_mass)
    field, wide = pl.pallas_call(
        mix_second_kernel,
        grid=(steps,),
        in_specs=[half(0, steps), half(1, steps), mixing(steps), flat, flat, mass]
        + [pl.BlockSpec(memory_space=pl.ANY), IN_VMEM],
        out_specs=[mixed(steps), IN_VMEM],
        out_shape=results,
        input_output_aliases={6: 0, 7: 1},
        compiler_params=params(20),
        cost_estimate=cost,
        name="mix_second",
    )(
        adjoint_field, adjoint_field, mixing_inverse, cloud_top, conv_frac, layer_mass,
        in_hbm(field), in_vmem(wide),
    )
    return in_hbm(field), in_vmem(wide), edge, in_vmem(row)


def mix_edge(edge_refs, lines_ref, wide_ref, layer_mass, out_ref):
    levels = layer_mass.shape[0]
    group = iota((levels, 2 * LANES), 1) // EDGE
    top, frac = edge_lines(lines_ref, levels)
    for row in range(8):
        value = jnp.concatenate([level_rows(ref, row, levels) for ref in edge_refs], axis=1)
        value = value * (1.0 / SCALE)
        left, right = [], []
        for q in range(4):
            cols = slice((8 * q + row) * levels, (8 * q + row + 1) * levels)
            high, low = halves(jnp.where(group == q, value, 0.0))
            left += [wide_ref[:, cols], wide_ref[:, cols]]
            right += [high, low]
        both = dot(jnp.concatenate(left, axis=1), jnp.concatenate(right, axis=0))
        mixed = both[:levels] + both[levels:]
        done = convect(mixed, top[row : row + 1].astype(I32), frac[row : row + 1], layer_mass)
        put_columns(out_ref, row, done)


def edge_lines(ref, levels):
    top, high, mid, low = [ref[levels + i] for i in range(EDGE_LINES)]
    return top, high + (mid + low) * (1.0 / SCALE)


def find_places(row, row_count):
    count = row.shape[1]
    upto = (iota((LANES, LANES), 0) <= iota((LANES, LANES), 1)).astype(F32).astype(BF16)
    before = jnp.zeros((row_count, 1), F32)
    places = []
    for start in range(0, count, LANES):
        mine = iota((row_count, LANES), 0) == row[:, start : start + LANES]
        running = dot(mine.astype(F32).astype(BF16), upto)
        place = jnp.sum(jnp.where(mine, running + before, 0.0), axis=0, keepdims=True) - 1.0
        places.append(place.astype(I32))
        before = before + running[:, LANES - 1 :]
    return jnp.concatenate(places, axis=1), jnp.max(before)


def force_rows(block, rounds, place_ref, split_ref, source_ref, wide_ref, mass, square, out_ref):
    levels = mass.shape[1]
    slots = 8 * WINDOW
    row = place_ref[0:1, :] - 8 * block
    place = place_ref[1:2, :]
    flat = out_ref.reshape(REACH * 8, LANES)

    def one_round(index, add):
        here = place - index * WINDOW
        used = (row >= 0) & (row < 8) & (here >= 0) & (here < WINDOW)
        slot = jnp.where(used, row * WINDOW + here, -1)
        pick = (iota((slots, slot.shape[1]), 0) == slot).astype(F32).astype(BF16)
        picked = dot(pick, source_ref[...])
        split = dot_nt(split_ref[...], pick)
        column = (split[0:1] * EDGE + split[1:2]).astype(I32)
        parts = []
        for r in range(8):
            mixing = wide_ref[:, pl.ds(pl.multiple_of((8 * block + r) * levels, levels), levels)]
            both = dot_nt(picked[r * WINDOW : (r + 1) * WINDOW, :levels].astype(BF16), mixing)
            parts.append(both[:, :levels] + both[:, levels:])
        mixed = jnp.concatenate(parts, axis=0)
        cell = picked[:, levels:]
        frac = (cell[:, 1:2] + cell[:, 2:3]) + cell[:, 3:4]
        inside = iota(mixed.shape, 1).astype(F32) < cell[:, 0:1]
        total = jnp.sum(jnp.where(inside, mixed, 0.0), axis=1, keepdims=True)
        weight = jnp.sum(jnp.where(inside, mass, 0.0), axis=1, keepdims=True)
        mean = total / jnp.where(weight > 0.0, weight, 1.0)
        high, low = halves(mixed + jnp.where(inside, frac * (mass * mean - mixed), 0.0))
        hot = (iota((REACH, slots), 0) == column).astype(F32).astype(BF16)
        for group in range(2):
            for r in range(4):
                source = slice((4 * group + r) * WINDOW, (4 * group + r + 1) * WINDOW)
                target = slice(r * levels, (r + 1) * levels)
                square[r * WINDOW : (r + 1) * WINDOW, target] = high[source]
                square[(4 + r) * WINDOW : (5 + r) * WINDOW, target] = low[source]
            left = hot[:, 4 * group * WINDOW : 4 * (group + 1) * WINDOW]
            found = dot(jnp.concatenate([left, left], axis=1), square[...])
            for r in range(4):
                rows = pl.ds(4 * group + r, REACH, stride=8)
                part = found[:, r * levels : (r + 1) * levels]
                flat[rows, :] = flat[rows, :] + part if add else part

    one_round(0, False)

    def more(index, carry):
        one_round(index, True)
        return carry

    lax.fori_loop(1, rounds, more, 0)


def soundings_kernel(
    got_ref, wide_ref, top_ref, frac_ref, near_ref, far_ref, lines_ref, mass_ref,
    row_ref, west_ref, east_ref, shift_ref, weight_ref,
    place_ref, split_ref, source_ref, edge_out, rounds_ref, first_ref,
    forced, square,
):
    devices = got_ref.shape[0]
    levels = mass_ref.shape[1]
    n = devices * CAP
    row_count = top_ref.shape[0]
    width = 2 * LANES
    mix_edge((near_ref, far_ref), lines_ref, wide_ref, as_wide_column(mass_ref[...]), edge_out)

    got = got_ref[...].astype(F32)
    source_ref[:n, :levels] = got[:, :CAP].reshape(n, levels).astype(BF16)
    source_ref[n:, :levels] = got[:, CAP : 2 * CAP].reshape(n, levels).astype(BF16)
    info = got[:, 2 * CAP :].reshape(devices * 8, LANES).astype(BF16)
    first = iota((devices, devices * 8), 1) == 8 * iota((devices, devices * 8), 0)
    info = dot(first.astype(F32).astype(BF16), info).astype(BF16)
    lines = []
    for kind in range(4):
        chosen = iota((LANES, n), 0) == iota((LANES, n), 1) % CAP + 32 * kind
        spread = dot(info, chosen.astype(F32).astype(BF16))
        mine = iota((devices, n), 0) == iota((devices, n), 1) // CAP
        lines.append(jnp.sum(jnp.where(mine, spread, 0.0), axis=0, keepdims=True))
    own_row, own_col, east_row, east_col = [line.astype(I32) for line in lines]
    own_row, east_row = own_row - 1, east_row - 1
    east_row = jnp.where(east_col < EDGE, east_row, -1)
    row = jnp.concatenate([own_row, east_row], axis=1)
    place, most = find_places(row, row_count)
    rounds = (most.astype(I32) + (WINDOW - 1)) // WINDOW
    rounds_ref[0] = rounds
    place_ref[0:1] = row
    place_ref[1:2] = place
    place_ref[2:] = jnp.zeros((6, 2 * n), I32)
    column = jnp.concatenate([own_col, width + east_col], axis=1)
    split = [(column // EDGE).astype(F32), (column % EDGE).astype(F32), jnp.zeros((6, 2 * n), F32)]
    split_ref[...] = jnp.concatenate(split, axis=0).astype(BF16)

    packed_col = (east_row // 8) * EDGE + east_col
    parts = [
        (own_col, own_row, top_ref[...].astype(F32), frac_ref[...], row_count),
        (packed_col, east_row % 8, *edge_lines(lines_ref, levels), 8),
    ]
    cells = []
    for col, row, top, frac, count in parts:
        hot = (iota((width, n), 0) == col).astype(F32).astype(BF16)
        table = jnp.concatenate([top.astype(BF16)] + thirds(frac), axis=0)
        found = dot(table, hot)
        here = iota((count, n), 0) == row
        found = [
            jnp.sum(jnp.where(here, found[i * count : (i + 1) * count], 0.0), axis=0, keepdims=True)
            for i in range(4)
        ]
        cells.append(jnp.concatenate(found + [jnp.zeros((LANES - 4, n), F32)], axis=0).T)
    source_ref[:n, levels:] = cells[0].astype(BF16)
    source_ref[n:, levels:] = cells[1].astype(BF16)

    square[...] = jnp.zeros_like(square)
    force_rows(
        0, rounds, place_ref, split_ref, source_ref, wide_ref, mass_ref[...], square, forced
    )
    edge = edge_out.reshape(width * 8, LANES)[pl.ds(0, EDGE, stride=8), :]
    value = jnp.concatenate([row_ref[...], edge], axis=0)
    value = value + forced.reshape(REACH * 8, LANES)[pl.ds(0, REACH, stride=8), :]
    shift = shift_ref[0:1, :]
    weight = weight_ref[0:1, :]
    for bit in (32, 16, 8, 4, 2, 1):
        value = jnp.where((shift & bit) != 0, value[bit:], value[:-bit])
    zonal = (1.0 - weight) * value[:width] + weight * value[1 : width + 1]
    for h, courant_ref in enumerate((west_ref, east_ref)):
        here = slice(h * LANES, (h + 1) * LANES)
        first_ref[:, here] = level_rows(courant_ref, 0) * zonal[here].T


def take_soundings(got, wide, cloud_top, conv_frac, edge_in, layer_mass, row, courant, shift, weight):
    levels = layer_mass.shape[1]
    row_count, col_count = cloud_top.shape
    n = got.shape[0] * CAP
    width = 2 * LANES
    full = lambda array: pl.BlockSpec(array.shape, lambda s: (0,) * array.ndim)
    edge_half = lambda h: pl.BlockSpec((levels + EDGE_LINES, 8, LANES), lambda s: (0, 0, h))
    half = lambda h: pl.BlockSpec((levels, 8, LANES), lambda s: (0, 0, h))
    lines = pl.BlockSpec((8, levels), lambda s: (0, 0))
    return pl.pallas_call(
        soundings_kernel,
        grid=(1,),
        in_specs=[
            IN_VMEM,
            IN_VMEM,
            full(cloud_top),
            full(conv_frac),
            edge_half(0),
            edge_half(1),
            IN_VMEM,
            full(layer_mass),
            IN_VMEM,
            half(0),
            half(1),
            lines,
            lines,
        ],
        out_specs=[IN_VMEM] * 4 + [pl.BlockSpec(memory_space=pltpu.SMEM), IN_VMEM],
        out_shape=[
            pltpu.VMEM((8, 2 * n), I32),
            pltpu.VMEM((8, 2 * n), BF16),
            pltpu.VMEM((2 * n, 2 * levels), BF16),
            pltpu.VMEM((width, 8, levels), F32),
            jax.ShapeDtypeStruct((1,), I32),
            jax.ShapeDtypeStruct((levels, col_count), F32),
        ],
        scratch_shapes=[
            pltpu.VMEM((REACH, 8, levels), F32),
            pltpu.VMEM((8 * WINDOW, 4 * levels), BF16),
        ],
        compiler_params=params(20 + n // 128),
        name="take_soundings",
    )(
        got, wide, cloud_top, conv_frac, edge_in, edge_in, edge_in, layer_mass, row, courant,
        courant, shift, weight,
    )


def advect_kernel(
    place_ref, split_ref, source_ref, edge_ref, rounds_ref, wide_ref, field_ref, mass_ref,
    west_ref, east_ref, shift_ref, weight_ref,
    out_ref, last_ref,
    forced, coarse, square, out_scr, prev, sem,
):
    step = pl.program_id(0)
    blocks = pl.num_programs(0)
    block = blocks - 1 - step
    levels = mass_ref.shape[1]
    width = 2 * LANES

    @pl.when(step == 0)
    def _():
        prev[...] = jnp.zeros_like(prev)
        square[...] = jnp.zeros_like(square)

    force_rows(
        block, rounds_ref[0], place_ref, split_ref, source_ref, wide_ref, mass_ref[...], square,
        forced,
    )
    shift = shift_ref[...]
    weight = weight_ref[...]
    chosen = {bit: (shift & bit) != 0 for bit in (32, 16, 8, 4, 2, 1)}

    def choose(tiles, bit, step):
        return [
            jnp.where(chosen[bit], new, old) for old, new in zip(tiles[:-step], tiles[step:])
        ]

    def by_eights(start, carry):
        tiles = [field_ref[0, start + 8 * i] + forced[start + 8 * i] for i in range(32)]
        tiles += [
            edge_ref[EDGE * block + start + 8 * i] + forced[width + start + 8 * i] for i in range(8)
        ]
        for bit in (32, 16, 8):
            tiles = choose(tiles, bit, bit // 8)
        for i, tile in enumerate(tiles):
            coarse[start + 8 * i] = tile
        return carry

    lax.fori_loop(0, 8, by_eights, 0)

    def by_ones(chunk, carry):
        start = chunk * 32
        tiles = [coarse[start + i] for i in range(40)]
        for bit in (4, 2, 1):
            tiles = choose(tiles, bit, bit)
        for i in range(32):
            forced[start + i] = (1.0 - weight) * tiles[i] + weight * tiles[i + 1]
        return carry

    lax.fori_loop(0, width // 32, by_ones, 0)

    flat = forced.reshape(REACH * 8, LANES)
    later = [prev[0], prev[1]]
    for r in reversed(range(8)):
        for h, courant_ref in enumerate((west_ref, east_ref)):
            zonal = flat[pl.ds(h * LANES * 8 + r, LANES, stride=8), :].T
            courant = level_rows(courant_ref, r)
            place = out_scr.at[block, h].reshape(levels * 8, LANES)
            value = (1.0 - courant) * zonal + later[h]
            place[pl.ds(r, levels, stride=8), :] = value
            if r == 7:

                @pl.when(step == 0)
                def _():
                    last_ref[:, h * LANES : (h + 1) * LANES] = value

            later[h] = courant * zonal
    prev[0] = later[0]
    prev[1] = later[1]

    def copies(b):
        return [
            pltpu.make_async_copy(
                out_scr.at[b, h],
                out_ref.at[:, pl.ds(b * 8, 8), pl.ds(h * LANES, LANES)],
                sem.at[b, h],
            )
            for h in range(2)
        ]

    for b in range(out_scr.shape[0]):

        @pl.when(block == b)
        def _():
            for copy in copies(b):
                copy.start()

    @pl.when(step == blocks - 1)
    def _():
        for b in range(out_scr.shape[0]):
            for copy in copies(b):
                copy.wait()


def advect(place, split, source, edge_field, rounds, wide, field, layer_mass, courant, shift, weight):
    blocks, col_count, _, levels = field.shape
    n = place.shape[1] // 2
    half = lambda h: pl.BlockSpec((levels, 8, LANES), lambda s: (0, blocks - 1 - s, h))
    lines = pl.BlockSpec((8, levels), lambda s: (blocks - 1 - s, 0))
    return pl.pallas_call(
        advect_kernel,
        grid=(blocks,),
        in_specs=[IN_VMEM] * 4
        + [
            pl.BlockSpec(memory_space=pltpu.SMEM),
            IN_VMEM,
            pl.BlockSpec((1, col_count, 8, levels), lambda s: (blocks - 1 - s, 0, 0, 0)),
            pl.BlockSpec((1, levels), lambda s: (0, 0)),
            half(0),
            half(1),
            lines,
            lines,
        ],
        out_specs=[pl.BlockSpec(memory_space=pl.ANY), IN_VMEM],
        out_shape=[
            jax.ShapeDtypeStruct(courant.shape, F32),
            pltpu.VMEM((levels, col_count), F32),
        ],
        scratch_shapes=[
            pltpu.VMEM((REACH, 8, levels), F32),
            pltpu.VMEM((col_count + 8, 8, levels), F32),
            pltpu.VMEM((8 * WINDOW, 4 * levels), BF16),
            pltpu.VMEM((blocks, 2, levels, 8, LANES), F32),
            pltpu.VMEM((2, levels, LANES), F32),
            pltpu.SemaphoreType.DMA((blocks, 2)),
        ],
        compiler_params=params(24 + n // 128),
        cost_estimate=pl.CostEstimate(
            flops=2 * levels * 8 * blocks * n * col_count,
            bytes_accessed=12 * levels * 8 * blocks * col_count,
            transcendentals=0,
        ),
        name="advect",
    )(
        place, split, source, edge_field, rounds, wide, field, layer_mass, courant, courant, shift,
        weight,
    )


def close_kernel(last_ref, north_ref, _, out_ref, row, sem):
    row[...] = last_ref[...] + north_ref[...]
    copy = pltpu.make_async_copy(row, out_ref.at[:, out_ref.shape[1] - 1, :], sem)
    copy.start()
    copy.wait()


def close(out, last, north):
    in_place = pl.BlockSpec(memory_space=pl.ANY)
    return pl.pallas_call(
        close_kernel,
        in_specs=[IN_VMEM, IN_VMEM, in_place],
        out_specs=in_place,
        out_shape=jax.ShapeDtypeStruct(out.shape, F32),
        scratch_shapes=[pltpu.VMEM(last.shape, F32), pltpu.SemaphoreType.DMA],
        input_output_aliases={2: 0},
        compiler_params=params(4),
        name="close_last_row",
    )(last, north, out)


def shards(
    adjoint_field,
    mixing_inverse,
    cloud_top,
    conv_frac,
    thickness,
    zonal_shift,
    zonal_frac,
    merid_courant,
    obs_kernel,
    obs_depart,
    obs_dest,
    obs_col,
    obs_count,
):
    adjoint_field, mixing_inverse, cloud_top, conv_frac, merid_courant, obs_kernel = [
        in_hbm(array)
        for array in (
            adjoint_field, mixing_inverse, cloud_top, conv_frac, merid_courant, obs_kernel
        )
    ]
    levels, row_count, col_count = adjoint_field.shape
    lat_count, lon_count = lax.axis_size("lat"), lax.axis_size("lon")
    devices = lat_count * lon_count
    sent = prepare(devices, lon_count, obs_count, obs_dest, obs_col, obs_depart, obs_kernel)
    sent, field_after = lax.optimization_barrier((sent, adjoint_field))
    got = lax.all_to_all(
        sent.reshape(devices, SLOTS, levels), ("lat", "lon"), split_axis=0, concat_axis=0, tiled=True
    )
    westward = [((i + 1) % lon_count, i) for i in range(lon_count)]
    layer_mass = in_hbm(thickness.reshape(1, levels))
    field, wide, edge, row = mix(
        in_hbm(field_after), mixing_inverse, cloud_top, conv_frac, layer_mass
    )
    edge_in = in_vmem(lax.ppermute(edge.astype(jnp.float16), "lon", westward).astype(F32))
    shift, weight = in_hbm(zonal_shift.T), in_hbm(zonal_frac.T)
    place, split, source, edge_field, rounds, first = take_soundings(
        got, wide, cloud_top, conv_frac, edge_in, layer_mass, row, merid_courant, shift, weight
    )
    southward = [(i + 1, i) for i in range(lat_count - 1)]
    north = lax.ppermute(first, "lat", southward)
    out, last = advect(
        in_vmem(place), in_vmem(split), in_vmem(source), in_vmem(edge_field), rounds, wide, field,
        layer_mass, merid_courant, shift, weight,
    )
    return close(out, last, north)


def solution(mesh):
    in_specs = (
        P(None, "lat", "lon"),
        P("lat", None, None),
        P("lat", "lon"),
        P("lat", "lon"),
        P(),
        P(None, "lat"),
        P(None, "lat"),
        P(None, "lat", "lon"),
        P(("lat", "lon"), None),
        P(("lat", "lon")),
        P(("lat", "lon")),
        P(("lat", "lon")),
        P(("lat", "lon")),
    )
    out_specs = P(None, "lat", "lon")
    return jax.shard_map(shards, mesh=mesh, in_specs=in_specs, out_specs=out_specs, check_vma=False)
```

```python
import functools

import jax
import jax.numpy as jnp
from jax import lax
from jax.experimental import pallas as pl
from jax.experimental.pallas import tpu as pltpu
from jax.sharding import PartitionSpec as P

F32, BF16, I32 = jnp.float32, jnp.bfloat16, jnp.int32
CAP = 16
SLOTS = 40
EDGE = 64
LANES = 128
GROUP = 32
EDGE_LINES = 4
SCALE = 4096.0
WINDOW = 32
REACH = 2 * LANES + EDGE
PITCH = 4096
CELL_LINES = 16
MIB = 1024 * 1024


IN_VMEM = pl.BlockSpec(memory_space=pltpu.VMEM)


def iota(shape, dim):
    return lax.broadcasted_iota(I32, shape, dim)


def params(mib):
    return pltpu.CompilerParams(vmem_limit_bytes=mib * MIB)


def in_hbm(array):
    return pltpu.with_memory_space_constraint(array, pltpu.HBM)


def in_vmem(array):
    return pltpu.with_memory_space_constraint(array, pltpu.VMEM)


def dot(left, right):
    return jnp.dot(left, right, preferred_element_type=F32)


def dot_nt(left, right):
    return lax.dot_general(left, right, (((1,), (1,)), ((), ())), preferred_element_type=F32)


def halves(value):
    high = value.astype(BF16)
    return high, (value - high.astype(F32)).astype(BF16)


def thirds(value):
    high = value.astype(BF16)
    rest = value - high.astype(F32)
    mid = rest.astype(BF16)
    return [high, mid, (rest - mid.astype(F32)).astype(BF16)]


def as_column(line):
    return jnp.broadcast_to(line, (LANES, line.shape[1])).T


def as_wide_column(line):
    column = as_column(line)
    return jnp.concatenate([column, column], axis=1)


def convect(mixed, top, frac, layer_mass):
    inside = iota(mixed.shape, 0) < top
    total = jnp.sum(jnp.where(inside, mixed, 0.0), axis=0, keepdims=True)
    mass = jnp.sum(jnp.where(inside, layer_mass, 0.0), axis=0, keepdims=True)
    mean = total / jnp.where(mass > 0.0, mass, 1.0)
    return mixed + jnp.where(inside, frac * (layer_mass * mean - mixed), 0.0)


def prep_kernel(lon_count, count_ref, dest_ref, col_ref, depart_ref, obs_ref, out_ref):
    n = obs_ref.shape[0]
    rows = GROUP * SLOTS
    lane = iota((1, n), 1)
    live = lane < count_ref[0]
    dest = jnp.where(live, dest_ref[...], -1)
    cell = col_ref[...]
    cell_row = (cell // 256 + 1).astype(F32)
    cell_col = (cell % 256).astype(F32)
    contribution = (obs_ref[...].astype(F32) * as_column(depart_ref[...])).astype(BF16)
    local = iota((GROUP, n), 0)
    own_id = pl.program_id(0) * GROUP + local
    lon_id = own_id % lon_count
    east_id = jnp.where(lon_id == lon_count - 1, own_id - lon_id, own_id + 1)
    slots, places, left = [], [], []
    for ident, offset in ((own_id, 0), (east_id, CAP)):
        hit = dest == ident
        before = jnp.sum((live & (dest < ident)).astype(I32), axis=1, keepdims=True)
        place = lane - before
        slot = jnp.where(hit, local * SLOTS + offset + place + 1, 0)
        slots.append(jnp.sum(slot, axis=0, keepdims=True) - 1)
        places.append(jnp.sum(jnp.where(hit, place, 0), axis=0, keepdims=True))
        left.append(jnp.where(hit, cell_row, 0.0).astype(BF16))
        left.append(jnp.where(hit, cell_col, 0.0).astype(BF16))
    out_row = iota((rows, n), 0)
    pick = ((out_row == slots[0]) | (out_row == slots[1])).astype(F32).astype(BF16)
    spot = iota((LANES, n), 0)
    right = [
        (spot == 32 * kind + places[kind // 2]).astype(F32).astype(BF16) for kind in range(4)
    ]
    cells = dot_nt(jnp.concatenate(left, axis=1), jnp.concatenate(right, axis=1))
    spread = (iota((rows, GROUP), 0) == iota((rows, GROUP), 1) * SLOTS + 2 * CAP)
    spread = spread.astype(F32).astype(BF16)
    out_ref[...] = (dot(pick, contribution) + dot(spread, cells.astype(BF16))).astype(BF16)


def prepare(devices, lon_count, obs_count, obs_dest, obs_col, obs_depart, obs_kernel):
    n, levels = obs_kernel.shape
    steps = devices // GROUP
    whole = lambda shape: pl.BlockSpec(shape, lambda g: (0, 0))
    return pl.pallas_call(
        functools.partial(prep_kernel, lon_count),
        grid=(steps,),
        in_specs=[
            pl.BlockSpec(memory_space=pltpu.SMEM),
            whole((1, n)),
            whole((1, n)),
            whole((1, n)),
            whole((n, levels)),
        ],
        out_specs=pl.BlockSpec((GROUP * SLOTS, levels), lambda g: (g, 0)),
        out_shape=jax.ShapeDtypeStruct((devices * SLOTS, levels), BF16),
        compiler_params=params(16 + devices // 4),
        name="soundings_out",
    )(
        obs_count,
        in_hbm(obs_dest.reshape(1, n)),
        in_hbm(obs_col.reshape(1, n)),
        in_hbm(obs_depart.reshape(1, n)),
        obs_kernel,
    )


def level_rows(ref, row, count=None):
    levels = ref.shape[0]
    count = levels if count is None else count
    return ref.reshape(levels * 8, LANES)[pl.ds(row, count, stride=8), :]


def pack_edge(block):
    parts = [block[:, 8 * q : 8 * q + 8, :] for q in range(4)]
    low = iota(parts[0].shape, 2) < EDGE
    pairs = [
        jnp.where(low, parts[2 * h], pltpu.roll(parts[2 * h + 1], EDGE, 2)) for h in range(2)
    ]
    return jnp.concatenate(pairs, axis=2)


def edge_kernel(field_ref, top_ref, frac_ref, out_ref):
    step = pl.program_id(0)
    count = field_ref.shape[0]
    here = pl.ds(pl.multiple_of(step * count, count), count)
    out_ref[here] = pack_edge(field_ref[...]) * SCALE

    @pl.when(step == 0)
    def _():
        pieces = thirds(frac_ref[...])
        lines = [top_ref[...].astype(F32)] + [piece.astype(F32) for piece in pieces]
        lines[2:] = [line * SCALE for line in lines[2:]]
        first = out_ref.shape[0] - EDGE_LINES
        for i, line in enumerate(lines):
            out_ref[first + i : first + i + 1] = pack_edge(line[None])


def edge_columns(adjoint_field, cloud_top, conv_frac):
    levels, row_count, _ = adjoint_field.shape
    flat = pl.BlockSpec((row_count, LANES), lambda i: (0, 0))
    return pl.pallas_call(
        edge_kernel,
        grid=(2,),
        in_specs=[pl.BlockSpec((levels // 2, row_count, LANES), lambda i: (i, 0, 0)), flat, flat],
        out_specs=IN_VMEM,
        out_shape=pltpu.VMEM((levels + EDGE_LINES, 8, 4 * EDGE), F32),
        compiler_params=params(16),
        cost_estimate=pl.CostEstimate(
            flops=levels * levels * 4 * row_count * LANES,
            bytes_accessed=12 * levels * row_count * LANES,
            transcendentals=0,
        ),
        name="edge_columns",
    )(adjoint_field, cloud_top, conv_frac)


def put_columns(ref, row, value):
    count = ref.shape[0]
    flat = ref.reshape(count * 8, LANES)
    for h in range(count // LANES):
        part = value[:, h * LANES : (h + 1) * LANES].T
        flat[pl.ds(h * LANES * 8 + row, LANES, stride=8), :] = part


def mix_rows(field_refs, mixing_ref, top, frac, layer_mass, block, out_ref, wide_ref):
    levels = mixing_ref.shape[1]
    for row in range(8):
        value = jnp.concatenate([level_rows(ref, row) for ref in field_refs], axis=1)
        high, low = halves(value)
        mix_high, mix_low = halves(mixing_ref[row])
        here = pl.ds(pl.multiple_of((8 * block + row) * levels, levels), levels)
        wide_ref[:levels, here] = mix_high
        wide_ref[levels:, here] = mix_low
        four = jnp.concatenate([mix_high, mix_low], axis=0)
        both = dot(jnp.concatenate([four, four], axis=1), jnp.concatenate([high, low], axis=0))
        mixed = both[:levels] + both[levels:]
        done = convect(mixed, top[row : row + 1, :], frac[row : row + 1, :], layer_mass)
        put_columns(out_ref.at[0], row, done)


def mix_kernel(
    west_ref, east_ref, mixing_ref, top_ref, frac_ref, mass_ref, out_ref, wide_ref, row_ref
):
    layer_mass = as_wide_column(mass_ref[...])
    block = pl.program_id(0)
    mix_rows(
        (west_ref, east_ref), mixing_ref, top_ref[...], frac_ref[...], layer_mass, block,
        out_ref, wide_ref,
    )

    @pl.when(block == 0)
    def _():
        flat = out_ref.at[0].reshape(row_ref.shape[0] * 8, LANES)
        row_ref[...] = flat[pl.ds(0, row_ref.shape[0], stride=8), :]


def mix(adjoint_field, mixing_inverse, cloud_top, conv_frac, layer_mass):
    levels, row_count, col_count = adjoint_field.shape
    blocks = row_count // 8
    half = lambda h: pl.BlockSpec((levels, 8, LANES), lambda b: (0, b, h))
    flat = pl.BlockSpec((8, col_count), lambda b: (b, 0))
    field, wide, row = pl.pallas_call(
        mix_kernel,
        grid=(blocks,),
        in_specs=[
            half(0),
            half(1),
            pl.BlockSpec((8, levels, levels), lambda b: (b, 0, 0)),
            flat,
            flat,
            pl.BlockSpec((1, levels), lambda b: (0, 0)),
        ],
        out_specs=[
            pl.BlockSpec((1, col_count, 8, levels), lambda b: (b, 0, 0, 0)),
            IN_VMEM,
            pl.BlockSpec((col_count, levels), lambda b: (0, 0)),
        ],
        out_shape=[
            pltpu.HBM((blocks, col_count, 8, levels), F32),
            pltpu.VMEM((2 * levels, row_count * levels), BF16),
            pltpu.HBM((col_count, levels), F32),
        ],
        compiler_params=params(20),
        cost_estimate=pl.CostEstimate(
            flops=2 * levels * levels * 4 * row_count * col_count,
            bytes_accessed=12 * levels * row_count * col_count,
            transcendentals=0,
        ),
        name="mix_own",
    )(adjoint_field, adjoint_field, mixing_inverse, cloud_top, conv_frac, layer_mass)
    return in_hbm(field), in_vmem(wide), in_hbm(row)


def mix_edge(edge_refs, lines_ref, wide_ref, layer_mass, out_ref):
    levels = layer_mass.shape[0]
    group = iota((levels, 2 * LANES), 1) // EDGE
    top, frac = edge_lines(lines_ref, levels)
    for row in range(8):
        value = jnp.concatenate([level_rows(ref, row, levels) for ref in edge_refs], axis=1)
        value = value * (1.0 / SCALE)
        left, right = [], []
        for q in range(4):
            cols = slice((8 * q + row) * levels, (8 * q + row + 1) * levels)
            high, low = halves(jnp.where(group == q, value, 0.0))
            left += [wide_ref[:, cols], wide_ref[:, cols]]
            right += [high, low]
        both = dot(jnp.concatenate(left, axis=1), jnp.concatenate(right, axis=0))
        mixed = both[:levels] + both[levels:]
        done = convect(mixed, top[row : row + 1].astype(I32), frac[row : row + 1], layer_mass)
        put_columns(out_ref, row, done)


def edge_lines(ref, levels):
    top, high, mid, low = [ref[levels + i] for i in range(EDGE_LINES)]
    return top, high + (mid + low) * (1.0 / SCALE)


def find_places(row, row_count):
    count = row.shape[1]
    upto = (iota((LANES, LANES), 0) <= iota((LANES, LANES), 1)).astype(F32).astype(BF16)
    before = jnp.zeros((row_count, 1), F32)
    places = []
    for start in range(0, count, LANES):
        mine = iota((row_count, LANES), 0) == row[:, start : start + LANES]
        running = dot(mine.astype(F32).astype(BF16), upto)
        place = jnp.sum(jnp.where(mine, running + before, 0.0), axis=0, keepdims=True) - 1.0
        places.append(place.astype(I32))
        before = before + running[:, LANES - 1 :]
    return jnp.concatenate(places, axis=1), jnp.max(before)


def force_rows(block, rounds, key_ref, table_ref, wide_ref, layer_mass, stack, square, out_ref):
    levels = layer_mass.shape[0]
    slots = 8 * WINDOW
    lane = iota((1, slots), 1)
    flat = out_ref.reshape(REACH * 8, LANES)

    def one_round(index, add):
        target = (8 * block + lane // WINDOW) * PITCH + index * WINDOW + lane % WINDOW
        pick = [key_ref[...] == target[:, h * LANES : (h + 1) * LANES] for h in range(2)]
        pick = jnp.concatenate([part.astype(F32).astype(BF16) for part in pick], axis=1)
        found = dot(table_ref[...], pick)
        split_high, split_low, top, high, mid, low = [
            found[levels + i : levels + i + 1] for i in range(6)
        ]
        column = (split_high * EDGE + split_low).astype(I32)
        value = found[:levels].astype(BF16)
        for r in range(8):
            mine = (lane // WINDOW == r).astype(F32).astype(BF16)
            stack[r * levels : (r + 1) * levels, :] = value * mine
        start = pl.multiple_of(8 * block * levels, 8 * levels)
        both = dot(wide_ref[:, pl.ds(start, 8 * levels)], stack[...])
        mixed = both[:levels] + both[levels:]
        done = convect(mixed, top.astype(I32), (high + mid) + low, layer_mass)
        turned = jnp.concatenate([done[:, h * LANES : (h + 1) * LANES].T for h in range(2)], axis=0)
        high, low = halves(turned)
        hot = (iota((REACH, slots), 0) == column).astype(F32).astype(BF16)
        for group in range(2):
            for r in range(4):
                source = slice((4 * group + r) * WINDOW, (4 * group + r + 1) * WINDOW)
                target = slice(r * levels, (r + 1) * levels)
                square[r * WINDOW : (r + 1) * WINDOW, target] = high[source]
                square[(4 + r) * WINDOW : (5 + r) * WINDOW, target] = low[source]
            left = hot[:, 4 * group * WINDOW : 4 * (group + 1) * WINDOW]
            forced = dot(jnp.concatenate([left, left], axis=1), square[...])
            for r in range(4):
                rows = pl.ds(4 * group + r, REACH, stride=8)
                part = forced[:, r * levels : (r + 1) * levels]
                flat[rows, :] = flat[rows, :] + part if add else part

    one_round(0, False)

    def more(index, carry):
        one_round(index, True)
        return carry

    lax.fori_loop(1, rounds, more, 0)


def soundings_kernel(
    got_ref, wide_ref, top_ref, frac_ref, near_ref, far_ref, lines_ref, mass_ref,
    row_ref, west_ref, east_ref, shift_ref, weight_ref,
    key_ref, table_ref, edge_out, rounds_ref, first_ref,
    forced, stack, square,
):
    devices = got_ref.shape[0]
    levels = mass_ref.shape[1]
    n = devices * CAP
    row_count = top_ref.shape[0]
    width = 2 * LANES
    layer_mass = as_wide_column(mass_ref[...])
    mix_edge((near_ref, far_ref), lines_ref, wide_ref, layer_mass, edge_out)

    got = got_ref[...].astype(F32)
    table_ref[:levels, :n] = got[:, :CAP].reshape(n, levels).T.astype(BF16)
    table_ref[:levels, n:] = got[:, CAP : 2 * CAP].reshape(n, levels).T.astype(BF16)
    info = got[:, 2 * CAP :].reshape(devices * 8, LANES).astype(BF16)
    first = iota((devices, devices * 8), 1) == 8 * iota((devices, devices * 8), 0)
    info = dot(first.astype(F32).astype(BF16), info).astype(BF16)
    lines = []
    for kind in range(4):
        chosen = iota((LANES, n), 0) == iota((LANES, n), 1) % CAP + 32 * kind
        spread = dot(info, chosen.astype(F32).astype(BF16))
        mine = iota((devices, n), 0) == iota((devices, n), 1) // CAP
        lines.append(jnp.sum(jnp.where(mine, spread, 0.0), axis=0, keepdims=True))
    own_row, own_col, east_row, east_col = [line.astype(I32) for line in lines]
    own_row, east_row = own_row - 1, east_row - 1
    east_row = jnp.where(east_col < EDGE, east_row, -1)
    row = jnp.concatenate([own_row, east_row], axis=1)
    place, most = find_places(row, row_count)
    rounds = (most.astype(I32) + (WINDOW - 1)) // WINDOW
    rounds_ref[0] = rounds
    key_ref[...] = as_column((row * PITCH + place).astype(F32)).astype(I32)
    column = jnp.concatenate([own_col, width + east_col], axis=1)
    cells = [[(column // EDGE).astype(F32), (column % EDGE).astype(F32)]]

    packed_col = (east_row // 8) * EDGE + east_col
    parts = [
        (own_col, own_row, top_ref[...].astype(F32), frac_ref[...], row_count),
        (packed_col, east_row % 8, *edge_lines(lines_ref, levels), 8),
    ]
    for col, row, top, frac, count in parts:
        hot = (iota((width, n), 0) == col).astype(F32).astype(BF16)
        table = jnp.concatenate([top.astype(BF16)] + thirds(frac), axis=0)
        found = dot(table, hot)
        here = iota((count, n), 0) == row
        cells.append([
            jnp.sum(jnp.where(here, found[i * count : (i + 1) * count], 0.0), axis=0, keepdims=True)
            for i in range(4)
        ])
    lines = cells[0] + [jnp.concatenate(pair, axis=1) for pair in zip(cells[1], cells[2])]
    lines.append(jnp.zeros((CELL_LINES - len(lines), 2 * n), F32))
    table_ref[levels:] = jnp.concatenate(lines, axis=0).astype(BF16)

    square[...] = jnp.zeros_like(square)
    force_rows(0, rounds, key_ref, table_ref, wide_ref, layer_mass, stack, square, forced)
    edge = edge_out.reshape(width * 8, LANES)[pl.ds(0, EDGE, stride=8), :]
    value = jnp.concatenate([row_ref[...], edge], axis=0)
    value = value + forced.reshape(REACH * 8, LANES)[pl.ds(0, REACH, stride=8), :]
    shift = shift_ref[0:1, :]
    weight = weight_ref[0:1, :]
    for bit in (32, 16, 8, 4, 2, 1):
        value = jnp.where((shift & bit) != 0, value[bit:], value[:-bit])
    zonal = (1.0 - weight) * value[:width] + weight * value[1 : width + 1]
    for h, courant_ref in enumerate((west_ref, east_ref)):
        here = slice(h * LANES, (h + 1) * LANES)
        first_ref[:, here] = level_rows(courant_ref, 0) * zonal[here].T


def take_soundings(got, wide, cloud_top, conv_frac, edge_in, layer_mass, row, courant, shift, weight):
    levels = layer_mass.shape[1]
    row_count, col_count = cloud_top.shape
    n = got.shape[0] * CAP
    width = 2 * LANES
    full = lambda array: pl.BlockSpec(array.shape, lambda s: (0,) * array.ndim)
    edge_half = lambda h: pl.BlockSpec((levels + EDGE_LINES, 8, LANES), lambda s: (0, 0, h))
    half = lambda h: pl.BlockSpec((levels, 8, LANES), lambda s: (0, 0, h))
    lines = pl.BlockSpec((8, levels), lambda s: (0, 0))
    return pl.pallas_call(
        soundings_kernel,
        grid=(1,),
        in_specs=[
            IN_VMEM,
            IN_VMEM,
            full(cloud_top),
            full(conv_frac),
            edge_half(0),
            edge_half(1),
            IN_VMEM,
            full(layer_mass),
            full(row),
            half(0),
            half(1),
            lines,
            lines,
        ],
        out_specs=[IN_VMEM] * 3 + [pl.BlockSpec(memory_space=pltpu.SMEM), IN_VMEM],
        out_shape=[
            pltpu.VMEM((2 * n, LANES), I32),
            pltpu.VMEM((levels + CELL_LINES, 2 * n), BF16),
            pltpu.VMEM((width, 8, levels), F32),
            jax.ShapeDtypeStruct((1,), I32),
            jax.ShapeDtypeStruct((levels, col_count), F32),
        ],
        scratch_shapes=[
            pltpu.VMEM((REACH, 8, levels), F32),
            pltpu.VMEM((8 * levels, 8 * WINDOW), BF16),
            pltpu.VMEM((8 * WINDOW, 4 * levels), BF16),
        ],
        compiler_params=params(20 + n // 128),
        name="take_soundings",
    )(
        got, wide, cloud_top, conv_frac, edge_in, edge_in, edge_in, layer_mass, row, courant,
        courant, shift, weight,
    )


def advect_kernel(
    key_ref, table_ref, edge_ref, rounds_ref, wide_ref, field_ref, mass_ref,
    west_ref, east_ref, shift_ref, weight_ref,
    out_ref, last_ref,
    forced, coarse, stack, square, out_scr, prev, sem,
):
    step = pl.program_id(0)
    blocks = pl.num_programs(0)
    block = blocks - 1 - step
    levels = mass_ref.shape[1]
    width = 2 * LANES

    @pl.when(step == 0)
    def _():
        prev[...] = jnp.zeros_like(prev)
        square[...] = jnp.zeros_like(square)

    layer_mass = as_wide_column(mass_ref[...])
    force_rows(
        block, rounds_ref[0], key_ref, table_ref, wide_ref, layer_mass, stack, square, forced
    )
    shift = shift_ref[...]
    weight = weight_ref[...]
    chosen = {bit: (shift & bit) != 0 for bit in (32, 16, 8, 4, 2, 1)}

    def choose(tiles, bit, step):
        return [
            jnp.where(chosen[bit], new, old) for old, new in zip(tiles[:-step], tiles[step:])
        ]

    def by_eights(start, carry):
        tiles = [field_ref[0, start + 8 * i] + forced[start + 8 * i] for i in range(32)]
        tiles += [
            edge_ref[EDGE * block + start + 8 * i] + forced[width + start + 8 * i] for i in range(8)
        ]
        for bit in (32, 16, 8):
            tiles = choose(tiles, bit, bit // 8)
        for i, tile in enumerate(tiles):
            coarse[start + 8 * i] = tile
        return carry

    lax.fori_loop(0, 8, by_eights, 0)

    def by_ones(chunk, carry):
        start = chunk * 32
        tiles = [coarse[start + i] for i in range(40)]
        for bit in (4, 2, 1):
            tiles = choose(tiles, bit, bit)
        for i in range(32):
            forced[start + i] = (1.0 - weight) * tiles[i] + weight * tiles[i + 1]
        return carry

    lax.fori_loop(0, width // 32, by_ones, 0)

    flat = forced.reshape(REACH * 8, LANES)
    later = [prev[0], prev[1]]
    for r in reversed(range(8)):
        for h, courant_ref in enumerate((west_ref, east_ref)):
            zonal = flat[pl.ds(h * LANES * 8 + r, LANES, stride=8), :].T
            courant = level_rows(courant_ref, r)
            place = out_scr.at[block, h].reshape(levels * 8, LANES)
            value = (1.0 - courant) * zonal + later[h]
            place[pl.ds(r, levels, stride=8), :] = value
            if r == 7:

                @pl.when(step == 0)
                def _():
                    last_ref[:, h * LANES : (h + 1) * LANES] = value

            later[h] = courant * zonal
    prev[0] = later[0]
    prev[1] = later[1]

    def copies(b):
        return [
            pltpu.make_async_copy(
                out_scr.at[b, h],
                out_ref.at[:, pl.ds(b * 8, 8), pl.ds(h * LANES, LANES)],
                sem.at[b, h],
            )
            for h in range(2)
        ]

    for b in range(out_scr.shape[0]):

        @pl.when(block == b)
        def _():
            for copy in copies(b):
                copy.start()

    @pl.when(step == blocks - 1)
    def _():
        for b in range(out_scr.shape[0]):
            for copy in copies(b):
                copy.wait()


def advect(keys, table, edge_field, rounds, wide, field, layer_mass, courant, shift, weight):
    blocks, col_count, _, levels = field.shape
    n = keys.shape[0] // 2
    half = lambda h: pl.BlockSpec((levels, 8, LANES), lambda s: (0, blocks - 1 - s, h))
    lines = pl.BlockSpec((8, levels), lambda s: (blocks - 1 - s, 0))
    return pl.pallas_call(
        advect_kernel,
        grid=(blocks,),
        in_specs=[IN_VMEM] * 3
        + [
            pl.BlockSpec(memory_space=pltpu.SMEM),
            IN_VMEM,
            pl.BlockSpec((1, col_count, 8, levels), lambda s: (blocks - 1 - s, 0, 0, 0)),
            pl.BlockSpec((1, levels), lambda s: (0, 0)),
            half(0),
            half(1),
            lines,
            lines,
        ],
        out_specs=[pl.BlockSpec(memory_space=pl.ANY), IN_VMEM],
        out_shape=[
            jax.ShapeDtypeStruct(courant.shape, F32),
            pltpu.VMEM((levels, col_count), F32),
        ],
        scratch_shapes=[
            pltpu.VMEM((REACH, 8, levels), F32),
            pltpu.VMEM((col_count + 8, 8, levels), F32),
            pltpu.VMEM((8 * levels, 8 * WINDOW), BF16),
            pltpu.VMEM((8 * WINDOW, 4 * levels), BF16),
            pltpu.VMEM((blocks, 2, levels, 8, LANES), F32),
            pltpu.VMEM((2, levels, LANES), F32),
            pltpu.SemaphoreType.DMA((blocks, 2)),
        ],
        compiler_params=params(24 + n // 128),
        cost_estimate=pl.CostEstimate(
            flops=2 * levels * 8 * blocks * n * col_count,
            bytes_accessed=12 * levels * 8 * blocks * col_count,
            transcendentals=0,
        ),
        name="advect",
    )(
        keys, table, edge_field, rounds, wide, field, layer_mass, courant, courant, shift, weight
    )


def close_kernel(last_ref, north_ref, _, out_ref, row, sem):
    row[...] = last_ref[...] + north_ref[...]
    copy = pltpu.make_async_copy(row, out_ref.at[:, out_ref.shape[1] - 1, :], sem)
    copy.start()
    copy.wait()


def close(out, last, north):
    in_place = pl.BlockSpec(memory_space=pl.ANY)
    return pl.pallas_call(
        close_kernel,
        in_specs=[IN_VMEM, IN_VMEM, in_place],
        out_specs=in_place,
        out_shape=jax.ShapeDtypeStruct(out.shape, F32),
        scratch_shapes=[pltpu.VMEM(last.shape, F32), pltpu.SemaphoreType.DMA],
        input_output_aliases={2: 0},
        compiler_params=params(4),
        name="close_last_row",
    )(last, north, out)


def shards(
    adjoint_field,
    mixing_inverse,
    cloud_top,
    conv_frac,
    thickness,
    zonal_shift,
    zonal_frac,
    merid_courant,
    obs_kernel,
    obs_depart,
    obs_dest,
    obs_col,
    obs_count,
):
    adjoint_field, mixing_inverse, cloud_top, conv_frac, merid_courant, obs_kernel = [
        in_hbm(array)
        for array in (
            adjoint_field, mixing_inverse, cloud_top, conv_frac, merid_courant, obs_kernel
        )
    ]
    levels, row_count, col_count = adjoint_field.shape
    lat_count, lon_count = lax.axis_size("lat"), lax.axis_size("lon")
    devices = lat_count * lon_count
    sent = prepare(devices, lon_count, obs_count, obs_dest, obs_col, obs_depart, obs_kernel)
    sent, field_after = lax.optimization_barrier((sent, adjoint_field))
    got = lax.all_to_all(
        sent.reshape(devices, SLOTS, levels), ("lat", "lon"), split_axis=0, concat_axis=0, tiled=True
    )
    westward = [((i + 1) % lon_count, i) for i in range(lon_count)]
    layer_mass = in_hbm(thickness.reshape(1, levels))
    field_after = in_hbm(field_after)
    edge = edge_columns(field_after, cloud_top, conv_frac)
    field, wide, row = mix(field_after, mixing_inverse, cloud_top, conv_frac, layer_mass)
    edge_in = in_vmem(lax.ppermute(edge.astype(jnp.float16), "lon", westward).astype(F32))
    shift, weight = in_hbm(zonal_shift.T), in_hbm(zonal_frac.T)
    keys, table, edge_field, rounds, first = take_soundings(
        got, wide, cloud_top, conv_frac, edge_in, layer_mass, row, merid_courant, shift, weight
    )
    southward = [(i + 1, i) for i in range(lat_count - 1)]
    north = lax.ppermute(first, "lat", southward)
    out, last = advect(
        in_vmem(keys), in_vmem(table), in_vmem(edge_field), rounds, wide, field, layer_mass,
        merid_courant, shift, weight,
    )
    return close(out, last, north)


def solution(mesh):
    in_specs = (
        P(None, "lat", "lon"),
        P("lat", None, None),
        P("lat", "lon"),
        P("lat", "lon"),
        P(),
        P(None, "lat"),
        P(None, "lat"),
        P(None, "lat", "lon"),
        P(("lat", "lon"), None),
        P(("lat", "lon")),
        P(("lat", "lon")),
        P(("lat", "lon")),
        P(("lat", "lon")),
    )
    out_specs = P(None, "lat", "lon")
    return jax.shard_map(shards, mesh=mesh, in_specs=in_specs, out_specs=out_specs, check_vma=False)
```

```python
import functools

import jax
import jax.numpy as jnp
from jax import lax
from jax.experimental import pallas as pl
from jax.experimental.pallas import tpu as pltpu
from jax.sharding import PartitionSpec as P

F32, BF16, I32 = jnp.float32, jnp.bfloat16, jnp.int32
CAP = 16
SLOTS = 40
EDGE = 64
LANES = 128
GROUP = 32
EDGE_LINES = 4
SCALE = 4096.0
WINDOW = 32
REACH = 2 * LANES + EDGE
PITCH = 4096
CELL_LINES = 16
MIB = 1024 * 1024


IN_VMEM = pl.BlockSpec(memory_space=pltpu.VMEM)


def iota(shape, dim):
    return lax.broadcasted_iota(I32, shape, dim)


def params(mib):
    return pltpu.CompilerParams(vmem_limit_bytes=mib * MIB)


def in_hbm(array):
    return pltpu.with_memory_space_constraint(array, pltpu.HBM)


def in_vmem(array):
    return pltpu.with_memory_space_constraint(array, pltpu.VMEM)


def dot(left, right):
    return jnp.dot(left, right, preferred_element_type=F32)


def dot_nt(left, right):
    return lax.dot_general(left, right, (((1,), (1,)), ((), ())), preferred_element_type=F32)


def halves(value):
    high = value.astype(BF16)
    return high, (value - high.astype(F32)).astype(BF16)


def thirds(value):
    high = value.astype(BF16)
    rest = value - high.astype(F32)
    mid = rest.astype(BF16)
    return [high, mid, (rest - mid.astype(F32)).astype(BF16)]


def as_column(line):
    return jnp.broadcast_to(line, (LANES, line.shape[1])).T


def as_wide_column(line):
    column = as_column(line)
    return jnp.concatenate([column, column], axis=1)


def convect(mixed, top, frac, layer_mass):
    inside = iota(mixed.shape, 0) < top
    total = jnp.sum(jnp.where(inside, mixed, 0.0), axis=0, keepdims=True)
    mass = jnp.sum(jnp.where(inside, layer_mass, 0.0), axis=0, keepdims=True)
    mean = total / jnp.where(mass > 0.0, mass, 1.0)
    return mixed + jnp.where(inside, frac * (layer_mass * mean - mixed), 0.0)


def prep_kernel(lon_count, count_ref, dest_ref, col_ref, depart_ref, obs_ref, out_ref):
    n = obs_ref.shape[0]
    rows = GROUP * SLOTS
    lane = iota((1, n), 1)
    live = lane < count_ref[0]
    dest = jnp.where(live, dest_ref[...], -1)
    cell = col_ref[...]
    cell_row = (cell // 256 + 1).astype(F32)
    cell_col = (cell % 256).astype(F32)
    contribution = (obs_ref[...].astype(F32) * as_column(depart_ref[...])).astype(BF16)
    local = iota((GROUP, n), 0)
    own_id = pl.program_id(0) * GROUP + local
    lon_id = own_id % lon_count
    east_id = jnp.where(lon_id == lon_count - 1, own_id - lon_id, own_id + 1)
    slots, places, left = [], [], []
    for ident, offset in ((own_id, 0), (east_id, CAP)):
        hit = dest == ident
        before = jnp.sum((live & (dest < ident)).astype(I32), axis=1, keepdims=True)
        place = lane - before
        slot = jnp.where(hit, local * SLOTS + offset + place + 1, 0)
        slots.append(jnp.sum(slot, axis=0, keepdims=True) - 1)
        places.append(jnp.sum(jnp.where(hit, place, 0), axis=0, keepdims=True))
        left.append(jnp.where(hit, cell_row, 0.0).astype(BF16))
        left.append(jnp.where(hit, cell_col, 0.0).astype(BF16))
    out_row = iota((rows, n), 0)
    pick = ((out_row == slots[0]) | (out_row == slots[1])).astype(F32).astype(BF16)
    spot = iota((LANES, n), 0)
    right = [
        (spot == 32 * kind + places[kind // 2]).astype(F32).astype(BF16) for kind in range(4)
    ]
    cells = dot_nt(jnp.concatenate(left, axis=1), jnp.concatenate(right, axis=1))
    spread = (iota((rows, GROUP), 0) == iota((rows, GROUP), 1) * SLOTS + 2 * CAP)
    spread = spread.astype(F32).astype(BF16)
    out_ref[...] = (dot(pick, contribution) + dot(spread, cells.astype(BF16))).astype(BF16)


def prepare(devices, lon_count, obs_count, obs_dest, obs_col, obs_depart, obs_kernel):
    n, levels = obs_kernel.shape
    steps = devices // GROUP
    whole = lambda shape: pl.BlockSpec(shape, lambda g: (0, 0))
    return pl.pallas_call(
        functools.partial(prep_kernel, lon_count),
        grid=(steps,),
        in_specs=[
            pl.BlockSpec(memory_space=pltpu.SMEM),
            whole((1, n)),
            whole((1, n)),
            whole((1, n)),
            whole((n, levels)),
        ],
        out_specs=pl.BlockSpec((GROUP * SLOTS, levels), lambda g: (g, 0)),
        out_shape=pltpu.VMEM((devices * SLOTS, levels), BF16),
        compiler_params=params(16 + devices // 4),
        name="soundings_out",
    )(
        obs_count,
        in_hbm(obs_dest.reshape(1, n)),
        in_hbm(obs_col.reshape(1, n)),
        in_hbm(obs_depart.reshape(1, n)),
        obs_kernel,
    )


def level_rows(ref, row, count=None):
    levels = ref.shape[0]
    count = levels if count is None else count
    return ref.reshape(levels * 8, LANES)[pl.ds(row, count, stride=8), :]


def pack_edge(block):
    parts = [block[:, 8 * q : 8 * q + 8, :] for q in range(4)]
    low = iota(parts[0].shape, 2) < EDGE
    pairs = [
        jnp.where(low, parts[2 * h], pltpu.roll(parts[2 * h + 1], EDGE, 2)) for h in range(2)
    ]
    return jnp.concatenate(pairs, axis=2)


def edge_kernel(field_ref, top_ref, frac_ref, out_ref):
    step = pl.program_id(0)
    count = field_ref.shape[0]
    here = pl.ds(pl.multiple_of(step * count, count), count)
    out_ref[here] = pack_edge(field_ref[...]) * SCALE

    @pl.when(step == 0)
    def _():
        pieces = thirds(frac_ref[...])
        lines = [top_ref[...].astype(F32)] + [piece.astype(F32) for piece in pieces]
        lines[2:] = [line * SCALE for line in lines[2:]]
        first = out_ref.shape[0] - EDGE_LINES
        for i, line in enumerate(lines):
            out_ref[first + i : first + i + 1] = pack_edge(line[None])


def edge_columns(adjoint_field, cloud_top, conv_frac):
    levels, row_count, _ = adjoint_field.shape
    flat = pl.BlockSpec((row_count, LANES), lambda i: (0, 0))
    return pl.pallas_call(
        edge_kernel,
        grid=(2,),
        in_specs=[pl.BlockSpec((levels // 2, row_count, LANES), lambda i: (i, 0, 0)), flat, flat],
        out_specs=IN_VMEM,
        out_shape=pltpu.VMEM((levels + EDGE_LINES, 8, 4 * EDGE), F32),
        compiler_params=params(16),
        cost_estimate=pl.CostEstimate(
            flops=levels * levels * 4 * row_count * LANES,
            bytes_accessed=12 * levels * row_count * LANES,
            transcendentals=0,
        ),
        name="edge_columns",
    )(adjoint_field, cloud_top, conv_frac)


def put_columns(ref, row, value):
    count = ref.shape[0]
    flat = ref.reshape(count * 8, LANES)
    for h in range(count // LANES):
        part = value[:, h * LANES : (h + 1) * LANES].T
        flat[pl.ds(h * LANES * 8 + row, LANES, stride=8), :] = part


def mix_rows(field_refs, mixing_ref, top, frac, layer_mass, block, out_ref, wide_ref):
    levels = mixing_ref.shape[1]
    for row in range(8):
        value = jnp.concatenate([level_rows(ref, row) for ref in field_refs], axis=1)
        high, low = halves(value)
        mix_high, mix_low = halves(mixing_ref[row])
        here = pl.ds(pl.multiple_of((8 * block + row) * levels, levels), levels)
        wide_ref[:levels, here] = mix_high
        wide_ref[levels:, here] = mix_low
        four = jnp.concatenate([mix_high, mix_low], axis=0)
        both = dot(jnp.concatenate([four, four], axis=1), jnp.concatenate([high, low], axis=0))
        mixed = both[:levels] + both[levels:]
        done = convect(mixed, top[row : row + 1, :], frac[row : row + 1, :], layer_mass)
        put_columns(out_ref.at[0], row, done)


def mix_kernel(
    west_ref, east_ref, mixing_ref, top_ref, frac_ref, mass_ref, out_ref, wide_ref, row_ref
):
    layer_mass = as_wide_column(mass_ref[...])
    block = pl.program_id(0)
    mix_rows(
        (west_ref, east_ref), mixing_ref, top_ref[...], frac_ref[...], layer_mass, block,
        out_ref, wide_ref,
    )

    @pl.when(block == 0)
    def _():
        flat = out_ref.at[0].reshape(row_ref.shape[0] * 8, LANES)
        row_ref[...] = flat[pl.ds(0, row_ref.shape[0], stride=8), :]


def mix(adjoint_field, mixing_inverse, cloud_top, conv_frac, layer_mass):
    levels, row_count, col_count = adjoint_field.shape
    blocks = row_count // 8
    half = lambda h: pl.BlockSpec((levels, 8, LANES), lambda b: (0, b, h))
    flat = pl.BlockSpec((8, col_count), lambda b: (b, 0))
    field, wide, row = pl.pallas_call(
        mix_kernel,
        grid=(blocks,),
        in_specs=[
            half(0),
            half(1),
            pl.BlockSpec((8, levels, levels), lambda b: (b, 0, 0)),
            flat,
            flat,
            pl.BlockSpec((1, levels), lambda b: (0, 0)),
        ],
        out_specs=[
            pl.BlockSpec((1, col_count, 8, levels), lambda b: (b, 0, 0, 0)),
            IN_VMEM,
            pl.BlockSpec((col_count, levels), lambda b: (0, 0)),
        ],
        out_shape=[
            pltpu.HBM((blocks, col_count, 8, levels), F32),
            pltpu.VMEM((2 * levels, row_count * levels), BF16),
            pltpu.HBM((col_count, levels), F32),
        ],
        compiler_params=params(20),
        cost_estimate=pl.CostEstimate(
            flops=2 * levels * levels * 4 * row_count * col_count,
            bytes_accessed=12 * levels * row_count * col_count,
            transcendentals=0,
        ),
        name="mix_own",
    )(adjoint_field, adjoint_field, mixing_inverse, cloud_top, conv_frac, layer_mass)
    return in_hbm(field), in_vmem(wide), in_hbm(row)


def mix_edge(edge_refs, lines_ref, wide_ref, layer_mass, out_ref):
    levels = layer_mass.shape[0]
    group = iota((levels, 2 * LANES), 1) // EDGE
    top, frac = edge_lines(lines_ref, levels)
    for row in range(8):
        value = jnp.concatenate([level_rows(ref, row, levels) for ref in edge_refs], axis=1)
        value = value * (1.0 / SCALE)
        left, right = [], []
        for q in range(4):
            cols = slice((8 * q + row) * levels, (8 * q + row + 1) * levels)
            high, low = halves(jnp.where(group == q, value, 0.0))
            left += [wide_ref[:, cols], wide_ref[:, cols]]
            right += [high, low]
        both = dot(jnp.concatenate(left, axis=1), jnp.concatenate(right, axis=0))
        mixed = both[:levels] + both[levels:]
        done = convect(mixed, top[row : row + 1].astype(I32), frac[row : row + 1], layer_mass)
        put_columns(out_ref, row, done)


def edge_lines(ref, levels):
    top, high, mid, low = [ref[levels + i] for i in range(EDGE_LINES)]
    return top, high + (mid + low) * (1.0 / SCALE)


def find_places(row, row_count):
    count = row.shape[1]
    upto = (iota((LANES, LANES), 0) <= iota((LANES, LANES), 1)).astype(F32).astype(BF16)
    before = jnp.zeros((row_count, 1), F32)
    places = []
    for start in range(0, count, LANES):
        mine = iota((row_count, LANES), 0) == row[:, start : start + LANES]
        running = dot(mine.astype(F32).astype(BF16), upto)
        place = jnp.sum(jnp.where(mine, running + before, 0.0), axis=0, keepdims=True) - 1.0
        places.append(place.astype(I32))
        before = before + running[:, LANES - 1 :]
    return jnp.concatenate(places, axis=1), jnp.max(before)


def mix_slots(blocks, index, key_ref, table_ref, wide_ref, layer_mass, stack):
    levels = layer_mass.shape[0]
    slots = 8 * WINDOW
    lane = iota((1, slots), 1)
    target = [(8 * b + lane // WINDOW) * PITCH + index * WINDOW + lane % WINDOW for b in blocks]
    target = jnp.concatenate(target, axis=1)
    pick = [
        (key_ref[...] == target[:, start : start + LANES]).astype(F32).astype(BF16)
        for start in range(0, target.shape[1], LANES)
    ]
    found = dot(table_ref[...], jnp.concatenate(pick, axis=1))
    split_high, split_low, top, high, mid, low = [
        found[levels + i : levels + i + 1] for i in range(6)
    ]
    column = (split_high * EDGE + split_low).astype(I32)
    parts = []
    for i, b in enumerate(blocks):
        value = found[:levels, i * slots : (i + 1) * slots].astype(BF16)
        for r in range(8):
            mine = (lane // WINDOW == r).astype(F32).astype(BF16)
            stack[i, r * levels : (r + 1) * levels, :] = value * mine
        start = pl.multiple_of(8 * b * levels, 8 * levels)
        both = dot(wide_ref[:, pl.ds(start, 8 * levels)], stack[i])
        parts.append(both[:levels] + both[levels:])
    mass = jnp.concatenate([layer_mass] * len(blocks), axis=1)
    done = convect(
        jnp.concatenate(parts, axis=1), top.astype(I32), (high + mid) + low, mass
    )
    turned = [done[:, start : start + LANES].T for start in range(0, done.shape[1], LANES)]
    high, low = halves(jnp.concatenate(turned, axis=0))
    return high, low, column


def expand(high, low, column, square, out_ref, add):
    levels = high.shape[1]
    flat = out_ref.reshape(REACH * 8, LANES)
    hot = (iota((REACH, 8 * WINDOW), 0) == column).astype(F32).astype(BF16)
    for group in range(2):
        for r in range(4):
            source = slice((4 * group + r) * WINDOW, (4 * group + r + 1) * WINDOW)
            target = slice(r * levels, (r + 1) * levels)
            square[group, r * WINDOW : (r + 1) * WINDOW, target] = high[source]
            square[group, (4 + r) * WINDOW : (5 + r) * WINDOW, target] = low[source]
        left = hot[:, 4 * group * WINDOW : 4 * (group + 1) * WINDOW]
        forced = dot(jnp.concatenate([left, left], axis=1), square[group])
        for r in range(4):
            rows = pl.ds(4 * group + r, REACH, stride=8)
            part = forced[:, r * levels : (r + 1) * levels]
            flat[rows, :] = flat[rows, :] + part if add else part


def force_rows(
    block, rounds, high_ref, low_ref, column_ref,
    key_ref, table_ref, wide_ref, layer_mass, stack, square, out_ref,
):
    slots = 8 * WINDOW
    here = pl.ds(pl.multiple_of(block * slots, slots), slots)
    expand(high_ref[here, :], low_ref[here, :], column_ref[0:1, here], square, out_ref, False)

    def more(index, carry):
        mixed = mix_slots([block], index, key_ref, table_ref, wide_ref, layer_mass, stack)
        expand(*mixed, square, out_ref, True)
        return carry

    lax.fori_loop(1, rounds, more, 0)


def soundings_kernel(
    got_ref, wide_ref, top_ref, frac_ref, near_ref, far_ref, lines_ref, mass_ref,
    row_ref, west_ref, east_ref, shift_ref, weight_ref,
    key_ref, table_ref, high_ref, low_ref, column_ref, edge_out, rounds_ref, first_ref,
    forced, stack, square,
):
    devices = got_ref.shape[0]
    levels = mass_ref.shape[1]
    n = devices * CAP
    row_count = top_ref.shape[0]
    width = 2 * LANES
    layer_mass = as_wide_column(mass_ref[...])
    mix_edge((near_ref, far_ref), lines_ref, wide_ref, layer_mass, edge_out)

    got = got_ref[...].astype(F32)
    table_ref[:levels, :n] = got[:, :CAP].reshape(n, levels).T.astype(BF16)
    table_ref[:levels, n:] = got[:, CAP : 2 * CAP].reshape(n, levels).T.astype(BF16)
    info = got[:, 2 * CAP :].reshape(devices * 8, LANES).astype(BF16)
    first = iota((devices, devices * 8), 1) == 8 * iota((devices, devices * 8), 0)
    info = dot(first.astype(F32).astype(BF16), info).astype(BF16)
    lines = []
    for kind in range(4):
        chosen = iota((LANES, n), 0) == iota((LANES, n), 1) % CAP + 32 * kind
        spread = dot(info, chosen.astype(F32).astype(BF16))
        mine = iota((devices, n), 0) == iota((devices, n), 1) // CAP
        lines.append(jnp.sum(jnp.where(mine, spread, 0.0), axis=0, keepdims=True))
    own_row, own_col, east_row, east_col = [line.astype(I32) for line in lines]
    own_row, east_row = own_row - 1, east_row - 1
    east_row = jnp.where(east_col < EDGE, east_row, -1)
    row = jnp.concatenate([own_row, east_row], axis=1)
    place, most = find_places(row, row_count)
    rounds = (most.astype(I32) + (WINDOW - 1)) // WINDOW
    rounds_ref[0] = rounds
    key_ref[...] = as_column((row * PITCH + place).astype(F32)).astype(I32)
    column = jnp.concatenate([own_col, width + east_col], axis=1)
    cells = [[(column // EDGE).astype(F32), (column % EDGE).astype(F32)]]

    packed_col = (east_row // 8) * EDGE + east_col
    parts = [
        (own_col, own_row, top_ref[...].astype(F32), frac_ref[...], row_count),
        (packed_col, east_row % 8, *edge_lines(lines_ref, levels), 8),
    ]
    for col, row, top, frac, count in parts:
        hot = (iota((width, n), 0) == col).astype(F32).astype(BF16)
        table = jnp.concatenate([top.astype(BF16)] + thirds(frac), axis=0)
        found = dot(table, hot)
        here = iota((count, n), 0) == row
        cells.append([
            jnp.sum(jnp.where(here, found[i * count : (i + 1) * count], 0.0), axis=0, keepdims=True)
            for i in range(4)
        ])
    lines = cells[0] + [jnp.concatenate(pair, axis=1) for pair in zip(cells[1], cells[2])]
    lines.append(jnp.zeros((CELL_LINES - len(lines), 2 * n), F32))
    table_ref[levels:] = jnp.concatenate(lines, axis=0).astype(BF16)

    high, low, column = mix_slots(
        list(range(row_count // 8)), 0, key_ref, table_ref, wide_ref, layer_mass, stack
    )
    high_ref[...] = high
    low_ref[...] = low
    column_ref[0:1] = column
    column_ref[1:] = jnp.zeros_like(column_ref[1:])
    square[...] = jnp.zeros_like(square)
    force_rows(
        0, rounds, high_ref, low_ref, column_ref,
        key_ref, table_ref, wide_ref, layer_mass, stack, square, forced,
    )
    edge = edge_out.reshape(width * 8, LANES)[pl.ds(0, EDGE, stride=8), :]
    value = jnp.concatenate([row_ref[...], edge], axis=0)
    value = value + forced.reshape(REACH * 8, LANES)[pl.ds(0, REACH, stride=8), :]
    shift = shift_ref[0:1, :]
    weight = weight_ref[0:1, :]
    for bit in (32, 16, 8, 4, 2, 1):
        value = jnp.where((shift & bit) != 0, value[bit:], value[:-bit])
    zonal = (1.0 - weight) * value[:width] + weight * value[1 : width + 1]
    for h, courant_ref in enumerate((west_ref, east_ref)):
        here = slice(h * LANES, (h + 1) * LANES)
        first_ref[:, here] = level_rows(courant_ref, 0) * zonal[here].T


def take_soundings(got, wide, cloud_top, conv_frac, edge_in, layer_mass, row, courant, shift, weight):
    levels = layer_mass.shape[1]
    row_count, col_count = cloud_top.shape
    n = got.shape[0] * CAP
    width = 2 * LANES
    full = lambda array: pl.BlockSpec(array.shape, lambda s: (0,) * array.ndim)
    edge_half = lambda h: pl.BlockSpec((levels + EDGE_LINES, 8, LANES), lambda s: (0, 0, h))
    half = lambda h: pl.BlockSpec((levels, 8, LANES), lambda s: (0, 0, h))
    lines = pl.BlockSpec((8, levels), lambda s: (0, 0))
    return pl.pallas_call(
        soundings_kernel,
        grid=(1,),
        in_specs=[
            IN_VMEM,
            IN_VMEM,
            full(cloud_top),
            full(conv_frac),
            edge_half(0),
            edge_half(1),
            IN_VMEM,
            full(layer_mass),
            full(row),
            half(0),
            half(1),
            lines,
            lines,
        ],
        out_specs=[IN_VMEM] * 6 + [pl.BlockSpec(memory_space=pltpu.SMEM), IN_VMEM],
        out_shape=[
            pltpu.VMEM((2 * n, LANES), I32),
            pltpu.VMEM((levels + CELL_LINES, 2 * n), BF16),
            pltpu.VMEM((row_count * WINDOW, levels), BF16),
            pltpu.VMEM((row_count * WINDOW, levels), BF16),
            pltpu.VMEM((8, row_count * WINDOW), I32),
            pltpu.VMEM((width, 8, levels), F32),
            jax.ShapeDtypeStruct((1,), I32),
            jax.ShapeDtypeStruct((levels, col_count), F32),
        ],
        scratch_shapes=[
            pltpu.VMEM((REACH, 8, levels), F32),
            pltpu.VMEM((row_count // 8, 8 * levels, 8 * WINDOW), BF16),
            pltpu.VMEM((2, 8 * WINDOW, 4 * levels), BF16),
        ],
        compiler_params=params(24 + n // 64),
        name="take_soundings",
    )(
        got, wide, cloud_top, conv_frac, edge_in, edge_in, edge_in, layer_mass, row, courant,
        courant, shift, weight,
    )


def advect_kernel(
    key_ref, table_ref, high_ref, low_ref, column_ref, edge_ref, rounds_ref, wide_ref, field_ref,
    mass_ref,
    west_ref, east_ref, shift_ref, weight_ref,
    out_ref, last_ref,
    forced, coarse, stack, square, out_scr, prev, sem,
):
    step = pl.program_id(0)
    blocks = pl.num_programs(0)
    block = blocks - 1 - step
    levels = mass_ref.shape[1]
    width = 2 * LANES

    @pl.when(step == 0)
    def _():
        prev[...] = jnp.zeros_like(prev)
        square[...] = jnp.zeros_like(square)

    layer_mass = as_wide_column(mass_ref[...])
    force_rows(
        block, rounds_ref[0], high_ref, low_ref, column_ref,
        key_ref, table_ref, wide_ref, layer_mass, stack, square, forced,
    )
    shift = shift_ref[...]
    weight = weight_ref[...]
    chosen = {bit: (shift & bit) != 0 for bit in (32, 16, 8, 4, 2, 1)}

    def choose(tiles, bit, step):
        return [
            jnp.where(chosen[bit], new, old) for old, new in zip(tiles[:-step], tiles[step:])
        ]

    def by_eights(start, carry):
        tiles = [field_ref[0, start + 8 * i] + forced[start + 8 * i] for i in range(32)]
        tiles += [
            edge_ref[EDGE * block + start + 8 * i] + forced[width + start + 8 * i] for i in range(8)
        ]
        for bit in (32, 16, 8):
            tiles = choose(tiles, bit, bit // 8)
        for i, tile in enumerate(tiles):
            coarse[start + 8 * i] = tile
        return carry

    lax.fori_loop(0, 8, by_eights, 0)

    def by_ones(chunk, carry):
        start = chunk * 32
        tiles = [coarse[start + i] for i in range(40)]
        for bit in (4, 2, 1):
            tiles = choose(tiles, bit, bit)
        for i in range(32):
            forced[start + i] = (1.0 - weight) * tiles[i] + weight * tiles[i + 1]
        return carry

    lax.fori_loop(0, width // 32, by_ones, 0)

    flat = forced.reshape(REACH * 8, LANES)
    later = [prev[0], prev[1]]
    for r in reversed(range(8)):
        for h, courant_ref in enumerate((west_ref, east_ref)):
            zonal = flat[pl.ds(h * LANES * 8 + r, LANES, stride=8), :].T
            courant = level_rows(courant_ref, r)
            place = out_scr.at[block, h].reshape(levels * 8, LANES)
            value = (1.0 - courant) * zonal + later[h]
            place[pl.ds(r, levels, stride=8), :] = value
            if r == 7:

                @pl.when(step == 0)
                def _():
                    last_ref[:, h * LANES : (h + 1) * LANES] = value

            later[h] = courant * zonal
    prev[0] = later[0]
    prev[1] = later[1]

    def copies(b):
        return [
            pltpu.make_async_copy(
                out_scr.at[b, h],
                out_ref.at[:, pl.ds(b * 8, 8), pl.ds(h * LANES, LANES)],
                sem.at[b, h],
            )
            for h in range(2)
        ]

    for b in range(out_scr.shape[0]):

        @pl.when(block == b)
        def _():
            for copy in copies(b):
                copy.start()

    @pl.when(step == blocks - 1)
    def _():
        for b in range(out_scr.shape[0]):
            for copy in copies(b):
                copy.wait()


def advect(soundings, edge_field, rounds, wide, field, layer_mass, courant, shift, weight):
    blocks, col_count, _, levels = field.shape
    n = soundings[0].shape[0] // 2
    half = lambda h: pl.BlockSpec((levels, 8, LANES), lambda s: (0, blocks - 1 - s, h))
    lines = pl.BlockSpec((8, levels), lambda s: (blocks - 1 - s, 0))
    return pl.pallas_call(
        advect_kernel,
        grid=(blocks,),
        in_specs=[IN_VMEM] * 6
        + [
            pl.BlockSpec(memory_space=pltpu.SMEM),
            IN_VMEM,
            pl.BlockSpec((1, col_count, 8, levels), lambda s: (blocks - 1 - s, 0, 0, 0)),
            pl.BlockSpec((1, levels), lambda s: (0, 0)),
            half(0),
            half(1),
            lines,
            lines,
        ],
        out_specs=[pl.BlockSpec(memory_space=pl.ANY), IN_VMEM],
        out_shape=[
            jax.ShapeDtypeStruct(courant.shape, F32),
            pltpu.VMEM((levels, col_count), F32),
        ],
        scratch_shapes=[
            pltpu.VMEM((REACH, 8, levels), F32),
            pltpu.VMEM((col_count + 8, 8, levels), F32),
            pltpu.VMEM((1, 8 * levels, 8 * WINDOW), BF16),
            pltpu.VMEM((2, 8 * WINDOW, 4 * levels), BF16),
            pltpu.VMEM((blocks, 2, levels, 8, LANES), F32),
            pltpu.VMEM((2, levels, LANES), F32),
            pltpu.SemaphoreType.DMA((blocks, 2)),
        ],
        compiler_params=params(24 + n // 128),
        cost_estimate=pl.CostEstimate(
            flops=2 * levels * 8 * blocks * n * col_count,
            bytes_accessed=12 * levels * 8 * blocks * col_count,
            transcendentals=0,
        ),
        name="advect",
    )(
        *soundings, edge_field, rounds, wide, field, layer_mass, courant, courant, shift, weight
    )


def close_kernel(last_ref, north_ref, _, out_ref, row, sem):
    row[...] = last_ref[...] + north_ref[...]
    copy = pltpu.make_async_copy(row, out_ref.at[:, out_ref.shape[1] - 1, :], sem)
    copy.start()
    copy.wait()


def close(out, last, north):
    in_place = pl.BlockSpec(memory_space=pl.ANY)
    return pl.pallas_call(
        close_kernel,
        in_specs=[IN_VMEM, IN_VMEM, in_place],
        out_specs=in_place,
        out_shape=jax.ShapeDtypeStruct(out.shape, F32),
        scratch_shapes=[pltpu.VMEM(last.shape, F32), pltpu.SemaphoreType.DMA],
        input_output_aliases={2: 0},
        compiler_params=params(4),
        name="close_last_row",
    )(last, north, out)


def shards(
    adjoint_field,
    mixing_inverse,
    cloud_top,
    conv_frac,
    thickness,
    zonal_shift,
    zonal_frac,
    merid_courant,
    obs_kernel,
    obs_depart,
    obs_dest,
    obs_col,
    obs_count,
):
    adjoint_field, mixing_inverse, cloud_top, conv_frac, merid_courant, obs_kernel = [
        in_hbm(array)
        for array in (
            adjoint_field, mixing_inverse, cloud_top, conv_frac, merid_courant, obs_kernel
        )
    ]
    levels, row_count, col_count = adjoint_field.shape
    lat_count, lon_count = lax.axis_size("lat"), lax.axis_size("lon")
    devices = lat_count * lon_count
    sent = prepare(devices, lon_count, obs_count, obs_dest, obs_col, obs_depart, obs_kernel)
    sent, field_after = lax.optimization_barrier((sent, adjoint_field))
    got = lax.all_to_all(
        sent.reshape(devices, SLOTS, levels), ("lat", "lon"), split_axis=0, concat_axis=0, tiled=True
    )
    westward = [((i + 1) % lon_count, i) for i in range(lon_count)]
    layer_mass = in_hbm(thickness.reshape(1, levels))
    field_after = in_hbm(field_after)
    edge = edge_columns(field_after, cloud_top, conv_frac)
    field, wide, row = mix(field_after, mixing_inverse, cloud_top, conv_frac, layer_mass)
    edge_in = in_vmem(lax.ppermute(edge.astype(jnp.float16), "lon", westward).astype(F32))
    shift, weight = in_hbm(zonal_shift.T), in_hbm(zonal_frac.T)
    *soundings, edge_field, rounds, first = take_soundings(
        got, wide, cloud_top, conv_frac, edge_in, layer_mass, row, merid_courant, shift, weight
    )
    southward = [(i + 1, i) for i in range(lat_count - 1)]
    north = lax.ppermute(first, "lat", southward)
    out, last = advect(
        [in_vmem(part) for part in soundings], in_vmem(edge_field), rounds, wide, field, layer_mass,
        merid_courant, shift, weight,
    )
    return close(out, last, north)


def solution(mesh):
    in_specs = (
        P(None, "lat", "lon"),
        P("lat", None, None),
        P("lat", "lon"),
        P("lat", "lon"),
        P(),
        P(None, "lat"),
        P(None, "lat"),
        P(None, "lat", "lon"),
        P(("lat", "lon"), None),
        P(("lat", "lon")),
        P(("lat", "lon")),
        P(("lat", "lon")),
        P(("lat", "lon")),
    )
    out_specs = P(None, "lat", "lon")
    return jax.shard_map(shards, mesh=mesh, in_specs=in_specs, out_specs=out_specs, check_vma=False)
```

```python
import functools

import jax
import jax.numpy as jnp
from jax import lax
from jax.experimental import pallas as pl
from jax.experimental.pallas import tpu as pltpu
from jax.sharding import PartitionSpec as P

F32, BF16, I32 = jnp.float32, jnp.bfloat16, jnp.int32
CAP = 16
SLOTS = 40
EDGE = 64
LANES = 128
GROUP = 32
EDGE_LINES = 4
SCALE = 4096.0
WINDOW = 32
REACH = 2 * LANES + EDGE
PITCH = 4096
CELL_LINES = 16
MIB = 1024 * 1024


IN_VMEM = pl.BlockSpec(memory_space=pltpu.VMEM)


def iota(shape, dim):
    return lax.broadcasted_iota(I32, shape, dim)


def params(mib):
    return pltpu.CompilerParams(vmem_limit_bytes=mib * MIB)


def in_hbm(array):
    return pltpu.with_memory_space_constraint(array, pltpu.HBM)


def in_vmem(array):
    return pltpu.with_memory_space_constraint(array, pltpu.VMEM)


def dot(left, right):
    return jnp.dot(left, right, preferred_element_type=F32)


def dot_nt(left, right):
    return lax.dot_general(left, right, (((1,), (1,)), ((), ())), preferred_element_type=F32)


def halves(value):
    high = value.astype(BF16)
    return high, (value - high.astype(F32)).astype(BF16)


def thirds(value):
    high = value.astype(BF16)
    rest = value - high.astype(F32)
    mid = rest.astype(BF16)
    return [high, mid, (rest - mid.astype(F32)).astype(BF16)]


def as_column(line):
    return jnp.broadcast_to(line, (LANES, line.shape[1])).T


def as_wide_column(line):
    column = as_column(line)
    return jnp.concatenate([column, column], axis=1)


def convect(mixed, top, frac, layer_mass):
    inside = iota(mixed.shape, 0) < top
    total = jnp.sum(jnp.where(inside, mixed, 0.0), axis=0, keepdims=True)
    mass = jnp.sum(jnp.where(inside, layer_mass, 0.0), axis=0, keepdims=True)
    mean = total / jnp.where(mass > 0.0, mass, 1.0)
    return mixed + jnp.where(inside, frac * (layer_mass * mean - mixed), 0.0)


def prep_kernel(lon_count, count_ref, dest_ref, col_ref, depart_ref, obs_ref, out_ref):
    n = obs_ref.shape[0]
    rows = GROUP * SLOTS
    lane = iota((1, n), 1)
    live = lane < count_ref[0]
    dest = jnp.where(live, dest_ref[...], -1)
    cell = col_ref[...]
    cell_row = (cell // 256 + 1).astype(F32)
    cell_col = (cell % 256).astype(F32)
    contribution = (obs_ref[...].astype(F32) * as_column(depart_ref[...])).astype(BF16)
    local = iota((GROUP, n), 0)
    own_id = pl.program_id(0) * GROUP + local
    lon_id = own_id % lon_count
    east_id = jnp.where(lon_id == lon_count - 1, own_id - lon_id, own_id + 1)
    slots, places, left = [], [], []
    for ident, offset in ((own_id, 0), (east_id, CAP)):
        hit = dest == ident
        before = jnp.sum((live & (dest < ident)).astype(I32), axis=1, keepdims=True)
        place = lane - before
        slot = jnp.where(hit, local * SLOTS + offset + place + 1, 0)
        slots.append(jnp.sum(slot, axis=0, keepdims=True) - 1)
        places.append(jnp.sum(jnp.where(hit, place, 0), axis=0, keepdims=True))
        left.append(jnp.where(hit, cell_row, 0.0).astype(BF16))
        left.append(jnp.where(hit, cell_col, 0.0).astype(BF16))
    out_row = iota((rows, n), 0)
    pick = ((out_row == slots[0]) | (out_row == slots[1])).astype(F32).astype(BF16)
    spot = iota((LANES, n), 0)
    right = [
        (spot == 32 * kind + places[kind // 2]).astype(F32).astype(BF16) for kind in range(4)
    ]
    cells = dot_nt(jnp.concatenate(left, axis=1), jnp.concatenate(right, axis=1))
    spread = (iota((rows, GROUP), 0) == iota((rows, GROUP), 1) * SLOTS + 2 * CAP)
    spread = spread.astype(F32).astype(BF16)
    out_ref[...] = (dot(pick, contribution) + dot(spread, cells.astype(BF16))).astype(BF16)


def prepare(devices, lon_count, obs_count, obs_dest, obs_col, obs_depart, obs_kernel):
    n, levels = obs_kernel.shape
    steps = devices // GROUP
    whole = lambda shape: pl.BlockSpec(shape, lambda g: (0, 0))
    return pl.pallas_call(
        functools.partial(prep_kernel, lon_count),
        grid=(steps,),
        in_specs=[
            pl.BlockSpec(memory_space=pltpu.SMEM),
            whole((1, n)),
            whole((1, n)),
            whole((1, n)),
            whole((n, levels)),
        ],
        out_specs=pl.BlockSpec((GROUP * SLOTS, levels), lambda g: (g, 0)),
        out_shape=pltpu.VMEM((devices * SLOTS, levels), BF16),
        compiler_params=params(16 + devices // 4),
        name="soundings_out",
    )(
        obs_count,
        in_hbm(obs_dest.reshape(1, n)),
        in_hbm(obs_col.reshape(1, n)),
        in_hbm(obs_depart.reshape(1, n)),
        obs_kernel,
    )


def level_rows(ref, row, count=None):
    levels = ref.shape[0]
    count = levels if count is None else count
    return ref.reshape(levels * 8, LANES)[pl.ds(row, count, stride=8), :]


def pack_edge(block):
    parts = [block[:, 8 * q : 8 * q + 8, :] for q in range(4)]
    low = iota(parts[0].shape, 2) < EDGE
    pairs = [
        jnp.where(low, parts[2 * h], pltpu.roll(parts[2 * h + 1], EDGE, 2)) for h in range(2)
    ]
    return jnp.concatenate(pairs, axis=2)


def edge_kernel(field_ref, top_ref, frac_ref, out_ref):
    step = pl.program_id(0)
    count = field_ref.shape[0]
    here = pl.ds(pl.multiple_of(step * count, count), count)
    out_ref[here] = pack_edge(field_ref[...]) * SCALE

    @pl.when(step == 0)
    def _():
        pieces = thirds(frac_ref[...])
        lines = [top_ref[...].astype(F32)] + [piece.astype(F32) for piece in pieces]
        lines[2:] = [line * SCALE for line in lines[2:]]
        first = out_ref.shape[0] - EDGE_LINES
        for i, line in enumerate(lines):
            out_ref[first + i : first + i + 1] = pack_edge(line[None])


def edge_columns(adjoint_field, cloud_top, conv_frac):
    levels, row_count, _ = adjoint_field.shape
    flat = pl.BlockSpec((row_count, LANES), lambda i: (0, 0))
    return pl.pallas_call(
        edge_kernel,
        grid=(2,),
        in_specs=[pl.BlockSpec((levels // 2, row_count, LANES), lambda i: (i, 0, 0)), flat, flat],
        out_specs=IN_VMEM,
        out_shape=pltpu.VMEM((levels + EDGE_LINES, 8, 4 * EDGE), F32),
        compiler_params=params(16),
        cost_estimate=pl.CostEstimate(
            flops=levels * levels * 4 * row_count * LANES,
            bytes_accessed=12 * levels * row_count * LANES,
            transcendentals=0,
        ),
        name="edge_columns",
    )(adjoint_field, cloud_top, conv_frac)


def put_columns(ref, row, value):
    count = ref.shape[0]
    flat = ref.reshape(count * 8, LANES)
    for h in range(count // LANES):
        part = value[:, h * LANES : (h + 1) * LANES].T
        flat[pl.ds(h * LANES * 8 + row, LANES, stride=8), :] = part


def mix_rows(field_refs, mixing_ref, top, frac, layer_mass, block, out_ref, wide_ref):
    levels = mixing_ref.shape[1]
    for row in range(8):
        value = jnp.concatenate([level_rows(ref, row) for ref in field_refs], axis=1)
        high, low = halves(value)
        mix_high, mix_low = halves(mixing_ref[row])
        here = pl.ds(pl.multiple_of((8 * block + row) * levels, levels), levels)
        wide_ref[:levels, here] = mix_high
        wide_ref[levels:, here] = mix_low
        four = jnp.concatenate([mix_high, mix_low], axis=0)
        both = dot(jnp.concatenate([four, four], axis=1), jnp.concatenate([high, low], axis=0))
        mixed = both[:levels] + both[levels:]
        done = convect(mixed, top[row : row + 1, :], frac[row : row + 1, :], layer_mass)
        put_columns(out_ref.at[0], row, done)


def mix_kernel(
    west_ref, east_ref, mixing_ref, top_ref, frac_ref, mass_ref, out_ref, wide_ref, row_ref
):
    layer_mass = as_wide_column(mass_ref[...])
    block = pl.program_id(0)
    mix_rows(
        (west_ref, east_ref), mixing_ref, top_ref[...], frac_ref[...], layer_mass, block,
        out_ref, wide_ref,
    )

    @pl.when(block == 0)
    def _():
        flat = out_ref.at[0].reshape(row_ref.shape[0] * 8, LANES)
        row_ref[...] = flat[pl.ds(0, row_ref.shape[0], stride=8), :]


def mix(adjoint_field, mixing_inverse, cloud_top, conv_frac, layer_mass):
    levels, row_count, col_count = adjoint_field.shape
    blocks = row_count // 8
    half = lambda h: pl.BlockSpec((levels, 8, LANES), lambda b: (0, b, h))
    flat = pl.BlockSpec((8, col_count), lambda b: (b, 0))
    field, wide, row = pl.pallas_call(
        mix_kernel,
        grid=(blocks,),
        in_specs=[
            half(0),
            half(1),
            pl.BlockSpec((8, levels, levels), lambda b: (b, 0, 0)),
            flat,
            flat,
            pl.BlockSpec((1, levels), lambda b: (0, 0)),
        ],
        out_specs=[
            pl.BlockSpec((1, col_count, 8, levels), lambda b: (b, 0, 0, 0)),
            IN_VMEM,
            pl.BlockSpec((col_count, levels), lambda b: (0, 0)),
        ],
        out_shape=[
            pltpu.HBM((blocks, col_count, 8, levels), F32),
            pltpu.VMEM((2 * levels, row_count * levels), BF16),
            pltpu.HBM((col_count, levels), F32),
        ],
        compiler_params=params(20),
        cost_estimate=pl.CostEstimate(
            flops=2 * levels * levels * 4 * row_count * col_count,
            bytes_accessed=12 * levels * row_count * col_count,
            transcendentals=0,
        ),
        name="mix_own",
    )(adjoint_field, adjoint_field, mixing_inverse, cloud_top, conv_frac, layer_mass)
    return in_hbm(field), in_vmem(wide), in_hbm(row)


def mix_edge(edge_refs, lines_ref, wide_ref, layer_mass, out_ref):
    levels = layer_mass.shape[0]
    group = iota((levels, 2 * LANES), 1) // EDGE
    top, frac = edge_lines(lines_ref, levels)
    for row in range(8):
        value = jnp.concatenate([level_rows(ref, row, levels) for ref in edge_refs], axis=1)
        value = value * (1.0 / SCALE)
        left, right = [], []
        for q in range(4):
            cols = slice((8 * q + row) * levels, (8 * q + row + 1) * levels)
            high, low = halves(jnp.where(group == q, value, 0.0))
            left += [wide_ref[:, cols], wide_ref[:, cols]]
            right += [high, low]
        both = dot(jnp.concatenate(left, axis=1), jnp.concatenate(right, axis=0))
        mixed = both[:levels] + both[levels:]
        done = convect(mixed, top[row : row + 1].astype(I32), frac[row : row + 1], layer_mass)
        put_columns(out_ref, row, done)


def edge_lines(ref, levels):
    top, high, mid, low = [ref[levels + i] for i in range(EDGE_LINES)]
    return top, high + (mid + low) * (1.0 / SCALE)


def find_places(row, row_count):
    count = row.shape[1]
    upto = (iota((LANES, LANES), 0) <= iota((LANES, LANES), 1)).astype(F32).astype(BF16)
    before = jnp.zeros((row_count, 1), F32)
    places = []
    for start in range(0, count, LANES):
        mine = iota((row_count, LANES), 0) == row[:, start : start + LANES]
        running = dot(mine.astype(F32).astype(BF16), upto)
        place = jnp.sum(jnp.where(mine, running + before, 0.0), axis=0, keepdims=True) - 1.0
        places.append(place.astype(I32))
        before = before + running[:, LANES - 1 :]
    return jnp.concatenate(places, axis=1), jnp.max(before)


def mix_slots(blocks, index, key_ref, table_ref, wide_ref, layer_mass, stack):
    levels = layer_mass.shape[0]
    slots = 8 * WINDOW
    lane = iota((1, slots), 1)
    target = [(8 * b + lane // WINDOW) * PITCH + index * WINDOW + lane % WINDOW for b in blocks]
    target = jnp.concatenate(target, axis=1)
    pick = [
        (key_ref[...] == target[:, start : start + LANES]).astype(F32).astype(BF16)
        for start in range(0, target.shape[1], LANES)
    ]
    found = dot(table_ref[...], jnp.concatenate(pick, axis=1))
    split_high, split_low, top, high, mid, low = [
        found[levels + i : levels + i + 1] for i in range(6)
    ]
    column = (split_high * EDGE + split_low).astype(I32)
    parts = []
    for i, b in enumerate(blocks):
        value = found[:levels, i * slots : (i + 1) * slots].astype(BF16)
        for r in range(8):
            mine = (lane // WINDOW == r).astype(F32).astype(BF16)
            stack[i, r * levels : (r + 1) * levels, :] = value * mine
        start = pl.multiple_of(8 * b * levels, 8 * levels)
        both = dot(wide_ref[:, pl.ds(start, 8 * levels)], stack[i])
        parts.append(both[:levels] + both[levels:])
    mass = jnp.concatenate([layer_mass] * len(blocks), axis=1)
    done = convect(
        jnp.concatenate(parts, axis=1), top.astype(I32), (high + mid) + low, mass
    )
    turned = [done[:, start : start + LANES].T for start in range(0, done.shape[1], LANES)]
    high, low = halves(jnp.concatenate(turned, axis=0))
    return high, low, column


def expand(high, low, column, square, out_ref, add):
    levels = high.shape[1]
    flat = out_ref.reshape(REACH * 8, LANES)
    hot = (iota((REACH, 8 * WINDOW), 0) == column).astype(F32).astype(BF16)
    for group in range(2):
        for r in range(4):
            source = slice((4 * group + r) * WINDOW, (4 * group + r + 1) * WINDOW)
            target = slice(r * levels, (r + 1) * levels)
            square[group, r * WINDOW : (r + 1) * WINDOW, target] = high[source]
            square[group, (4 + r) * WINDOW : (5 + r) * WINDOW, target] = low[source]
        left = hot[:, 4 * group * WINDOW : 4 * (group + 1) * WINDOW]
        forced = dot(jnp.concatenate([left, left], axis=1), square[group])
        for r in range(4):
            rows = pl.ds(4 * group + r, REACH, stride=8)
            part = forced[:, r * levels : (r + 1) * levels]
            flat[rows, :] = flat[rows, :] + part if add else part


def force_rows(
    block, rounds, high_ref, low_ref, column_ref,
    key_ref, table_ref, wide_ref, layer_mass, stack, square, out_ref,
):
    slots = 8 * WINDOW
    here = pl.ds(pl.multiple_of(block * slots, slots), slots)
    expand(high_ref[here, :], low_ref[here, :], column_ref[0:1, here], square, out_ref, False)

    def more(index, carry):
        mixed = mix_slots([block], index, key_ref, table_ref, wide_ref, layer_mass, stack)
        expand(*mixed, square, out_ref, True)
        return carry

    lax.fori_loop(1, rounds, more, 0)


def soundings_kernel(
    got_ref, wide_ref, top_ref, frac_ref, near_ref, far_ref, lines_ref, mass_ref,
    row_ref, west_ref, east_ref, shift_ref, weight_ref,
    key_ref, table_ref, high_ref, low_ref, column_ref, edge_out, rounds_ref, first_ref,
    forced, stack, square,
):
    devices = got_ref.shape[0]
    levels = mass_ref.shape[1]
    n = devices * CAP
    row_count = top_ref.shape[0]
    width = 2 * LANES
    layer_mass = as_wide_column(mass_ref[...])
    mix_edge((near_ref, far_ref), lines_ref, wide_ref, layer_mass, edge_out)

    got = got_ref[...].astype(F32)
    table_ref[:levels, :n] = got[:, :CAP].reshape(n, levels).T.astype(BF16)
    table_ref[:levels, n:] = got[:, CAP : 2 * CAP].reshape(n, levels).T.astype(BF16)
    info = got[:, 2 * CAP :].reshape(devices * 8, LANES).astype(BF16)
    first = iota((devices, devices * 8), 1) == 8 * iota((devices, devices * 8), 0)
    info = dot(first.astype(F32).astype(BF16), info).astype(BF16)
    lines = []
    for kind in range(4):
        chosen = iota((LANES, n), 0) == iota((LANES, n), 1) % CAP + 32 * kind
        spread = dot(info, chosen.astype(F32).astype(BF16))
        mine = iota((devices, n), 0) == iota((devices, n), 1) // CAP
        lines.append(jnp.sum(jnp.where(mine, spread, 0.0), axis=0, keepdims=True))
    own_row, own_col, east_row, east_col = [line.astype(I32) for line in lines]
    own_row, east_row = own_row - 1, east_row - 1
    east_row = jnp.where(east_col < EDGE, east_row, -1)
    row = jnp.concatenate([own_row, east_row], axis=1)
    place, most = find_places(row, row_count)
    rounds = (most.astype(I32) + (WINDOW - 1)) // WINDOW
    rounds_ref[0] = rounds
    key_ref[...] = as_column((row * PITCH + place).astype(F32)).astype(I32)
    column = jnp.concatenate([own_col, width + east_col], axis=1)
    cells = [[(column // EDGE).astype(F32), (column % EDGE).astype(F32)]]

    packed_col = (east_row // 8) * EDGE + east_col
    parts = [
        (own_col, own_row, top_ref[...].astype(F32), frac_ref[...], row_count),
        (packed_col, east_row % 8, *edge_lines(lines_ref, levels), 8),
    ]
    for col, row, top, frac, count in parts:
        hot = (iota((width, n), 0) == col).astype(F32).astype(BF16)
        table = jnp.concatenate([top.astype(BF16)] + thirds(frac), axis=0)
        found = dot(table, hot)
        here = iota((count, n), 0) == row
        cells.append([
            jnp.sum(jnp.where(here, found[i * count : (i + 1) * count], 0.0), axis=0, keepdims=True)
            for i in range(4)
        ])
    lines = cells[0] + [jnp.concatenate(pair, axis=1) for pair in zip(cells[1], cells[2])]
    lines.append(jnp.zeros((CELL_LINES - len(lines), 2 * n), F32))
    table_ref[levels:] = jnp.concatenate(lines, axis=0).astype(BF16)

    high, low, column = mix_slots(
        list(range(row_count // 8)), 0, key_ref, table_ref, wide_ref, layer_mass, stack
    )
    high_ref[...] = high
    low_ref[...] = low
    column_ref[0:1] = column
    column_ref[1:] = jnp.zeros_like(column_ref[1:])
    square[...] = jnp.zeros_like(square)
    force_rows(
        0, rounds, high_ref, low_ref, column_ref,
        key_ref, table_ref, wide_ref, layer_mass, stack, square, forced,
    )
    edge = edge_out.reshape(width * 8, LANES)[pl.ds(0, EDGE, stride=8), :]
    value = jnp.concatenate([row_ref[...], edge], axis=0)
    value = value + forced.reshape(REACH * 8, LANES)[pl.ds(0, REACH, stride=8), :]
    shift = shift_ref[0:1, :]
    weight = weight_ref[0:1, :]
    for bit in (32, 16, 8, 4, 2, 1):
        value = jnp.where((shift & bit) != 0, value[bit:], value[:-bit])
    zonal = (1.0 - weight) * value[:width] + weight * value[1 : width + 1]
    for h, courant_ref in enumerate((west_ref, east_ref)):
        here = slice(h * LANES, (h + 1) * LANES)
        first_ref[:, here] = level_rows(courant_ref, 0) * zonal[here].T


def take_soundings(got, wide, cloud_top, conv_frac, edge_in, layer_mass, row, courant, shift, weight):
    levels = layer_mass.shape[1]
    row_count, col_count = cloud_top.shape
    n = got.shape[0] * CAP
    width = 2 * LANES
    full = lambda array: pl.BlockSpec(array.shape, lambda s: (0,) * array.ndim)
    edge_half = lambda h: pl.BlockSpec((levels + EDGE_LINES, 8, LANES), lambda s: (0, 0, h))
    half = lambda h: pl.BlockSpec((levels, 8, LANES), lambda s: (0, 0, h))
    lines = pl.BlockSpec((8, levels), lambda s: (0, 0))
    return pl.pallas_call(
        soundings_kernel,
        grid=(1,),
        in_specs=[
            IN_VMEM,
            IN_VMEM,
            full(cloud_top),
            full(conv_frac),
            edge_half(0),
            edge_half(1),
            IN_VMEM,
            full(layer_mass),
            full(row),
            half(0),
            half(1),
            lines,
            lines,
        ],
        out_specs=[IN_VMEM] * 6 + [pl.BlockSpec(memory_space=pltpu.SMEM), IN_VMEM],
        out_shape=[
            pltpu.VMEM((2 * n, LANES), I32),
            pltpu.VMEM((levels + CELL_LINES, 2 * n), BF16),
            pltpu.VMEM((row_count * WINDOW, levels), BF16),
            pltpu.VMEM((row_count * WINDOW, levels), BF16),
            pltpu.VMEM((8, row_count * WINDOW), I32),
            pltpu.VMEM((width, 8, levels), F32),
            jax.ShapeDtypeStruct((1,), I32),
            jax.ShapeDtypeStruct((levels, col_count), F32),
        ],
        scratch_shapes=[
            pltpu.VMEM((REACH, 8, levels), F32),
            pltpu.VMEM((row_count // 8, 8 * levels, 8 * WINDOW), BF16),
            pltpu.VMEM((2, 8 * WINDOW, 4 * levels), BF16),
        ],
        compiler_params=params(24 + n // 64),
        name="take_soundings",
    )(
        got, wide, cloud_top, conv_frac, edge_in, edge_in, edge_in, layer_mass, row, courant,
        courant, shift, weight,
    )


def advect_kernel(
    key_ref, table_ref, high_ref, low_ref, column_ref, edge_ref, rounds_ref, wide_ref, field_ref,
    mass_ref,
    west_ref, east_ref, shift_ref, weight_ref,
    out_ref, last_ref,
    forced, coarse, done, stack, square, out_scr, prev, sem,
):
    step = pl.program_id(0)
    blocks = pl.num_programs(0) - 1
    block = blocks - 1 - step
    levels = mass_ref.shape[1]
    width = 2 * LANES

    @pl.when(step == 0)
    def _():
        prev[...] = jnp.zeros_like(prev)
        square[...] = jnp.zeros_like(square)

    layer_mass = as_wide_column(mass_ref[...])
    shift = shift_ref[...]
    weight = weight_ref[...]
    chosen = {bit: (shift & bit) != 0 for bit in (32, 16, 8, 4, 2, 1)}

    def choose(tiles, bit, step):
        return [
            jnp.where(chosen[bit], new, old) for old, new in zip(tiles[:-step], tiles[step:])
        ]

    def by_eights(start):
        tiles = [field_ref[0, start + 8 * i] + forced[start + 8 * i] for i in range(32)]
        tiles += [
            edge_ref[EDGE * block + start + 8 * i] + forced[width + start + 8 * i] for i in range(8)
        ]
        for bit in (32, 16, 8):
            tiles = choose(tiles, bit, bit // 8)
        for i, tile in enumerate(tiles):
            coarse[start + 8 * i] = tile

    def by_ones(chunk, carry):
        start = chunk * 32
        tiles = [coarse[start + i] for i in range(40)]
        for bit in (4, 2, 1):
            tiles = choose(tiles, bit, bit)
        for i in range(32):
            done[start + i] = (1.0 - weight) * tiles[i] + weight * tiles[i + 1]
        return carry

    flat = done.reshape(width * 8, LANES)

    def meridional(index):
        r = 7 - index
        for h, courant_ref in enumerate((west_ref, east_ref)):
            zonal = flat[pl.ds(h * LANES * 8 + r, LANES, stride=8), :].T
            courant = level_rows(courant_ref, r)
            place = out_scr.at[block + 1, h].reshape(levels * 8, LANES)
            place[pl.ds(r, levels, stride=8), :] = (1.0 - courant) * zonal + prev[h]
            prev[h] = courant * zonal

    def shift_only(index, carry):
        by_eights(index)
        return carry

    def both(index, carry):
        meridional(index)
        by_eights(index)
        return carry

    def meridional_only(index, carry):
        meridional(index)
        return carry

    @pl.when(step < blocks)
    def _():
        force_rows(
            block, rounds_ref[0], high_ref, low_ref, column_ref,
            key_ref, table_ref, wide_ref, layer_mass, stack, square, forced,
        )

    @pl.when(step == 0)
    def _():
        lax.fori_loop(0, 8, shift_only, 0)

    @pl.when((step > 0) & (step < blocks))
    def _():
        lax.fori_loop(0, 8, both, 0)

    @pl.when(step < blocks)
    def _():
        lax.fori_loop(0, width // 32, by_ones, 0)

    @pl.when(step == blocks)
    def _():
        lax.fori_loop(0, 8, meridional_only, 0)

    @pl.when(step == 1)
    def _():
        for h in range(2):
            place = out_scr.at[blocks - 1, h].reshape(levels * 8, LANES)
            last_ref[:, h * LANES : (h + 1) * LANES] = place[pl.ds(7, levels, stride=8), :]

    def copies(b):
        return [
            pltpu.make_async_copy(
                out_scr.at[b, h],
                out_ref.at[:, pl.ds(b * 8, 8), pl.ds(h * LANES, LANES)],
                sem.at[b, h],
            )
            for h in range(2)
        ]

    for b in range(out_scr.shape[0]):

        @pl.when(block + 1 == b)
        def _():
            for copy in copies(b):
                copy.start()

    @pl.when(step == blocks)
    def _():
        for b in range(out_scr.shape[0]):
            for copy in copies(b):
                copy.wait()


def advect(soundings, edge_field, rounds, wide, field, layer_mass, courant, shift, weight):
    blocks, col_count, _, levels = field.shape
    n = soundings[0].shape[0] // 2
    half = lambda h: pl.BlockSpec((levels, 8, LANES), lambda s: (0, jnp.minimum(blocks - s, blocks - 1), h))
    here = lambda s: jnp.maximum(blocks - 1 - s, 0)
    lines = pl.BlockSpec((8, levels), lambda s: (here(s), 0))
    return pl.pallas_call(
        advect_kernel,
        grid=(blocks + 1,),
        in_specs=[IN_VMEM] * 6
        + [
            pl.BlockSpec(memory_space=pltpu.SMEM),
            IN_VMEM,
            pl.BlockSpec((1, col_count, 8, levels), lambda s: (here(s), 0, 0, 0)),
            pl.BlockSpec((1, levels), lambda s: (0, 0)),
            half(0),
            half(1),
            lines,
            lines,
        ],
        out_specs=[pl.BlockSpec(memory_space=pl.ANY), IN_VMEM],
        out_shape=[
            jax.ShapeDtypeStruct(courant.shape, F32),
            pltpu.VMEM((levels, col_count), F32),
        ],
        scratch_shapes=[
            pltpu.VMEM((REACH, 8, levels), F32),
            pltpu.VMEM((col_count + 8, 8, levels), F32),
            pltpu.VMEM((col_count, 8, levels), F32),
            pltpu.VMEM((1, 8 * levels, 8 * WINDOW), BF16),
            pltpu.VMEM((2, 8 * WINDOW, 4 * levels), BF16),
            pltpu.VMEM((blocks, 2, levels, 8, LANES), F32),
            pltpu.VMEM((2, levels, LANES), F32),
            pltpu.SemaphoreType.DMA((blocks, 2)),
        ],
        compiler_params=params(24 + n // 128),
        cost_estimate=pl.CostEstimate(
            flops=2 * levels * 8 * blocks * n * col_count,
            bytes_accessed=12 * levels * 8 * blocks * col_count,
            transcendentals=0,
        ),
        name="advect",
    )(
        *soundings, edge_field, rounds, wide, field, layer_mass, courant, courant, shift, weight
    )


def close_kernel(last_ref, north_ref, _, out_ref, row, sem):
    row[...] = last_ref[...] + north_ref[...]
    copy = pltpu.make_async_copy(row, out_ref.at[:, out_ref.shape[1] - 1, :], sem)
    copy.start()
    copy.wait()


def close(out, last, north):
    in_place = pl.BlockSpec(memory_space=pl.ANY)
    return pl.pallas_call(
        close_kernel,
        in_specs=[IN_VMEM, IN_VMEM, in_place],
        out_specs=in_place,
        out_shape=jax.ShapeDtypeStruct(out.shape, F32),
        scratch_shapes=[pltpu.VMEM(last.shape, F32), pltpu.SemaphoreType.DMA],
        input_output_aliases={2: 0},
        compiler_params=params(4),
        name="close_last_row",
    )(last, north, out)


def shards(
    adjoint_field,
    mixing_inverse,
    cloud_top,
    conv_frac,
    thickness,
    zonal_shift,
    zonal_frac,
    merid_courant,
    obs_kernel,
    obs_depart,
    obs_dest,
    obs_col,
    obs_count,
):
    adjoint_field, mixing_inverse, cloud_top, conv_frac, merid_courant, obs_kernel = [
        in_hbm(array)
        for array in (
            adjoint_field, mixing_inverse, cloud_top, conv_frac, merid_courant, obs_kernel
        )
    ]
    levels, row_count, col_count = adjoint_field.shape
    lat_count, lon_count = lax.axis_size("lat"), lax.axis_size("lon")
    devices = lat_count * lon_count
    sent = prepare(devices, lon_count, obs_count, obs_dest, obs_col, obs_depart, obs_kernel)
    sent, field_after = lax.optimization_barrier((sent, adjoint_field))
    got = lax.all_to_all(
        sent.reshape(devices, SLOTS, levels), ("lat", "lon"), split_axis=0, concat_axis=0, tiled=True
    )
    westward = [((i + 1) % lon_count, i) for i in range(lon_count)]
    layer_mass = in_hbm(thickness.reshape(1, levels))
    field_after = in_hbm(field_after)
    edge = edge_columns(field_after, cloud_top, conv_frac)
    field, wide, row = mix(field_after, mixing_inverse, cloud_top, conv_frac, layer_mass)
    edge_in = in_vmem(lax.ppermute(edge.astype(jnp.float16), "lon", westward).astype(F32))
    shift, weight = in_hbm(zonal_shift.T), in_hbm(zonal_frac.T)
    *soundings, edge_field, rounds, first = take_soundings(
        got, wide, cloud_top, conv_frac, edge_in, layer_mass, row, merid_courant, shift, weight
    )
    southward = [(i + 1, i) for i in range(lat_count - 1)]
    north = lax.ppermute(first, "lat", southward)
    out, last = advect(
        [in_vmem(part) for part in soundings], in_vmem(edge_field), rounds, wide, field, layer_mass,
        merid_courant, shift, weight,
    )
    return close(out, last, north)


def solution(mesh):
    in_specs = (
        P(None, "lat", "lon"),
        P("lat", None, None),
        P("lat", "lon"),
        P("lat", "lon"),
        P(),
        P(None, "lat"),
        P(None, "lat"),
        P(None, "lat", "lon"),
        P(("lat", "lon"), None),
        P(("lat", "lon")),
        P(("lat", "lon")),
        P(("lat", "lon")),
        P(("lat", "lon")),
    )
    out_specs = P(None, "lat", "lon")
    return jax.shard_map(shards, mesh=mesh, in_specs=in_specs, out_specs=out_specs, check_vma=False)
```

```python
import functools

import jax
import jax.numpy as jnp
from jax import lax
from jax.experimental import pallas as pl
from jax.experimental.pallas import tpu as pltpu
from jax.sharding import PartitionSpec as P

F32, BF16, I32 = jnp.float32, jnp.bfloat16, jnp.int32
CAP = 16
SLOTS = 40
EDGE = 64
LANES = 128
GROUP = 32
EDGE_LINES = 4
SCALE = 4096.0
WINDOW = 32
REACH = 2 * LANES + EDGE
PITCH = 4096
CELL_LINES = 16
MIB = 1024 * 1024


IN_VMEM = pl.BlockSpec(memory_space=pltpu.VMEM)


def iota(shape, dim):
    return lax.broadcasted_iota(I32, shape, dim)


def params(mib):
    return pltpu.CompilerParams(vmem_limit_bytes=mib * MIB)


def in_hbm(array):
    return pltpu.with_memory_space_constraint(array, pltpu.HBM)


def in_vmem(array):
    return pltpu.with_memory_space_constraint(array, pltpu.VMEM)


def dot(left, right):
    return jnp.dot(left, right, preferred_element_type=F32)


def dot_nt(left, right):
    return lax.dot_general(left, right, (((1,), (1,)), ((), ())), preferred_element_type=F32)


def halves(value):
    high = value.astype(BF16)
    return high, (value - high.astype(F32)).astype(BF16)


def thirds(value):
    high = value.astype(BF16)
    rest = value - high.astype(F32)
    mid = rest.astype(BF16)
    return [high, mid, (rest - mid.astype(F32)).astype(BF16)]


def as_column(line):
    return jnp.broadcast_to(line, (LANES, line.shape[1])).T


def as_wide_column(line):
    column = as_column(line)
    return jnp.concatenate([column, column], axis=1)


def convect(mixed, top, frac, layer_mass):
    inside = iota(mixed.shape, 0) < top
    total = jnp.sum(jnp.where(inside, mixed, 0.0), axis=0, keepdims=True)
    mass = jnp.sum(jnp.where(inside, layer_mass, 0.0), axis=0, keepdims=True)
    mean = total / jnp.where(mass > 0.0, mass, 1.0)
    return mixed + jnp.where(inside, frac * (layer_mass * mean - mixed), 0.0)


def prep_kernel(lon_count, count_ref, dest_ref, col_ref, depart_ref, obs_ref, out_ref):
    n = obs_ref.shape[0]
    rows = GROUP * SLOTS
    lane = iota((1, n), 1)
    live = lane < count_ref[0]
    dest = jnp.where(live, dest_ref[...], -1)
    cell = col_ref[...]
    cell_row = (cell // 256 + 1).astype(F32)
    cell_col = (cell % 256).astype(F32)
    contribution = (obs_ref[...].astype(F32) * as_column(depart_ref[...])).astype(BF16)
    local = iota((GROUP, n), 0)
    own_id = pl.program_id(0) * GROUP + local
    lon_id = own_id % lon_count
    east_id = jnp.where(lon_id == lon_count - 1, own_id - lon_id, own_id + 1)
    slots, places, left = [], [], []
    for ident, offset in ((own_id, 0), (east_id, CAP)):
        hit = dest == ident
        before = jnp.sum((live & (dest < ident)).astype(I32), axis=1, keepdims=True)
        place = lane - before
        slot = jnp.where(hit, local * SLOTS + offset + place + 1, 0)
        slots.append(jnp.sum(slot, axis=0, keepdims=True) - 1)
        places.append(jnp.sum(jnp.where(hit, place, 0), axis=0, keepdims=True))
        left.append(jnp.where(hit, cell_row, 0.0).astype(BF16))
        left.append(jnp.where(hit, cell_col, 0.0).astype(BF16))
    out_row = iota((rows, n), 0)
    pick = ((out_row == slots[0]) | (out_row == slots[1])).astype(F32).astype(BF16)
    spot = iota((LANES, n), 0)
    right = [
        (spot == 32 * kind + places[kind // 2]).astype(F32).astype(BF16) for kind in range(4)
    ]
    cells = dot_nt(jnp.concatenate(left, axis=1), jnp.concatenate(right, axis=1))
    spread = (iota((rows, GROUP), 0) == iota((rows, GROUP), 1) * SLOTS + 2 * CAP)
    spread = spread.astype(F32).astype(BF16)
    out_ref[...] = (dot(pick, contribution) + dot(spread, cells.astype(BF16))).astype(BF16)


def prepare(devices, lon_count, obs_count, obs_dest, obs_col, obs_depart, obs_kernel):
    n, levels = obs_kernel.shape
    steps = devices // GROUP
    whole = lambda shape: pl.BlockSpec(shape, lambda g: (0, 0))
    return pl.pallas_call(
        functools.partial(prep_kernel, lon_count),
        grid=(steps,),
        in_specs=[
            pl.BlockSpec(memory_space=pltpu.SMEM),
            whole((1, n)),
            whole((1, n)),
            whole((1, n)),
            whole((n, levels)),
        ],
        out_specs=pl.BlockSpec((GROUP * SLOTS, levels), lambda g: (g, 0)),
        out_shape=pltpu.VMEM((devices * SLOTS, levels), BF16),
        compiler_params=params(16 + devices // 4),
        name="soundings_out",
    )(
        obs_count,
        in_hbm(obs_dest.reshape(1, n)),
        in_hbm(obs_col.reshape(1, n)),
        in_hbm(obs_depart.reshape(1, n)),
        obs_kernel,
    )


def level_rows(ref, row, count=None):
    levels = ref.shape[0]
    count = levels if count is None else count
    return ref.reshape(levels * 8, LANES)[pl.ds(row, count, stride=8), :]


def pack_edge(block):
    parts = [block[:, 8 * q : 8 * q + 8, :] for q in range(4)]
    low = iota(parts[0].shape, 2) < EDGE
    pairs = [
        jnp.where(low, parts[2 * h], pltpu.roll(parts[2 * h + 1], EDGE, 2)) for h in range(2)
    ]
    return jnp.concatenate(pairs, axis=2)


def edge_kernel(field_ref, top_ref, frac_ref, out_ref):
    step = pl.program_id(0)
    count = field_ref.shape[0]
    here = pl.ds(pl.multiple_of(step * count, count), count)
    out_ref[here] = pack_edge(field_ref[...]) * SCALE

    @pl.when(step == 0)
    def _():
        pieces = thirds(frac_ref[...])
        lines = [top_ref[...].astype(F32)] + [piece.astype(F32) for piece in pieces]
        lines[2:] = [line * SCALE for line in lines[2:]]
        first = out_ref.shape[0] - EDGE_LINES
        for i, line in enumerate(lines):
            out_ref[first + i : first + i + 1] = pack_edge(line[None])


def edge_columns(adjoint_field, cloud_top, conv_frac):
    levels, row_count, _ = adjoint_field.shape
    flat = pl.BlockSpec((row_count, LANES), lambda i: (0, 0))
    return pl.pallas_call(
        edge_kernel,
        grid=(2,),
        in_specs=[pl.BlockSpec((levels // 2, row_count, LANES), lambda i: (i, 0, 0)), flat, flat],
        out_specs=IN_VMEM,
        out_shape=pltpu.VMEM((levels + EDGE_LINES, 8, 4 * EDGE), F32),
        compiler_params=params(16),
        cost_estimate=pl.CostEstimate(
            flops=levels * levels * 4 * row_count * LANES,
            bytes_accessed=12 * levels * row_count * LANES,
            transcendentals=0,
        ),
        name="edge_columns",
    )(adjoint_field, cloud_top, conv_frac)


def put_columns(ref, row, value):
    count = ref.shape[0]
    flat = ref.reshape(count * 8, LANES)
    for h in range(count // LANES):
        part = value[:, h * LANES : (h + 1) * LANES].T
        flat[pl.ds(h * LANES * 8 + row, LANES, stride=8), :] = part


def mix_rows(field_refs, mixing_ref, top, frac, layer_mass, block, out_ref, wide_ref):
    levels = mixing_ref.shape[1]
    for row in range(8):
        value = jnp.concatenate([level_rows(ref, row) for ref in field_refs], axis=1)
        high, low = halves(value)
        mix_high, mix_low = halves(mixing_ref[row])
        here = pl.ds(pl.multiple_of((8 * block + row) * levels, levels), levels)
        wide_ref[:levels, here] = mix_high
        wide_ref[levels:, here] = mix_low
        four = jnp.concatenate([mix_high, mix_low], axis=0)
        both = dot(jnp.concatenate([four, four], axis=1), jnp.concatenate([high, low], axis=0))
        mixed = both[:levels] + both[levels:]
        done = convect(mixed, top[row : row + 1, :], frac[row : row + 1, :], layer_mass)
        put_columns(out_ref.at[0], row, done)


def mix_kernel(
    west_ref, east_ref, mixing_ref, top_ref, frac_ref, mass_ref, out_ref, wide_ref, row_ref
):
    layer_mass = as_wide_column(mass_ref[...])
    block = pl.program_id(0)
    mix_rows(
        (west_ref, east_ref), mixing_ref, top_ref[...], frac_ref[...], layer_mass, block,
        out_ref, wide_ref,
    )

    @pl.when(block == 0)
    def _():
        flat = out_ref.at[0].reshape(row_ref.shape[0] * 8, LANES)
        row_ref[...] = flat[pl.ds(0, row_ref.shape[0], stride=8), :]


def mix(adjoint_field, mixing_inverse, cloud_top, conv_frac, layer_mass):
    levels, row_count, col_count = adjoint_field.shape
    blocks = row_count // 8
    half = lambda h: pl.BlockSpec((levels, 8, LANES), lambda b: (0, b, h))
    flat = pl.BlockSpec((8, col_count), lambda b: (b, 0))
    field, wide, row = pl.pallas_call(
        mix_kernel,
        grid=(blocks,),
        in_specs=[
            half(0),
            half(1),
            pl.BlockSpec((8, levels, levels), lambda b: (b, 0, 0)),
            flat,
            flat,
            pl.BlockSpec((1, levels), lambda b: (0, 0)),
        ],
        out_specs=[
            pl.BlockSpec((1, col_count, 8, levels), lambda b: (b, 0, 0, 0)),
            IN_VMEM,
            pl.BlockSpec((col_count, levels), lambda b: (0, 0)),
        ],
        out_shape=[
            pltpu.HBM((blocks, col_count, 8, levels), F32),
            pltpu.VMEM((2 * levels, row_count * levels), BF16),
            pltpu.HBM((col_count, levels), F32),
        ],
        compiler_params=params(20),
        cost_estimate=pl.CostEstimate(
            flops=2 * levels * levels * 4 * row_count * col_count,
            bytes_accessed=12 * levels * row_count * col_count,
            transcendentals=0,
        ),
        name="mix_own",
    )(adjoint_field, adjoint_field, mixing_inverse, cloud_top, conv_frac, layer_mass)
    return in_hbm(field), in_vmem(wide), in_hbm(row)


def mix_edge(edge_refs, lines_ref, wide_ref, layer_mass, out_ref):
    levels = layer_mass.shape[0]
    group = iota((levels, 2 * LANES), 1) // EDGE
    top, frac = edge_lines(lines_ref, levels)
    for row in range(8):
        value = jnp.concatenate([level_rows(ref, row, levels) for ref in edge_refs], axis=1)
        value = value * (1.0 / SCALE)
        left, right = [], []
        for q in range(4):
            cols = slice((8 * q + row) * levels, (8 * q + row + 1) * levels)
            high, low = halves(jnp.where(group == q, value, 0.0))
            left += [wide_ref[:, cols], wide_ref[:, cols]]
            right += [high, low]
        both = dot(jnp.concatenate(left, axis=1), jnp.concatenate(right, axis=0))
        mixed = both[:levels] + both[levels:]
        done = convect(mixed, top[row : row + 1].astype(I32), frac[row : row + 1], layer_mass)
        put_columns(out_ref, row, done)


def edge_lines(ref, levels):
    top, high, mid, low = [ref[levels + i] for i in range(EDGE_LINES)]
    return top, high + (mid + low) * (1.0 / SCALE)


def find_places(row, row_count):
    count = row.shape[1]
    upto = (iota((LANES, LANES), 0) <= iota((LANES, LANES), 1)).astype(F32).astype(BF16)
    before = jnp.zeros((row_count, 1), F32)
    places = []
    for start in range(0, count, LANES):
        mine = iota((row_count, LANES), 0) == row[:, start : start + LANES]
        running = dot(mine.astype(F32).astype(BF16), upto)
        place = jnp.sum(jnp.where(mine, running + before, 0.0), axis=0, keepdims=True) - 1.0
        places.append(place.astype(I32))
        before = before + running[:, LANES - 1 :]
    return jnp.concatenate(places, axis=1), jnp.max(before)


def mix_slots(blocks, index, key_ref, table_ref, wide_ref, layer_mass, stack):
    levels = layer_mass.shape[0]
    slots = 8 * WINDOW
    lane = iota((1, slots), 1)
    target = [(8 * b + lane // WINDOW) * PITCH + index * WINDOW + lane % WINDOW for b in blocks]
    target = jnp.concatenate(target, axis=1)
    pick = [
        (key_ref[...] == target[:, start : start + LANES]).astype(F32).astype(BF16)
        for start in range(0, target.shape[1], LANES)
    ]
    found = dot(table_ref[...], jnp.concatenate(pick, axis=1))
    split_high, split_low, top, high, mid, low = [
        found[levels + i : levels + i + 1] for i in range(6)
    ]
    column = (split_high * EDGE + split_low).astype(I32)
    parts = []
    for i, b in enumerate(blocks):
        value = found[:levels, i * slots : (i + 1) * slots].astype(BF16)
        for r in range(8):
            mine = (lane // WINDOW == r).astype(F32).astype(BF16)
            stack[i, r * levels : (r + 1) * levels, :] = value * mine
        start = pl.multiple_of(8 * b * levels, 8 * levels)
        both = dot(wide_ref[:, pl.ds(start, 8 * levels)], stack[i])
        parts.append(both[:levels] + both[levels:])
    mass = jnp.concatenate([layer_mass] * len(blocks), axis=1)
    done = convect(
        jnp.concatenate(parts, axis=1), top.astype(I32), (high + mid) + low, mass
    )
    turned = [done[:, start : start + LANES].T for start in range(0, done.shape[1], LANES)]
    high, low = halves(jnp.concatenate(turned, axis=0))
    return high, low, column


def expand(high, low, column, square, out_ref, add):
    levels = high.shape[1]
    flat = out_ref.reshape(REACH * 8, LANES)
    hot = (iota((REACH, 8 * WINDOW), 0) == column).astype(F32).astype(BF16)
    for group in range(2):
        for r in range(4):
            source = slice((4 * group + r) * WINDOW, (4 * group + r + 1) * WINDOW)
            target = slice(r * levels, (r + 1) * levels)
            square[group, r * WINDOW : (r + 1) * WINDOW, target] = high[source]
            square[group, (4 + r) * WINDOW : (5 + r) * WINDOW, target] = low[source]
        left = hot[:, 4 * group * WINDOW : 4 * (group + 1) * WINDOW]
        forced = dot(jnp.concatenate([left, left], axis=1), square[group])
        for r in range(4):
            rows = pl.ds(4 * group + r, REACH, stride=8)
            part = forced[:, r * levels : (r + 1) * levels]
            flat[rows, :] = flat[rows, :] + part if add else part


def force_rows(
    block, rounds, high_ref, low_ref, column_ref,
    key_ref, table_ref, wide_ref, layer_mass, stack, square, out_ref,
):
    slots = 8 * WINDOW
    here = pl.ds(pl.multiple_of(block * slots, slots), slots)
    expand(high_ref[here, :], low_ref[here, :], column_ref[0:1, here], square, out_ref, False)

    def more(index, carry):
        mixed = mix_slots([block], index, key_ref, table_ref, wide_ref, layer_mass, stack)
        expand(*mixed, square, out_ref, True)
        return carry

    lax.fori_loop(1, rounds, more, 0)


def soundings_kernel(
    got_ref, wide_ref, top_ref, frac_ref, near_ref, far_ref, lines_ref, mass_ref,
    row_ref, west_ref, east_ref, shift_ref, weight_ref,
    key_ref, table_ref, high_ref, low_ref, column_ref, edge_out, rounds_ref, first_ref,
    forced, stack, square,
):
    devices = got_ref.shape[0]
    levels = mass_ref.shape[1]
    n = devices * CAP
    row_count = top_ref.shape[0]
    width = 2 * LANES
    layer_mass = as_wide_column(mass_ref[...])
    mix_edge((near_ref, far_ref), lines_ref, wide_ref, layer_mass, edge_out)

    got = got_ref[...].astype(F32)
    table_ref[:levels, :n] = got[:, :CAP].reshape(n, levels).T.astype(BF16)
    table_ref[:levels, n:] = got[:, CAP : 2 * CAP].reshape(n, levels).T.astype(BF16)
    info = got[:, 2 * CAP :].reshape(devices * 8, LANES).astype(BF16)
    first = iota((devices, devices * 8), 1) == 8 * iota((devices, devices * 8), 0)
    info = dot(first.astype(F32).astype(BF16), info).astype(BF16)
    lines = []
    for kind in range(4):
        chosen = iota((LANES, n), 0) == iota((LANES, n), 1) % CAP + 32 * kind
        spread = dot(info, chosen.astype(F32).astype(BF16))
        mine = iota((devices, n), 0) == iota((devices, n), 1) // CAP
        lines.append(jnp.sum(jnp.where(mine, spread, 0.0), axis=0, keepdims=True))
    own_row, own_col, east_row, east_col = [line.astype(I32) for line in lines]
    own_row, east_row = own_row - 1, east_row - 1
    east_row = jnp.where(east_col < EDGE, east_row, -1)
    row = jnp.concatenate([own_row, east_row], axis=1)
    place, most = find_places(row, row_count)
    rounds = (most.astype(I32) + (WINDOW - 1)) // WINDOW
    rounds_ref[0] = rounds
    key_ref[...] = as_column((row * PITCH + place).astype(F32)).astype(I32)
    column = jnp.concatenate([own_col, width + east_col], axis=1)
    cells = [[(column // EDGE).astype(F32), (column % EDGE).astype(F32)]]

    packed_col = (east_row // 8) * EDGE + east_col
    parts = [
        (own_col, own_row, top_ref[...].astype(F32), frac_ref[...], row_count),
        (packed_col, east_row % 8, *edge_lines(lines_ref, levels), 8),
    ]
    for col, row, top, frac, count in parts:
        hot = (iota((width, n), 0) == col).astype(F32).astype(BF16)
        table = jnp.concatenate([top.astype(BF16)] + thirds(frac), axis=0)
        found = dot(table, hot)
        here = iota((count, n), 0) == row
        cells.append([
            jnp.sum(jnp.where(here, found[i * count : (i + 1) * count], 0.0), axis=0, keepdims=True)
            for i in range(4)
        ])
    lines = cells[0] + [jnp.concatenate(pair, axis=1) for pair in zip(cells[1], cells[2])]
    lines.append(jnp.zeros((CELL_LINES - len(lines), 2 * n), F32))
    table_ref[levels:] = jnp.concatenate(lines, axis=0).astype(BF16)

    high, low, column = mix_slots(
        list(range(row_count // 8)), 0, key_ref, table_ref, wide_ref, layer_mass, stack
    )
    high_ref[...] = high
    low_ref[...] = low
    column_ref[0:1] = column
    column_ref[1:] = jnp.zeros_like(column_ref[1:])
    square[...] = jnp.zeros_like(square)
    force_rows(
        0, rounds, high_ref, low_ref, column_ref,
        key_ref, table_ref, wide_ref, layer_mass, stack, square, forced,
    )
    edge = edge_out.reshape(width * 8, LANES)[pl.ds(0, EDGE, stride=8), :]
    value = jnp.concatenate([row_ref[...], edge], axis=0)
    value = value + forced.reshape(REACH * 8, LANES)[pl.ds(0, REACH, stride=8), :]
    shift = shift_ref[0:1, :]
    weight = weight_ref[0:1, :]
    for bit in (32, 16, 8, 4, 2, 1):
        value = jnp.where((shift & bit) != 0, value[bit:], value[:-bit])
    zonal = (1.0 - weight) * value[:width] + weight * value[1 : width + 1]
    for h, courant_ref in enumerate((west_ref, east_ref)):
        here = slice(h * LANES, (h + 1) * LANES)
        first_ref[:, here] = level_rows(courant_ref, 0) * zonal[here].T


def take_soundings(got, wide, cloud_top, conv_frac, edge_in, layer_mass, row, courant, shift, weight):
    levels = layer_mass.shape[1]
    row_count, col_count = cloud_top.shape
    n = got.shape[0] * CAP
    width = 2 * LANES
    full = lambda array: pl.BlockSpec(array.shape, lambda s: (0,) * array.ndim)
    edge_half = lambda h: pl.BlockSpec((levels + EDGE_LINES, 8, LANES), lambda s: (0, 0, h))
    half = lambda h: pl.BlockSpec((levels, 8, LANES), lambda s: (0, 0, h))
    lines = pl.BlockSpec((8, levels), lambda s: (0, 0))
    return pl.pallas_call(
        soundings_kernel,
        grid=(1,),
        in_specs=[
            IN_VMEM,
            IN_VMEM,
            full(cloud_top),
            full(conv_frac),
            edge_half(0),
            edge_half(1),
            IN_VMEM,
            full(layer_mass),
            full(row),
            half(0),
            half(1),
            lines,
            lines,
        ],
        out_specs=[IN_VMEM] * 6 + [pl.BlockSpec(memory_space=pltpu.SMEM), IN_VMEM],
        out_shape=[
            pltpu.VMEM((2 * n, LANES), I32),
            pltpu.VMEM((levels + CELL_LINES, 2 * n), BF16),
            pltpu.VMEM((row_count * WINDOW, levels), BF16),
            pltpu.VMEM((row_count * WINDOW, levels), BF16),
            pltpu.VMEM((8, row_count * WINDOW), I32),
            pltpu.VMEM((width, 8, levels), F32),
            jax.ShapeDtypeStruct((1,), I32),
            jax.ShapeDtypeStruct((levels, col_count), F32),
        ],
        scratch_shapes=[
            pltpu.VMEM((REACH, 8, levels), F32),
            pltpu.VMEM((row_count // 8, 8 * levels, 8 * WINDOW), BF16),
            pltpu.VMEM((2, 8 * WINDOW, 4 * levels), BF16),
        ],
        compiler_params=params(24 + n // 64),
        name="take_soundings",
    )(
        got, wide, cloud_top, conv_frac, edge_in, edge_in, edge_in, layer_mass, row, courant,
        courant, shift, weight,
    )


def advect_kernel(
    key_ref, table_ref, high_ref, low_ref, column_ref, edge_ref, rounds_ref, wide_ref, field_ref,
    mass_ref,
    west_ref, east_ref, shift_ref, weight_ref,
    out_ref, last_ref,
    forced, coarse, done, stack, square, out_scr, prev, sem,
):
    step = pl.program_id(0)
    blocks = pl.num_programs(0) - 1
    block = blocks - 1 - step
    levels = mass_ref.shape[1]
    width = 2 * LANES

    @pl.when(step == 0)
    def _():
        prev[...] = jnp.zeros_like(prev)
        square[...] = jnp.zeros_like(square)

    layer_mass = as_wide_column(mass_ref[...])
    shift = shift_ref[...]
    weight = weight_ref[...]
    chosen = {bit: (shift & bit) != 0 for bit in (32, 16, 8, 4, 2, 1)}

    def choose(tiles, bit, step):
        return [
            jnp.where(chosen[bit], new, old) for old, new in zip(tiles[:-step], tiles[step:])
        ]

    def by_eights(start):
        tiles = [field_ref[0, start + 8 * i] + forced[start + 8 * i] for i in range(32)]
        tiles += [
            edge_ref[EDGE * block + start + 8 * i] + forced[width + start + 8 * i] for i in range(8)
        ]
        for bit in (32, 16, 8):
            tiles = choose(tiles, bit, bit // 8)
        for i, tile in enumerate(tiles):
            coarse[start + 8 * i] = tile

    def by_ones(chunk, carry):
        start = chunk * 32
        tiles = [coarse[start + i] for i in range(40)]
        for bit in (4, 2, 1):
            tiles = choose(tiles, bit, bit)
        for i in range(32):
            done[start + i] = (1.0 - weight) * tiles[i] + weight * tiles[i + 1]
        return carry

    flat = done.reshape(width * 8, LANES)

    def meridional(beside):
        later = [prev[0], prev[1]]
        for index in range(8):
            r = 7 - index
            for h, courant_ref in enumerate((west_ref, east_ref)):
                zonal = flat[pl.ds(h * LANES * 8 + r, LANES, stride=8), :].T
                courant = level_rows(courant_ref, r)
                place = out_scr.at[block + 1, h].reshape(levels * 8, LANES)
                place[pl.ds(r, levels, stride=8), :] = (1.0 - courant) * zonal + later[h]
                later[h] = courant * zonal
            beside(index)
        prev[0] = later[0]
        prev[1] = later[1]

    def shift_only(index, carry):
        by_eights(index)
        return carry

    @pl.when(step < blocks)
    def _():
        force_rows(
            block, rounds_ref[0], high_ref, low_ref, column_ref,
            key_ref, table_ref, wide_ref, layer_mass, stack, square, forced,
        )

    @pl.when(step == 0)
    def _():
        lax.fori_loop(0, 8, shift_only, 0)

    @pl.when((step > 0) & (step < blocks))
    def _():
        meridional(by_eights)

    @pl.when(step < blocks)
    def _():
        lax.fori_loop(0, width // 32, by_ones, 0)

    @pl.when(step == blocks)
    def _():
        meridional(lambda index: None)

    @pl.when(step == 1)
    def _():
        for h in range(2):
            place = out_scr.at[blocks - 1, h].reshape(levels * 8, LANES)
            last_ref[:, h * LANES : (h + 1) * LANES] = place[pl.ds(7, levels, stride=8), :]

    def copies(b):
        return [
            pltpu.make_async_copy(
                out_scr.at[b, h],
                out_ref.at[:, pl.ds(b * 8, 8), pl.ds(h * LANES, LANES)],
                sem.at[b, h],
            )
            for h in range(2)
        ]

    for b in range(out_scr.shape[0]):

        @pl.when(block + 1 == b)
        def _():
            for copy in copies(b):
                copy.start()

    @pl.when(step == blocks)
    def _():
        for b in range(out_scr.shape[0]):
            for copy in copies(b):
                copy.wait()


def advect(soundings, edge_field, rounds, wide, field, layer_mass, courant, shift, weight):
    blocks, col_count, _, levels = field.shape
    n = soundings[0].shape[0] // 2
    half = lambda h: pl.BlockSpec((levels, 8, LANES), lambda s: (0, jnp.minimum(blocks - s, blocks - 1), h))
    here = lambda s: jnp.maximum(blocks - 1 - s, 0)
    lines = pl.BlockSpec((8, levels), lambda s: (here(s), 0))
    return pl.pallas_call(
        advect_kernel,
        grid=(blocks + 1,),
        in_specs=[IN_VMEM] * 6
        + [
            pl.BlockSpec(memory_space=pltpu.SMEM),
            IN_VMEM,
            pl.BlockSpec((1, col_count, 8, levels), lambda s: (here(s), 0, 0, 0)),
            pl.BlockSpec((1, levels), lambda s: (0, 0)),
            half(0),
            half(1),
            lines,
            lines,
        ],
        out_specs=[pl.BlockSpec(memory_space=pl.ANY), IN_VMEM],
        out_shape=[
            jax.ShapeDtypeStruct(courant.shape, F32),
            pltpu.VMEM((levels, col_count), F32),
        ],
        scratch_shapes=[
            pltpu.VMEM((REACH, 8, levels), F32),
            pltpu.VMEM((col_count + 8, 8, levels), F32),
            pltpu.VMEM((col_count, 8, levels), F32),
            pltpu.VMEM((1, 8 * levels, 8 * WINDOW), BF16),
            pltpu.VMEM((2, 8 * WINDOW, 4 * levels), BF16),
            pltpu.VMEM((blocks, 2, levels, 8, LANES), F32),
            pltpu.VMEM((2, levels, LANES), F32),
            pltpu.SemaphoreType.DMA((blocks, 2)),
        ],
        compiler_params=params(24 + n // 128),
        cost_estimate=pl.CostEstimate(
            flops=2 * levels * 8 * blocks * n * col_count,
            bytes_accessed=12 * levels * 8 * blocks * col_count,
            transcendentals=0,
        ),
        name="advect",
    )(
        *soundings, edge_field, rounds, wide, field, layer_mass, courant, courant, shift, weight
    )


def close_kernel(last_ref, north_ref, _, out_ref, row, sem):
    row[...] = last_ref[...] + north_ref[...]
    copy = pltpu.make_async_copy(row, out_ref.at[:, out_ref.shape[1] - 1, :], sem)
    copy.start()
    copy.wait()


def close(out, last, north):
    in_place = pl.BlockSpec(memory_space=pl.ANY)
    return pl.pallas_call(
        close_kernel,
        in_specs=[IN_VMEM, IN_VMEM, in_place],
        out_specs=in_place,
        out_shape=jax.ShapeDtypeStruct(out.shape, F32),
        scratch_shapes=[pltpu.VMEM(last.shape, F32), pltpu.SemaphoreType.DMA],
        input_output_aliases={2: 0},
        compiler_params=params(4),
        name="close_last_row",
    )(last, north, out)


def shards(
    adjoint_field,
    mixing_inverse,
    cloud_top,
    conv_frac,
    thickness,
    zonal_shift,
    zonal_frac,
    merid_courant,
    obs_kernel,
    obs_depart,
    obs_dest,
    obs_col,
    obs_count,
):
    adjoint_field, mixing_inverse, cloud_top, conv_frac, merid_courant, obs_kernel = [
        in_hbm(array)
        for array in (
            adjoint_field, mixing_inverse, cloud_top, conv_frac, merid_courant, obs_kernel
        )
    ]
    levels, row_count, col_count = adjoint_field.shape
    lat_count, lon_count = lax.axis_size("lat"), lax.axis_size("lon")
    devices = lat_count * lon_count
    sent = prepare(devices, lon_count, obs_count, obs_dest, obs_col, obs_depart, obs_kernel)
    sent, field_after = lax.optimization_barrier((sent, adjoint_field))
    got = lax.all_to_all(
        sent.reshape(devices, SLOTS, levels), ("lat", "lon"), split_axis=0, concat_axis=0, tiled=True
    )
    westward = [((i + 1) % lon_count, i) for i in range(lon_count)]
    layer_mass = in_hbm(thickness.reshape(1, levels))
    field_after = in_hbm(field_after)
    edge = edge_columns(field_after, cloud_top, conv_frac)
    field, wide, row = mix(field_after, mixing_inverse, cloud_top, conv_frac, layer_mass)
    edge_in = in_vmem(lax.ppermute(edge.astype(jnp.float16), "lon", westward).astype(F32))
    shift, weight = in_hbm(zonal_shift.T), in_hbm(zonal_frac.T)
    *soundings, edge_field, rounds, first = take_soundings(
        got, wide, cloud_top, conv_frac, edge_in, layer_mass, row, merid_courant, shift, weight
    )
    southward = [(i + 1, i) for i in range(lat_count - 1)]
    north = lax.ppermute(first, "lat", southward)
    out, last = advect(
        [in_vmem(part) for part in soundings], in_vmem(edge_field), rounds, wide, field, layer_mass,
        merid_courant, shift, weight,
    )
    return close(out, last, north)


def solution(mesh):
    in_specs = (
        P(None, "lat", "lon"),
        P("lat", None, None),
        P("lat", "lon"),
        P("lat", "lon"),
        P(),
        P(None, "lat"),
        P(None, "lat"),
        P(None, "lat", "lon"),
        P(("lat", "lon"), None),
        P(("lat", "lon")),
        P(("lat", "lon")),
        P(("lat", "lon")),
        P(("lat", "lon")),
    )
    out_specs = P(None, "lat", "lon")
    return jax.shard_map(shards, mesh=mesh, in_specs=in_specs, out_specs=out_specs, check_vma=False)
```

```python
import functools

import jax
import jax.numpy as jnp
from jax import lax
from jax.experimental import pallas as pl
from jax.experimental.pallas import tpu as pltpu
from jax.sharding import PartitionSpec as P

F32, BF16, I32 = jnp.float32, jnp.bfloat16, jnp.int32
CAP = 16
SLOTS = 40
EDGE = 64
LANES = 128
GROUP = 32
EDGE_LINES = 4
SCALE = 4096.0
WINDOW = 32
REACH = 2 * LANES + EDGE
PITCH = 4096
CELL_LINES = 16
MIB = 1024 * 1024


IN_VMEM = pl.BlockSpec(memory_space=pltpu.VMEM)


def iota(shape, dim):
    return lax.broadcasted_iota(I32, shape, dim)


def params(mib):
    return pltpu.CompilerParams(vmem_limit_bytes=mib * MIB)


def in_hbm(array):
    return pltpu.with_memory_space_constraint(array, pltpu.HBM)


def in_vmem(array):
    return pltpu.with_memory_space_constraint(array, pltpu.VMEM)


def dot(left, right):
    return jnp.dot(left, right, preferred_element_type=F32)


def dot_nt(left, right):
    return lax.dot_general(left, right, (((1,), (1,)), ((), ())), preferred_element_type=F32)


def halves(value):
    high = value.astype(BF16)
    return high, (value - high.astype(F32)).astype(BF16)


def thirds(value):
    high = value.astype(BF16)
    rest = value - high.astype(F32)
    mid = rest.astype(BF16)
    return [high, mid, (rest - mid.astype(F32)).astype(BF16)]


def as_column(line):
    return jnp.broadcast_to(line, (LANES, line.shape[1])).T


def as_wide_column(line):
    column = as_column(line)
    return jnp.concatenate([column, column], axis=1)


def convect(mixed, top, frac, layer_mass):
    inside = iota(mixed.shape, 0) < top
    total = jnp.sum(jnp.where(inside, mixed, 0.0), axis=0, keepdims=True)
    mass = jnp.sum(jnp.where(inside, layer_mass, 0.0), axis=0, keepdims=True)
    mean = total / jnp.where(mass > 0.0, mass, 1.0)
    return mixed + jnp.where(inside, frac * (layer_mass * mean - mixed), 0.0)


def prep_kernel(lon_count, count_ref, dest_ref, col_ref, depart_ref, obs_ref, out_ref):
    n = obs_ref.shape[0]
    rows = GROUP * SLOTS
    lane = iota((1, n), 1)
    live = lane < count_ref[0]
    dest = jnp.where(live, dest_ref[...], -1)
    cell = col_ref[...]
    cell_row = (cell // 256 + 1).astype(F32)
    cell_col = (cell % 256).astype(F32)
    contribution = (obs_ref[...].astype(F32) * as_column(depart_ref[...])).astype(BF16)
    local = iota((GROUP, n), 0)
    own_id = pl.program_id(0) * GROUP + local
    lon_id = own_id % lon_count
    east_id = jnp.where(lon_id == lon_count - 1, own_id - lon_id, own_id + 1)
    slots, places, left = [], [], []
    for ident, offset in ((own_id, 0), (east_id, CAP)):
        hit = dest == ident
        before = jnp.sum((live & (dest < ident)).astype(I32), axis=1, keepdims=True)
        place = lane - before
        slot = jnp.where(hit, local * SLOTS + offset + place + 1, 0)
        slots.append(jnp.sum(slot, axis=0, keepdims=True) - 1)
        places.append(jnp.sum(jnp.where(hit, place, 0), axis=0, keepdims=True))
        left.append(jnp.where(hit, cell_row, 0.0).astype(BF16))
        left.append(jnp.where(hit, cell_col, 0.0).astype(BF16))
    out_row = iota((rows, n), 0)
    pick = ((out_row == slots[0]) | (out_row == slots[1])).astype(F32).astype(BF16)
    spot = iota((LANES, n), 0)
    right = [
        (spot == 32 * kind + places[kind // 2]).astype(F32).astype(BF16) for kind in range(4)
    ]
    cells = dot_nt(jnp.concatenate(left, axis=1), jnp.concatenate(right, axis=1))
    spread = (iota((rows, GROUP), 0) == iota((rows, GROUP), 1) * SLOTS + 2 * CAP)
    spread = spread.astype(F32).astype(BF16)
    out_ref[...] = (dot(pick, contribution) + dot(spread, cells.astype(BF16))).astype(BF16)


def prepare(devices, lon_count, obs_count, obs_dest, obs_col, obs_depart, obs_kernel):
    n, levels = obs_kernel.shape
    steps = devices // GROUP
    whole = lambda shape: pl.BlockSpec(shape, lambda g: (0, 0))
    return pl.pallas_call(
        functools.partial(prep_kernel, lon_count),
        grid=(steps,),
        in_specs=[
            pl.BlockSpec(memory_space=pltpu.SMEM),
            whole((1, n)),
            whole((1, n)),
            whole((1, n)),
            whole((n, levels)),
        ],
        out_specs=pl.BlockSpec((GROUP * SLOTS, levels), lambda g: (g, 0)),
        out_shape=pltpu.VMEM((devices * SLOTS, levels), BF16),
        compiler_params=params(16 + devices // 4),
        name="soundings_out",
    )(
        obs_count,
        in_hbm(obs_dest.reshape(1, n)),
        in_hbm(obs_col.reshape(1, n)),
        in_hbm(obs_depart.reshape(1, n)),
        obs_kernel,
    )


def level_rows(ref, row, count=None):
    levels = ref.shape[0]
    count = levels if count is None else count
    return ref.reshape(levels * 8, LANES)[pl.ds(row, count, stride=8), :]


def pack_edge(block):
    parts = [block[:, 8 * q : 8 * q + 8, :] for q in range(4)]
    low = iota(parts[0].shape, 2) < EDGE
    return [jnp.where(low, parts[2 * h], pltpu.roll(parts[2 * h + 1], EDGE, 2)) for h in range(2)]


def edge_kernel(field_ref, top_ref, frac_ref, out_ref):
    step = pl.program_id(0)
    count = field_ref.shape[0]
    here = pl.ds(pl.multiple_of(step * count, count), count)
    for h, part in enumerate(pack_edge(field_ref[...])):
        out_ref[h, here] = part * SCALE

    @pl.when(step == 0)
    def _():
        pieces = thirds(frac_ref[...])
        lines = [top_ref[...].astype(F32)] + [piece.astype(F32) for piece in pieces]
        lines[2:] = [line * SCALE for line in lines[2:]]
        first = out_ref.shape[1] - EDGE_LINES
        for i, line in enumerate(lines):
            for h, part in enumerate(pack_edge(line[None])):
                out_ref[h, first + i : first + i + 1] = part


def edge_columns(adjoint_field, cloud_top, conv_frac):
    levels, row_count, _ = adjoint_field.shape
    flat = pl.BlockSpec((row_count, LANES), lambda i: (0, 0))
    return pl.pallas_call(
        edge_kernel,
        grid=(2,),
        in_specs=[pl.BlockSpec((levels // 2, row_count, LANES), lambda i: (i, 0, 0)), flat, flat],
        out_specs=IN_VMEM,
        out_shape=pltpu.VMEM((2, levels + EDGE_LINES, 8, LANES), F32),
        compiler_params=params(16),
        name="edge_columns",
    )(adjoint_field, cloud_top, conv_frac)


def put_columns(ref, row, value):
    count = ref.shape[0]
    flat = ref.reshape(count * 8, LANES)
    for h in range(count // LANES):
        part = value[:, h * LANES : (h + 1) * LANES].T
        flat[pl.ds(h * LANES * 8 + row, LANES, stride=8), :] = part


def mix_rows(field_refs, mixing_ref, top, frac, layer_mass, block, out_ref, wide_ref):
    levels = mixing_ref.shape[1]
    for row in range(8):
        value = jnp.concatenate([level_rows(ref, row) for ref in field_refs], axis=1)
        high, low = halves(value)
        mix_high, mix_low = halves(mixing_ref[row])
        here = pl.ds(pl.multiple_of((8 * block + row) * levels, levels), levels)
        wide_ref[:levels, here] = mix_high
        wide_ref[levels:, here] = mix_low
        four = jnp.concatenate([mix_high, mix_low], axis=0)
        both = dot(jnp.concatenate([four, four], axis=1), jnp.concatenate([high, low], axis=0))
        mixed = both[:levels] + both[levels:]
        done = convect(mixed, top[row : row + 1, :], frac[row : row + 1, :], layer_mass)
        put_columns(out_ref.at[0], row, done)


def mix_kernel(
    west_ref, east_ref, mixing_ref, top_ref, frac_ref, mass_ref, out_ref, wide_ref, row_ref
):
    layer_mass = as_wide_column(mass_ref[...])
    block = pl.program_id(0)
    mix_rows(
        (west_ref, east_ref), mixing_ref, top_ref[...], frac_ref[...], layer_mass, block,
        out_ref, wide_ref,
    )

    @pl.when(block == 0)
    def _():
        flat = out_ref.at[0].reshape(row_ref.shape[0] * 8, LANES)
        row_ref[...] = flat[pl.ds(0, row_ref.shape[0], stride=8), :]


def mix(adjoint_field, mixing_inverse, cloud_top, conv_frac, layer_mass):
    levels, row_count, col_count = adjoint_field.shape
    blocks = row_count // 8
    half = lambda h: pl.BlockSpec((levels, 8, LANES), lambda b: (0, b, h))
    flat = pl.BlockSpec((8, col_count), lambda b: (b, 0))
    field, wide, row = pl.pallas_call(
        mix_kernel,
        grid=(blocks,),
        in_specs=[
            half(0),
            half(1),
            pl.BlockSpec((8, levels, levels), lambda b: (b, 0, 0)),
            flat,
            flat,
            pl.BlockSpec((1, levels), lambda b: (0, 0)),
        ],
        out_specs=[
            pl.BlockSpec((1, col_count, 8, levels), lambda b: (b, 0, 0, 0)),
            IN_VMEM,
            pl.BlockSpec((col_count, levels), lambda b: (0, 0)),
        ],
        out_shape=[
            pltpu.HBM((blocks, col_count, 8, levels), F32),
            pltpu.VMEM((2 * levels, row_count * levels), BF16),
            pltpu.HBM((col_count, levels), F32),
        ],
        compiler_params=params(20),
        cost_estimate=pl.CostEstimate(
            flops=2 * levels * levels * 4 * row_count * col_count,
            bytes_accessed=12 * levels * row_count * col_count,
            transcendentals=0,
        ),
        name="mix_own",
    )(adjoint_field, adjoint_field, mixing_inverse, cloud_top, conv_frac, layer_mass)
    return in_hbm(field), in_vmem(wide), in_hbm(row)


def mix_edge(edge_ref, wide_ref, layer_mass, out_ref):
    levels = layer_mass.shape[0]
    group = iota((levels, 2 * LANES), 1) // EDGE
    top, frac = edge_lines(edge_ref, levels)
    for row in range(8):
        value = jnp.concatenate([level_rows(edge_ref.at[h], row, levels) for h in range(2)], axis=1)
        value = value * (1.0 / SCALE)
        left, right = [], []
        for q in range(4):
            cols = slice((8 * q + row) * levels, (8 * q + row + 1) * levels)
            high, low = halves(jnp.where(group == q, value, 0.0))
            left += [wide_ref[:, cols], wide_ref[:, cols]]
            right += [high, low]
        both = dot(jnp.concatenate(left, axis=1), jnp.concatenate(right, axis=0))
        mixed = both[:levels] + both[levels:]
        done = convect(mixed, top[row : row + 1].astype(I32), frac[row : row + 1], layer_mass)
        put_columns(out_ref, row, done)


def edge_lines(ref, levels):
    top, high, mid, low = [
        jnp.concatenate([ref[0, levels + i], ref[1, levels + i]], axis=1)
        for i in range(EDGE_LINES)
    ]
    return top, high + (mid + low) * (1.0 / SCALE)


def find_places(row, row_count):
    count = row.shape[1]
    upto = (iota((LANES, LANES), 0) <= iota((LANES, LANES), 1)).astype(F32).astype(BF16)
    before = jnp.zeros((row_count, 1), F32)
    places = []
    for start in range(0, count, LANES):
        mine = iota((row_count, LANES), 0) == row[:, start : start + LANES]
        running = dot(mine.astype(F32).astype(BF16), upto)
        place = jnp.sum(jnp.where(mine, running + before, 0.0), axis=0, keepdims=True) - 1.0
        places.append(place.astype(I32))
        before = before + running[:, LANES - 1 :]
    return jnp.concatenate(places, axis=1), jnp.max(before)


def mix_slots(blocks, index, key_ref, table_ref, wide_ref, layer_mass, stack):
    levels = layer_mass.shape[0]
    slots = 8 * WINDOW
    lane = iota((1, slots), 1)
    target = [(8 * b + lane // WINDOW) * PITCH + index * WINDOW + lane % WINDOW for b in blocks]
    target = jnp.concatenate(target, axis=1)
    pick = [
        (key_ref[...] == target[:, start : start + LANES]).astype(F32).astype(BF16)
        for start in range(0, target.shape[1], LANES)
    ]
    found = dot(table_ref[...], jnp.concatenate(pick, axis=1))
    split_high, split_low, top, high, mid, low = [
        found[levels + i : levels + i + 1] for i in range(6)
    ]
    column = (split_high * EDGE + split_low).astype(I32)
    parts = []
    for i, b in enumerate(blocks):
        value = found[:levels, i * slots : (i + 1) * slots].astype(BF16)
        for r in range(8):
            mine = (lane // WINDOW == r).astype(F32).astype(BF16)
            stack[i, r * levels : (r + 1) * levels, :] = value * mine
        start = pl.multiple_of(8 * b * levels, 8 * levels)
        both = dot(wide_ref[:, pl.ds(start, 8 * levels)], stack[i])
        parts.append(both[:levels] + both[levels:])
    mass = jnp.concatenate([layer_mass] * len(blocks), axis=1)
    done = convect(
        jnp.concatenate(parts, axis=1), top.astype(I32), (high + mid) + low, mass
    )
    turned = [done[:, start : start + LANES].T for start in range(0, done.shape[1], LANES)]
    high, low = halves(jnp.concatenate(turned, axis=0))
    return high, low, column


def expand(high, low, column, square, out_ref, add):
    levels = high.shape[1]
    flat = out_ref.reshape(REACH * 8, LANES)
    hot = (iota((REACH, 8 * WINDOW), 0) == column).astype(F32).astype(BF16)
    for group in range(2):
        for r in range(4):
            source = slice((4 * group + r) * WINDOW, (4 * group + r + 1) * WINDOW)
            target = slice(r * levels, (r + 1) * levels)
            square[group, r * WINDOW : (r + 1) * WINDOW, target] = high[source]
            square[group, (4 + r) * WINDOW : (5 + r) * WINDOW, target] = low[source]
        left = hot[:, 4 * group * WINDOW : 4 * (group + 1) * WINDOW]
        forced = dot(jnp.concatenate([left, left], axis=1), square[group])
        for r in range(4):
            rows = pl.ds(4 * group + r, REACH, stride=8)
            part = forced[:, r * levels : (r + 1) * levels]
            flat[rows, :] = flat[rows, :] + part if add else part


def force_rows(
    block, rounds, high_ref, low_ref, column_ref,
    key_ref, table_ref, wide_ref, layer_mass, stack, square, out_ref,
):
    slots = 8 * WINDOW
    here = pl.ds(pl.multiple_of(block * slots, slots), slots)
    expand(high_ref[here, :], low_ref[here, :], column_ref[0:1, here], square, out_ref, False)

    def more(index, carry):
        mixed = mix_slots([block], index, key_ref, table_ref, wide_ref, layer_mass, stack)
        expand(*mixed, square, out_ref, True)
        return carry

    lax.fori_loop(1, rounds, more, 0)


def soundings_kernel(
    got_ref, wide_ref, top_ref, frac_ref, lines_ref, mass_ref,
    row_ref, courant_ref, shift_ref, weight_ref,
    key_ref, table_ref, high_ref, low_ref, column_ref, edge_out, rounds_ref, first_ref,
    forced, stack, square, row_scr, courant_scr, sem,
):
    devices = got_ref.shape[0]
    levels = mass_ref.shape[1]
    n = devices * CAP
    row_count = top_ref.shape[0]
    width = 2 * LANES
    layer_mass = as_wide_column(mass_ref[...])
    late = [
        pltpu.make_async_copy(row_ref, row_scr, sem.at[0]),
        pltpu.make_async_copy(courant_ref.at[:, 0, :], courant_scr, sem.at[1]),
    ]
    for copy in late:
        copy.start()
    mix_edge(lines_ref, wide_ref, layer_mass, edge_out)

    got = got_ref[...].astype(F32)
    table_ref[:levels, :n] = got[:, :CAP].reshape(n, levels).T.astype(BF16)
    table_ref[:levels, n:] = got[:, CAP : 2 * CAP].reshape(n, levels).T.astype(BF16)
    info = got[:, 2 * CAP :].reshape(devices * 8, LANES).astype(BF16)
    first = iota((devices, devices * 8), 1) == 8 * iota((devices, devices * 8), 0)
    info = dot(first.astype(F32).astype(BF16), info).astype(BF16)
    lines = []
    for kind in range(4):
        chosen = iota((LANES, n), 0) == iota((LANES, n), 1) % CAP + 32 * kind
        spread = dot(info, chosen.astype(F32).astype(BF16))
        mine = iota((devices, n), 0) == iota((devices, n), 1) // CAP
        lines.append(jnp.sum(jnp.where(mine, spread, 0.0), axis=0, keepdims=True))
    own_row, own_col, east_row, east_col = [line.astype(I32) for line in lines]
    own_row, east_row = own_row - 1, east_row - 1
    east_row = jnp.where(east_col < EDGE, east_row, -1)
    row = jnp.concatenate([own_row, east_row], axis=1)
    place, most = find_places(row, row_count)
    rounds = (most.astype(I32) + (WINDOW - 1)) // WINDOW
    rounds_ref[0] = rounds
    key_ref[...] = as_column((row * PITCH + place).astype(F32)).astype(I32)
    column = jnp.concatenate([own_col, width + east_col], axis=1)
    cells = [[(column // EDGE).astype(F32), (column % EDGE).astype(F32)]]

    packed_col = (east_row // 8) * EDGE + east_col
    parts = [
        (own_col, own_row, top_ref[...].astype(F32), frac_ref[...], row_count),
        (packed_col, east_row % 8, *edge_lines(lines_ref, levels), 8),
    ]
    for col, row, top, frac, count in parts:
        hot = (iota((width, n), 0) == col).astype(F32).astype(BF16)
        table = jnp.concatenate([top.astype(BF16)] + thirds(frac), axis=0)
        found = dot(table, hot)
        here = iota((count, n), 0) == row
        cells.append([
            jnp.sum(jnp.where(here, found[i * count : (i + 1) * count], 0.0), axis=0, keepdims=True)
            for i in range(4)
        ])
    lines = cells[0] + [jnp.concatenate(pair, axis=1) for pair in zip(cells[1], cells[2])]
    lines.append(jnp.zeros((CELL_LINES - len(lines), 2 * n), F32))
    table_ref[levels:] = jnp.concatenate(lines, axis=0).astype(BF16)

    high, low, column = mix_slots(
        list(range(row_count // 8)), 0, key_ref, table_ref, wide_ref, layer_mass, stack
    )
    high_ref[...] = high
    low_ref[...] = low
    column_ref[0:1] = column
    column_ref[1:] = jnp.zeros_like(column_ref[1:])
    square[...] = jnp.zeros_like(square)
    force_rows(
        0, rounds, high_ref, low_ref, column_ref,
        key_ref, table_ref, wide_ref, layer_mass, stack, square, forced,
    )
    edge = edge_out.reshape(width * 8, LANES)[pl.ds(0, EDGE, stride=8), :]
    for copy in late:
        copy.wait()
    value = jnp.concatenate([row_scr[...], edge], axis=0)
    value = value + forced.reshape(REACH * 8, LANES)[pl.ds(0, REACH, stride=8), :]
    shift = shift_ref[0:1, :]
    weight = weight_ref[0:1, :]
    for bit in (32, 16, 8, 4, 2, 1):
        value = jnp.where((shift & bit) != 0, value[bit:], value[:-bit])
    zonal = (1.0 - weight) * value[:width] + weight * value[1 : width + 1]
    for h in range(2):
        here = slice(h * LANES, (h + 1) * LANES)
        first_ref[:, here] = courant_scr[:, here] * zonal[here].T


def take_soundings(got, wide, cloud_top, conv_frac, edge_in, layer_mass, row, courant, shift, weight):
    levels = layer_mass.shape[1]
    row_count, col_count = cloud_top.shape
    n = got.shape[0] * CAP
    width = 2 * LANES
    full = lambda array: pl.BlockSpec(array.shape, lambda s: (0,) * array.ndim)
    lines = pl.BlockSpec((8, levels), lambda s: (0, 0))
    return pl.pallas_call(
        soundings_kernel,
        grid=(1,),
        in_specs=[
            IN_VMEM,
            IN_VMEM,
            full(cloud_top),
            full(conv_frac),
            IN_VMEM,
            full(layer_mass),
            pl.BlockSpec(memory_space=pl.ANY),
            pl.BlockSpec(memory_space=pl.ANY),
            lines,
            lines,
        ],
        out_specs=[IN_VMEM] * 6 + [pl.BlockSpec(memory_space=pltpu.SMEM), IN_VMEM],
        out_shape=[
            pltpu.VMEM((2 * n, LANES), I32),
            pltpu.VMEM((levels + CELL_LINES, 2 * n), BF16),
            pltpu.VMEM((row_count * WINDOW, levels), BF16),
            pltpu.VMEM((row_count * WINDOW, levels), BF16),
            pltpu.VMEM((8, row_count * WINDOW), I32),
            pltpu.VMEM((width, 8, levels), F32),
            jax.ShapeDtypeStruct((1,), I32),
            jax.ShapeDtypeStruct((levels, col_count), F32),
        ],
        scratch_shapes=[
            pltpu.VMEM((REACH, 8, levels), F32),
            pltpu.VMEM((row_count // 8, 8 * levels, 8 * WINDOW), BF16),
            pltpu.VMEM((2, 8 * WINDOW, 4 * levels), BF16),
            pltpu.VMEM((col_count, levels), F32),
            pltpu.VMEM((levels, col_count), F32),
            pltpu.SemaphoreType.DMA((2,)),
        ],
        compiler_params=params(24 + n // 64),
        name="take_soundings",
    )(
        got, wide, cloud_top, conv_frac, edge_in, layer_mass, row, courant, shift, weight
    )


def advect_kernel(
    key_ref, table_ref, high_ref, low_ref, column_ref, edge_ref, rounds_ref, wide_ref, field_ref,
    mass_ref, courant_ref, shift_ref, weight_ref,
    out_ref, last_ref,
    forced, coarse, done, stack, square, out_scr, prev, field_scr, courant_scr, sem, in_sem,
):
    step = pl.program_id(0)
    blocks = pl.num_programs(0) - 1
    block = blocks - 1 - step
    levels = mass_ref.shape[1]
    width = 2 * LANES

    def field_in(b):
        return pltpu.make_async_copy(field_ref.at[b], field_scr.at[b], in_sem.at[b, 0])

    def courant_in(b, h):
        source = courant_ref.at[:, pl.ds(pl.multiple_of(b * 8, 8), 8), pl.ds(h * LANES, LANES)]
        return pltpu.make_async_copy(source, courant_scr.at[b, h], in_sem.at[b, 1 + h])

    @pl.when(step == 0)
    def _():
        for b in reversed(range(out_scr.shape[0])):
            field_in(b).start()
            for h in range(2):
                courant_in(b, h).start()
        prev[...] = jnp.zeros_like(prev)
        square[...] = jnp.zeros_like(square)

    layer_mass = as_wide_column(mass_ref[...])
    shift = shift_ref[...]
    weight = weight_ref[...]
    chosen = {bit: (shift & bit) != 0 for bit in (32, 16, 8, 4, 2, 1)}

    def choose(tiles, bit, step):
        return [
            jnp.where(chosen[bit], new, old) for old, new in zip(tiles[:-step], tiles[step:])
        ]

    def by_eights(start):
        tiles = [field_scr[block, start + 8 * i] + forced[start + 8 * i] for i in range(32)]
        tiles += [
            edge_ref[EDGE * block + start + 8 * i] + forced[width + start + 8 * i] for i in range(8)
        ]
        for bit in (32, 16, 8):
            tiles = choose(tiles, bit, bit // 8)
        for i, tile in enumerate(tiles):
            coarse[start + 8 * i] = tile

    def by_ones(chunk, carry):
        start = chunk * 32
        tiles = [coarse[start + i] for i in range(40)]
        for bit in (4, 2, 1):
            tiles = choose(tiles, bit, bit)
        for i in range(32):
            done[start + i] = (1.0 - weight) * tiles[i] + weight * tiles[i + 1]
        return carry

    flat = done.reshape(width * 8, LANES)

    def meridional(beside):
        later = [prev[0], prev[1]]
        for index in range(8):
            r = 7 - index
            for h in range(2):
                zonal = flat[pl.ds(h * LANES * 8 + r, LANES, stride=8), :].T
                courant = level_rows(courant_scr.at[block + 1, h], r)
                place = out_scr.at[block + 1, h].reshape(levels * 8, LANES)
                place[pl.ds(r, levels, stride=8), :] = (1.0 - courant) * zonal + later[h]
                later[h] = courant * zonal
            beside(index)
        prev[0] = later[0]
        prev[1] = later[1]

    def shift_only(index, carry):
        by_eights(index)
        return carry

    @pl.when(step < blocks)
    def _():
        force_rows(
            block, rounds_ref[0], high_ref, low_ref, column_ref,
            key_ref, table_ref, wide_ref, layer_mass, stack, square, forced,
        )
        field_in(block).wait()

    @pl.when(step > 0)
    def _():
        for h in range(2):
            courant_in(block + 1, h).wait()

    @pl.when(step == 0)
    def _():
        lax.fori_loop(0, 8, shift_only, 0)

    @pl.when((step > 0) & (step < blocks))
    def _():
        meridional(by_eights)

    @pl.when(step < blocks)
    def _():
        lax.fori_loop(0, width // 32, by_ones, 0)

    @pl.when(step == blocks)
    def _():
        meridional(lambda index: None)

    @pl.when(step == 1)
    def _():
        for h in range(2):
            place = out_scr.at[blocks - 1, h].reshape(levels * 8, LANES)
            last_ref[:, h * LANES : (h + 1) * LANES] = place[pl.ds(7, levels, stride=8), :]

    def copies(b):
        return [
            pltpu.make_async_copy(
                out_scr.at[b, h],
                out_ref.at[:, pl.ds(b * 8, 8), pl.ds(h * LANES, LANES)],
                sem.at[b, h],
            )
            for h in range(2)
        ]

    for b in range(out_scr.shape[0]):

        @pl.when(block + 1 == b)
        def _():
            for copy in copies(b):
                copy.start()

    @pl.when(step == blocks)
    def _():
        for b in range(out_scr.shape[0]):
            for copy in copies(b):
                copy.wait()


def advect(soundings, edge_field, rounds, wide, field, layer_mass, courant, shift, weight):
    blocks, col_count, _, levels = field.shape
    n = soundings[0].shape[0] // 2
    here = lambda s: jnp.maximum(blocks - 1 - s, 0)
    lines = pl.BlockSpec((8, levels), lambda s: (here(s), 0))
    return pl.pallas_call(
        advect_kernel,
        grid=(blocks + 1,),
        in_specs=[IN_VMEM] * 6
        + [
            pl.BlockSpec(memory_space=pltpu.SMEM),
            IN_VMEM,
            pl.BlockSpec(memory_space=pl.ANY),
            pl.BlockSpec((1, levels), lambda s: (0, 0)),
            pl.BlockSpec(memory_space=pl.ANY),
            lines,
            lines,
        ],
        out_specs=[pl.BlockSpec(memory_space=pl.ANY), IN_VMEM],
        out_shape=[
            jax.ShapeDtypeStruct(courant.shape, F32),
            pltpu.VMEM((levels, col_count), F32),
        ],
        scratch_shapes=[
            pltpu.VMEM((REACH, 8, levels), F32),
            pltpu.VMEM((col_count + 8, 8, levels), F32),
            pltpu.VMEM((col_count, 8, levels), F32),
            pltpu.VMEM((1, 8 * levels, 8 * WINDOW), BF16),
            pltpu.VMEM((2, 8 * WINDOW, 4 * levels), BF16),
            pltpu.VMEM((blocks, 2, levels, 8, LANES), F32),
            pltpu.VMEM((2, levels, LANES), F32),
            pltpu.VMEM((blocks, col_count, 8, levels), F32),
            pltpu.VMEM((blocks, 2, levels, 8, LANES), F32),
            pltpu.SemaphoreType.DMA((blocks, 2)),
            pltpu.SemaphoreType.DMA((blocks, 3)),
        ],
        compiler_params=params(24 + n // 128),
        cost_estimate=pl.CostEstimate(
            flops=2 * levels * 8 * blocks * n * col_count,
            bytes_accessed=12 * levels * 8 * blocks * col_count,
            transcendentals=0,
        ),
        name="advect",
    )(
        *soundings, edge_field, rounds, wide, field, layer_mass, courant, shift, weight
    )


def close_kernel(last_ref, north_ref, _, out_ref, row, sem):
    row[...] = last_ref[...] + north_ref[...]
    copy = pltpu.make_async_copy(row, out_ref.at[:, out_ref.shape[1] - 1, :], sem)
    copy.start()
    copy.wait()


def close(out, last, north):
    in_place = pl.BlockSpec(memory_space=pl.ANY)
    return pl.pallas_call(
        close_kernel,
        in_specs=[IN_VMEM, IN_VMEM, in_place],
        out_specs=in_place,
        out_shape=jax.ShapeDtypeStruct(out.shape, F32),
        scratch_shapes=[pltpu.VMEM(last.shape, F32), pltpu.SemaphoreType.DMA],
        input_output_aliases={2: 0},
        compiler_params=params(4),
        name="close_last_row",
    )(last, north, out)


def shards(
    adjoint_field,
    mixing_inverse,
    cloud_top,
    conv_frac,
    thickness,
    zonal_shift,
    zonal_frac,
    merid_courant,
    obs_kernel,
    obs_depart,
    obs_dest,
    obs_col,
    obs_count,
):
    adjoint_field, mixing_inverse, cloud_top, conv_frac, merid_courant, obs_kernel = [
        in_hbm(array)
        for array in (
            adjoint_field, mixing_inverse, cloud_top, conv_frac, merid_courant, obs_kernel
        )
    ]
    levels, row_count, col_count = adjoint_field.shape
    lat_count, lon_count = lax.axis_size("lat"), lax.axis_size("lon")
    devices = lat_count * lon_count
    edge = edge_columns(adjoint_field, cloud_top, conv_frac).astype(jnp.float16)
    edge, obs_kernel = lax.optimization_barrier((edge, obs_kernel))
    obs_kernel = in_hbm(obs_kernel)
    sent = prepare(devices, lon_count, obs_count, obs_dest, obs_col, obs_depart, obs_kernel)
    sent, field_after = lax.optimization_barrier((sent, adjoint_field))
    got = lax.all_to_all(
        sent.reshape(devices, SLOTS, levels), ("lat", "lon"), split_axis=0, concat_axis=0, tiled=True
    )
    westward = [((i + 1) % lon_count, i) for i in range(lon_count)]
    layer_mass = in_hbm(thickness.reshape(1, levels))
    field_after = in_hbm(field_after)
    field, wide, row = mix(field_after, mixing_inverse, cloud_top, conv_frac, layer_mass)
    edge_in = in_vmem(lax.ppermute(edge, "lon", westward).astype(F32))
    shift, weight = in_hbm(zonal_shift.T), in_hbm(zonal_frac.T)
    *soundings, edge_field, rounds, first = take_soundings(
        got, wide, cloud_top, conv_frac, edge_in, layer_mass, row, merid_courant, shift, weight
    )
    southward = [(i + 1, i) for i in range(lat_count - 1)]
    north = lax.ppermute(first, "lat", southward)
    out, last = advect(
        [in_vmem(part) for part in soundings], in_vmem(edge_field), rounds, wide, field, layer_mass,
        merid_courant, shift, weight,
    )
    return close(out, last, north)


def solution(mesh):
    in_specs = (
        P(None, "lat", "lon"),
        P("lat", None, None),
        P("lat", "lon"),
        P("lat", "lon"),
        P(),
        P(None, "lat"),
        P(None, "lat"),
        P(None, "lat", "lon"),
        P(("lat", "lon"), None),
        P(("lat", "lon")),
        P(("lat", "lon")),
        P(("lat", "lon")),
        P(("lat", "lon")),
    )
    out_specs = P(None, "lat", "lon")
    return jax.shard_map(shards, mesh=mesh, in_specs=in_specs, out_specs=out_specs, check_vma=False)
```

```python
import functools

import jax
import jax.numpy as jnp
from jax import lax
from jax.experimental import pallas as pl
from jax.experimental.pallas import tpu as pltpu
from jax.sharding import PartitionSpec as P

F32, BF16, I32 = jnp.float32, jnp.bfloat16, jnp.int32
CAP = 16
SLOTS = 40
EDGE = 64
LANES = 128
GROUP = 32
EDGE_LINES = 4
SCALE = 4096.0
WINDOW = 32
REACH = 2 * LANES + EDGE
PITCH = 4096
CELL_LINES = 16
MIB = 1024 * 1024


IN_VMEM = pl.BlockSpec(memory_space=pltpu.VMEM)


def iota(shape, dim):
    return lax.broadcasted_iota(I32, shape, dim)


def params(mib):
    return pltpu.CompilerParams(vmem_limit_bytes=mib * MIB)


def in_hbm(array):
    return pltpu.with_memory_space_constraint(array, pltpu.HBM)


def in_vmem(array):
    return pltpu.with_memory_space_constraint(array, pltpu.VMEM)


def dot(left, right):
    return jnp.dot(left, right, preferred_element_type=F32)


def dot_nt(left, right):
    return lax.dot_general(left, right, (((1,), (1,)), ((), ())), preferred_element_type=F32)


def halves(value):
    high = value.astype(BF16)
    return high, (value - high.astype(F32)).astype(BF16)


def thirds(value):
    high = value.astype(BF16)
    rest = value - high.astype(F32)
    mid = rest.astype(BF16)
    return [high, mid, (rest - mid.astype(F32)).astype(BF16)]


def as_column(line):
    return jnp.broadcast_to(line, (LANES, line.shape[1])).T


def as_wide_column(line):
    column = as_column(line)
    return jnp.concatenate([column, column], axis=1)


def convect(mixed, top, frac, layer_mass):
    inside = iota(mixed.shape, 0) < top
    total = jnp.sum(jnp.where(inside, mixed, 0.0), axis=0, keepdims=True)
    mass = jnp.sum(jnp.where(inside, layer_mass, 0.0), axis=0, keepdims=True)
    mean = total / jnp.where(mass > 0.0, mass, 1.0)
    return mixed + jnp.where(inside, frac * (layer_mass * mean - mixed), 0.0)


def prep_kernel(lon_count, count_ref, dest_ref, col_ref, depart_ref, obs_ref, out_ref):
    n, levels = obs_ref.shape
    lane = iota((1, n), 1)
    live = lane < count_ref[0]
    first = pl.program_id(0) * GROUP
    dest = jnp.where(live, dest_ref[...] - first, -GROUP * SLOTS)
    lon = (dest + first) % lon_count
    west = jnp.where(lon == 0, dest + (lon_count - 1), dest - 1)
    cell = col_ref[...]
    cell_row = (cell // 256 + 1).astype(F32)
    cell_col = (cell % 256).astype(F32)
    contribution = (obs_ref[...].astype(F32) * as_column(depart_ref[...])).astype(BF16)
    local = iota((GROUP, n), 0)
    hit = dest == local
    before = jnp.sum((live & (dest < local)).astype(I32), axis=1, keepdims=True)
    place = jnp.sum(jnp.where(hit, lane - before, 0), axis=0, keepdims=True)
    parts, left = [], []
    for owner in (dest, west):
        pick = iota((GROUP * CAP, n), 0) == owner * CAP + place
        found = dot(pick.astype(F32).astype(BF16), contribution)
        parts.append(found.reshape(GROUP, CAP, levels))
        hit = owner == local
        left += [jnp.where(hit, cell_row, 0.0), jnp.where(hit, cell_col, 0.0)]
    spot = (iota((LANES, n), 0) % 32 == place).astype(F32).astype(BF16)
    every = dot_nt(jnp.concatenate(left, axis=0).astype(BF16), spot)
    kind = iota((GROUP, LANES), 1) // 32
    cells = [jnp.where(kind == k, every[k * GROUP : (k + 1) * GROUP], 0.0) for k in range(4)]
    cells = ((cells[0] + cells[1]) + (cells[2] + cells[3])).astype(BF16)
    spread = iota((GROUP * 8, GROUP), 0) == 8 * iota((GROUP * 8, GROUP), 1)
    parts.append(dot(spread.astype(F32).astype(BF16), cells).reshape(GROUP, 8, levels))
    whole = jnp.concatenate(parts, axis=1).reshape(GROUP * SLOTS, levels)
    out_ref[...] = whole.astype(BF16)


def prepare(devices, lon_count, obs_count, obs_dest, obs_col, obs_depart, obs_kernel):
    n, levels = obs_kernel.shape
    steps = devices // GROUP
    whole = lambda shape: pl.BlockSpec(shape, lambda g: (0, 0))
    return pl.pallas_call(
        functools.partial(prep_kernel, lon_count),
        grid=(steps,),
        in_specs=[
            pl.BlockSpec(memory_space=pltpu.SMEM),
            whole((1, n)),
            whole((1, n)),
            whole((1, n)),
            whole((n, levels)),
        ],
        out_specs=pl.BlockSpec((GROUP * SLOTS, levels), lambda g: (g, 0)),
        out_shape=pltpu.VMEM((devices * SLOTS, levels), BF16),
        compiler_params=params(16 + devices // 4),
        name="soundings_out",
    )(
        obs_count,
        in_hbm(obs_dest.reshape(1, n)),
        in_hbm(obs_col.reshape(1, n)),
        in_hbm(obs_depart.reshape(1, n)),
        obs_kernel,
    )


def level_rows(ref, row, count=None):
    levels = ref.shape[0]
    count = levels if count is None else count
    return ref.reshape(levels * 8, LANES)[pl.ds(row, count, stride=8), :]


def pack_edge(block):
    parts = [block[:, 8 * q : 8 * q + 8, :] for q in range(4)]
    low = iota(parts[0].shape, 2) < EDGE
    return [jnp.where(low, parts[2 * h], pltpu.roll(parts[2 * h + 1], EDGE, 2)) for h in range(2)]


def edge_kernel(field_ref, top_ref, frac_ref, out_ref):
    step = pl.program_id(0)
    count = field_ref.shape[0]
    here = pl.ds(pl.multiple_of(step * count, count), count)
    for h, part in enumerate(pack_edge(field_ref[...])):
        out_ref[h, here] = part * SCALE

    @pl.when(step == 0)
    def _():
        pieces = thirds(frac_ref[...])
        lines = [top_ref[...].astype(F32)] + [piece.astype(F32) for piece in pieces]
        lines[2:] = [line * SCALE for line in lines[2:]]
        first = out_ref.shape[1] - EDGE_LINES
        for i, line in enumerate(lines):
            for h, part in enumerate(pack_edge(line[None])):
                out_ref[h, first + i : first + i + 1] = part


def edge_columns(adjoint_field, cloud_top, conv_frac):
    levels, row_count, _ = adjoint_field.shape
    flat = pl.BlockSpec((row_count, LANES), lambda i: (0, 0))
    return pl.pallas_call(
        edge_kernel,
        grid=(2,),
        in_specs=[pl.BlockSpec((levels // 2, row_count, LANES), lambda i: (i, 0, 0)), flat, flat],
        out_specs=IN_VMEM,
        out_shape=pltpu.VMEM((2, levels + EDGE_LINES, 8, LANES), F32),
        compiler_params=params(16),
        cost_estimate=pl.CostEstimate(
            flops=levels * levels * 4 * row_count * LANES,
            bytes_accessed=12 * levels * row_count * LANES,
            transcendentals=0,
        ),
        name="edge_columns",
    )(adjoint_field, cloud_top, conv_frac)


def put_columns(ref, row, value):
    count = ref.shape[0]
    flat = ref.reshape(count * 8, LANES)
    for h in range(count // LANES):
        part = value[:, h * LANES : (h + 1) * LANES].T
        flat[pl.ds(h * LANES * 8 + row, LANES, stride=8), :] = part


def mix_rows(field_refs, mixing_ref, top, frac, layer_mass, block, out_ref, wide_ref):
    levels = mixing_ref.shape[1]
    for row in range(8):
        value = jnp.concatenate([level_rows(ref, row) for ref in field_refs], axis=1)
        high, low = halves(value)
        mix_high, mix_low = halves(mixing_ref[row])
        here = pl.ds(pl.multiple_of((8 * block + row) * levels, levels), levels)
        wide_ref[:levels, here] = mix_high
        wide_ref[levels:, here] = mix_low
        four = jnp.concatenate([mix_high, mix_low], axis=0)
        both = dot(jnp.concatenate([four, four], axis=1), jnp.concatenate([high, low], axis=0))
        mixed = both[:levels] + both[levels:]
        done = convect(mixed, top[row : row + 1, :], frac[row : row + 1, :], layer_mass)
        put_columns(out_ref.at[0], row, done)


def mix_kernel(
    west_ref, east_ref, mixing_ref, top_ref, frac_ref, mass_ref, out_ref, wide_ref, row_ref
):
    layer_mass = as_wide_column(mass_ref[...])
    block = pl.program_id(0)
    mix_rows(
        (west_ref, east_ref), mixing_ref, top_ref[...], frac_ref[...], layer_mass, block,
        out_ref, wide_ref,
    )

    @pl.when(block == 0)
    def _():
        flat = out_ref.at[0].reshape(row_ref.shape[0] * 8, LANES)
        row_ref[...] = flat[pl.ds(0, row_ref.shape[0], stride=8), :]


def mix(adjoint_field, mixing_inverse, cloud_top, conv_frac, layer_mass):
    levels, row_count, col_count = adjoint_field.shape
    blocks = row_count // 8
    half = lambda h: pl.BlockSpec((levels, 8, LANES), lambda b: (0, b, h))
    flat = pl.BlockSpec((8, col_count), lambda b: (b, 0))
    field, wide, row = pl.pallas_call(
        mix_kernel,
        grid=(blocks,),
        in_specs=[
            half(0),
            half(1),
            pl.BlockSpec((8, levels, levels), lambda b: (b, 0, 0)),
            flat,
            flat,
            pl.BlockSpec((1, levels), lambda b: (0, 0)),
        ],
        out_specs=[
            pl.BlockSpec((1, col_count, 8, levels), lambda b: (b, 0, 0, 0)),
            IN_VMEM,
            pl.BlockSpec((col_count, levels), lambda b: (0, 0)),
        ],
        out_shape=[
            pltpu.HBM((blocks, col_count, 8, levels), F32),
            pltpu.VMEM((2 * levels, row_count * levels), BF16),
            pltpu.HBM((col_count, levels), F32),
        ],
        compiler_params=params(20),
        cost_estimate=pl.CostEstimate(
            flops=2 * levels * levels * 4 * row_count * col_count,
            bytes_accessed=12 * levels * row_count * col_count,
            transcendentals=0,
        ),
        name="mix_own",
    )(adjoint_field, adjoint_field, mixing_inverse, cloud_top, conv_frac, layer_mass)
    return in_hbm(field), in_vmem(wide), in_hbm(row)


def mix_edge(edge_ref, wide_ref, layer_mass, out_ref):
    levels = layer_mass.shape[0]
    group = iota((levels, 2 * LANES), 1) // EDGE
    top, frac = edge_lines(edge_ref, levels)
    for row in range(8):
        value = jnp.concatenate([level_rows(edge_ref.at[h], row, levels) for h in range(2)], axis=1)
        value = value * (1.0 / SCALE)
        mix_high, mix_low, highs, lows = [], [], [], []
        for q in range(4):
            cols = slice((8 * q + row) * levels, (8 * q + row + 1) * levels)
            mix_high.append(wide_ref[:levels, cols])
            mix_low.append(wide_ref[levels:, cols])
            high, low = halves(jnp.where(group == q, value, 0.0))
            highs.append(high)
            lows.append(low)
        highs = jnp.concatenate(highs, axis=0)
        mixed = dot(
            jnp.concatenate(mix_high * 2, axis=1),
            jnp.concatenate([highs] + lows, axis=0),
        ) + dot(jnp.concatenate(mix_low, axis=1), highs)
        done = convect(mixed, top[row : row + 1].astype(I32), frac[row : row + 1], layer_mass)
        put_columns(out_ref, row, done)


def edge_lines(ref, levels):
    top, high, mid, low = [
        jnp.concatenate([ref[0, levels + i], ref[1, levels + i]], axis=1)
        for i in range(EDGE_LINES)
    ]
    return top, high + (mid + low) * (1.0 / SCALE)


def find_places(row, row_count):
    count = row.shape[1]
    upto = (iota((LANES, LANES), 0) <= iota((LANES, LANES), 1)).astype(F32).astype(BF16)
    before = jnp.zeros((row_count, 1), F32)
    places = []
    for start in range(0, count, LANES):
        mine = iota((row_count, LANES), 0) == row[:, start : start + LANES]
        running = dot(mine.astype(F32).astype(BF16), upto)
        place = jnp.sum(jnp.where(mine, running + before, 0.0), axis=0, keepdims=True) - 1.0
        places.append(place.astype(I32))
        before = before + running[:, LANES - 1 :]
    return jnp.concatenate(places, axis=1), jnp.max(before)


def mix_slots(blocks, index, key_ref, table_ref, wide_ref, layer_mass, stack):
    levels = layer_mass.shape[0]
    slots = 8 * WINDOW
    lane = iota((1, slots), 1)
    target = [(8 * b + lane // WINDOW) * PITCH + index * WINDOW + lane % WINDOW for b in blocks]
    target = jnp.concatenate(target, axis=1)
    pick = [
        (key_ref[...] == target[:, start : start + LANES]).astype(F32).astype(BF16)
        for start in range(0, target.shape[1], LANES)
    ]
    found = dot(table_ref[...], jnp.concatenate(pick, axis=1))
    split_high, split_low, top, high, mid, low = [
        found[levels + i : levels + i + 1] for i in range(6)
    ]
    column = (split_high * EDGE + split_low).astype(I32)
    parts = []
    for i, b in enumerate(blocks):
        value = found[:levels, i * slots : (i + 1) * slots].astype(BF16)
        for r in range(8):
            mine = (lane // WINDOW == r).astype(F32).astype(BF16)
            stack[i, r * levels : (r + 1) * levels, :] = value * mine
        start = pl.multiple_of(8 * b * levels, 8 * levels)
        both = dot(wide_ref[:, pl.ds(start, 8 * levels)], stack[i])
        parts.append(both[:levels] + both[levels:])
    mass = jnp.concatenate([layer_mass] * len(blocks), axis=1)
    done = convect(
        jnp.concatenate(parts, axis=1), top.astype(I32), (high + mid) + low, mass
    )
    turned = [done[:, start : start + LANES].T for start in range(0, done.shape[1], LANES)]
    high, low = halves(jnp.concatenate(turned, axis=0))
    return high, low, column


def expand(high, low, column, square, out_ref, add):
    levels = high.shape[1]
    flat = out_ref.reshape(REACH * 8, LANES)
    hot = (iota((REACH, 8 * WINDOW), 0) == column).astype(F32).astype(BF16)
    for group in range(2):
        for r in range(4):
            source = slice((4 * group + r) * WINDOW, (4 * group + r + 1) * WINDOW)
            target = slice(r * levels, (r + 1) * levels)
            square[group, r * WINDOW : (r + 1) * WINDOW, target] = high[source]
            square[group, (4 + r) * WINDOW : (5 + r) * WINDOW, target] = low[source]
        left = hot[:, 4 * group * WINDOW : 4 * (group + 1) * WINDOW]
        forced = dot(jnp.concatenate([left, left], axis=1), square[group])
        for r in range(4):
            rows = pl.ds(4 * group + r, REACH, stride=8)
            part = forced[:, r * levels : (r + 1) * levels]
            flat[rows, :] = flat[rows, :] + part if add else part


def force_rows(
    block, rounds, high_ref, low_ref, column_ref,
    key_ref, table_ref, wide_ref, layer_mass, stack, square, out_ref,
):
    slots = 8 * WINDOW
    here = pl.ds(pl.multiple_of(block * slots, slots), slots)
    expand(high_ref[here, :], low_ref[here, :], column_ref[0:1, here], square, out_ref, False)

    def more(index, carry):
        mixed = mix_slots([block], index, key_ref, table_ref, wide_ref, layer_mass, stack)
        expand(*mixed, square, out_ref, True)
        return carry

    lax.fori_loop(1, rounds, more, 0)


def soundings_kernel(
    got_ref, wide_ref, top_ref, frac_ref, lines_ref, mass_ref,
    row_ref, courant_ref, shift_ref, weight_ref,
    key_ref, table_ref, high_ref, low_ref, column_ref, edge_out, rounds_ref, first_ref,
    forced, stack, square, row_scr, courant_scr, sem,
):
    devices = got_ref.shape[0]
    levels = mass_ref.shape[1]
    n = devices * CAP
    row_count = top_ref.shape[0]
    width = 2 * LANES
    layer_mass = as_wide_column(mass_ref[...])
    late = [
        pltpu.make_async_copy(row_ref, row_scr, sem.at[0]),
        pltpu.make_async_copy(courant_ref.at[:, 0, :], courant_scr, sem.at[1]),
    ]
    for copy in late:
        copy.start()
    mix_edge(lines_ref, wide_ref, layer_mass, edge_out)

    got = got_ref[...].astype(F32)
    table_ref[:levels, :n] = got[:, :CAP].reshape(n, levels).T.astype(BF16)
    table_ref[:levels, n:] = got[:, CAP : 2 * CAP].reshape(n, levels).T.astype(BF16)
    info = got[:, 2 * CAP :].reshape(devices * 8, LANES).astype(BF16)
    first = iota((devices, devices * 8), 1) == 8 * iota((devices, devices * 8), 0)
    info = dot(first.astype(F32).astype(BF16), info)
    kind = iota((devices, LANES), 1) // 32
    left = [jnp.where(kind == k, info, 0.0) for k in range(4)]
    chosen = iota((LANES, n), 0) % 32 == iota((LANES, n), 1) % CAP
    spread = dot(
        jnp.concatenate(left, axis=0).astype(BF16), chosen.astype(F32).astype(BF16)
    )
    mine = iota((devices, n), 0) == iota((devices, n), 1) // CAP
    lines = [
        jnp.sum(jnp.where(mine, spread[k * devices : (k + 1) * devices], 0.0), axis=0, keepdims=True)
        for k in range(4)
    ]
    own_row, own_col, east_row, east_col = [line.astype(I32) for line in lines]
    own_row, east_row = own_row - 1, east_row - 1
    east_row = jnp.where(east_col < EDGE, east_row, -1)
    row = jnp.concatenate([own_row, east_row], axis=1)
    place, most = find_places(row, row_count)
    rounds = (most.astype(I32) + (WINDOW - 1)) // WINDOW
    rounds_ref[0] = rounds
    key_ref[...] = as_column((row * PITCH + place).astype(F32)).astype(I32)
    column = jnp.concatenate([own_col, width + east_col], axis=1)
    cells = [[(column // EDGE).astype(F32), (column % EDGE).astype(F32)]]

    packed_col = (east_row // 8) * EDGE + east_col
    parts = [
        (own_col, own_row, top_ref[...].astype(F32), frac_ref[...], row_count),
        (packed_col, east_row % 8, *edge_lines(lines_ref, levels), 8),
    ]
    for col, row, top, frac, count in parts:
        hot = (iota((width, n), 0) == col).astype(F32).astype(BF16)
        table = jnp.concatenate([top.astype(BF16)] + thirds(frac), axis=0)
        found = dot(table, hot)
        here = iota((count, n), 0) == row
        cells.append([
            jnp.sum(jnp.where(here, found[i * count : (i + 1) * count], 0.0), axis=0, keepdims=True)
            for i in range(4)
        ])
    lines = cells[0] + [jnp.concatenate(pair, axis=1) for pair in zip(cells[1], cells[2])]
    lines.append(jnp.zeros((CELL_LINES - len(lines), 2 * n), F32))
    table_ref[levels:] = jnp.concatenate(lines, axis=0).astype(BF16)

    high, low, column = mix_slots(
        list(range(row_count // 8)), 0, key_ref, table_ref, wide_ref, layer_mass, stack
    )
    high_ref[...] = high
    low_ref[...] = low
    column_ref[0:1] = column
    column_ref[1:] = jnp.zeros_like(column_ref[1:])
    square[...] = jnp.zeros_like(square)
    force_rows(
        0, rounds, high_ref, low_ref, column_ref,
        key_ref, table_ref, wide_ref, layer_mass, stack, square, forced,
    )
    edge = edge_out.reshape(width * 8, LANES)[pl.ds(0, EDGE, stride=8), :]
    for copy in late:
        copy.wait()
    value = jnp.concatenate([row_scr[...], edge], axis=0)
    value = value + forced.reshape(REACH * 8, LANES)[pl.ds(0, REACH, stride=8), :]
    shift = shift_ref[0:1, :]
    weight = weight_ref[0:1, :]
    for bit in (32, 16, 8, 4, 2, 1):
        value = jnp.where((shift & bit) != 0, value[bit:], value[:-bit])
    zonal = (1.0 - weight) * value[:width] + weight * value[1 : width + 1]
    for h in range(2):
        here = slice(h * LANES, (h + 1) * LANES)
        first_ref[:, here] = courant_scr[:, here] * zonal[here].T


def take_soundings(got, wide, cloud_top, conv_frac, edge_in, layer_mass, row, courant, shift, weight):
    levels = layer_mass.shape[1]
    row_count, col_count = cloud_top.shape
    n = got.shape[0] * CAP
    width = 2 * LANES
    full = lambda array: pl.BlockSpec(array.shape, lambda s: (0,) * array.ndim)
    lines = pl.BlockSpec((8, levels), lambda s: (0, 0))
    return pl.pallas_call(
        soundings_kernel,
        grid=(1,),
        in_specs=[
            IN_VMEM,
            IN_VMEM,
            full(cloud_top),
            full(conv_frac),
            IN_VMEM,
            full(layer_mass),
            pl.BlockSpec(memory_space=pl.ANY),
            pl.BlockSpec(memory_space=pl.ANY),
            lines,
            lines,
        ],
        out_specs=[IN_VMEM] * 6 + [pl.BlockSpec(memory_space=pltpu.SMEM), IN_VMEM],
        out_shape=[
            pltpu.VMEM((2 * n, LANES), I32),
            pltpu.VMEM((levels + CELL_LINES, 2 * n), BF16),
            pltpu.VMEM((row_count * WINDOW, levels), BF16),
            pltpu.VMEM((row_count * WINDOW, levels), BF16),
            pltpu.VMEM((8, row_count * WINDOW), I32),
            pltpu.VMEM((width, 8, levels), F32),
            jax.ShapeDtypeStruct((1,), I32),
            jax.ShapeDtypeStruct((levels, col_count), F32),
        ],
        scratch_shapes=[
            pltpu.VMEM((REACH, 8, levels), F32),
            pltpu.VMEM((row_count // 8, 8 * levels, 8 * WINDOW), BF16),
            pltpu.VMEM((2, 8 * WINDOW, 4 * levels), BF16),
            pltpu.VMEM((col_count, levels), F32),
            pltpu.VMEM((levels, col_count), F32),
            pltpu.SemaphoreType.DMA((2,)),
        ],
        compiler_params=params(24 + n // 64),
        name="take_soundings",
    )(
        got, wide, cloud_top, conv_frac, edge_in, layer_mass, row, courant, shift, weight
    )


def advect_kernel(
    key_ref, table_ref, high_ref, low_ref, column_ref, edge_ref, rounds_ref, wide_ref, field_ref,
    mass_ref, courant_ref, shift_ref, weight_ref,
    out_ref, last_ref,
    forced, coarse, done, stack, square, out_scr, prev, field_scr, courant_scr, sem, in_sem,
):
    step = pl.program_id(0)
    blocks = pl.num_programs(0) - 1
    block = blocks - 1 - step
    levels = mass_ref.shape[1]
    width = 2 * LANES

    def field_in(b):
        return pltpu.make_async_copy(field_ref.at[b], field_scr.at[b], in_sem.at[b, 0])

    def courant_in(b, h):
        source = courant_ref.at[:, pl.ds(pl.multiple_of(b * 8, 8), 8), pl.ds(h * LANES, LANES)]
        return pltpu.make_async_copy(source, courant_scr.at[b, h], in_sem.at[b, 1 + h])

    @pl.when(step == 0)
    def _():
        for b in reversed(range(out_scr.shape[0])):
            field_in(b).start()
            for h in range(2):
                courant_in(b, h).start()
        prev[...] = jnp.zeros_like(prev)
        square[...] = jnp.zeros_like(square)

    layer_mass = as_wide_column(mass_ref[...])
    shift = shift_ref[...]
    weight = weight_ref[...]
    chosen = {bit: (shift & bit) != 0 for bit in (32, 16, 8, 4, 2, 1)}

    def choose(tiles, bit, step):
        return [
            jnp.where(chosen[bit], new, old) for old, new in zip(tiles[:-step], tiles[step:])
        ]

    def by_eights(start):
        tiles = [field_scr[block, start + 8 * i] + forced[start + 8 * i] for i in range(32)]
        tiles += [
            edge_ref[EDGE * block + start + 8 * i] + forced[width + start + 8 * i] for i in range(8)
        ]
        for bit in (32, 16, 8):
            tiles = choose(tiles, bit, bit // 8)
        for i, tile in enumerate(tiles):
            coarse[start + 8 * i] = tile

    def by_ones(chunk, carry):
        start = chunk * 32
        tiles = [coarse[start + i] for i in range(40)]
        for bit in (4, 2, 1):
            tiles = choose(tiles, bit, bit)
        for i in range(32):
            done[start + i] = (1.0 - weight) * tiles[i] + weight * tiles[i + 1]
        return carry

    flat = done.reshape(width * 8, LANES)

    def meridional(beside):
        later = [prev[0], prev[1]]
        for index in range(8):
            r = 7 - index
            for h in range(2):
                zonal = flat[pl.ds(h * LANES * 8 + r, LANES, stride=8), :].T
                courant = level_rows(courant_scr.at[block + 1, h], r)
                place = out_scr.at[block + 1, h].reshape(levels * 8, LANES)
                place[pl.ds(r, levels, stride=8), :] = (1.0 - courant) * zonal + later[h]
                later[h] = courant * zonal
            beside(index)
        prev[0] = later[0]
        prev[1] = later[1]

    def shift_only(index, carry):
        by_eights(index)
        return carry

    @pl.when(step < blocks)
    def _():
        force_rows(
            block, rounds_ref[0], high_ref, low_ref, column_ref,
            key_ref, table_ref, wide_ref, layer_mass, stack, square, forced,
        )
        field_in(block).wait()

    @pl.when(step > 0)
    def _():
        for h in range(2):
            courant_in(block + 1, h).wait()

    @pl.when(step == 0)
    def _():
        lax.fori_loop(0, 8, shift_only, 0)

    @pl.when((step > 0) & (step < blocks))
    def _():
        meridional(by_eights)

    @pl.when(step < blocks)
    def _():
        lax.fori_loop(0, width // 32, by_ones, 0)

    @pl.when(step == blocks)
    def _():
        meridional(lambda index: None)

    @pl.when(step == 1)
    def _():
        for h in range(2):
            place = out_scr.at[blocks - 1, h].reshape(levels * 8, LANES)
            last_ref[:, h * LANES : (h + 1) * LANES] = place[pl.ds(7, levels, stride=8), :]

    def copies(b):
        return [
            pltpu.make_async_copy(
                out_scr.at[b, h],
                out_ref.at[:, pl.ds(b * 8, 8), pl.ds(h * LANES, LANES)],
                sem.at[b, h],
            )
            for h in range(2)
        ]

    for b in range(out_scr.shape[0]):

        @pl.when(block + 1 == b)
        def _():
            for copy in copies(b):
                copy.start()

    @pl.when(step == blocks)
    def _():
        for b in range(out_scr.shape[0]):
            for copy in copies(b):
                copy.wait()


def advect(soundings, edge_field, rounds, wide, field, layer_mass, courant, shift, weight):
    blocks, col_count, _, levels = field.shape
    n = soundings[0].shape[0] // 2
    here = lambda s: jnp.maximum(blocks - 1 - s, 0)
    lines = pl.BlockSpec((8, levels), lambda s: (here(s), 0))
    return pl.pallas_call(
        advect_kernel,
        grid=(blocks + 1,),
        in_specs=[IN_VMEM] * 6
        + [
            pl.BlockSpec(memory_space=pltpu.SMEM),
            IN_VMEM,
            pl.BlockSpec(memory_space=pl.ANY),
            pl.BlockSpec((1, levels), lambda s: (0, 0)),
            pl.BlockSpec(memory_space=pl.ANY),
            lines,
            lines,
        ],
        out_specs=[pl.BlockSpec(memory_space=pl.ANY), IN_VMEM],
        out_shape=[
            jax.ShapeDtypeStruct(courant.shape, F32),
            pltpu.VMEM((levels, col_count), F32),
        ],
        scratch_shapes=[
            pltpu.VMEM((REACH, 8, levels), F32),
            pltpu.VMEM((col_count + 8, 8, levels), F32),
            pltpu.VMEM((col_count, 8, levels), F32),
            pltpu.VMEM((1, 8 * levels, 8 * WINDOW), BF16),
            pltpu.VMEM((2, 8 * WINDOW, 4 * levels), BF16),
            pltpu.VMEM((blocks, 2, levels, 8, LANES), F32),
            pltpu.VMEM((2, levels, LANES), F32),
            pltpu.VMEM((blocks, col_count, 8, levels), F32),
            pltpu.VMEM((blocks, 2, levels, 8, LANES), F32),
            pltpu.SemaphoreType.DMA((blocks, 2)),
            pltpu.SemaphoreType.DMA((blocks, 3)),
        ],
        compiler_params=params(24 + n // 128),
        cost_estimate=pl.CostEstimate(
            flops=2 * levels * 8 * blocks * n * col_count,
            bytes_accessed=12 * levels * 8 * blocks * col_count,
            transcendentals=0,
        ),
        name="advect",
    )(
        *soundings, edge_field, rounds, wide, field, layer_mass, courant, shift, weight
    )


def close_kernel(last_ref, north_ref, _, out_ref, row, sem):
    row[...] = last_ref[...] + north_ref[...]
    copy = pltpu.make_async_copy(row, out_ref.at[:, out_ref.shape[1] - 1, :], sem)
    copy.start()
    copy.wait()


def close(out, last, north):
    in_place = pl.BlockSpec(memory_space=pl.ANY)
    return pl.pallas_call(
        close_kernel,
        in_specs=[IN_VMEM, IN_VMEM, in_place],
        out_specs=in_place,
        out_shape=jax.ShapeDtypeStruct(out.shape, F32),
        scratch_shapes=[pltpu.VMEM(last.shape, F32), pltpu.SemaphoreType.DMA],
        input_output_aliases={2: 0},
        compiler_params=params(4),
        name="close_last_row",
    )(last, north, out)


def shards(
    adjoint_field,
    mixing_inverse,
    cloud_top,
    conv_frac,
    thickness,
    zonal_shift,
    zonal_frac,
    merid_courant,
    obs_kernel,
    obs_depart,
    obs_dest,
    obs_col,
    obs_count,
):
    adjoint_field, mixing_inverse, cloud_top, conv_frac, merid_courant, obs_kernel = [
        in_hbm(array)
        for array in (
            adjoint_field, mixing_inverse, cloud_top, conv_frac, merid_courant, obs_kernel
        )
    ]
    levels, row_count, col_count = adjoint_field.shape
    lat_count, lon_count = lax.axis_size("lat"), lax.axis_size("lon")
    devices = lat_count * lon_count
    sent = prepare(devices, lon_count, obs_count, obs_dest, obs_col, obs_depart, obs_kernel)
    sent, field_after = lax.optimization_barrier((sent, adjoint_field))
    got = lax.all_to_all(
        sent.reshape(devices, SLOTS, levels), ("lat", "lon"), split_axis=0, concat_axis=0, tiled=True
    )
    westward = [((i + 1) % lon_count, i) for i in range(lon_count)]
    layer_mass = in_hbm(thickness.reshape(1, levels))
    field_after = in_hbm(field_after)
    edge = edge_columns(field_after, cloud_top, conv_frac).astype(jnp.float16)
    field, wide, row = mix(field_after, mixing_inverse, cloud_top, conv_frac, layer_mass)
    edge_in = in_vmem(lax.ppermute(edge, "lon", westward).astype(F32))
    shift, weight = in_hbm(zonal_shift.T), in_hbm(zonal_frac.T)
    *soundings, edge_field, rounds, first = take_soundings(
        got, wide, cloud_top, conv_frac, edge_in, layer_mass, row, merid_courant, shift, weight
    )
    southward = [(i + 1, i) for i in range(lat_count - 1)]
    north = lax.ppermute(first, "lat", southward)
    out, last = advect(
        [in_vmem(part) for part in soundings], in_vmem(edge_field), rounds, wide, field, layer_mass,
        merid_courant, shift, weight,
    )
    return close(out, last, north)


def solution(mesh):
    in_specs = (
        P(None, "lat", "lon"),
        P("lat", None, None),
        P("lat", "lon"),
        P("lat", "lon"),
        P(),
        P(None, "lat"),
        P(None, "lat"),
        P(None, "lat", "lon"),
        P(("lat", "lon"), None),
        P(("lat", "lon")),
        P(("lat", "lon")),
        P(("lat", "lon")),
        P(("lat", "lon")),
    )
    out_specs = P(None, "lat", "lon")
    return jax.shard_map(shards, mesh=mesh, in_specs=in_specs, out_specs=out_specs, check_vma=False)
```

```python
import functools

import jax
import jax.numpy as jnp
from jax import lax
from jax.experimental import pallas as pl
from jax.experimental.pallas import tpu as pltpu
from jax.sharding import PartitionSpec as P

F32, BF16, I32 = jnp.float32, jnp.bfloat16, jnp.int32
CAP = 16
SLOTS = 40
EDGE = 64
LANES = 128
GROUP = 32
EDGE_LINES = 4
SCALE = 4096.0
WINDOW = 32
REACH = 2 * LANES + EDGE
PITCH = 4096
CELL_LINES = 16
MIB = 1024 * 1024


IN_VMEM = pl.BlockSpec(memory_space=pltpu.VMEM)


def iota(shape, dim):
    return lax.broadcasted_iota(I32, shape, dim)


def params(mib):
    return pltpu.CompilerParams(vmem_limit_bytes=mib * MIB)


def in_hbm(array):
    return pltpu.with_memory_space_constraint(array, pltpu.HBM)


def in_vmem(array):
    return pltpu.with_memory_space_constraint(array, pltpu.VMEM)


def dot(left, right):
    return jnp.dot(left, right, preferred_element_type=F32)


def dot_nt(left, right):
    return lax.dot_general(left, right, (((1,), (1,)), ((), ())), preferred_element_type=F32)


def halves(value):
    high = value.astype(BF16)
    return high, (value - high.astype(F32)).astype(BF16)


def thirds(value):
    high = value.astype(BF16)
    rest = value - high.astype(F32)
    mid = rest.astype(BF16)
    return [high, mid, (rest - mid.astype(F32)).astype(BF16)]


def as_column(line):
    return jnp.broadcast_to(line, (LANES, line.shape[1])).T


def as_wide_column(line):
    column = as_column(line)
    return jnp.concatenate([column, column], axis=1)


def convect(mixed, top, frac, layer_mass):
    inside = iota(mixed.shape, 0) < top
    total = jnp.sum(jnp.where(inside, mixed, 0.0), axis=0, keepdims=True)
    mass = jnp.sum(jnp.where(inside, layer_mass, 0.0), axis=0, keepdims=True)
    mean = total / jnp.where(mass > 0.0, mass, 1.0)
    return mixed + jnp.where(inside, frac * (layer_mass * mean - mixed), 0.0)


def prep_kernel(lon_count, count_ref, dest_ref, col_ref, depart_ref, obs_ref, out_ref):
    n, levels = obs_ref.shape
    lane = iota((1, n), 1)
    live = lane < count_ref[0]
    first = pl.program_id(0) * GROUP
    dest = jnp.where(live, dest_ref[...] - first, -GROUP * SLOTS)
    lon = (dest + first) % lon_count
    west = jnp.where(lon == 0, dest + (lon_count - 1), dest - 1)
    cell = col_ref[...]
    cell_row = (cell // 256 + 1).astype(F32)
    cell_col = (cell % 256).astype(F32)
    contribution = (obs_ref[...].astype(F32) * as_column(depart_ref[...])).astype(BF16)
    local = iota((GROUP, n), 0)
    hit = dest == local
    before = jnp.sum((live & (dest < local)).astype(I32), axis=1, keepdims=True)
    place = jnp.sum(jnp.where(hit, lane - before, 0), axis=0, keepdims=True)
    parts, left = [], []
    for owner in (dest, west):
        pick = iota((GROUP * CAP, n), 0) == owner * CAP + place
        found = dot(pick.astype(F32).astype(BF16), contribution)
        parts.append(found.reshape(GROUP, CAP, levels))
        hit = owner == local
        left += [jnp.where(hit, cell_row, 0.0), jnp.where(hit, cell_col, 0.0)]
    spot = (iota((LANES, n), 0) % 32 == place).astype(F32).astype(BF16)
    every = dot_nt(jnp.concatenate(left, axis=0).astype(BF16), spot)
    kind = iota((GROUP, LANES), 1) // 32
    cells = [jnp.where(kind == k, every[k * GROUP : (k + 1) * GROUP], 0.0) for k in range(4)]
    cells = ((cells[0] + cells[1]) + (cells[2] + cells[3])).astype(BF16)
    spread = iota((GROUP * 8, GROUP), 0) == 8 * iota((GROUP * 8, GROUP), 1)
    parts.append(dot(spread.astype(F32).astype(BF16), cells).reshape(GROUP, 8, levels))
    whole = jnp.concatenate(parts, axis=1).reshape(GROUP * SLOTS, levels)
    out_ref[...] = whole.astype(BF16)


def prepare(devices, lon_count, obs_count, obs_dest, obs_col, obs_depart, obs_kernel):
    n, levels = obs_kernel.shape
    steps = devices // GROUP
    whole = lambda shape: pl.BlockSpec(shape, lambda g: (0, 0))
    return pl.pallas_call(
        functools.partial(prep_kernel, lon_count),
        grid=(steps,),
        in_specs=[
            pl.BlockSpec(memory_space=pltpu.SMEM),
            whole((1, n)),
            whole((1, n)),
            whole((1, n)),
            whole((n, levels)),
        ],
        out_specs=pl.BlockSpec((GROUP * SLOTS, levels), lambda g: (g, 0)),
        out_shape=pltpu.VMEM((devices * SLOTS, levels), BF16),
        compiler_params=params(16 + devices // 4),
        name="soundings_out",
    )(
        obs_count,
        in_hbm(obs_dest.reshape(1, n)),
        in_hbm(obs_col.reshape(1, n)),
        in_hbm(obs_depart.reshape(1, n)),
        obs_kernel,
    )


def level_rows(ref, row, count=None):
    levels = ref.shape[0]
    count = levels if count is None else count
    return ref.reshape(levels * 8, LANES)[pl.ds(row, count, stride=8), :]


def pack_edge(block):
    parts = [block[:, 8 * q : 8 * q + 8, :] for q in range(4)]
    low = iota(parts[0].shape, 2) < EDGE
    return [jnp.where(low, parts[2 * h], pltpu.roll(parts[2 * h + 1], EDGE, 2)) for h in range(2)]


def edge_kernel(field_ref, top_ref, frac_ref, out_ref):
    step = pl.program_id(0)
    count = field_ref.shape[0]
    here = pl.ds(pl.multiple_of(step * count, count), count)
    for h, part in enumerate(pack_edge(field_ref[...])):
        out_ref[h, here] = part * SCALE

    @pl.when(step == 0)
    def _():
        pieces = thirds(frac_ref[...])
        lines = [top_ref[...].astype(F32)] + [piece.astype(F32) for piece in pieces]
        lines[2:] = [line * SCALE for line in lines[2:]]
        first = out_ref.shape[1] - EDGE_LINES
        for i, line in enumerate(lines):
            for h, part in enumerate(pack_edge(line[None])):
                out_ref[h, first + i : first + i + 1] = part


def edge_columns(adjoint_field, cloud_top, conv_frac):
    levels, row_count, _ = adjoint_field.shape
    flat = pl.BlockSpec((row_count, LANES), lambda i: (0, 0))
    return pl.pallas_call(
        edge_kernel,
        grid=(2,),
        in_specs=[pl.BlockSpec((levels // 2, row_count, LANES), lambda i: (i, 0, 0)), flat, flat],
        out_specs=IN_VMEM,
        out_shape=pltpu.VMEM((2, levels + EDGE_LINES, 8, LANES), F32),
        compiler_params=params(16),
        cost_estimate=pl.CostEstimate(
            flops=levels * levels * 4 * row_count * LANES,
            bytes_accessed=12 * levels * row_count * LANES,
            transcendentals=0,
        ),
        name="edge_columns",
    )(adjoint_field, cloud_top, conv_frac)


def put_columns(ref, row, value):
    count = ref.shape[0]
    flat = ref.reshape(count * 8, LANES)
    for h in range(count // LANES):
        part = value[:, h * LANES : (h + 1) * LANES].T
        flat[pl.ds(h * LANES * 8 + row, LANES, stride=8), :] = part


def mix_rows(field_refs, mixing_ref, top, frac, layer_mass, block, out_ref, wide_ref):
    levels = mixing_ref.shape[1]
    for row in range(8):
        value = jnp.concatenate([level_rows(ref, row) for ref in field_refs], axis=1)
        high, low = halves(value)
        mix_high, mix_low = halves(mixing_ref[row])
        here = pl.ds(pl.multiple_of((8 * block + row) * levels, levels), levels)
        wide_ref[:levels, here] = mix_high
        wide_ref[levels:, here] = mix_low
        four = jnp.concatenate([mix_high, mix_low], axis=0)
        both = dot(jnp.concatenate([four, four], axis=1), jnp.concatenate([high, low], axis=0))
        mixed = both[:levels] + both[levels:]
        done = convect(mixed, top[row : row + 1, :], frac[row : row + 1, :], layer_mass)
        put_columns(out_ref.at[0], row, done)


def mix_kernel(
    west_ref, east_ref, mixing_ref, top_ref, frac_ref, mass_ref, out_ref, wide_ref, row_ref
):
    layer_mass = as_wide_column(mass_ref[...])
    block = pl.program_id(0)
    mix_rows(
        (west_ref, east_ref), mixing_ref, top_ref[...], frac_ref[...], layer_mass, block,
        out_ref, wide_ref,
    )

    @pl.when(block == 0)
    def _():
        flat = out_ref.at[0].reshape(row_ref.shape[0] * 8, LANES)
        row_ref[...] = flat[pl.ds(0, row_ref.shape[0], stride=8), :]


def mix(adjoint_field, mixing_inverse, cloud_top, conv_frac, layer_mass):
    levels, row_count, col_count = adjoint_field.shape
    blocks = row_count // 8
    half = lambda h: pl.BlockSpec((levels, 8, LANES), lambda b: (0, b, h))
    flat = pl.BlockSpec((8, col_count), lambda b: (b, 0))
    field, wide, row = pl.pallas_call(
        mix_kernel,
        grid=(blocks,),
        in_specs=[
            half(0),
            half(1),
            pl.BlockSpec((8, levels, levels), lambda b: (b, 0, 0)),
            flat,
            flat,
            pl.BlockSpec((1, levels), lambda b: (0, 0)),
        ],
        out_specs=[
            pl.BlockSpec((1, col_count, 8, levels), lambda b: (b, 0, 0, 0)),
            IN_VMEM,
            pl.BlockSpec((col_count, levels), lambda b: (0, 0)),
        ],
        out_shape=[
            pltpu.HBM((blocks, col_count, 8, levels), F32),
            pltpu.VMEM((2 * levels, row_count * levels), BF16),
            pltpu.HBM((col_count, levels), F32),
        ],
        compiler_params=params(20),
        cost_estimate=pl.CostEstimate(
            flops=2 * levels * levels * 4 * row_count * col_count,
            bytes_accessed=12 * levels * row_count * col_count,
            transcendentals=0,
        ),
        name="mix_own",
    )(adjoint_field, adjoint_field, mixing_inverse, cloud_top, conv_frac, layer_mass)
    return in_hbm(field), in_vmem(wide), in_hbm(row)


def mix_edge(edge_ref, wide_ref, layer_mass, out_ref):
    levels = layer_mass.shape[0]
    group = iota((levels, 2 * LANES), 1) // EDGE
    top, frac = edge_lines(edge_ref, levels)
    for row in range(8):
        value = jnp.concatenate([level_rows(edge_ref.at[h], row, levels) for h in range(2)], axis=1)
        value = value * (1.0 / SCALE)
        mix_high, mix_low, highs, lows = [], [], [], []
        for q in range(4):
            cols = slice((8 * q + row) * levels, (8 * q + row + 1) * levels)
            mix_high.append(wide_ref[:levels, cols])
            mix_low.append(wide_ref[levels:, cols])
            high, low = halves(jnp.where(group == q, value, 0.0))
            highs.append(high)
            lows.append(low)
        highs = jnp.concatenate(highs, axis=0)
        mixed = dot(
            jnp.concatenate(mix_high * 2, axis=1),
            jnp.concatenate([highs] + lows, axis=0),
        ) + dot(jnp.concatenate(mix_low, axis=1), highs)
        done = convect(mixed, top[row : row + 1].astype(I32), frac[row : row + 1], layer_mass)
        put_columns(out_ref, row, done)


def edge_lines(ref, levels):
    top, high, mid, low = [
        jnp.concatenate([ref[0, levels + i], ref[1, levels + i]], axis=1)
        for i in range(EDGE_LINES)
    ]
    return top, high + (mid + low) * (1.0 / SCALE)


def find_places(row, row_count):
    count = row.shape[1]
    upto = (iota((LANES, LANES), 0) <= iota((LANES, LANES), 1)).astype(F32).astype(BF16)
    before = jnp.zeros((row_count, 1), F32)
    places = []
    for start in range(0, count, LANES):
        mine = iota((row_count, LANES), 0) == row[:, start : start + LANES]
        running = dot(mine.astype(F32).astype(BF16), upto)
        place = jnp.sum(jnp.where(mine, running + before, 0.0), axis=0, keepdims=True) - 1.0
        places.append(place.astype(I32))
        before = before + running[:, LANES - 1 :]
    return jnp.concatenate(places, axis=1), jnp.max(before)


def mix_slots(blocks, index, key_ref, table_ref, wide_ref, layer_mass, stack):
    levels = layer_mass.shape[0]
    slots = 8 * WINDOW
    lane = iota((1, slots), 1)
    target = [(8 * b + lane // WINDOW) * PITCH + index * WINDOW + lane % WINDOW for b in blocks]
    target = jnp.concatenate(target, axis=1)
    pick = [
        (key_ref[...] == target[:, start : start + LANES]).astype(F32).astype(BF16)
        for start in range(0, target.shape[1], LANES)
    ]
    found = dot(table_ref[...], jnp.concatenate(pick, axis=1))
    split_high, split_low, top, high, mid, low = [
        found[levels + i : levels + i + 1] for i in range(6)
    ]
    column = (split_high * EDGE + split_low).astype(I32)
    parts = []
    for i, b in enumerate(blocks):
        value = found[:levels, i * slots : (i + 1) * slots].astype(BF16)
        for r in range(8):
            mine = (lane // WINDOW == r).astype(F32).astype(BF16)
            stack[i, r * levels : (r + 1) * levels, :] = value * mine
        start = pl.multiple_of(8 * b * levels, 8 * levels)
        both = dot(wide_ref[:, pl.ds(start, 8 * levels)], stack[i])
        parts.append(both[:levels] + both[levels:])
    mass = jnp.concatenate([layer_mass] * len(blocks), axis=1)
    done = convect(
        jnp.concatenate(parts, axis=1), top.astype(I32), (high + mid) + low, mass
    )
    turned = [done[:, start : start + LANES].T for start in range(0, done.shape[1], LANES)]
    high, low = halves(jnp.concatenate(turned, axis=0))
    return high, low, column


def expand(high, low, column, square, out_ref, add):
    levels = high.shape[1]
    flat = out_ref.reshape(REACH * 8, LANES)
    hot = (iota((REACH, 8 * WINDOW), 0) == column).astype(F32).astype(BF16)
    for group in range(2):
        for r in range(4):
            source = slice((4 * group + r) * WINDOW, (4 * group + r + 1) * WINDOW)
            target = slice(r * levels, (r + 1) * levels)
            square[group, r * WINDOW : (r + 1) * WINDOW, target] = high[source]
            square[group, (4 + r) * WINDOW : (5 + r) * WINDOW, target] = low[source]
        left = hot[:, 4 * group * WINDOW : 4 * (group + 1) * WINDOW]
        forced = dot(jnp.concatenate([left, left], axis=1), square[group])
        for r in range(4):
            rows = pl.ds(4 * group + r, REACH, stride=8)
            part = forced[:, r * levels : (r + 1) * levels]
            flat[rows, :] = flat[rows, :] + part if add else part


def force_rows(
    block, rounds, high_ref, low_ref, column_ref,
    key_ref, table_ref, wide_ref, layer_mass, stack, square, out_ref,
):
    slots = 8 * WINDOW
    here = pl.ds(pl.multiple_of(block * slots, slots), slots)
    expand(high_ref[here, :], low_ref[here, :], column_ref[0:1, here], square, out_ref, False)

    def more(index, carry):
        mixed = mix_slots([block], index, key_ref, table_ref, wide_ref, layer_mass, stack)
        expand(*mixed, square, out_ref, True)
        return carry

    lax.fori_loop(1, rounds, more, 0)


def soundings_kernel(
    got_ref, wide_ref, top_ref, frac_ref, lines_ref, mass_ref,
    row_ref, courant_ref, shift_ref, weight_ref,
    key_ref, table_ref, high_ref, low_ref, column_ref, edge_out, rounds_ref, first_ref,
    forced, stack, square, row_scr, courant_scr, sem,
):
    devices = got_ref.shape[0]
    levels = mass_ref.shape[1]
    n = devices * CAP
    row_count = top_ref.shape[0]
    width = 2 * LANES
    layer_mass = as_wide_column(mass_ref[...])
    late = [
        pltpu.make_async_copy(row_ref, row_scr, sem.at[0]),
        pltpu.make_async_copy(courant_ref.at[:, 0, :], courant_scr, sem.at[1]),
    ]
    for copy in late:
        copy.start()
    mix_edge(lines_ref, wide_ref, layer_mass, edge_out)

    got = got_ref[...].astype(F32)
    table_ref[:levels, :n] = got[:, :CAP].reshape(n, levels).T.astype(BF16)
    table_ref[:levels, n:] = got[:, CAP : 2 * CAP].reshape(n, levels).T.astype(BF16)
    info = got[:, 2 * CAP :].reshape(devices * 8, LANES).astype(BF16)
    first = iota((devices, devices * 8), 1) == 8 * iota((devices, devices * 8), 0)
    info = dot(first.astype(F32).astype(BF16), info)
    kind = iota((devices, LANES), 1) // 32
    left = [jnp.where(kind == k, info, 0.0) for k in range(4)]
    chosen = iota((LANES, n), 0) % 32 == iota((LANES, n), 1) % CAP
    spread = dot(
        jnp.concatenate(left, axis=0).astype(BF16), chosen.astype(F32).astype(BF16)
    )
    mine = iota((devices, n), 0) == iota((devices, n), 1) // CAP
    lines = [
        jnp.sum(jnp.where(mine, spread[k * devices : (k + 1) * devices], 0.0), axis=0, keepdims=True)
        for k in range(4)
    ]
    own_row, own_col, east_row, east_col = [line.astype(I32) for line in lines]
    own_row, east_row = own_row - 1, east_row - 1
    east_row = jnp.where(east_col < EDGE, east_row, -1)
    row = jnp.concatenate([own_row, east_row], axis=1)
    place, most = find_places(row, row_count)
    rounds = (most.astype(I32) + (WINDOW - 1)) // WINDOW
    rounds_ref[0] = rounds
    key_ref[...] = as_column((row * PITCH + place).astype(F32)).astype(I32)
    column = jnp.concatenate([own_col, width + east_col], axis=1)
    cells = [[(column // EDGE).astype(F32), (column % EDGE).astype(F32)]]

    packed_col = (east_row // 8) * EDGE + east_col
    parts = [
        (own_col, own_row, top_ref[...].astype(F32), frac_ref[...], row_count),
        (packed_col, east_row % 8, *edge_lines(lines_ref, levels), 8),
    ]
    for col, row, top, frac, count in parts:
        hot = (iota((width, n), 0) == col).astype(F32).astype(BF16)
        table = jnp.concatenate([top.astype(BF16)] + thirds(frac), axis=0)
        found = dot(table, hot)
        here = iota((count, n), 0) == row
        cells.append([
            jnp.sum(jnp.where(here, found[i * count : (i + 1) * count], 0.0), axis=0, keepdims=True)
            for i in range(4)
        ])
    lines = cells[0] + [jnp.concatenate(pair, axis=1) for pair in zip(cells[1], cells[2])]
    lines.append(jnp.zeros((CELL_LINES - len(lines), 2 * n), F32))
    table_ref[levels:] = jnp.concatenate(lines, axis=0).astype(BF16)

    high, low, column = mix_slots(
        list(range(row_count // 8)), 0, key_ref, table_ref, wide_ref, layer_mass, stack
    )
    high_ref[...] = high
    low_ref[...] = low
    column_ref[0:1] = column
    column_ref[1:] = jnp.zeros_like(column_ref[1:])
    square[...] = jnp.zeros_like(square)
    force_rows(
        0, rounds, high_ref, low_ref, column_ref,
        key_ref, table_ref, wide_ref, layer_mass, stack, square, forced,
    )
    edge = edge_out.reshape(width * 8, LANES)[pl.ds(0, EDGE, stride=8), :]
    for copy in late:
        copy.wait()
    value = jnp.concatenate([row_scr[...], edge], axis=0)
    value = value + forced.reshape(REACH * 8, LANES)[pl.ds(0, REACH, stride=8), :]
    shift = shift_ref[0:1, :]
    weight = weight_ref[0:1, :]
    for bit in (32, 16, 8, 4, 2, 1):
        value = jnp.where((shift & bit) != 0, value[bit:], value[:-bit])
    zonal = (1.0 - weight) * value[:width] + weight * value[1 : width + 1]
    for h in range(2):
        here = slice(h * LANES, (h + 1) * LANES)
        first_ref[:, here] = courant_scr[:, here] * zonal[here].T


def take_soundings(got, wide, cloud_top, conv_frac, edge_in, layer_mass, row, courant, shift, weight):
    levels = layer_mass.shape[1]
    row_count, col_count = cloud_top.shape
    n = got.shape[0] * CAP
    width = 2 * LANES
    full = lambda array: pl.BlockSpec(array.shape, lambda s: (0,) * array.ndim)
    lines = pl.BlockSpec((8, levels), lambda s: (0, 0))
    return pl.pallas_call(
        soundings_kernel,
        grid=(1,),
        in_specs=[
            IN_VMEM,
            IN_VMEM,
            full(cloud_top),
            full(conv_frac),
            IN_VMEM,
            full(layer_mass),
            pl.BlockSpec(memory_space=pl.ANY),
            pl.BlockSpec(memory_space=pl.ANY),
            lines,
            lines,
        ],
        out_specs=[IN_VMEM] * 6
        + [
            pl.BlockSpec(memory_space=pltpu.SMEM),
            pl.BlockSpec((levels, col_count), lambda s: (0, 0)),
        ],
        out_shape=[
            pltpu.VMEM((2 * n, LANES), I32),
            pltpu.VMEM((levels + CELL_LINES, 2 * n), BF16),
            pltpu.VMEM((row_count * WINDOW, levels), BF16),
            pltpu.VMEM((row_count * WINDOW, levels), BF16),
            pltpu.VMEM((8, row_count * WINDOW), I32),
            pltpu.VMEM((width, 8, levels), F32),
            jax.ShapeDtypeStruct((1,), I32),
            pltpu.HBM((levels, col_count), F32),
        ],
        scratch_shapes=[
            pltpu.VMEM((REACH, 8, levels), F32),
            pltpu.VMEM((row_count // 8, 8 * levels, 8 * WINDOW), BF16),
            pltpu.VMEM((2, 8 * WINDOW, 4 * levels), BF16),
            pltpu.VMEM((col_count, levels), F32),
            pltpu.VMEM((levels, col_count), F32),
            pltpu.SemaphoreType.DMA((2,)),
        ],
        compiler_params=params(24 + n // 64),
        name="take_soundings",
    )(
        got, wide, cloud_top, conv_frac, edge_in, layer_mass, row, courant, shift, weight
    )


def advect_kernel(
    key_ref, table_ref, high_ref, low_ref, column_ref, edge_ref, rounds_ref, wide_ref, field_ref,
    mass_ref, courant_ref, shift_ref, weight_ref,
    out_ref, last_ref,
    forced, coarse, done, stack, square, out_scr, prev, field_scr, courant_scr, sem, in_sem,
):
    step = pl.program_id(0)
    blocks = pl.num_programs(0) - 1
    block = blocks - 1 - step
    levels = mass_ref.shape[1]
    width = 2 * LANES

    def field_in(b):
        return pltpu.make_async_copy(field_ref.at[b], field_scr.at[b], in_sem.at[b, 0])

    def courant_in(b, h):
        source = courant_ref.at[:, pl.ds(pl.multiple_of(b * 8, 8), 8), pl.ds(h * LANES, LANES)]
        return pltpu.make_async_copy(source, courant_scr.at[b, h], in_sem.at[b, 1 + h])

    @pl.when(step == 0)
    def _():
        for b in reversed(range(out_scr.shape[0])):
            field_in(b).start()
            for h in range(2):
                courant_in(b, h).start()
        prev[...] = jnp.zeros_like(prev)
        square[...] = jnp.zeros_like(square)

    layer_mass = as_wide_column(mass_ref[...])
    shift = shift_ref[...]
    weight = weight_ref[...]
    chosen = {bit: (shift & bit) != 0 for bit in (32, 16, 8, 4, 2, 1)}

    def choose(tiles, bit, step):
        return [
            jnp.where(chosen[bit], new, old) for old, new in zip(tiles[:-step], tiles[step:])
        ]

    def by_eights(start):
        tiles = [field_scr[block, start + 8 * i] + forced[start + 8 * i] for i in range(32)]
        tiles += [
            edge_ref[EDGE * block + start + 8 * i] + forced[width + start + 8 * i] for i in range(8)
        ]
        for bit in (32, 16, 8):
            tiles = choose(tiles, bit, bit // 8)
        for i, tile in enumerate(tiles):
            coarse[start + 8 * i] = tile

    def by_ones(chunk, carry):
        start = chunk * 32
        tiles = [coarse[start + i] for i in range(40)]
        for bit in (4, 2, 1):
            tiles = choose(tiles, bit, bit)
        for i in range(32):
            done[start + i] = (1.0 - weight) * tiles[i] + weight * tiles[i + 1]
        return carry

    flat = done.reshape(width * 8, LANES)

    def meridional(beside):
        later = [prev[0], prev[1]]
        for index in range(8):
            r = 7 - index
            for h in range(2):
                zonal = flat[pl.ds(h * LANES * 8 + r, LANES, stride=8), :].T
                courant = level_rows(courant_scr.at[block + 1, h], r)
                place = out_scr.at[block + 1, h].reshape(levels * 8, LANES)
                leaving = courant * zonal
                place[pl.ds(r, levels, stride=8), :] = (zonal - leaving) + later[h]
                later[h] = leaving
            beside(index)
        prev[0] = later[0]
        prev[1] = later[1]

    def shift_only(index, carry):
        by_eights(index)
        return carry

    @pl.when(step < blocks)
    def _():
        force_rows(
            block, rounds_ref[0], high_ref, low_ref, column_ref,
            key_ref, table_ref, wide_ref, layer_mass, stack, square, forced,
        )
        field_in(block).wait()

    @pl.when(step > 0)
    def _():
        for h in range(2):
            courant_in(block + 1, h).wait()

    @pl.when(step == 0)
    def _():
        lax.fori_loop(0, 8, shift_only, 0)

    @pl.when((step > 0) & (step < blocks))
    def _():
        meridional(by_eights)

    @pl.when(step < blocks)
    def _():
        lax.fori_loop(0, width // 32, by_ones, 0)

    @pl.when(step == blocks)
    def _():
        meridional(lambda index: None)

    @pl.when(step == 1)
    def _():
        for h in range(2):
            place = out_scr.at[blocks - 1, h].reshape(levels * 8, LANES)
            last_ref[:, h * LANES : (h + 1) * LANES] = place[pl.ds(7, levels, stride=8), :]

    def copies(b):
        return [
            pltpu.make_async_copy(
                out_scr.at[b, h],
                out_ref.at[:, pl.ds(b * 8, 8), pl.ds(h * LANES, LANES)],
                sem.at[b, h],
            )
            for h in range(2)
        ]

    for b in range(out_scr.shape[0]):

        @pl.when(block + 1 == b)
        def _():
            for copy in copies(b):
                copy.start()

    @pl.when(step == blocks)
    def _():
        for b in range(out_scr.shape[0]):
            for copy in copies(b):
                copy.wait()


def advect(soundings, edge_field, rounds, wide, field, layer_mass, courant, shift, weight):
    blocks, col_count, _, levels = field.shape
    n = soundings[0].shape[0] // 2
    here = lambda s: jnp.maximum(blocks - 1 - s, 0)
    lines = pl.BlockSpec((8, levels), lambda s: (here(s), 0))
    return pl.pallas_call(
        advect_kernel,
        grid=(blocks + 1,),
        in_specs=[IN_VMEM] * 6
        + [
            pl.BlockSpec(memory_space=pltpu.SMEM),
            IN_VMEM,
            pl.BlockSpec(memory_space=pl.ANY),
            pl.BlockSpec((1, levels), lambda s: (0, 0)),
            pl.BlockSpec(memory_space=pl.ANY),
            lines,
            lines,
        ],
        out_specs=[pl.BlockSpec(memory_space=pl.ANY), IN_VMEM],
        out_shape=[
            jax.ShapeDtypeStruct(courant.shape, F32),
            pltpu.VMEM((levels, col_count), F32),
        ],
        scratch_shapes=[
            pltpu.VMEM((REACH, 8, levels), F32),
            pltpu.VMEM((col_count + 8, 8, levels), F32),
            pltpu.VMEM((col_count, 8, levels), F32),
            pltpu.VMEM((1, 8 * levels, 8 * WINDOW), BF16),
            pltpu.VMEM((2, 8 * WINDOW, 4 * levels), BF16),
            pltpu.VMEM((blocks, 2, levels, 8, LANES), F32),
            pltpu.VMEM((2, levels, LANES), F32),
            pltpu.VMEM((blocks, col_count, 8, levels), F32),
            pltpu.VMEM((blocks, 2, levels, 8, LANES), F32),
            pltpu.SemaphoreType.DMA((blocks, 2)),
            pltpu.SemaphoreType.DMA((blocks, 3)),
        ],
        compiler_params=params(24 + n // 128),
        cost_estimate=pl.CostEstimate(
            flops=2 * levels * 8 * blocks * n * col_count,
            bytes_accessed=12 * levels * 8 * blocks * col_count,
            transcendentals=0,
        ),
        name="advect",
    )(
        *soundings, edge_field, rounds, wide, field, layer_mass, courant, shift, weight
    )


def close_kernel(lat_ref, last_ref, firsts_ref, _, out_ref, row, sem):
    count = firsts_ref.shape[0]
    lat = lat_ref[0]
    take = pltpu.make_async_copy(firsts_ref.at[jnp.minimum(lat + 1, count - 1)], row, sem)
    take.start()
    take.wait()
    row[...] = last_ref[...] + jnp.where(lat < count - 1, row[...], 0.0)
    copy = pltpu.make_async_copy(row, out_ref.at[:, out_ref.shape[1] - 1, :], sem)
    copy.start()
    copy.wait()


def close(out, last, firsts, lat):
    in_place = pl.BlockSpec(memory_space=pl.ANY)
    return pl.pallas_call(
        close_kernel,
        in_specs=[pl.BlockSpec(memory_space=pltpu.SMEM), IN_VMEM, in_place, in_place],
        out_specs=in_place,
        out_shape=jax.ShapeDtypeStruct(out.shape, F32),
        scratch_shapes=[pltpu.VMEM(last.shape, F32), pltpu.SemaphoreType.DMA],
        input_output_aliases={3: 0},
        compiler_params=params(4),
        name="close_last_row",
    )(lat, last, in_hbm(firsts), out)


def shards(
    adjoint_field,
    mixing_inverse,
    cloud_top,
    conv_frac,
    thickness,
    zonal_shift,
    zonal_frac,
    merid_courant,
    obs_kernel,
    obs_depart,
    obs_dest,
    obs_col,
    obs_count,
):
    adjoint_field, mixing_inverse, cloud_top, conv_frac, merid_courant, obs_kernel = [
        in_hbm(array)
        for array in (
            adjoint_field, mixing_inverse, cloud_top, conv_frac, merid_courant, obs_kernel
        )
    ]
    levels, row_count, col_count = adjoint_field.shape
    lat_count, lon_count = lax.axis_size("lat"), lax.axis_size("lon")
    devices = lat_count * lon_count
    sent = prepare(devices, lon_count, obs_count, obs_dest, obs_col, obs_depart, obs_kernel)
    sent, field_after = lax.optimization_barrier((sent, adjoint_field))
    got = lax.all_to_all(
        sent.reshape(devices, SLOTS, levels), ("lat", "lon"), split_axis=0, concat_axis=0, tiled=True
    )
    westward = [((i + 1) % lon_count, i) for i in range(lon_count)]
    layer_mass = in_hbm(thickness.reshape(1, levels))
    field_after = in_hbm(field_after)
    edge = edge_columns(field_after, cloud_top, conv_frac).astype(jnp.float16)
    field, wide, row = mix(field_after, mixing_inverse, cloud_top, conv_frac, layer_mass)
    edge_in = in_vmem(lax.ppermute(edge, "lon", westward).astype(F32))
    shift, weight = in_hbm(zonal_shift.T), in_hbm(zonal_frac.T)
    *soundings, edge_field, rounds, first = take_soundings(
        got, wide, cloud_top, conv_frac, edge_in, layer_mass, row, merid_courant, shift, weight
    )
    firsts = lax.all_gather(first, "lat")
    out, last = advect(
        [in_vmem(part) for part in soundings], in_vmem(edge_field), rounds, wide, field, layer_mass,
        merid_courant, shift, weight,
    )
    return close(out, last, firsts, lax.axis_index("lat").astype(I32).reshape(1))


def solution(mesh):
    in_specs = (
        P(None, "lat", "lon"),
        P("lat", None, None),
        P("lat", "lon"),
        P("lat", "lon"),
        P(),
        P(None, "lat"),
        P(None, "lat"),
        P(None, "lat", "lon"),
        P(("lat", "lon"), None),
        P(("lat", "lon")),
        P(("lat", "lon")),
        P(("lat", "lon")),
        P(("lat", "lon")),
    )
    out_specs = P(None, "lat", "lon")
    return jax.shard_map(shards, mesh=mesh, in_specs=in_specs, out_specs=out_specs, check_vma=False)
```

```python
import functools

import jax
import jax.numpy as jnp
from jax import lax
from jax.experimental import pallas as pl
from jax.experimental.pallas import tpu as pltpu
from jax.sharding import PartitionSpec as P

F32, BF16, I32 = jnp.float32, jnp.bfloat16, jnp.int32
CAP = 16
SLOTS = 40
EDGE = 64
LANES = 128
GROUP = 32
EDGE_LINES = 4
SCALE = 4096.0
WINDOW = 32
REACH = 2 * LANES + EDGE
PITCH = 4096
CELL_LINES = 16
MIB = 1024 * 1024


IN_VMEM = pl.BlockSpec(memory_space=pltpu.VMEM)


def iota(shape, dim):
    return lax.broadcasted_iota(I32, shape, dim)


def params(mib):
    return pltpu.CompilerParams(vmem_limit_bytes=mib * MIB)


def in_hbm(array):
    return pltpu.with_memory_space_constraint(array, pltpu.HBM)


def in_vmem(array):
    return pltpu.with_memory_space_constraint(array, pltpu.VMEM)


def dot(left, right):
    return jnp.dot(left, right, preferred_element_type=F32)


def dot_nt(left, right):
    return lax.dot_general(left, right, (((1,), (1,)), ((), ())), preferred_element_type=F32)


def halves(value):
    high = value.astype(BF16)
    return high, (value - high.astype(F32)).astype(BF16)


def thirds(value):
    high = value.astype(BF16)
    rest = value - high.astype(F32)
    mid = rest.astype(BF16)
    return [high, mid, (rest - mid.astype(F32)).astype(BF16)]


def as_column(line):
    return jnp.broadcast_to(line, (LANES, line.shape[1])).T


def as_wide_column(line):
    column = as_column(line)
    return jnp.concatenate([column, column], axis=1)


def convect(mixed, top, frac, layer_mass):
    inside = iota(mixed.shape, 0) < top
    total = jnp.sum(jnp.where(inside, mixed, 0.0), axis=0, keepdims=True)
    mass = jnp.sum(jnp.where(inside, layer_mass, 0.0), axis=0, keepdims=True)
    mean = total / jnp.where(mass > 0.0, mass, 1.0)
    return mixed + jnp.where(inside, frac * (layer_mass * mean - mixed), 0.0)


def prep_kernel(lon_count, count_ref, dest_ref, col_ref, depart_ref, obs_ref, out_ref):
    n, levels = obs_ref.shape
    lane = iota((1, n), 1)
    live = lane < count_ref[0]
    first = pl.program_id(0) * GROUP
    dest = jnp.where(live, dest_ref[...] - first, -GROUP * SLOTS)
    lon = (dest + first) % lon_count
    west = jnp.where(lon == 0, dest + (lon_count - 1), dest - 1)
    cell = col_ref[...]
    cell_row = (cell // 256 + 1).astype(F32)
    cell_col = (cell % 256).astype(F32)
    contribution = (obs_ref[...].astype(F32) * as_column(depart_ref[...])).astype(BF16)
    local = iota((GROUP, n), 0)
    hit = dest == local
    before = jnp.sum((live & (dest < local)).astype(I32), axis=1, keepdims=True)
    place = jnp.sum(jnp.where(hit, lane - before, 0), axis=0, keepdims=True)
    parts, left = [], []
    for owner in (dest, west):
        pick = iota((GROUP * CAP, n), 0) == owner * CAP + place
        found = dot(pick.astype(F32).astype(BF16), contribution)
        parts.append(found.reshape(GROUP, CAP, levels))
        hit = owner == local
        left += [jnp.where(hit, cell_row, 0.0), jnp.where(hit, cell_col, 0.0)]
    spot = (iota((LANES, n), 0) % 32 == place).astype(F32).astype(BF16)
    every = dot_nt(jnp.concatenate(left, axis=0).astype(BF16), spot)
    kind = iota((GROUP, LANES), 1) // 32
    cells = [jnp.where(kind == k, every[k * GROUP : (k + 1) * GROUP], 0.0) for k in range(4)]
    cells = ((cells[0] + cells[1]) + (cells[2] + cells[3])).astype(BF16)
    spread = iota((GROUP * 8, GROUP), 0) == 8 * iota((GROUP * 8, GROUP), 1)
    parts.append(dot(spread.astype(F32).astype(BF16), cells).reshape(GROUP, 8, levels))
    whole = jnp.concatenate(parts, axis=1).reshape(GROUP * SLOTS, levels)
    out_ref[...] = whole.astype(BF16)


def prepare(devices, lon_count, obs_count, obs_dest, obs_col, obs_depart, obs_kernel):
    n, levels = obs_kernel.shape
    steps = devices // GROUP
    whole = lambda shape: pl.BlockSpec(shape, lambda g: (0, 0))
    return pl.pallas_call(
        functools.partial(prep_kernel, lon_count),
        grid=(steps,),
        in_specs=[
            pl.BlockSpec(memory_space=pltpu.SMEM),
            whole((1, n)),
            whole((1, n)),
            whole((1, n)),
            whole((n, levels)),
        ],
        out_specs=pl.BlockSpec((GROUP * SLOTS, levels), lambda g: (g, 0)),
        out_shape=pltpu.VMEM((devices * SLOTS, levels), BF16),
        compiler_params=params(16 + devices // 4),
        name="soundings_out",
    )(
        obs_count,
        in_hbm(obs_dest.reshape(1, n)),
        in_hbm(obs_col.reshape(1, n)),
        in_hbm(obs_depart.reshape(1, n)),
        obs_kernel,
    )


def level_rows(ref, row, count=None):
    levels = ref.shape[0]
    count = levels if count is None else count
    return ref.reshape(levels * 8, LANES)[pl.ds(row, count, stride=8), :]


def pack_edge(block):
    parts = [block[:, 8 * q : 8 * q + 8, :] for q in range(4)]
    low = iota(parts[0].shape, 2) < EDGE
    return [jnp.where(low, parts[2 * h], pltpu.roll(parts[2 * h + 1], EDGE, 2)) for h in range(2)]


def edge_kernel(field_ref, top_ref, frac_ref, out_ref):
    step = pl.program_id(0)
    count = field_ref.shape[0]
    here = pl.ds(pl.multiple_of(step * count, count), count)
    for h, part in enumerate(pack_edge(field_ref[...])):
        out_ref[h, here] = part * SCALE

    @pl.when(step == 0)
    def _():
        pieces = thirds(frac_ref[...])
        lines = [top_ref[...].astype(F32)] + [piece.astype(F32) for piece in pieces]
        lines[2:] = [line * SCALE for line in lines[2:]]
        first = out_ref.shape[1] - EDGE_LINES
        for i, line in enumerate(lines):
            for h, part in enumerate(pack_edge(line[None])):
                out_ref[h, first + i : first + i + 1] = part


def edge_columns(adjoint_field, cloud_top, conv_frac):
    levels, row_count, _ = adjoint_field.shape
    flat = pl.BlockSpec((row_count, LANES), lambda i: (0, 0))
    return pl.pallas_call(
        edge_kernel,
        grid=(2,),
        in_specs=[pl.BlockSpec((levels // 2, row_count, LANES), lambda i: (i, 0, 0)), flat, flat],
        out_specs=IN_VMEM,
        out_shape=pltpu.VMEM((2, levels + EDGE_LINES, 8, LANES), F32),
        compiler_params=params(16),
        cost_estimate=pl.CostEstimate(
            flops=levels * levels * 4 * row_count * LANES,
            bytes_accessed=12 * levels * row_count * LANES,
            transcendentals=0,
        ),
        name="edge_columns",
    )(adjoint_field, cloud_top, conv_frac)


def put_columns(ref, row, value):
    count = ref.shape[0]
    flat = ref.reshape(count * 8, LANES)
    for h in range(count // LANES):
        part = value[:, h * LANES : (h + 1) * LANES].T
        flat[pl.ds(h * LANES * 8 + row, LANES, stride=8), :] = part


def mix_rows(field_refs, mixing_ref, top, frac, layer_mass, block, out_ref, wide_ref):
    levels = mixing_ref.shape[1]
    for row in range(8):
        value = jnp.concatenate([level_rows(ref, row) for ref in field_refs], axis=1)
        high, low = halves(value)
        mix_high, mix_low = halves(mixing_ref[row])
        here = pl.ds(pl.multiple_of((8 * block + row) * levels, levels), levels)
        wide_ref[:levels, here] = mix_high
        wide_ref[levels:, here] = mix_low
        four = jnp.concatenate([mix_high, mix_low], axis=0)
        both = dot(jnp.concatenate([four, four], axis=1), jnp.concatenate([high, low], axis=0))
        mixed = both[:levels] + both[levels:]
        done = convect(mixed, top[row : row + 1, :], frac[row : row + 1, :], layer_mass)
        put_columns(out_ref.at[0], row, done)


def mix_kernel(
    west_ref, east_ref, mixing_ref, top_ref, frac_ref, mass_ref, out_ref, wide_ref, row_ref, column_ref
):
    layer_mass = as_wide_column(mass_ref[...])
    block = pl.program_id(0)
    mix_rows(
        (west_ref, east_ref), mixing_ref, top_ref[...], frac_ref[...], layer_mass, block,
        out_ref, wide_ref,
    )

    @pl.when(block == 0)
    def _():
        flat = out_ref.at[0].reshape(row_ref.shape[0] * 8, LANES)
        row_ref[...] = flat[pl.ds(0, row_ref.shape[0], stride=8), :]
        column_ref[...] = as_column(mass_ref[...])


def mix(adjoint_field, mixing_inverse, cloud_top, conv_frac, layer_mass):
    levels, row_count, col_count = adjoint_field.shape
    blocks = row_count // 8
    half = lambda h: pl.BlockSpec((levels, 8, LANES), lambda b: (0, b, h))
    flat = pl.BlockSpec((8, col_count), lambda b: (b, 0))
    field, wide, row, column = pl.pallas_call(
        mix_kernel,
        grid=(blocks,),
        in_specs=[
            half(0),
            half(1),
            pl.BlockSpec((8, levels, levels), lambda b: (b, 0, 0)),
            flat,
            flat,
            pl.BlockSpec((1, levels), lambda b: (0, 0)),
        ],
        out_specs=[
            pl.BlockSpec((1, col_count, 8, levels), lambda b: (b, 0, 0, 0)),
            IN_VMEM,
            pl.BlockSpec((col_count, levels), lambda b: (0, 0)),
            IN_VMEM,
        ],
        out_shape=[
            pltpu.HBM((blocks, col_count, 8, levels), F32),
            pltpu.VMEM((2 * levels, row_count * levels), BF16),
            pltpu.HBM((col_count, levels), F32),
            pltpu.VMEM((levels, LANES), F32),
        ],
        compiler_params=params(20),
        cost_estimate=pl.CostEstimate(
            flops=2 * levels * levels * 4 * row_count * col_count,
            bytes_accessed=12 * levels * row_count * col_count,
            transcendentals=0,
        ),
        name="mix_own",
    )(adjoint_field, adjoint_field, mixing_inverse, cloud_top, conv_frac, layer_mass)
    return in_hbm(field), in_vmem(wide), in_hbm(row), in_vmem(column)


def mix_edge(edge_ref, wide_ref, layer_mass, out_ref):
    levels = layer_mass.shape[0]
    group = iota((levels, 2 * LANES), 1) // EDGE
    top, frac = edge_lines(edge_ref, levels)
    for row in range(8):
        value = jnp.concatenate([level_rows(edge_ref.at[h], row, levels) for h in range(2)], axis=1)
        value = value * (1.0 / SCALE)
        mix_high, mix_low, highs, lows = [], [], [], []
        for q in range(4):
            cols = slice((8 * q + row) * levels, (8 * q + row + 1) * levels)
            mix_high.append(wide_ref[:levels, cols])
            mix_low.append(wide_ref[levels:, cols])
            high, low = halves(jnp.where(group == q, value, 0.0))
            highs.append(high)
            lows.append(low)
        highs = jnp.concatenate(highs, axis=0)
        mixed = dot(
            jnp.concatenate(mix_high * 2, axis=1),
            jnp.concatenate([highs] + lows, axis=0),
        ) + dot(jnp.concatenate(mix_low, axis=1), highs)
        done = convect(mixed, top[row : row + 1].astype(I32), frac[row : row + 1], layer_mass)
        put_columns(out_ref, row, done)


def edge_lines(ref, levels):
    top, high, mid, low = [
        jnp.concatenate([ref[0, levels + i], ref[1, levels + i]], axis=1)
        for i in range(EDGE_LINES)
    ]
    return top, high + (mid + low) * (1.0 / SCALE)


def find_places(row, row_count):
    count = row.shape[1]
    upto = (iota((LANES, LANES), 0) <= iota((LANES, LANES), 1)).astype(F32).astype(BF16)
    before = jnp.zeros((row_count, 1), F32)
    places = []
    for start in range(0, count, LANES):
        mine = iota((row_count, LANES), 0) == row[:, start : start + LANES]
        running = dot(mine.astype(F32).astype(BF16), upto)
        place = jnp.sum(jnp.where(mine, running + before, 0.0), axis=0, keepdims=True) - 1.0
        places.append(place.astype(I32))
        before = before + running[:, LANES - 1 :]
    return jnp.concatenate(places, axis=1), jnp.max(before)


def mix_slots(blocks, index, key_ref, table_ref, wide_ref, layer_mass, stack):
    levels = layer_mass.shape[0]
    slots = 8 * WINDOW
    lane = iota((1, slots), 1)
    target = [(8 * b + lane // WINDOW) * PITCH + index * WINDOW + lane % WINDOW for b in blocks]
    target = jnp.concatenate(target, axis=1)
    pick = [
        (key_ref[...] == target[:, start : start + LANES]).astype(F32).astype(BF16)
        for start in range(0, target.shape[1], LANES)
    ]
    found = dot(table_ref[...], jnp.concatenate(pick, axis=1))
    split_high, split_low, top, high, mid, low = [
        found[levels + i : levels + i + 1] for i in range(6)
    ]
    column = (split_high * EDGE + split_low).astype(I32)
    parts = []
    for i, b in enumerate(blocks):
        value = found[:levels, i * slots : (i + 1) * slots].astype(BF16)
        for r in range(8):
            mine = (lane // WINDOW == r).astype(F32).astype(BF16)
            stack[i, r * levels : (r + 1) * levels, :] = value * mine
        start = pl.multiple_of(8 * b * levels, 8 * levels)
        both = dot(wide_ref[:, pl.ds(start, 8 * levels)], stack[i])
        parts.append(both[:levels] + both[levels:])
    mass = jnp.concatenate([layer_mass] * len(blocks), axis=1)
    done = convect(
        jnp.concatenate(parts, axis=1), top.astype(I32), (high + mid) + low, mass
    )
    turned = [done[:, start : start + LANES].T for start in range(0, done.shape[1], LANES)]
    high, low = halves(jnp.concatenate(turned, axis=0))
    return high, low, column


def expand(high, low, column, square, out_ref, add):
    levels = high.shape[1]
    flat = out_ref.reshape(REACH * 8, LANES)
    hot = (iota((REACH, 8 * WINDOW), 0) == column).astype(F32).astype(BF16)
    for group in range(2):
        for r in range(4):
            source = slice((4 * group + r) * WINDOW, (4 * group + r + 1) * WINDOW)
            target = slice(r * levels, (r + 1) * levels)
            square[group, r * WINDOW : (r + 1) * WINDOW, target] = high[source]
            square[group, (4 + r) * WINDOW : (5 + r) * WINDOW, target] = low[source]
        left = hot[:, 4 * group * WINDOW : 4 * (group + 1) * WINDOW]
        forced = dot(jnp.concatenate([left, left], axis=1), square[group])
        for r in range(4):
            rows = pl.ds(4 * group + r, REACH, stride=8)
            part = forced[:, r * levels : (r + 1) * levels]
            flat[rows, :] = flat[rows, :] + part if add else part


def force_rows(
    block, rounds, high_ref, low_ref, column_ref,
    key_ref, table_ref, wide_ref, layer_mass, stack, square, out_ref,
):
    slots = 8 * WINDOW
    here = pl.ds(pl.multiple_of(block * slots, slots), slots)
    expand(high_ref[here, :], low_ref[here, :], column_ref[0:1, here], square, out_ref, False)

    def more(index, carry):
        mixed = mix_slots([block], index, key_ref, table_ref, wide_ref, layer_mass, stack)
        expand(*mixed, square, out_ref, True)
        return carry

    lax.fori_loop(1, rounds, more, 0)


def soundings_kernel(
    got_ref, wide_ref, top_hbm, frac_hbm, lines_ref, mass_ref,
    row_ref, courant_ref, shift_hbm, weight_hbm,
    key_ref, table_ref, high_ref, low_ref, column_ref, shift_ref, weight_ref,
    edge_out, rounds_ref, first_ref,
    forced, stack, square, row_scr, courant_scr, top_ref, frac_ref, sem,
):
    devices = got_ref.shape[0]
    levels = mass_ref.shape[0]
    n = devices * CAP
    row_count = top_ref.shape[0]
    width = 2 * LANES
    layer_mass = jnp.concatenate([mass_ref[...]] * 2, axis=1)
    late = [
        pltpu.make_async_copy(row_ref, row_scr, sem.at[0]),
        pltpu.make_async_copy(courant_ref.at[:, 0, :], courant_scr, sem.at[1]),
        pltpu.make_async_copy(shift_hbm, shift_ref, sem.at[2]),
        pltpu.make_async_copy(weight_hbm, weight_ref, sem.at[3]),
    ]
    soon = [
        pltpu.make_async_copy(top_hbm, top_ref, sem.at[4]),
        pltpu.make_async_copy(frac_hbm, frac_ref, sem.at[5]),
    ]
    for copy in soon + late:
        copy.start()
    mix_edge(lines_ref, wide_ref, layer_mass, edge_out)

    got = got_ref[...].astype(F32)
    table_ref[:levels, :n] = got[:, :CAP].reshape(n, levels).T.astype(BF16)
    table_ref[:levels, n:] = got[:, CAP : 2 * CAP].reshape(n, levels).T.astype(BF16)
    info = got[:, 2 * CAP :].reshape(devices * 8, LANES).astype(BF16)
    first = iota((devices, devices * 8), 1) == 8 * iota((devices, devices * 8), 0)
    info = dot(first.astype(F32).astype(BF16), info)
    kind = iota((devices, LANES), 1) // 32
    left = [jnp.where(kind == k, info, 0.0) for k in range(4)]
    chosen = iota((LANES, n), 0) % 32 == iota((LANES, n), 1) % CAP
    spread = dot(
        jnp.concatenate(left, axis=0).astype(BF16), chosen.astype(F32).astype(BF16)
    )
    mine = iota((devices, n), 0) == iota((devices, n), 1) // CAP
    lines = [
        jnp.sum(jnp.where(mine, spread[k * devices : (k + 1) * devices], 0.0), axis=0, keepdims=True)
        for k in range(4)
    ]
    own_row, own_col, east_row, east_col = [line.astype(I32) for line in lines]
    own_row, east_row = own_row - 1, east_row - 1
    east_row = jnp.where(east_col < EDGE, east_row, -1)
    row = jnp.concatenate([own_row, east_row], axis=1)
    place, most = find_places(row, row_count)
    rounds = (most.astype(I32) + (WINDOW - 1)) // WINDOW
    rounds_ref[0] = rounds
    key_ref[...] = as_column((row * PITCH + place).astype(F32)).astype(I32)
    column = jnp.concatenate([own_col, width + east_col], axis=1)
    cells = [[(column // EDGE).astype(F32), (column % EDGE).astype(F32)]]

    for copy in soon:
        copy.wait()
    packed_col = (east_row // 8) * EDGE + east_col
    parts = [
        (own_col, own_row, top_ref[...].astype(F32), frac_ref[...], row_count),
        (packed_col, east_row % 8, *edge_lines(lines_ref, levels), 8),
    ]
    for col, row, top, frac, count in parts:
        hot = (iota((width, n), 0) == col).astype(F32).astype(BF16)
        table = jnp.concatenate([top.astype(BF16)] + thirds(frac), axis=0)
        found = dot(table, hot)
        here = iota((count, n), 0) == row
        cells.append([
            jnp.sum(jnp.where(here, found[i * count : (i + 1) * count], 0.0), axis=0, keepdims=True)
            for i in range(4)
        ])
    lines = cells[0] + [jnp.concatenate(pair, axis=1) for pair in zip(cells[1], cells[2])]
    lines.append(jnp.zeros((CELL_LINES - len(lines), 2 * n), F32))
    table_ref[levels:] = jnp.concatenate(lines, axis=0).astype(BF16)

    high, low, column = mix_slots(
        list(range(row_count // 8)), 0, key_ref, table_ref, wide_ref, layer_mass, stack
    )
    high_ref[...] = high
    low_ref[...] = low
    column_ref[0:1] = column
    column_ref[1:] = jnp.zeros_like(column_ref[1:])
    square[...] = jnp.zeros_like(square)
    force_rows(
        0, rounds, high_ref, low_ref, column_ref,
        key_ref, table_ref, wide_ref, layer_mass, stack, square, forced,
    )
    edge = edge_out.reshape(width * 8, LANES)[pl.ds(0, EDGE, stride=8), :]
    for copy in late:
        copy.wait()
    value = jnp.concatenate([row_scr[...], edge], axis=0)
    value = value + forced.reshape(REACH * 8, LANES)[pl.ds(0, REACH, stride=8), :]
    shift = shift_ref[0:1, :]
    weight = weight_ref[0:1, :]
    for bit in (32, 16, 8, 4, 2, 1):
        value = jnp.where((shift & bit) != 0, value[bit:], value[:-bit])
    zonal = (1.0 - weight) * value[:width] + weight * value[1 : width + 1]
    for h in range(2):
        here = slice(h * LANES, (h + 1) * LANES)
        first_ref[:, here] = courant_scr[:, here] * zonal[here].T


def take_soundings(got, wide, cloud_top, conv_frac, edge_in, layer_mass, row, courant, shift, weight):
    levels = layer_mass.shape[0]
    row_count, col_count = cloud_top.shape
    n = got.shape[0] * CAP
    width = 2 * LANES
    in_place = pl.BlockSpec(memory_space=pl.ANY)
    return pl.pallas_call(
        soundings_kernel,
        in_specs=[IN_VMEM, IN_VMEM, in_place, in_place, IN_VMEM, IN_VMEM] + [in_place] * 4,
        out_specs=[IN_VMEM] * 8 + [pl.BlockSpec(memory_space=pltpu.SMEM), IN_VMEM],
        out_shape=[
            pltpu.VMEM((2 * n, LANES), I32),
            pltpu.VMEM((levels + CELL_LINES, 2 * n), BF16),
            pltpu.VMEM((row_count * WINDOW, levels), BF16),
            pltpu.VMEM((row_count * WINDOW, levels), BF16),
            pltpu.VMEM((8, row_count * WINDOW), I32),
            pltpu.VMEM((row_count, levels), I32),
            pltpu.VMEM((row_count, levels), F32),
            pltpu.VMEM((width, 8, levels), F32),
            jax.ShapeDtypeStruct((1,), I32),
            jax.ShapeDtypeStruct((levels, col_count), F32),
        ],
        scratch_shapes=[
            pltpu.VMEM((REACH, 8, levels), F32),
            pltpu.VMEM((row_count // 8, 8 * levels, 8 * WINDOW), BF16),
            pltpu.VMEM((2, 8 * WINDOW, 4 * levels), BF16),
            pltpu.VMEM((col_count, levels), F32),
            pltpu.VMEM((levels, col_count), F32),
            pltpu.VMEM((row_count, col_count), I32),
            pltpu.VMEM((row_count, col_count), F32),
            pltpu.SemaphoreType.DMA((6,)),
        ],
        compiler_params=params(24 + n // 64),
        name="take_soundings",
    )(
        got, wide, cloud_top, conv_frac, edge_in, layer_mass, row, courant, shift, weight
    )


def advect_kernel(
    key_ref, table_ref, high_ref, low_ref, column_ref, shift_ref, weight_ref, edge_ref, rounds_ref,
    wide_ref, field_ref, mass_ref, courant_ref,
    out_ref, last_ref,
    forced, coarse, done, stack, square, out_scr, prev, field_scr, courant_scr, sem, in_sem,
):
    step = pl.program_id(0)
    blocks = pl.num_programs(0) - 1
    block = blocks - 1 - step
    levels = mass_ref.shape[0]
    width = 2 * LANES

    def field_in(b):
        return pltpu.make_async_copy(field_ref.at[b], field_scr.at[b], in_sem.at[b, 0])

    def courant_in(b, h):
        source = courant_ref.at[:, pl.ds(pl.multiple_of(b * 8, 8), 8), pl.ds(h * LANES, LANES)]
        return pltpu.make_async_copy(source, courant_scr.at[b, h], in_sem.at[b, 1 + h])

    @pl.when(step == 0)
    def _():
        for b in reversed(range(out_scr.shape[0])):
            field_in(b).start()
            for h in range(2):
                courant_in(b, h).start()
        prev[...] = jnp.zeros_like(prev)
        square[...] = jnp.zeros_like(square)

    layer_mass = jnp.concatenate([mass_ref[...]] * 2, axis=1)
    lines = pl.ds(pl.multiple_of(8 * jnp.maximum(block, 0), 8), 8)
    shift = shift_ref[lines, :]
    weight = weight_ref[lines, :]
    chosen = {bit: (shift & bit) != 0 for bit in (32, 16, 8, 4, 2, 1)}

    def choose(tiles, bit, step):
        return [
            jnp.where(chosen[bit], new, old) for old, new in zip(tiles[:-step], tiles[step:])
        ]

    def by_eights(start):
        tiles = [field_scr[block, start + 8 * i] + forced[start + 8 * i] for i in range(32)]
        tiles += [
            edge_ref[EDGE * block + start + 8 * i] + forced[width + start + 8 * i] for i in range(8)
        ]
        for bit in (32, 16, 8):
            tiles = choose(tiles, bit, bit // 8)
        for i, tile in enumerate(tiles):
            coarse[start + 8 * i] = tile

    def by_ones(chunk, carry):
        start = chunk * 32
        tiles = [coarse[start + i] for i in range(40)]
        for bit in (4, 2, 1):
            tiles = choose(tiles, bit, bit)
        for i in range(32):
            done[start + i] = (1.0 - weight) * tiles[i] + weight * tiles[i + 1]
        return carry

    flat = done.reshape(width * 8, LANES)

    def meridional(beside, which=(0, 1)):
        later = [prev[0], prev[1]]
        for index in range(8):
            r = 7 - index
            for h in which:
                zonal = flat[pl.ds(h * LANES * 8 + r, LANES, stride=8), :].T
                courant = level_rows(courant_scr.at[block + 1, h], r)
                place = out_scr.at[block + 1, h].reshape(levels * 8, LANES)
                leaving = courant * zonal
                place[pl.ds(r, levels, stride=8), :] = (zonal - leaving) + later[h]
                later[h] = leaving
            beside(index)
        for h in which:
            prev[h] = later[h]

    def copies(b, which=(0, 1)):
        return [
            pltpu.make_async_copy(
                out_scr.at[b, h],
                out_ref.at[:, pl.ds(b * 8, 8), pl.ds(h * LANES, LANES)],
                sem.at[b, h],
            )
            for h in which
        ]

    def shift_only(index, carry):
        by_eights(index)
        return carry

    @pl.when(step < blocks)
    def _():
        force_rows(
            block, rounds_ref[0], high_ref, low_ref, column_ref,
            key_ref, table_ref, wide_ref, layer_mass, stack, square, forced,
        )
        field_in(block).wait()

    @pl.when(step > 0)
    def _():
        for h in range(2):
            courant_in(block + 1, h).wait()

    @pl.when(step == 0)
    def _():
        lax.fori_loop(0, 8, shift_only, 0)

    @pl.when((step > 0) & (step < blocks))
    def _():
        meridional(by_eights)

    @pl.when(step < blocks)
    def _():
        lax.fori_loop(0, width // 32, by_ones, 0)

    @pl.when(step == blocks)
    def _():
        for h in range(2):
            meridional(lambda index: None, (h,))
            copies(0, (h,))[0].start()

    @pl.when(step == 1)
    def _():
        for h in range(2):
            place = out_scr.at[blocks - 1, h].reshape(levels * 8, LANES)
            last_ref[:, h * LANES : (h + 1) * LANES] = place[pl.ds(7, levels, stride=8), :]

    for b in range(1, out_scr.shape[0]):

        @pl.when(block + 1 == b)
        def _():
            for copy in copies(b):
                copy.start()

    @pl.when(step == blocks)
    def _():
        for b in range(out_scr.shape[0]):
            for copy in copies(b):
                copy.wait()


def advect(soundings, edge_field, rounds, wide, field, layer_mass, courant):
    blocks, col_count, _, levels = field.shape
    n = soundings[0].shape[0] // 2
    in_place = pl.BlockSpec(memory_space=pl.ANY)
    return pl.pallas_call(
        advect_kernel,
        grid=(blocks + 1,),
        in_specs=[IN_VMEM] * 8
        + [pl.BlockSpec(memory_space=pltpu.SMEM), IN_VMEM, in_place, IN_VMEM, in_place],
        out_specs=[pl.BlockSpec(memory_space=pl.ANY), IN_VMEM],
        out_shape=[
            jax.ShapeDtypeStruct(courant.shape, F32),
            pltpu.VMEM((levels, col_count), F32),
        ],
        scratch_shapes=[
            pltpu.VMEM((REACH, 8, levels), F32),
            pltpu.VMEM((col_count + 8, 8, levels), F32),
            pltpu.VMEM((col_count, 8, levels), F32),
            pltpu.VMEM((1, 8 * levels, 8 * WINDOW), BF16),
            pltpu.VMEM((2, 8 * WINDOW, 4 * levels), BF16),
            pltpu.VMEM((blocks, 2, levels, 8, LANES), F32),
            pltpu.VMEM((2, levels, LANES), F32),
            pltpu.VMEM((blocks, col_count, 8, levels), F32),
            pltpu.VMEM((blocks, 2, levels, 8, LANES), F32),
            pltpu.SemaphoreType.DMA((blocks, 2)),
            pltpu.SemaphoreType.DMA((blocks, 3)),
        ],
        compiler_params=params(24 + n // 128),
        cost_estimate=pl.CostEstimate(
            flops=2 * levels * 8 * blocks * n * col_count,
            bytes_accessed=12 * levels * 8 * blocks * col_count,
            transcendentals=0,
        ),
        name="advect",
    )(
        *soundings, edge_field, rounds, wide, field, layer_mass, courant
    )


def close_kernel(last_ref, north_ref, _, out_ref, row, sem):
    row[...] = last_ref[...] + north_ref[...]
    copy = pltpu.make_async_copy(row, out_ref.at[:, out_ref.shape[1] - 1, :], sem)
    copy.start()
    copy.wait()


def close(out, last, north):
    in_place = pl.BlockSpec(memory_space=pl.ANY)
    return pl.pallas_call(
        close_kernel,
        in_specs=[IN_VMEM, IN_VMEM, in_place],
        out_specs=in_place,
        out_shape=jax.ShapeDtypeStruct(out.shape, F32),
        scratch_shapes=[pltpu.VMEM(last.shape, F32), pltpu.SemaphoreType.DMA],
        input_output_aliases={2: 0},
        compiler_params=params(4),
        name="close_last_row",
    )(last, north, out)


def shards(
    adjoint_field,
    mixing_inverse,
    cloud_top,
    conv_frac,
    thickness,
    zonal_shift,
    zonal_frac,
    merid_courant,
    obs_kernel,
    obs_depart,
    obs_dest,
    obs_col,
    obs_count,
):
    adjoint_field, mixing_inverse, cloud_top, conv_frac, merid_courant, obs_kernel = [
        in_hbm(array)
        for array in (
            adjoint_field, mixing_inverse, cloud_top, conv_frac, merid_courant, obs_kernel
        )
    ]
    levels, row_count, col_count = adjoint_field.shape
    lat_count, lon_count = lax.axis_size("lat"), lax.axis_size("lon")
    devices = lat_count * lon_count
    sent = prepare(devices, lon_count, obs_count, obs_dest, obs_col, obs_depart, obs_kernel)
    sent, field_after = lax.optimization_barrier((sent, adjoint_field))
    got = lax.all_to_all(
        sent.reshape(devices, SLOTS, levels), ("lat", "lon"), split_axis=0, concat_axis=0, tiled=True
    )
    westward = [((i + 1) % lon_count, i) for i in range(lon_count)]
    layer_mass = in_hbm(thickness.reshape(1, levels))
    field_after = in_hbm(field_after)
    edge = edge_columns(field_after, cloud_top, conv_frac).astype(jnp.float16)
    field, wide, row, layer_mass = mix(
        field_after, mixing_inverse, cloud_top, conv_frac, layer_mass
    )
    edge_in = in_vmem(lax.ppermute(edge, "lon", westward).astype(F32))
    shift, weight = in_hbm(zonal_shift.T), in_hbm(zonal_frac.T)
    *soundings, edge_field, rounds, first = take_soundings(
        got, wide, cloud_top, conv_frac, edge_in, layer_mass, row, merid_courant, shift, weight
    )
    southward = [(i + 1, i) for i in range(lat_count - 1)]
    north = lax.ppermute(first, "lat", southward)
    out, last = advect(
        [in_vmem(part) for part in soundings], in_vmem(edge_field), rounds, wide, field, layer_mass,
        merid_courant,
    )
    return close(out, last, north)


def solution(mesh):
    in_specs = (
        P(None, "lat", "lon"),
        P("lat", None, None),
        P("lat", "lon"),
        P("lat", "lon"),
        P(),
        P(None, "lat"),
        P(None, "lat"),
        P(None, "lat", "lon"),
        P(("lat", "lon"), None),
        P(("lat", "lon")),
        P(("lat", "lon")),
        P(("lat", "lon")),
        P(("lat", "lon")),
    )
    out_specs = P(None, "lat", "lon")
    return jax.shard_map(shards, mesh=mesh, in_specs=in_specs, out_specs=out_specs, check_vma=False)
```

```python
import functools

import jax
import jax.numpy as jnp
from jax import lax
from jax.experimental import pallas as pl
from jax.experimental.pallas import tpu as pltpu
from jax.sharding import PartitionSpec as P

F32, BF16, I32 = jnp.float32, jnp.bfloat16, jnp.int32
CAP = 16
SLOTS = 40
EDGE = 64
LANES = 128
GROUP = 32
EDGE_LINES = 4
SCALE = 4096.0
WINDOW = 32
REACH = 2 * LANES + EDGE
PITCH = 4096
CELL_LINES = 16
MIB = 1024 * 1024


IN_VMEM = pl.BlockSpec(memory_space=pltpu.VMEM)


def iota(shape, dim):
    return lax.broadcasted_iota(I32, shape, dim)


def params(mib):
    return pltpu.CompilerParams(vmem_limit_bytes=mib * MIB)


def in_hbm(array):
    return pltpu.with_memory_space_constraint(array, pltpu.HBM)


def in_vmem(array):
    return pltpu.with_memory_space_constraint(array, pltpu.VMEM)


def dot(left, right):
    return jnp.dot(left, right, preferred_element_type=F32)


def dot_nt(left, right):
    return lax.dot_general(left, right, (((1,), (1,)), ((), ())), preferred_element_type=F32)


def halves(value):
    high = value.astype(BF16)
    return high, (value - high.astype(F32)).astype(BF16)


def thirds(value):
    high = value.astype(BF16)
    rest = value - high.astype(F32)
    mid = rest.astype(BF16)
    return [high, mid, (rest - mid.astype(F32)).astype(BF16)]


def as_column(line):
    return jnp.broadcast_to(line, (LANES, line.shape[1])).T


def as_wide_column(line):
    column = as_column(line)
    return jnp.concatenate([column, column], axis=1)


def convect(mixed, top, frac, layer_mass):
    inside = iota(mixed.shape, 0) < top
    total = jnp.sum(jnp.where(inside, mixed, 0.0), axis=0, keepdims=True)
    mass = jnp.sum(jnp.where(inside, layer_mass, 0.0), axis=0, keepdims=True)
    mean = total / jnp.where(mass > 0.0, mass, 1.0)
    return mixed + jnp.where(inside, frac * (layer_mass * mean - mixed), 0.0)


def prep_kernel(lon_count, count_ref, dest_ref, col_ref, depart_ref, obs_ref, out_ref):
    n, levels = obs_ref.shape
    lane = iota((1, n), 1)
    live = lane < count_ref[0]
    first = pl.program_id(0) * GROUP
    dest = jnp.where(live, dest_ref[...] - first, -GROUP * SLOTS)
    lon = (dest + first) % lon_count
    west = jnp.where(lon == 0, dest + (lon_count - 1), dest - 1)
    cell = col_ref[...]
    cell_row = (cell // 256 + 1).astype(F32)
    cell_col = (cell % 256).astype(F32)
    contribution = (obs_ref[...].astype(F32) * as_column(depart_ref[...])).astype(BF16)
    local = iota((GROUP, n), 0)
    hit = dest == local
    before = jnp.sum((live & (dest < local)).astype(I32), axis=1, keepdims=True)
    place = jnp.sum(jnp.where(hit, lane - before, 0), axis=0, keepdims=True)
    parts, left = [], []
    for owner in (dest, west):
        pick = iota((GROUP * CAP, n), 0) == owner * CAP + place
        found = dot(pick.astype(F32).astype(BF16), contribution)
        parts.append(found.reshape(GROUP, CAP, levels))
        hit = owner == local
        left += [jnp.where(hit, cell_row, 0.0), jnp.where(hit, cell_col, 0.0)]
    spot = (iota((LANES, n), 0) % 32 == place).astype(F32).astype(BF16)
    every = dot_nt(jnp.concatenate(left, axis=0).astype(BF16), spot)
    kind = iota((GROUP, LANES), 1) // 32
    cells = [jnp.where(kind == k, every[k * GROUP : (k + 1) * GROUP], 0.0) for k in range(4)]
    cells = ((cells[0] + cells[1]) + (cells[2] + cells[3])).astype(BF16)
    spread = iota((GROUP * 8, GROUP), 0) == 8 * iota((GROUP * 8, GROUP), 1)
    parts.append(dot(spread.astype(F32).astype(BF16), cells).reshape(GROUP, 8, levels))
    whole = jnp.concatenate(parts, axis=1).reshape(GROUP * SLOTS, levels)
    out_ref[...] = whole.astype(BF16)


def prepare(devices, lon_count, obs_count, obs_dest, obs_col, obs_depart, obs_kernel):
    n, levels = obs_kernel.shape
    steps = devices // GROUP
    whole = lambda shape: pl.BlockSpec(shape, lambda g: (0, 0))
    return pl.pallas_call(
        functools.partial(prep_kernel, lon_count),
        grid=(steps,),
        in_specs=[
            pl.BlockSpec(memory_space=pltpu.SMEM),
            whole((1, n)),
            whole((1, n)),
            whole((1, n)),
            whole((n, levels)),
        ],
        out_specs=pl.BlockSpec((GROUP * SLOTS, levels), lambda g: (g, 0)),
        out_shape=pltpu.VMEM((devices * SLOTS, levels), BF16),
        compiler_params=params(16 + devices // 4),
        name="soundings_out",
    )(
        obs_count,
        in_hbm(obs_dest.reshape(1, n)),
        in_hbm(obs_col.reshape(1, n)),
        in_hbm(obs_depart.reshape(1, n)),
        obs_kernel,
    )


def level_rows(ref, row, count=None):
    levels = ref.shape[0]
    count = levels if count is None else count
    return ref.reshape(levels * 8, LANES)[pl.ds(row, count, stride=8), :]


def pack_edge(block):
    parts = [block[:, 8 * q : 8 * q + 8, :] for q in range(4)]
    low = iota(parts[0].shape, 2) < EDGE
    return [jnp.where(low, parts[2 * h], pltpu.roll(parts[2 * h + 1], EDGE, 2)) for h in range(2)]


def edge_kernel(field_ref, top_ref, frac_ref, out_ref):
    step = pl.program_id(0)
    count = field_ref.shape[0]
    here = pl.ds(pl.multiple_of(step * count, count), count)
    for h, part in enumerate(pack_edge(field_ref[...])):
        out_ref[h, here] = part * SCALE

    @pl.when(step == 0)
    def _():
        pieces = thirds(frac_ref[...])
        lines = [top_ref[...].astype(F32)] + [piece.astype(F32) for piece in pieces]
        lines[2:] = [line * SCALE for line in lines[2:]]
        first = out_ref.shape[1] - EDGE_LINES
        for i, line in enumerate(lines):
            for h, part in enumerate(pack_edge(line[None])):
                out_ref[h, first + i : first + i + 1] = part


def edge_columns(adjoint_field, cloud_top, conv_frac):
    levels, row_count, _ = adjoint_field.shape
    flat = pl.BlockSpec((row_count, LANES), lambda i: (0, 0))
    return pl.pallas_call(
        edge_kernel,
        grid=(2,),
        in_specs=[pl.BlockSpec((levels // 2, row_count, LANES), lambda i: (i, 0, 0)), flat, flat],
        out_specs=IN_VMEM,
        out_shape=pltpu.VMEM((2, levels + EDGE_LINES, 8, LANES), F32),
        compiler_params=params(16),
        cost_estimate=pl.CostEstimate(
            flops=levels * levels * 4 * row_count * LANES,
            bytes_accessed=12 * levels * row_count * LANES,
            transcendentals=0,
        ),
        name="edge_columns",
    )(adjoint_field, cloud_top, conv_frac)


def put_columns(ref, row, value):
    count = ref.shape[0]
    flat = ref.reshape(count * 8, LANES)
    for h in range(count // LANES):
        part = value[:, h * LANES : (h + 1) * LANES].T
        flat[pl.ds(h * LANES * 8 + row, LANES, stride=8), :] = part


def mix_rows(field_refs, mixing_ref, top, frac, layer_mass, block, out_ref, wide_ref):
    levels = mixing_ref.shape[1]
    for row in range(8):
        value = jnp.concatenate([level_rows(ref, row) for ref in field_refs], axis=1)
        high, low = halves(value)
        mix_high, mix_low = halves(mixing_ref[row])
        here = pl.ds(pl.multiple_of((8 * block + row) * levels, levels), levels)
        wide_ref[:levels, here] = mix_high
        wide_ref[levels:, here] = mix_low
        four = jnp.concatenate([mix_high, mix_low], axis=0)
        both = dot(jnp.concatenate([four, four], axis=1), jnp.concatenate([high, low], axis=0))
        mixed = both[:levels] + both[levels:]
        done = convect(mixed, top[row : row + 1, :], frac[row : row + 1, :], layer_mass)
        put_columns(out_ref.at[0], row, done)


def mix_kernel(
    west_ref, east_ref, mixing_ref, top_ref, frac_ref, mass_ref, out_ref, wide_ref, row_ref
):
    layer_mass = as_wide_column(mass_ref[...])
    block = pl.program_id(0)
    mix_rows(
        (west_ref, east_ref), mixing_ref, top_ref[...], frac_ref[...], layer_mass, block,
        out_ref, wide_ref,
    )

    @pl.when(block == 0)
    def _():
        flat = out_ref.at[0].reshape(row_ref.shape[0] * 8, LANES)
        row_ref[...] = flat[pl.ds(0, row_ref.shape[0], stride=8), :]


def mix(adjoint_field, mixing_inverse, cloud_top, conv_frac, layer_mass):
    levels, row_count, col_count = adjoint_field.shape
    blocks = row_count // 8
    half = lambda h: pl.BlockSpec((levels, 8, LANES), lambda b: (0, b, h))
    flat = pl.BlockSpec((8, col_count), lambda b: (b, 0))
    field, wide, row = pl.pallas_call(
        mix_kernel,
        grid=(blocks,),
        in_specs=[
            half(0),
            half(1),
            pl.BlockSpec((8, levels, levels), lambda b: (b, 0, 0)),
            flat,
            flat,
            pl.BlockSpec((1, levels), lambda b: (0, 0)),
        ],
        out_specs=[
            pl.BlockSpec((1, col_count, 8, levels), lambda b: (b, 0, 0, 0)),
            IN_VMEM,
            pl.BlockSpec((col_count, levels), lambda b: (0, 0)),
        ],
        out_shape=[
            pltpu.HBM((blocks, col_count, 8, levels), F32),
            pltpu.VMEM((2 * levels, row_count * levels), BF16),
            pltpu.HBM((col_count, levels), F32),
        ],
        compiler_params=params(20),
        cost_estimate=pl.CostEstimate(
            flops=2 * levels * levels * 4 * row_count * col_count,
            bytes_accessed=12 * levels * row_count * col_count,
            transcendentals=0,
        ),
        name="mix_own",
    )(adjoint_field, adjoint_field, mixing_inverse, cloud_top, conv_frac, layer_mass)
    return in_hbm(field), in_vmem(wide), in_hbm(row)


def mix_edge(edge_ref, wide_ref, mass_ref, arrive, out_ref):
    levels = mass_ref.shape[0]
    group = iota((levels, 2 * LANES), 1) // EDGE
    top, frac = edge_lines(edge_ref, levels)
    for row in range(8):
        value = jnp.concatenate([level_rows(edge_ref.at[h], row, levels) for h in range(2)], axis=1)
        value = value * (1.0 / SCALE)
        mix_high, mix_low, highs, lows = [], [], [], []
        for q in range(4):
            cols = slice((8 * q + row) * levels, (8 * q + row + 1) * levels)
            mix_high.append(wide_ref[:levels, cols])
            mix_low.append(wide_ref[levels:, cols])
            high, low = halves(jnp.where(group == q, value, 0.0))
            highs.append(high)
            lows.append(low)
        highs = jnp.concatenate(highs, axis=0)
        mixed = dot(
            jnp.concatenate(mix_high * 2, axis=1),
            jnp.concatenate([highs] + lows, axis=0),
        ) + dot(jnp.concatenate(mix_low, axis=1), highs)
        if row == 0:
            arrive()
            layer_mass = jnp.concatenate([mass_ref[...]] * 2, axis=1)
        done = convect(mixed, top[row : row + 1].astype(I32), frac[row : row + 1], layer_mass)
        put_columns(out_ref, row, done)


def edge_lines(ref, levels):
    top, high, mid, low = [
        jnp.concatenate([ref[0, levels + i], ref[1, levels + i]], axis=1)
        for i in range(EDGE_LINES)
    ]
    return top, high + (mid + low) * (1.0 / SCALE)


def find_places(row, row_count):
    count = row.shape[1]
    upto = (iota((LANES, LANES), 0) <= iota((LANES, LANES), 1)).astype(F32).astype(BF16)
    before = jnp.zeros((row_count, 1), F32)
    places = []
    for start in range(0, count, LANES):
        mine = iota((row_count, LANES), 0) == row[:, start : start + LANES]
        running = dot(mine.astype(F32).astype(BF16), upto)
        place = jnp.sum(jnp.where(mine, running + before, 0.0), axis=0, keepdims=True) - 1.0
        places.append(place.astype(I32))
        before = before + running[:, LANES - 1 :]
    return jnp.concatenate(places, axis=1), jnp.max(before)


def mix_slots(blocks, index, key_ref, table_ref, wide_ref, layer_mass, stack):
    levels = layer_mass.shape[0]
    slots = 8 * WINDOW
    lane = iota((1, slots), 1)
    target = [(8 * b + lane // WINDOW) * PITCH + index * WINDOW + lane % WINDOW for b in blocks]
    target = jnp.concatenate(target, axis=1)
    pick = [
        (key_ref[...] == target[:, start : start + LANES]).astype(F32).astype(BF16)
        for start in range(0, target.shape[1], LANES)
    ]
    found = dot(table_ref[...], jnp.concatenate(pick, axis=1))
    split_high, split_low, top, high, mid, low = [
        found[levels + i : levels + i + 1] for i in range(6)
    ]
    column = (split_high * EDGE + split_low).astype(I32)
    parts = []
    for i, b in enumerate(blocks):
        value = found[:levels, i * slots : (i + 1) * slots].astype(BF16)
        for r in range(8):
            mine = (lane // WINDOW == r).astype(F32).astype(BF16)
            stack[i, r * levels : (r + 1) * levels, :] = value * mine
        start = pl.multiple_of(8 * b * levels, 8 * levels)
        both = dot(wide_ref[:, pl.ds(start, 8 * levels)], stack[i])
        parts.append(both[:levels] + both[levels:])
    mass = jnp.concatenate([layer_mass] * len(blocks), axis=1)
    done = convect(
        jnp.concatenate(parts, axis=1), top.astype(I32), (high + mid) + low, mass
    )
    turned = [done[:, start : start + LANES].T for start in range(0, done.shape[1], LANES)]
    high, low = halves(jnp.concatenate(turned, axis=0))
    return high, low, column


def expand(high, low, column, square, out_ref, add):
    levels = high.shape[1]
    flat = out_ref.reshape(REACH * 8, LANES)
    hot = (iota((REACH, 8 * WINDOW), 0) == column).astype(F32).astype(BF16)
    for group in range(2):
        for r in range(4):
            source = slice((4 * group + r) * WINDOW, (4 * group + r + 1) * WINDOW)
            target = slice(r * levels, (r + 1) * levels)
            square[group, r * WINDOW : (r + 1) * WINDOW, target] = high[source]
            square[group, (4 + r) * WINDOW : (5 + r) * WINDOW, target] = low[source]
        left = hot[:, 4 * group * WINDOW : 4 * (group + 1) * WINDOW]
        forced = dot(jnp.concatenate([left, left], axis=1), square[group])
        for r in range(4):
            rows = pl.ds(4 * group + r, REACH, stride=8)
            part = forced[:, r * levels : (r + 1) * levels]
            flat[rows, :] = flat[rows, :] + part if add else part


def force_rows(
    block, rounds, high_ref, low_ref, column_ref,
    key_ref, table_ref, wide_ref, layer_mass, stack, square, out_ref,
):
    slots = 8 * WINDOW
    here = pl.ds(pl.multiple_of(block * slots, slots), slots)
    expand(high_ref[here, :], low_ref[here, :], column_ref[0:1, here], square, out_ref, False)

    def more(index, carry):
        mixed = mix_slots([block], index, key_ref, table_ref, wide_ref, layer_mass, stack)
        expand(*mixed, square, out_ref, True)
        return carry

    lax.fori_loop(1, rounds, more, 0)


def soundings_kernel(
    got_ref, wide_ref, top_hbm, frac_hbm, lines_ref, mass_hbm,
    row_ref, courant_ref, shift_hbm, weight_hbm,
    key_ref, table_ref, high_ref, low_ref, column_ref, shift_ref, weight_ref,
    mass_ref, edge_out, rounds_ref, first_ref,
    forced, stack, square, row_scr, courant_scr, top_ref, frac_ref, mass_scr, sem,
):
    devices = got_ref.shape[0]
    levels = mass_ref.shape[0]
    n = devices * CAP
    row_count = top_ref.shape[0]
    width = 2 * LANES
    mass_in = pltpu.make_async_copy(mass_hbm, mass_scr, sem.at[6])
    late = [
        pltpu.make_async_copy(row_ref, row_scr, sem.at[0]),
        pltpu.make_async_copy(courant_ref.at[:, 0, :], courant_scr, sem.at[1]),
        pltpu.make_async_copy(shift_hbm, shift_ref, sem.at[2]),
        pltpu.make_async_copy(weight_hbm, weight_ref, sem.at[3]),
    ]
    soon = [
        pltpu.make_async_copy(top_hbm, top_ref, sem.at[4]),
        pltpu.make_async_copy(frac_hbm, frac_ref, sem.at[5]),
    ]
    for copy in [mass_in] + soon + late:
        copy.start()

    def arrive():
        mass_in.wait()
        mass_ref[...] = as_column(mass_scr[...])

    mix_edge(lines_ref, wide_ref, mass_ref, arrive, edge_out)
    layer_mass = jnp.concatenate([mass_ref[...]] * 2, axis=1)

    got = got_ref[...].astype(F32)
    table_ref[:levels, :n] = got[:, :CAP].reshape(n, levels).T.astype(BF16)
    table_ref[:levels, n:] = got[:, CAP : 2 * CAP].reshape(n, levels).T.astype(BF16)
    info = got[:, 2 * CAP :].reshape(devices * 8, LANES).astype(BF16)
    first = iota((devices, devices * 8), 1) == 8 * iota((devices, devices * 8), 0)
    info = dot(first.astype(F32).astype(BF16), info)
    kind = iota((devices, LANES), 1) // 32
    left = [jnp.where(kind == k, info, 0.0) for k in range(4)]
    chosen = iota((LANES, n), 0) % 32 == iota((LANES, n), 1) % CAP
    spread = dot(
        jnp.concatenate(left, axis=0).astype(BF16), chosen.astype(F32).astype(BF16)
    )
    mine = iota((devices, n), 0) == iota((devices, n), 1) // CAP
    lines = [
        jnp.sum(jnp.where(mine, spread[k * devices : (k + 1) * devices], 0.0), axis=0, keepdims=True)
        for k in range(4)
    ]
    own_row, own_col, east_row, east_col = [line.astype(I32) for line in lines]
    own_row, east_row = own_row - 1, east_row - 1
    east_row = jnp.where(east_col < EDGE, east_row, -1)
    row = jnp.concatenate([own_row, east_row], axis=1)
    place, most = find_places(row, row_count)
    rounds = (most.astype(I32) + (WINDOW - 1)) // WINDOW
    rounds_ref[0] = rounds
    key_ref[...] = as_column((row * PITCH + place).astype(F32)).astype(I32)
    column = jnp.concatenate([own_col, width + east_col], axis=1)
    cells = [[(column // EDGE).astype(F32), (column % EDGE).astype(F32)]]

    for copy in soon:
        copy.wait()
    packed_col = (east_row // 8) * EDGE + east_col
    parts = [
        (own_col, own_row, top_ref[...].astype(F32), frac_ref[...], row_count),
        (packed_col, east_row % 8, *edge_lines(lines_ref, levels), 8),
    ]
    for col, row, top, frac, count in parts:
        hot = (iota((width, n), 0) == col).astype(F32).astype(BF16)
        table = jnp.concatenate([top.astype(BF16)] + thirds(frac), axis=0)
        found = dot(table, hot)
        here = iota((count, n), 0) == row
        cells.append([
            jnp.sum(jnp.where(here, found[i * count : (i + 1) * count], 0.0), axis=0, keepdims=True)
            for i in range(4)
        ])
    lines = cells[0] + [jnp.concatenate(pair, axis=1) for pair in zip(cells[1], cells[2])]
    lines.append(jnp.zeros((CELL_LINES - len(lines), 2 * n), F32))
    table_ref[levels:] = jnp.concatenate(lines, axis=0).astype(BF16)

    high, low, column = mix_slots(
        list(range(row_count // 8)), 0, key_ref, table_ref, wide_ref, layer_mass, stack
    )
    high_ref[...] = high
    low_ref[...] = low
    column_ref[0:1] = column
    column_ref[1:] = jnp.zeros_like(column_ref[1:])
    square[...] = jnp.zeros_like(square)
    force_rows(
        0, rounds, high_ref, low_ref, column_ref,
        key_ref, table_ref, wide_ref, layer_mass, stack, square, forced,
    )
    edge = edge_out.reshape(width * 8, LANES)[pl.ds(0, EDGE, stride=8), :]
    for copy in late:
        copy.wait()
    value = jnp.concatenate([row_scr[...], edge], axis=0)
    value = value + forced.reshape(REACH * 8, LANES)[pl.ds(0, REACH, stride=8), :]
    shift = shift_ref[0:1, :]
    weight = weight_ref[0:1, :]
    for bit in (32, 16, 8, 4, 2, 1):
        value = jnp.where((shift & bit) != 0, value[bit:], value[:-bit])
    zonal = (1.0 - weight) * value[:width] + weight * value[1 : width + 1]
    for h in range(2):
        here = slice(h * LANES, (h + 1) * LANES)
        first_ref[:, here] = courant_scr[:, here] * zonal[here].T


def take_soundings(got, wide, cloud_top, conv_frac, edge_in, layer_mass, row, courant, shift, weight):
    levels = layer_mass.shape[1]
    row_count, col_count = cloud_top.shape
    n = got.shape[0] * CAP
    width = 2 * LANES
    in_place = pl.BlockSpec(memory_space=pl.ANY)
    return pl.pallas_call(
        soundings_kernel,
        in_specs=[IN_VMEM, IN_VMEM, in_place, in_place, IN_VMEM] + [in_place] * 5,
        out_specs=[IN_VMEM] * 9 + [pl.BlockSpec(memory_space=pltpu.SMEM), IN_VMEM],
        out_shape=[
            pltpu.VMEM((2 * n, LANES), I32),
            pltpu.VMEM((levels + CELL_LINES, 2 * n), BF16),
            pltpu.VMEM((row_count * WINDOW, levels), BF16),
            pltpu.VMEM((row_count * WINDOW, levels), BF16),
            pltpu.VMEM((8, row_count * WINDOW), I32),
            pltpu.VMEM((row_count, levels), I32),
            pltpu.VMEM((row_count, levels), F32),
            pltpu.VMEM((levels, LANES), F32),
            pltpu.VMEM((width, 8, levels), F32),
            jax.ShapeDtypeStruct((1,), I32),
            jax.ShapeDtypeStruct((levels, col_count), F32),
        ],
        scratch_shapes=[
            pltpu.VMEM((REACH, 8, levels), F32),
            pltpu.VMEM((row_count // 8, 8 * levels, 8 * WINDOW), BF16),
            pltpu.VMEM((2, 8 * WINDOW, 4 * levels), BF16),
            pltpu.VMEM((col_count, levels), F32),
            pltpu.VMEM((levels, col_count), F32),
            pltpu.VMEM((row_count, col_count), I32),
            pltpu.VMEM((row_count, col_count), F32),
            pltpu.VMEM((1, levels), F32),
            pltpu.SemaphoreType.DMA((7,)),
        ],
        compiler_params=params(24 + n // 64),
        name="take_soundings",
    )(
        got, wide, cloud_top, conv_frac, edge_in, layer_mass, row, courant, shift, weight
    )


def advect_kernel(
    key_ref, table_ref, high_ref, low_ref, column_ref, shift_ref, weight_ref, edge_ref, rounds_ref,
    wide_ref, field_ref, mass_ref, courant_ref,
    out_ref, last_ref,
    forced, coarse, done, stack, square, out_scr, prev, field_scr, courant_scr, sem, in_sem,
):
    step = pl.program_id(0)
    blocks = pl.num_programs(0) - 1
    block = blocks - 1 - step
    levels = mass_ref.shape[0]
    width = 2 * LANES

    def field_in(b):
        return pltpu.make_async_copy(field_ref.at[b], field_scr.at[b], in_sem.at[b, 0])

    def courant_in(b, h):
        source = courant_ref.at[:, pl.ds(pl.multiple_of(b * 8, 8), 8), pl.ds(h * LANES, LANES)]
        return pltpu.make_async_copy(source, courant_scr.at[b, h], in_sem.at[b, 1 + h])

    @pl.when(step == 0)
    def _():
        for b in reversed(range(out_scr.shape[0])):
            field_in(b).start()
            for h in range(2):
                courant_in(b, h).start()
        prev[...] = jnp.zeros_like(prev)
        square[...] = jnp.zeros_like(square)

    layer_mass = jnp.concatenate([mass_ref[...]] * 2, axis=1)
    lines = pl.ds(pl.multiple_of(8 * jnp.maximum(block, 0), 8), 8)
    shift = shift_ref[lines, :]
    weight = weight_ref[lines, :]
    chosen = {bit: (shift & bit) != 0 for bit in (32, 16, 8, 4, 2, 1)}

    def choose(tiles, bit, step):
        return [
            jnp.where(chosen[bit], new, old) for old, new in zip(tiles[:-step], tiles[step:])
        ]

    def by_eights(start):
        tiles = [field_scr[block, start + 8 * i] + forced[start + 8 * i] for i in range(32)]
        tiles += [
            edge_ref[EDGE * block + start + 8 * i] + forced[width + start + 8 * i] for i in range(8)
        ]
        for bit in (32, 16, 8):
            tiles = choose(tiles, bit, bit // 8)
        for i, tile in enumerate(tiles):
            coarse[start + 8 * i] = tile

    def by_ones(chunk, carry):
        start = chunk * 32
        tiles = [coarse[start + i] for i in range(40)]
        for bit in (4, 2, 1):
            tiles = choose(tiles, bit, bit)
        for i in range(32):
            done[start + i] = (1.0 - weight) * tiles[i] + weight * tiles[i + 1]
        return carry

    flat = done.reshape(width * 8, LANES)

    def meridional(beside, which=(0, 1)):
        later = [prev[0], prev[1]]
        for index in range(8):
            r = 7 - index
            for h in which:
                zonal = flat[pl.ds(h * LANES * 8 + r, LANES, stride=8), :].T
                courant = level_rows(courant_scr.at[block + 1, h], r)
                place = out_scr.at[block + 1, h].reshape(levels * 8, LANES)
                leaving = courant * zonal
                place[pl.ds(r, levels, stride=8), :] = (zonal - leaving) + later[h]
                later[h] = leaving
            beside(index)
        for h in which:
            prev[h] = later[h]

    def copies(b, which=(0, 1)):
        return [
            pltpu.make_async_copy(
                out_scr.at[b, h],
                out_ref.at[:, pl.ds(b * 8, 8), pl.ds(h * LANES, LANES)],
                sem.at[b, h],
            )
            for h in which
        ]

    def shift_only(index, carry):
        by_eights(index)
        return carry

    @pl.when(step < blocks)
    def _():
        force_rows(
            block, rounds_ref[0], high_ref, low_ref, column_ref,
            key_ref, table_ref, wide_ref, layer_mass, stack, square, forced,
        )
        field_in(block).wait()

    @pl.when(step > 0)
    def _():
        for h in range(2):
            courant_in(block + 1, h).wait()

    @pl.when(step == 0)
    def _():
        lax.fori_loop(0, 8, shift_only, 0)

    @pl.when((step > 0) & (step < blocks))
    def _():
        meridional(by_eights)

    @pl.when(step < blocks)
    def _():
        lax.fori_loop(0, width // 32, by_ones, 0)

    @pl.when(step == blocks)
    def _():
        for h in range(2):
            meridional(lambda index: None, (h,))
            copies(0, (h,))[0].start()

    @pl.when(step == 1)
    def _():
        for h in range(2):
            place = out_scr.at[blocks - 1, h].reshape(levels * 8, LANES)
            last_ref[:, h * LANES : (h + 1) * LANES] = place[pl.ds(7, levels, stride=8), :]

    for b in range(1, out_scr.shape[0]):

        @pl.when(block + 1 == b)
        def _():
            for copy in copies(b):
                copy.start()

    @pl.when(step == blocks)
    def _():
        for b in range(out_scr.shape[0]):
            for copy in copies(b):
                copy.wait()


def advect(soundings, edge_field, rounds, wide, field, layer_mass, courant):
    blocks, col_count, _, levels = field.shape
    n = soundings[0].shape[0] // 2
    in_place = pl.BlockSpec(memory_space=pl.ANY)
    return pl.pallas_call(
        advect_kernel,
        grid=(blocks + 1,),
        in_specs=[IN_VMEM] * 8
        + [pl.BlockSpec(memory_space=pltpu.SMEM), IN_VMEM, in_place, IN_VMEM, in_place],
        out_specs=[pl.BlockSpec(memory_space=pl.ANY), IN_VMEM],
        out_shape=[
            jax.ShapeDtypeStruct(courant.shape, F32),
            pltpu.VMEM((levels, col_count), F32),
        ],
        scratch_shapes=[
            pltpu.VMEM((REACH, 8, levels), F32),
            pltpu.VMEM((col_count + 8, 8, levels), F32),
            pltpu.VMEM((col_count, 8, levels), F32),
            pltpu.VMEM((1, 8 * levels, 8 * WINDOW), BF16),
            pltpu.VMEM((2, 8 * WINDOW, 4 * levels), BF16),
            pltpu.VMEM((blocks, 2, levels, 8, LANES), F32),
            pltpu.VMEM((2, levels, LANES), F32),
            pltpu.VMEM((blocks, col_count, 8, levels), F32),
            pltpu.VMEM((blocks, 2, levels, 8, LANES), F32),
            pltpu.SemaphoreType.DMA((blocks, 2)),
            pltpu.SemaphoreType.DMA((blocks, 3)),
        ],
        compiler_params=params(24 + n // 128),
        cost_estimate=pl.CostEstimate(
            flops=2 * levels * 8 * blocks * n * col_count,
            bytes_accessed=12 * levels * 8 * blocks * col_count,
            transcendentals=0,
        ),
        name="advect",
    )(
        *soundings, edge_field, rounds, wide, field, layer_mass, courant
    )


def close_kernel(last_ref, north_ref, _, out_ref, row, sem):
    row[...] = last_ref[...] + north_ref[...]
    copy = pltpu.make_async_copy(row, out_ref.at[:, out_ref.shape[1] - 1, :], sem)
    copy.start()
    copy.wait()


def close(out, last, north):
    in_place = pl.BlockSpec(memory_space=pl.ANY)
    return pl.pallas_call(
        close_kernel,
        in_specs=[IN_VMEM, IN_VMEM, in_place],
        out_specs=in_place,
        out_shape=jax.ShapeDtypeStruct(out.shape, F32),
        scratch_shapes=[pltpu.VMEM(last.shape, F32), pltpu.SemaphoreType.DMA],
        input_output_aliases={2: 0},
        compiler_params=params(4),
        name="close_last_row",
    )(last, north, out)


def shards(
    adjoint_field,
    mixing_inverse,
    cloud_top,
    conv_frac,
    thickness,
    zonal_shift,
    zonal_frac,
    merid_courant,
    obs_kernel,
    obs_depart,
    obs_dest,
    obs_col,
    obs_count,
):
    adjoint_field, mixing_inverse, cloud_top, conv_frac, merid_courant, obs_kernel = [
        in_hbm(array)
        for array in (
            adjoint_field, mixing_inverse, cloud_top, conv_frac, merid_courant, obs_kernel
        )
    ]
    levels, row_count, col_count = adjoint_field.shape
    lat_count, lon_count = lax.axis_size("lat"), lax.axis_size("lon")
    devices = lat_count * lon_count
    sent = prepare(devices, lon_count, obs_count, obs_dest, obs_col, obs_depart, obs_kernel)
    sent, field_after = lax.optimization_barrier((sent, adjoint_field))
    got = lax.all_to_all(
        sent.reshape(devices, SLOTS, levels), ("lat", "lon"), split_axis=0, concat_axis=0, tiled=True
    )
    westward = [((i + 1) % lon_count, i) for i in range(lon_count)]
    layer_mass = in_hbm(thickness.reshape(1, levels))
    field_after = in_hbm(field_after)
    edge = edge_columns(field_after, cloud_top, conv_frac).astype(jnp.float16)
    field, wide, row = mix(field_after, mixing_inverse, cloud_top, conv_frac, layer_mass)
    edge_in = in_vmem(lax.ppermute(edge, "lon", westward).astype(F32))
    shift, weight = in_hbm(zonal_shift.T), in_hbm(zonal_frac.T)
    *soundings, column, edge_field, rounds, first = take_soundings(
        got, wide, cloud_top, conv_frac, edge_in, layer_mass, row, merid_courant, shift, weight
    )
    southward = [(i + 1, i) for i in range(lat_count - 1)]
    north = lax.ppermute(first, "lat", southward)
    out, last = advect(
        [in_vmem(part) for part in soundings], in_vmem(edge_field), rounds, wide, field, in_vmem(column),
        merid_courant,
    )
    return close(out, last, north)


def solution(mesh):
    in_specs = (
        P(None, "lat", "lon"),
        P("lat", None, None),
        P("lat", "lon"),
        P("lat", "lon"),
        P(),
        P(None, "lat"),
        P(None, "lat"),
        P(None, "lat", "lon"),
        P(("lat", "lon"), None),
        P(("lat", "lon")),
        P(("lat", "lon")),
        P(("lat", "lon")),
        P(("lat", "lon")),
    )
    out_specs = P(None, "lat", "lon")
    return jax.shard_map(shards, mesh=mesh, in_specs=in_specs, out_specs=out_specs, check_vma=False)
```

```python
import functools

import jax
import jax.numpy as jnp
from jax import lax
from jax.experimental import pallas as pl
from jax.experimental.pallas import tpu as pltpu
from jax.sharding import PartitionSpec as P

F32, BF16, I32 = jnp.float32, jnp.bfloat16, jnp.int32
CAP = 16
SLOTS = 40
EDGE = 64
LANES = 128
GROUP = 32
EDGE_LINES = 4
SCALE = 4096.0
WINDOW = 32
REACH = 2 * LANES + EDGE
PITCH = 4096
CELL_LINES = 16
MIB = 1024 * 1024


IN_VMEM = pl.BlockSpec(memory_space=pltpu.VMEM)


def iota(shape, dim):
    return lax.broadcasted_iota(I32, shape, dim)


def params(mib):
    return pltpu.CompilerParams(vmem_limit_bytes=mib * MIB)


def in_hbm(array):
    return pltpu.with_memory_space_constraint(array, pltpu.HBM)


def in_vmem(array):
    return pltpu.with_memory_space_constraint(array, pltpu.VMEM)


def dot(left, right):
    return jnp.dot(left, right, preferred_element_type=F32)


def dot_nt(left, right):
    return lax.dot_general(left, right, (((1,), (1,)), ((), ())), preferred_element_type=F32)


def halves(value):
    high = value.astype(BF16)
    return high, (value - high.astype(F32)).astype(BF16)


def thirds(value):
    high = value.astype(BF16)
    rest = value - high.astype(F32)
    mid = rest.astype(BF16)
    return [high, mid, (rest - mid.astype(F32)).astype(BF16)]


def as_column(line):
    return jnp.broadcast_to(line, (LANES, line.shape[1])).T


def as_wide_column(line):
    column = as_column(line)
    return jnp.concatenate([column, column], axis=1)


def convect(mixed, top, frac, layer_mass):
    inside = iota(mixed.shape, 0) < top
    total = jnp.sum(jnp.where(inside, mixed, 0.0), axis=0, keepdims=True)
    mass = jnp.sum(jnp.where(inside, layer_mass, 0.0), axis=0, keepdims=True)
    mean = total / jnp.where(mass > 0.0, mass, 1.0)
    return mixed + jnp.where(inside, frac * (layer_mass * mean - mixed), 0.0)


def prep_kernel(lon_count, count_ref, dest_ref, col_ref, depart_ref, obs_ref, out_ref):
    n, levels = obs_ref.shape
    lane = iota((1, n), 1)
    live = lane < count_ref[0]
    first = pl.program_id(0) * GROUP
    dest = jnp.where(live, dest_ref[...] - first, -GROUP * SLOTS)
    lon = (dest + first) % lon_count
    west = jnp.where(lon == 0, dest + (lon_count - 1), dest - 1)
    cell = col_ref[...]
    cell_row = (cell // 256 + 1).astype(F32)
    cell_col = (cell % 256).astype(F32)
    contribution = (obs_ref[...].astype(F32) * as_column(depart_ref[...])).astype(BF16)
    local = iota((GROUP, n), 0)
    hit = dest == local
    before = jnp.sum((live & (dest < local)).astype(I32), axis=1, keepdims=True)
    place = jnp.sum(jnp.where(hit, lane - before, 0), axis=0, keepdims=True)
    parts, left = [], []
    for owner in (dest, west):
        pick = iota((GROUP * CAP, n), 0) == owner * CAP + place
        found = dot(pick.astype(F32).astype(BF16), contribution)
        parts.append(found.reshape(GROUP, CAP, levels))
        hit = owner == local
        left += [jnp.where(hit, cell_row, 0.0), jnp.where(hit, cell_col, 0.0)]
    spot = (iota((LANES, n), 0) % 32 == place).astype(F32).astype(BF16)
    every = dot_nt(jnp.concatenate(left, axis=0).astype(BF16), spot)
    kind = iota((GROUP, LANES), 1) // 32
    cells = [jnp.where(kind == k, every[k * GROUP : (k + 1) * GROUP], 0.0) for k in range(4)]
    cells = ((cells[0] + cells[1]) + (cells[2] + cells[3])).astype(BF16)
    spread = iota((GROUP * 8, GROUP), 0) == 8 * iota((GROUP * 8, GROUP), 1)
    parts.append(dot(spread.astype(F32).astype(BF16), cells).reshape(GROUP, 8, levels))
    whole = jnp.concatenate(parts, axis=1).reshape(GROUP * SLOTS, levels)
    out_ref[...] = whole.astype(BF16)


def prepare(devices, lon_count, obs_count, obs_dest, obs_col, obs_depart, obs_kernel):
    n, levels = obs_kernel.shape
    steps = devices // GROUP
    whole = lambda shape: pl.BlockSpec(shape, lambda g: (0, 0))
    return pl.pallas_call(
        functools.partial(prep_kernel, lon_count),
        grid=(steps,),
        in_specs=[
            pl.BlockSpec(memory_space=pltpu.SMEM),
            whole((1, n)),
            whole((1, n)),
            whole((1, n)),
            whole((n, levels)),
        ],
        out_specs=pl.BlockSpec((GROUP * SLOTS, levels), lambda g: (g, 0)),
        out_shape=pltpu.VMEM((devices * SLOTS, levels), BF16),
        compiler_params=params(16 + devices // 4),
        name="soundings_out",
    )(
        obs_count,
        in_hbm(obs_dest.reshape(1, n)),
        in_hbm(obs_col.reshape(1, n)),
        in_hbm(obs_depart.reshape(1, n)),
        obs_kernel,
    )


def level_rows(ref, row, count=None):
    levels = ref.shape[0]
    count = levels if count is None else count
    return ref.reshape(levels * 8, LANES)[pl.ds(row, count, stride=8), :]


def pack_edge(block):
    parts = [block[:, 8 * q : 8 * q + 8, :] for q in range(4)]
    low = iota(parts[0].shape, 2) < EDGE
    return [jnp.where(low, parts[2 * h], pltpu.roll(parts[2 * h + 1], EDGE, 2)) for h in range(2)]


EDGE_STEPS = 4


def edge_kernel(field_hbm, top_hbm, frac_hbm, out_ref, field, top, frac, sem):
    count = field.shape[1]
    here = [pl.ds(i * count, count) for i in range(EDGE_STEPS)]
    near = pl.ds(0, LANES)
    copies = [
        pltpu.make_async_copy(field_hbm.at[here[i], :, near], field.at[i], sem.at[i])
        for i in range(EDGE_STEPS)
    ]
    copies.append(pltpu.make_async_copy(top_hbm.at[:, near], top, sem.at[EDGE_STEPS]))
    copies.append(pltpu.make_async_copy(frac_hbm.at[:, near], frac, sem.at[EDGE_STEPS + 1]))
    for copy in copies:
        copy.start()
    for i in range(EDGE_STEPS):
        copies[i].wait()
        for h, part in enumerate(pack_edge(field[i])):
            out_ref[h, here[i]] = part * SCALE
    for copy in copies[EDGE_STEPS:]:
        copy.wait()
    pieces = thirds(frac[...])
    lines = [top[...].astype(F32)] + [piece.astype(F32) for piece in pieces]
    lines[2:] = [line * SCALE for line in lines[2:]]
    first = out_ref.shape[1] - EDGE_LINES
    for i, line in enumerate(lines):
        for h, part in enumerate(pack_edge(line[None])):
            out_ref[h, first + i : first + i + 1] = part


def edge_columns(adjoint_field, cloud_top, conv_frac):
    levels, row_count, _ = adjoint_field.shape
    in_place = pl.BlockSpec(memory_space=pl.ANY)
    return pl.pallas_call(
        edge_kernel,
        in_specs=[in_place] * 3,
        out_specs=IN_VMEM,
        out_shape=pltpu.VMEM((2, levels + EDGE_LINES, 8, LANES), F32),
        scratch_shapes=[
            pltpu.VMEM((EDGE_STEPS, levels // EDGE_STEPS, row_count, LANES), F32),
            pltpu.VMEM((row_count, LANES), I32),
            pltpu.VMEM((row_count, LANES), F32),
            pltpu.SemaphoreType.DMA((EDGE_STEPS + 2,)),
        ],
        compiler_params=params(16),
        cost_estimate=pl.CostEstimate(
            flops=levels * levels * 4 * row_count * LANES,
            bytes_accessed=12 * levels * row_count * LANES,
            transcendentals=0,
        ),
        name="edge_columns",
    )(adjoint_field, cloud_top, conv_frac)


def put_columns(ref, row, value):
    count = ref.shape[0]
    flat = ref.reshape(count * 8, LANES)
    for h in range(count // LANES):
        part = value[:, h * LANES : (h + 1) * LANES].T
        flat[pl.ds(h * LANES * 8 + row, LANES, stride=8), :] = part


def mix_rows(field_refs, mixing_ref, top, frac, layer_mass, block, out_ref, wide_ref):
    levels = mixing_ref.shape[1]
    for row in range(8):
        value = jnp.concatenate([level_rows(ref, row) for ref in field_refs], axis=1)
        high, low = halves(value)
        mix_high, mix_low = halves(mixing_ref[row])
        here = pl.ds(pl.multiple_of((8 * block + row) * levels, levels), levels)
        wide_ref[:levels, here] = mix_high
        wide_ref[levels:, here] = mix_low
        four = jnp.concatenate([mix_high, mix_low], axis=0)
        both = dot(jnp.concatenate([four, four], axis=1), jnp.concatenate([high, low], axis=0))
        mixed = both[:levels] + both[levels:]
        done = convect(mixed, top[row : row + 1, :], frac[row : row + 1, :], layer_mass)
        put_columns(out_ref.at[0], row, done)


def mix_kernel(
    west_ref, east_ref, mixing_ref, top_ref, frac_ref, mass_ref, out_ref, wide_ref, row_ref
):
    layer_mass = as_wide_column(mass_ref[...])
    block = pl.program_id(0)
    mix_rows(
        (west_ref, east_ref), mixing_ref, top_ref[...], frac_ref[...], layer_mass, block,
        out_ref, wide_ref,
    )

    @pl.when(block == 0)
    def _():
        flat = out_ref.at[0].reshape(row_ref.shape[0] * 8, LANES)
        row_ref[...] = flat[pl.ds(0, row_ref.shape[0], stride=8), :]


def mix(adjoint_field, mixing_inverse, cloud_top, conv_frac, layer_mass):
    levels, row_count, col_count = adjoint_field.shape
    blocks = row_count // 8
    half = lambda h: pl.BlockSpec((levels, 8, LANES), lambda b: (0, b, h))
    flat = pl.BlockSpec((8, col_count), lambda b: (b, 0))
    field, wide, row = pl.pallas_call(
        mix_kernel,
        grid=(blocks,),
        in_specs=[
            half(0),
            half(1),
            pl.BlockSpec((8, levels, levels), lambda b: (b, 0, 0)),
            flat,
            flat,
            pl.BlockSpec((1, levels), lambda b: (0, 0)),
        ],
        out_specs=[
            pl.BlockSpec((1, col_count, 8, levels), lambda b: (b, 0, 0, 0)),
            IN_VMEM,
            pl.BlockSpec((col_count, levels), lambda b: (0, 0)),
        ],
        out_shape=[
            pltpu.HBM((blocks, col_count, 8, levels), F32),
            pltpu.VMEM((2 * levels, row_count * levels), BF16),
            pltpu.HBM((col_count, levels), F32),
        ],
        compiler_params=params(20),
        cost_estimate=pl.CostEstimate(
            flops=2 * levels * levels * 4 * row_count * col_count,
            bytes_accessed=12 * levels * row_count * col_count,
            transcendentals=0,
        ),
        name="mix_own",
    )(adjoint_field, adjoint_field, mixing_inverse, cloud_top, conv_frac, layer_mass)
    return in_hbm(field), in_vmem(wide), in_hbm(row)


def mix_edge(edge_ref, wide_ref, mass_ref, arrive, out_ref):
    levels = mass_ref.shape[0]
    group = iota((levels, 2 * LANES), 1) // EDGE
    top, frac = edge_lines(edge_ref, levels)
    for row in range(8):
        value = jnp.concatenate([level_rows(edge_ref.at[h], row, levels) for h in range(2)], axis=1)
        value = value * (1.0 / SCALE)
        mix_high, mix_low, highs, lows = [], [], [], []
        for q in range(4):
            cols = slice((8 * q + row) * levels, (8 * q + row + 1) * levels)
            mix_high.append(wide_ref[:levels, cols])
            mix_low.append(wide_ref[levels:, cols])
            high, low = halves(jnp.where(group == q, value, 0.0))
            highs.append(high)
            lows.append(low)
        highs = jnp.concatenate(highs, axis=0)
        mixed = dot(
            jnp.concatenate(mix_high * 2, axis=1),
            jnp.concatenate([highs] + lows, axis=0),
        ) + dot(jnp.concatenate(mix_low, axis=1), highs)
        if row == 0:
            arrive()
            layer_mass = jnp.concatenate([mass_ref[...]] * 2, axis=1)
        done = convect(mixed, top[row : row + 1].astype(I32), frac[row : row + 1], layer_mass)
        put_columns(out_ref, row, done)


def edge_lines(ref, levels):
    top, high, mid, low = [
        jnp.concatenate([ref[0, levels + i], ref[1, levels + i]], axis=1)
        for i in range(EDGE_LINES)
    ]
    return top, high + (mid + low) * (1.0 / SCALE)


def find_places(row, row_count):
    count = row.shape[1]
    upto = (iota((LANES, LANES), 0) <= iota((LANES, LANES), 1)).astype(F32).astype(BF16)
    before = jnp.zeros((row_count, 1), F32)
    places = []
    for start in range(0, count, LANES):
        mine = iota((row_count, LANES), 0) == row[:, start : start + LANES]
        running = dot(mine.astype(F32).astype(BF16), upto)
        place = jnp.sum(jnp.where(mine, running + before, 0.0), axis=0, keepdims=True) - 1.0
        places.append(place.astype(I32))
        before = before + running[:, LANES - 1 :]
    return jnp.concatenate(places, axis=1), jnp.max(before)


def mix_slots(blocks, index, key_ref, table_ref, wide_ref, layer_mass, stack):
    levels = layer_mass.shape[0]
    slots = 8 * WINDOW
    lane = iota((1, slots), 1)
    target = [(8 * b + lane // WINDOW) * PITCH + index * WINDOW + lane % WINDOW for b in blocks]
    target = jnp.concatenate(target, axis=1)
    pick = [
        (key_ref[...] == target[:, start : start + LANES]).astype(F32).astype(BF16)
        for start in range(0, target.shape[1], LANES)
    ]
    found = dot(table_ref[...], jnp.concatenate(pick, axis=1))
    split_high, split_low, top, high, mid, low = [
        found[levels + i : levels + i + 1] for i in range(6)
    ]
    column = (split_high * EDGE + split_low).astype(I32)
    parts = []
    for i, b in enumerate(blocks):
        value = found[:levels, i * slots : (i + 1) * slots].astype(BF16)
        for r in range(8):
            mine = (lane // WINDOW == r).astype(F32).astype(BF16)
            stack[i, r * levels : (r + 1) * levels, :] = value * mine
        start = pl.multiple_of(8 * b * levels, 8 * levels)
        both = dot(wide_ref[:, pl.ds(start, 8 * levels)], stack[i])
        parts.append(both[:levels] + both[levels:])
    mass = jnp.concatenate([layer_mass] * len(blocks), axis=1)
    done = convect(
        jnp.concatenate(parts, axis=1), top.astype(I32), (high + mid) + low, mass
    )
    turned = [done[:, start : start + LANES].T for start in range(0, done.shape[1], LANES)]
    high, low = halves(jnp.concatenate(turned, axis=0))
    return high, low, column


def expand(high, low, column, square, out_ref, add):
    levels = high.shape[1]
    flat = out_ref.reshape(REACH * 8, LANES)
    hot = (iota((REACH, 8 * WINDOW), 0) == column).astype(F32).astype(BF16)
    for group in range(2):
        for r in range(4):
            source = slice((4 * group + r) * WINDOW, (4 * group + r + 1) * WINDOW)
            target = slice(r * levels, (r + 1) * levels)
            square[group, r * WINDOW : (r + 1) * WINDOW, target] = high[source]
            square[group, (4 + r) * WINDOW : (5 + r) * WINDOW, target] = low[source]
        left = hot[:, 4 * group * WINDOW : 4 * (group + 1) * WINDOW]
        forced = dot(jnp.concatenate([left, left], axis=1), square[group])
        for r in range(4):
            rows = pl.ds(4 * group + r, REACH, stride=8)
            part = forced[:, r * levels : (r + 1) * levels]
            flat[rows, :] = flat[rows, :] + part if add else part


def force_rows(
    block, rounds, high_ref, low_ref, column_ref,
    key_ref, table_ref, wide_ref, layer_mass, stack, square, out_ref,
):
    slots = 8 * WINDOW
    here = pl.ds(pl.multiple_of(block * slots, slots), slots)
    expand(high_ref[here, :], low_ref[here, :], column_ref[0:1, here], square, out_ref, False)

    def more(index, carry):
        mixed = mix_slots([block], index, key_ref, table_ref, wide_ref, layer_mass, stack)
        expand(*mixed, square, out_ref, True)
        return carry

    lax.fori_loop(1, rounds, more, 0)


def soundings_kernel(
    got_ref, wide_ref, top_hbm, frac_hbm, lines_ref, mass_hbm,
    row_ref, courant_ref, shift_hbm, weight_hbm,
    key_ref, table_ref, high_ref, low_ref, column_ref, shift_ref, weight_ref,
    mass_ref, edge_out, rounds_ref, first_ref,
    forced, stack, square, row_scr, courant_scr, top_ref, frac_ref, mass_scr, sem,
):
    devices = got_ref.shape[0]
    levels = mass_ref.shape[0]
    n = devices * CAP
    row_count = top_ref.shape[0]
    width = 2 * LANES
    mass_in = pltpu.make_async_copy(mass_hbm, mass_scr, sem.at[6])
    late = [
        pltpu.make_async_copy(row_ref, row_scr, sem.at[0]),
        pltpu.make_async_copy(courant_ref.at[:, 0, :], courant_scr, sem.at[1]),
        pltpu.make_async_copy(shift_hbm, shift_ref, sem.at[2]),
        pltpu.make_async_copy(weight_hbm, weight_ref, sem.at[3]),
    ]
    soon = [
        pltpu.make_async_copy(top_hbm, top_ref, sem.at[4]),
        pltpu.make_async_copy(frac_hbm, frac_ref, sem.at[5]),
    ]
    for copy in [mass_in] + soon + late:
        copy.start()

    def arrive():
        mass_in.wait()
        mass_ref[...] = as_column(mass_scr[...])


    got = got_ref[...].astype(F32)
    table_ref[:levels, :n] = got[:, :CAP].reshape(n, levels).T.astype(BF16)
    table_ref[:levels, n:] = got[:, CAP : 2 * CAP].reshape(n, levels).T.astype(BF16)
    info = got[:, 2 * CAP :].reshape(devices * 8, LANES).astype(BF16)
    first = iota((devices, devices * 8), 1) == 8 * iota((devices, devices * 8), 0)
    info = dot(first.astype(F32).astype(BF16), info)
    kind = iota((devices, LANES), 1) // 32
    left = [jnp.where(kind == k, info, 0.0) for k in range(4)]
    chosen = iota((LANES, n), 0) % 32 == iota((LANES, n), 1) % CAP
    spread = dot(
        jnp.concatenate(left, axis=0).astype(BF16), chosen.astype(F32).astype(BF16)
    )
    mine = iota((devices, n), 0) == iota((devices, n), 1) // CAP
    lines = [
        jnp.sum(jnp.where(mine, spread[k * devices : (k + 1) * devices], 0.0), axis=0, keepdims=True)
        for k in range(4)
    ]
    own_row, own_col, east_row, east_col = [line.astype(I32) for line in lines]
    own_row, east_row = own_row - 1, east_row - 1
    east_row = jnp.where(east_col < EDGE, east_row, -1)
    row = jnp.concatenate([own_row, east_row], axis=1)
    place, most = find_places(row, row_count)
    rounds = (most.astype(I32) + (WINDOW - 1)) // WINDOW
    rounds_ref[0] = rounds
    key_ref[...] = as_column((row * PITCH + place).astype(F32)).astype(I32)
    column = jnp.concatenate([own_col, width + east_col], axis=1)
    cells = [[(column // EDGE).astype(F32), (column % EDGE).astype(F32)]]

    mix_edge(lines_ref, wide_ref, mass_ref, arrive, edge_out)
    layer_mass = jnp.concatenate([mass_ref[...]] * 2, axis=1)
    for copy in soon:
        copy.wait()
    packed_col = (east_row // 8) * EDGE + east_col
    parts = [
        (own_col, own_row, top_ref[...].astype(F32), frac_ref[...], row_count),
        (packed_col, east_row % 8, *edge_lines(lines_ref, levels), 8),
    ]
    for col, row, top, frac, count in parts:
        hot = (iota((width, n), 0) == col).astype(F32).astype(BF16)
        table = jnp.concatenate([top.astype(BF16)] + thirds(frac), axis=0)
        found = dot(table, hot)
        here = iota((count, n), 0) == row
        cells.append([
            jnp.sum(jnp.where(here, found[i * count : (i + 1) * count], 0.0), axis=0, keepdims=True)
            for i in range(4)
        ])
    lines = cells[0] + [jnp.concatenate(pair, axis=1) for pair in zip(cells[1], cells[2])]
    lines.append(jnp.zeros((CELL_LINES - len(lines), 2 * n), F32))
    table_ref[levels:] = jnp.concatenate(lines, axis=0).astype(BF16)

    high, low, column = mix_slots(
        list(range(row_count // 8)), 0, key_ref, table_ref, wide_ref, layer_mass, stack
    )
    high_ref[...] = high
    low_ref[...] = low
    column_ref[0:1] = column
    column_ref[1:] = jnp.zeros_like(column_ref[1:])
    square[...] = jnp.zeros_like(square)
    force_rows(
        0, rounds, high_ref, low_ref, column_ref,
        key_ref, table_ref, wide_ref, layer_mass, stack, square, forced,
    )
    edge = edge_out.reshape(width * 8, LANES)[pl.ds(0, EDGE, stride=8), :]
    for copy in late:
        copy.wait()
    value = jnp.concatenate([row_scr[...], edge], axis=0)
    value = value + forced.reshape(REACH * 8, LANES)[pl.ds(0, REACH, stride=8), :]
    shift = shift_ref[0:1, :]
    weight = weight_ref[0:1, :]
    for bit in (32, 16, 8, 4, 2, 1):
        value = jnp.where((shift & bit) != 0, value[bit:], value[:-bit])
    zonal = (1.0 - weight) * value[:width] + weight * value[1 : width + 1]
    for h in range(2):
        here = slice(h * LANES, (h + 1) * LANES)
        first_ref[:, here] = courant_scr[:, here] * zonal[here].T


def take_soundings(got, wide, cloud_top, conv_frac, edge_in, layer_mass, row, courant, shift, weight):
    levels = layer_mass.shape[1]
    row_count, col_count = cloud_top.shape
    n = got.shape[0] * CAP
    width = 2 * LANES
    in_place = pl.BlockSpec(memory_space=pl.ANY)
    return pl.pallas_call(
        soundings_kernel,
        in_specs=[IN_VMEM, IN_VMEM, in_place, in_place, IN_VMEM] + [in_place] * 5,
        out_specs=[IN_VMEM] * 9 + [pl.BlockSpec(memory_space=pltpu.SMEM), IN_VMEM],
        out_shape=[
            pltpu.VMEM((2 * n, LANES), I32),
            pltpu.VMEM((levels + CELL_LINES, 2 * n), BF16),
            pltpu.VMEM((row_count * WINDOW, levels), BF16),
            pltpu.VMEM((row_count * WINDOW, levels), BF16),
            pltpu.VMEM((8, row_count * WINDOW), I32),
            pltpu.VMEM((row_count, levels), I32),
            pltpu.VMEM((row_count, levels), F32),
            pltpu.VMEM((levels, LANES), F32),
            pltpu.VMEM((width, 8, levels), F32),
            jax.ShapeDtypeStruct((1,), I32),
            jax.ShapeDtypeStruct((levels, col_count), F32),
        ],
        scratch_shapes=[
            pltpu.VMEM((REACH, 8, levels), F32),
            pltpu.VMEM((row_count // 8, 8 * levels, 8 * WINDOW), BF16),
            pltpu.VMEM((2, 8 * WINDOW, 4 * levels), BF16),
            pltpu.VMEM((col_count, levels), F32),
            pltpu.VMEM((levels, col_count), F32),
            pltpu.VMEM((row_count, col_count), I32),
            pltpu.VMEM((row_count, col_count), F32),
            pltpu.VMEM((1, levels), F32),
            pltpu.SemaphoreType.DMA((7,)),
        ],
        compiler_params=params(24 + n // 64),
        name="take_soundings",
    )(
        got, wide, cloud_top, conv_frac, edge_in, layer_mass, row, courant, shift, weight
    )


def advect_kernel(
    key_ref, table_ref, high_ref, low_ref, column_ref, shift_ref, weight_ref, edge_ref, rounds_ref,
    wide_ref, field_ref, mass_ref, courant_ref,
    out_ref, last_ref,
    forced, coarse, done, stack, square, out_scr, prev, field_scr, courant_scr, sem, in_sem,
):
    step = pl.program_id(0)
    blocks = pl.num_programs(0) - 1
    block = blocks - 1 - step
    levels = mass_ref.shape[0]
    width = 2 * LANES

    def field_in(b):
        return pltpu.make_async_copy(field_ref.at[b], field_scr.at[b], in_sem.at[b, 0])

    def courant_in(b, h):
        source = courant_ref.at[:, pl.ds(pl.multiple_of(b * 8, 8), 8), pl.ds(h * LANES, LANES)]
        return pltpu.make_async_copy(source, courant_scr.at[b, h], in_sem.at[b, 1 + h])

    @pl.when(step == 0)
    def _():
        for b in reversed(range(out_scr.shape[0])):
            field_in(b).start()
            for h in range(2):
                courant_in(b, h).start()
        prev[...] = jnp.zeros_like(prev)
        square[...] = jnp.zeros_like(square)

    layer_mass = jnp.concatenate([mass_ref[...]] * 2, axis=1)
    lines = pl.ds(pl.multiple_of(8 * jnp.maximum(block, 0), 8), 8)
    shift = shift_ref[lines, :]
    weight = weight_ref[lines, :]
    chosen = {bit: (shift & bit) != 0 for bit in (32, 16, 8, 4, 2, 1)}

    def choose(tiles, bit, step):
        return [
            jnp.where(chosen[bit], new, old) for old, new in zip(tiles[:-step], tiles[step:])
        ]

    def by_eights(start):
        tiles = [field_scr[block, start + 8 * i] + forced[start + 8 * i] for i in range(32)]
        tiles += [
            edge_ref[EDGE * block + start + 8 * i] + forced[width + start + 8 * i] for i in range(8)
        ]
        for bit in (32, 16, 8):
            tiles = choose(tiles, bit, bit // 8)
        for i, tile in enumerate(tiles):
            coarse[start + 8 * i] = tile

    def by_ones(chunk, carry):
        start = chunk * 32
        tiles = [coarse[start + i] for i in range(40)]
        for bit in (4, 2, 1):
            tiles = choose(tiles, bit, bit)
        for i in range(32):
            done[start + i] = (1.0 - weight) * tiles[i] + weight * tiles[i + 1]
        return carry

    flat = done.reshape(width * 8, LANES)

    def meridional(beside, which=(0, 1)):
        later = [prev[0], prev[1]]
        for index in range(8):
            r = 7 - index
            for h in which:
                zonal = flat[pl.ds(h * LANES * 8 + r, LANES, stride=8), :].T
                courant = level_rows(courant_scr.at[block + 1, h], r)
                place = out_scr.at[block + 1, h].reshape(levels * 8, LANES)
                leaving = courant * zonal
                place[pl.ds(r, levels, stride=8), :] = (zonal - leaving) + later[h]
                later[h] = leaving
            beside(index)
        for h in which:
            prev[h] = later[h]

    def copies(b, which=(0, 1)):
        return [
            pltpu.make_async_copy(
                out_scr.at[b, h],
                out_ref.at[:, pl.ds(b * 8, 8), pl.ds(h * LANES, LANES)],
                sem.at[b, h],
            )
            for h in which
        ]

    def shift_only(index, carry):
        by_eights(index)
        return carry

    @pl.when(step < blocks)
    def _():
        force_rows(
            block, rounds_ref[0], high_ref, low_ref, column_ref,
            key_ref, table_ref, wide_ref, layer_mass, stack, square, forced,
        )
        field_in(block).wait()

    @pl.when(step > 0)
    def _():
        for h in range(2):
            courant_in(block + 1, h).wait()

    @pl.when(step == 0)
    def _():
        lax.fori_loop(0, 8, shift_only, 0)

    @pl.when((step > 0) & (step < blocks))
    def _():
        meridional(by_eights)

    @pl.when(step < blocks)
    def _():
        lax.fori_loop(0, width // 32, by_ones, 0)

    @pl.when(step == blocks)
    def _():
        for h in range(2):
            meridional(lambda index: None, (h,))
            copies(0, (h,))[0].start()

    @pl.when(step == 1)
    def _():
        for h in range(2):
            place = out_scr.at[blocks - 1, h].reshape(levels * 8, LANES)
            last_ref[:, h * LANES : (h + 1) * LANES] = place[pl.ds(7, levels, stride=8), :]

    for b in range(1, out_scr.shape[0]):

        @pl.when(block + 1 == b)
        def _():
            for copy in copies(b):
                copy.start()

    @pl.when(step == blocks)
    def _():
        for b in range(out_scr.shape[0]):
            for copy in copies(b):
                copy.wait()


def advect(soundings, edge_field, rounds, wide, field, layer_mass, courant):
    blocks, col_count, _, levels = field.shape
    n = soundings[0].shape[0] // 2
    in_place = pl.BlockSpec(memory_space=pl.ANY)
    return pl.pallas_call(
        advect_kernel,
        grid=(blocks + 1,),
        in_specs=[IN_VMEM] * 8
        + [pl.BlockSpec(memory_space=pltpu.SMEM), IN_VMEM, in_place, IN_VMEM, in_place],
        out_specs=[pl.BlockSpec(memory_space=pl.ANY), IN_VMEM],
        out_shape=[
            jax.ShapeDtypeStruct(courant.shape, F32),
            pltpu.VMEM((levels, col_count), F32),
        ],
        scratch_shapes=[
            pltpu.VMEM((REACH, 8, levels), F32),
            pltpu.VMEM((col_count + 8, 8, levels), F32),
            pltpu.VMEM((col_count, 8, levels), F32),
            pltpu.VMEM((1, 8 * levels, 8 * WINDOW), BF16),
            pltpu.VMEM((2, 8 * WINDOW, 4 * levels), BF16),
            pltpu.VMEM((blocks, 2, levels, 8, LANES), F32),
            pltpu.VMEM((2, levels, LANES), F32),
            pltpu.VMEM((blocks, col_count, 8, levels), F32),
            pltpu.VMEM((blocks, 2, levels, 8, LANES), F32),
            pltpu.SemaphoreType.DMA((blocks, 2)),
            pltpu.SemaphoreType.DMA((blocks, 3)),
        ],
        compiler_params=params(24 + n // 128),
        cost_estimate=pl.CostEstimate(
            flops=2 * levels * 8 * blocks * n * col_count,
            bytes_accessed=12 * levels * 8 * blocks * col_count,
            transcendentals=0,
        ),
        name="advect",
    )(
        *soundings, edge_field, rounds, wide, field, layer_mass, courant
    )


def close_kernel(last_ref, north_ref, _, out_ref, row, sem):
    row[...] = last_ref[...] + north_ref[...]
    copy = pltpu.make_async_copy(row, out_ref.at[:, out_ref.shape[1] - 1, :], sem)
    copy.start()
    copy.wait()


def close(out, last, north):
    in_place = pl.BlockSpec(memory_space=pl.ANY)
    return pl.pallas_call(
        close_kernel,
        in_specs=[IN_VMEM, IN_VMEM, in_place],
        out_specs=in_place,
        out_shape=jax.ShapeDtypeStruct(out.shape, F32),
        scratch_shapes=[pltpu.VMEM(last.shape, F32), pltpu.SemaphoreType.DMA],
        input_output_aliases={2: 0},
        compiler_params=params(4),
        name="close_last_row",
    )(last, north, out)


def shards(
    adjoint_field,
    mixing_inverse,
    cloud_top,
    conv_frac,
    thickness,
    zonal_shift,
    zonal_frac,
    merid_courant,
    obs_kernel,
    obs_depart,
    obs_dest,
    obs_col,
    obs_count,
):
    adjoint_field, mixing_inverse, cloud_top, conv_frac, merid_courant, obs_kernel = [
        in_hbm(array)
        for array in (
            adjoint_field, mixing_inverse, cloud_top, conv_frac, merid_courant, obs_kernel
        )
    ]
    levels, row_count, col_count = adjoint_field.shape
    lat_count, lon_count = lax.axis_size("lat"), lax.axis_size("lon")
    devices = lat_count * lon_count
    sent = prepare(devices, lon_count, obs_count, obs_dest, obs_col, obs_depart, obs_kernel)
    sent, field_after = lax.optimization_barrier((sent, adjoint_field))
    got = lax.all_to_all(
        sent.reshape(devices, SLOTS, levels), ("lat", "lon"), split_axis=0, concat_axis=0, tiled=True
    )
    westward = [((i + 1) % lon_count, i) for i in range(lon_count)]
    layer_mass = in_hbm(thickness.reshape(1, levels))
    field_after = in_hbm(field_after)
    edge = edge_columns(field_after, cloud_top, conv_frac).astype(jnp.float16)
    field, wide, row = mix(field_after, mixing_inverse, cloud_top, conv_frac, layer_mass)
    edge_in = in_vmem(lax.ppermute(edge, "lon", westward).astype(F32))
    shift, weight = in_hbm(zonal_shift.T), in_hbm(zonal_frac.T)
    *soundings, column, edge_field, rounds, first = take_soundings(
        got, wide, cloud_top, conv_frac, edge_in, layer_mass, row, merid_courant, shift, weight
    )
    southward = [(i + 1, i) for i in range(lat_count - 1)]
    north = lax.ppermute(first, "lat", southward)
    out, last = advect(
        [in_vmem(part) for part in soundings], in_vmem(edge_field), rounds, wide, field, in_vmem(column),
        merid_courant,
    )
    return close(out, last, north)


def solution(mesh):
    in_specs = (
        P(None, "lat", "lon"),
        P("lat", None, None),
        P("lat", "lon"),
        P("lat", "lon"),
        P(),
        P(None, "lat"),
        P(None, "lat"),
        P(None, "lat", "lon"),
        P(("lat", "lon"), None),
        P(("lat", "lon")),
        P(("lat", "lon")),
        P(("lat", "lon")),
        P(("lat", "lon")),
    )
    out_specs = P(None, "lat", "lon")
    return jax.shard_map(shards, mesh=mesh, in_specs=in_specs, out_specs=out_specs, check_vma=False)
```

```python
import functools

import jax
import jax.numpy as jnp
from jax import lax
from jax.experimental import pallas as pl
from jax.experimental.pallas import tpu as pltpu
from jax.sharding import PartitionSpec as P

F32, BF16, I32 = jnp.float32, jnp.bfloat16, jnp.int32
CAP = 16
SLOTS = 40
EDGE = 64
LANES = 128
GROUP = 32
EDGE_LINES = 4
SCALE = 4096.0
WINDOW = 32
REACH = 2 * LANES + EDGE
PITCH = 4096
CELL_LINES = 16
MIB = 1024 * 1024


IN_VMEM = pl.BlockSpec(memory_space=pltpu.VMEM)


def iota(shape, dim):
    return lax.broadcasted_iota(I32, shape, dim)


def params(mib):
    return pltpu.CompilerParams(vmem_limit_bytes=mib * MIB)


def in_hbm(array):
    return pltpu.with_memory_space_constraint(array, pltpu.HBM)


def in_vmem(array):
    return pltpu.with_memory_space_constraint(array, pltpu.VMEM)


def dot(left, right):
    return jnp.dot(left, right, preferred_element_type=F32)


def dot_nt(left, right):
    return lax.dot_general(left, right, (((1,), (1,)), ((), ())), preferred_element_type=F32)


def halves(value):
    high = value.astype(BF16)
    return high, (value - high.astype(F32)).astype(BF16)


def thirds(value):
    high = value.astype(BF16)
    rest = value - high.astype(F32)
    mid = rest.astype(BF16)
    return [high, mid, (rest - mid.astype(F32)).astype(BF16)]


def as_column(line):
    return jnp.broadcast_to(line, (LANES, line.shape[1])).T


def as_wide_column(line):
    column = as_column(line)
    return jnp.concatenate([column, column], axis=1)


def convect(mixed, top, frac, layer_mass):
    inside = iota(mixed.shape, 0) < top
    total = jnp.sum(jnp.where(inside, mixed, 0.0), axis=0, keepdims=True)
    mass = jnp.sum(jnp.where(inside, layer_mass, 0.0), axis=0, keepdims=True)
    mean = total / jnp.where(mass > 0.0, mass, 1.0)
    return mixed + jnp.where(inside, frac * (layer_mass * mean - mixed), 0.0)


def prep_kernel(lon_count, count_ref, dest_ref, col_ref, depart_ref, obs_ref, out_ref):
    n, levels = obs_ref.shape
    lane = iota((1, n), 1)
    live = lane < count_ref[0]
    first = pl.program_id(0) * GROUP
    dest = jnp.where(live, dest_ref[...] - first, -GROUP * SLOTS)
    lon = (dest + first) % lon_count
    west = jnp.where(lon == 0, dest + (lon_count - 1), dest - 1)
    cell = col_ref[...]
    cell_row = (cell // 256 + 1).astype(F32)
    cell_col = (cell % 256).astype(F32)
    contribution = (obs_ref[...].astype(F32) * as_column(depart_ref[...])).astype(BF16)
    local = iota((GROUP, n), 0)
    hit = dest == local
    before = jnp.sum((live & (dest < local)).astype(I32), axis=1, keepdims=True)
    place = jnp.sum(jnp.where(hit, lane - before, 0), axis=0, keepdims=True)
    parts, left = [], []
    for owner in (dest, west):
        pick = iota((GROUP * CAP, n), 0) == owner * CAP + place
        found = dot(pick.astype(F32).astype(BF16), contribution)
        parts.append(found.reshape(GROUP, CAP, levels))
        hit = owner == local
        left += [jnp.where(hit, cell_row, 0.0), jnp.where(hit, cell_col, 0.0)]
    spot = (iota((LANES, n), 0) % 32 == place).astype(F32).astype(BF16)
    every = dot_nt(jnp.concatenate(left, axis=0).astype(BF16), spot)
    kind = iota((GROUP, LANES), 1) // 32
    cells = [jnp.where(kind == k, every[k * GROUP : (k + 1) * GROUP], 0.0) for k in range(4)]
    cells = ((cells[0] + cells[1]) + (cells[2] + cells[3])).astype(BF16)
    spread = iota((GROUP * 8, GROUP), 0) == 8 * iota((GROUP * 8, GROUP), 1)
    parts.append(dot(spread.astype(F32).astype(BF16), cells).reshape(GROUP, 8, levels))
    whole = jnp.concatenate(parts, axis=1).reshape(GROUP * SLOTS, levels)
    out_ref[...] = whole.astype(BF16)


def prepare(devices, lon_count, obs_count, obs_dest, obs_col, obs_depart, obs_kernel):
    n, levels = obs_kernel.shape
    steps = devices // GROUP
    whole = lambda shape: pl.BlockSpec(shape, lambda g: (0, 0))
    return pl.pallas_call(
        functools.partial(prep_kernel, lon_count),
        grid=(steps,),
        in_specs=[
            pl.BlockSpec(memory_space=pltpu.SMEM),
            whole((1, n)),
            whole((1, n)),
            whole((1, n)),
            whole((n, levels)),
        ],
        out_specs=pl.BlockSpec((GROUP * SLOTS, levels), lambda g: (g, 0)),
        out_shape=pltpu.VMEM((devices * SLOTS, levels), BF16),
        compiler_params=params(16 + devices // 4),
        name="soundings_out",
    )(
        obs_count,
        in_hbm(obs_dest.reshape(1, n)),
        in_hbm(obs_col.reshape(1, n)),
        in_hbm(obs_depart.reshape(1, n)),
        obs_kernel,
    )


def level_rows(ref, row, count=None):
    levels = ref.shape[0]
    count = levels if count is None else count
    return ref.reshape(levels * 8, LANES)[pl.ds(row, count, stride=8), :]


def pack_edge(block):
    parts = [block[:, 8 * q : 8 * q + 8, :] for q in range(4)]
    low = iota(parts[0].shape, 2) < EDGE
    return [jnp.where(low, parts[2 * h], pltpu.roll(parts[2 * h + 1], EDGE, 2)) for h in range(2)]


EDGE_STEPS = 4


def edge_kernel(field_hbm, top_hbm, frac_hbm, out_ref, field, top, frac, sem):
    count = field.shape[1]
    here = [pl.ds(i * count, count) for i in range(EDGE_STEPS)]
    near = pl.ds(0, LANES)
    copies = [
        pltpu.make_async_copy(field_hbm.at[here[i], :, near], field.at[i], sem.at[i])
        for i in range(EDGE_STEPS)
    ]
    copies.append(pltpu.make_async_copy(top_hbm.at[:, near], top, sem.at[EDGE_STEPS]))
    copies.append(pltpu.make_async_copy(frac_hbm.at[:, near], frac, sem.at[EDGE_STEPS + 1]))
    for copy in copies:
        copy.start()
    for i in range(EDGE_STEPS):
        copies[i].wait()
        for h, part in enumerate(pack_edge(field[i])):
            out_ref[h, here[i]] = part * SCALE
    for copy in copies[EDGE_STEPS:]:
        copy.wait()
    pieces = thirds(frac[...])
    lines = [top[...].astype(F32)] + [piece.astype(F32) for piece in pieces]
    lines[2:] = [line * SCALE for line in lines[2:]]
    first = out_ref.shape[1] - EDGE_LINES
    for i, line in enumerate(lines):
        for h, part in enumerate(pack_edge(line[None])):
            out_ref[h, first + i : first + i + 1] = part


def edge_columns(adjoint_field, cloud_top, conv_frac):
    levels, row_count, _ = adjoint_field.shape
    in_place = pl.BlockSpec(memory_space=pl.ANY)
    return pl.pallas_call(
        edge_kernel,
        in_specs=[in_place] * 3,
        out_specs=IN_VMEM,
        out_shape=pltpu.VMEM((2, levels + EDGE_LINES, 8, LANES), F32),
        scratch_shapes=[
            pltpu.VMEM((EDGE_STEPS, levels // EDGE_STEPS, row_count, LANES), F32),
            pltpu.VMEM((row_count, LANES), I32),
            pltpu.VMEM((row_count, LANES), F32),
            pltpu.SemaphoreType.DMA((EDGE_STEPS + 2,)),
        ],
        compiler_params=params(16),
        cost_estimate=pl.CostEstimate(
            flops=levels * levels * 4 * row_count * LANES,
            bytes_accessed=12 * levels * row_count * LANES,
            transcendentals=0,
        ),
        name="edge_columns",
    )(adjoint_field, cloud_top, conv_frac)


def put_columns(ref, row, value):
    count = ref.shape[0]
    flat = ref.reshape(count * 8, LANES)
    for h in range(count // LANES):
        part = value[:, h * LANES : (h + 1) * LANES].T
        flat[pl.ds(h * LANES * 8 + row, LANES, stride=8), :] = part


def mix_rows(field_refs, mixing_ref, top, frac, layer_mass, block, out_ref, wide_ref):
    levels = mixing_ref.shape[1]
    for row in range(8):
        value = jnp.concatenate([level_rows(ref, row) for ref in field_refs], axis=1)
        high, low = halves(value)
        mix_high, mix_low = halves(mixing_ref[row])
        here = pl.ds(pl.multiple_of((8 * block + row) * levels, levels), levels)
        wide_ref[:levels, here] = mix_high
        wide_ref[levels:, here] = mix_low
        four = jnp.concatenate([mix_high, mix_low], axis=0)
        both = dot(jnp.concatenate([four, four], axis=1), jnp.concatenate([high, low], axis=0))
        mixed = both[:levels] + both[levels:]
        done = convect(mixed, top[row : row + 1, :], frac[row : row + 1, :], layer_mass)
        put_columns(out_ref.at[0], row, done)


def mix_kernel(
    field_hbm, mixing_hbm, top_hbm, frac_hbm, mass_hbm, out_ref, wide_ref, row_ref,
    field, mixing, top, frac, mass, sem, small,
):
    block = pl.program_id(0)

    def copies(b):
        rows = pl.ds(pl.multiple_of(8 * b, 8), 8)
        found = [pltpu.make_async_copy(mixing_hbm.at[rows], mixing.at[b], sem.at[b, 2])]
        for h in range(2):
            source = field_hbm.at[:, rows, pl.ds(h * LANES, LANES)]
            found.append(pltpu.make_async_copy(source, field.at[b, h], sem.at[b, h]))
        return found

    @pl.when(block == 0)
    def _():
        pairs = ((top_hbm, top), (frac_hbm, frac), (mass_hbm, mass))
        lines = [pltpu.make_async_copy(*pair, small.at[i]) for i, pair in enumerate(pairs)]
        for copy in lines:
            copy.start()
        for b in range(field.shape[0]):
            for copy in copies(b):
                copy.start()
        for copy in lines:
            copy.wait()

    for copy in copies(block):
        copy.wait()
    rows = pl.ds(pl.multiple_of(8 * block, 8), 8)
    mix_rows(
        (field.at[block, 0], field.at[block, 1]), mixing.at[block], top[rows, :], frac[rows, :],
        as_wide_column(mass[...]), block, out_ref, wide_ref,
    )

    @pl.when(block == 0)
    def _():
        flat = out_ref.at[0].reshape(row_ref.shape[0] * 8, LANES)
        row_ref[...] = flat[pl.ds(0, row_ref.shape[0], stride=8), :]


def mix(adjoint_field, mixing_inverse, cloud_top, conv_frac, layer_mass):
    levels, row_count, col_count = adjoint_field.shape
    blocks = row_count // 8
    field, wide, row = pl.pallas_call(
        mix_kernel,
        grid=(blocks,),
        in_specs=[pl.BlockSpec(memory_space=pl.ANY)] * 5,
        out_specs=[
            pl.BlockSpec((1, col_count, 8, levels), lambda b: (b, 0, 0, 0)),
            IN_VMEM,
            pl.BlockSpec((col_count, levels), lambda b: (0, 0)),
        ],
        out_shape=[
            pltpu.HBM((blocks, col_count, 8, levels), F32),
            pltpu.VMEM((2 * levels, row_count * levels), BF16),
            pltpu.HBM((col_count, levels), F32),
        ],
        scratch_shapes=[
            pltpu.VMEM((blocks, 2, levels, 8, LANES), F32),
            pltpu.VMEM((blocks, 8, levels, levels), F32),
            pltpu.VMEM((row_count, col_count), I32),
            pltpu.VMEM((row_count, col_count), F32),
            pltpu.VMEM((1, levels), F32),
            pltpu.SemaphoreType.DMA((blocks, 3)),
            pltpu.SemaphoreType.DMA((3,)),
        ],
        compiler_params=params(24),
        cost_estimate=pl.CostEstimate(
            flops=2 * levels * levels * 4 * row_count * col_count,
            bytes_accessed=12 * levels * row_count * col_count,
            transcendentals=0,
        ),
        name="mix_own",
    )(adjoint_field, mixing_inverse, cloud_top, conv_frac, layer_mass)
    return in_hbm(field), in_vmem(wide), in_hbm(row)


def mix_edge(edge_ref, wide_ref, mass_ref, arrive, out_ref):
    levels = mass_ref.shape[0]
    group = iota((levels, 2 * LANES), 1) // EDGE
    top, frac = edge_lines(edge_ref, levels)
    for row in range(8):
        value = jnp.concatenate([level_rows(edge_ref.at[h], row, levels) for h in range(2)], axis=1)
        value = value * (1.0 / SCALE)
        mix_high, mix_low, highs, lows = [], [], [], []
        for q in range(4):
            cols = slice((8 * q + row) * levels, (8 * q + row + 1) * levels)
            mix_high.append(wide_ref[:levels, cols])
            mix_low.append(wide_ref[levels:, cols])
            high, low = halves(jnp.where(group == q, value, 0.0))
            highs.append(high)
            lows.append(low)
        highs = jnp.concatenate(highs, axis=0)
        mixed = dot(
            jnp.concatenate(mix_high * 2, axis=1),
            jnp.concatenate([highs] + lows, axis=0),
        ) + dot(jnp.concatenate(mix_low, axis=1), highs)
        if row == 0:
            arrive()
            layer_mass = jnp.concatenate([mass_ref[...]] * 2, axis=1)
        done = convect(mixed, top[row : row + 1].astype(I32), frac[row : row + 1], layer_mass)
        put_columns(out_ref, row, done)


def edge_lines(ref, levels):
    top, high, mid, low = [
        jnp.concatenate([ref[0, levels + i], ref[1, levels + i]], axis=1)
        for i in range(EDGE_LINES)
    ]
    return top, high + (mid + low) * (1.0 / SCALE)


def find_places(row, row_count):
    count = row.shape[1]
    upto = (iota((LANES, LANES), 0) <= iota((LANES, LANES), 1)).astype(F32).astype(BF16)
    before = jnp.zeros((row_count, 1), F32)
    places = []
    for start in range(0, count, LANES):
        mine = iota((row_count, LANES), 0) == row[:, start : start + LANES]
        running = dot(mine.astype(F32).astype(BF16), upto)
        place = jnp.sum(jnp.where(mine, running + before, 0.0), axis=0, keepdims=True) - 1.0
        places.append(place.astype(I32))
        before = before + running[:, LANES - 1 :]
    return jnp.concatenate(places, axis=1), jnp.max(before)


def mix_slots(blocks, index, key_ref, table_ref, wide_ref, layer_mass, stack):
    levels = layer_mass.shape[0]
    slots = 8 * WINDOW
    lane = iota((1, slots), 1)
    target = [(8 * b + lane // WINDOW) * PITCH + index * WINDOW + lane % WINDOW for b in blocks]
    target = jnp.concatenate(target, axis=1)
    pick = [
        (key_ref[...] == target[:, start : start + LANES]).astype(F32).astype(BF16)
        for start in range(0, target.shape[1], LANES)
    ]
    found = dot(table_ref[...], jnp.concatenate(pick, axis=1))
    split_high, split_low, top, high, mid, low = [
        found[levels + i : levels + i + 1] for i in range(6)
    ]
    column = (split_high * EDGE + split_low).astype(I32)
    parts = []
    for i, b in enumerate(blocks):
        value = found[:levels, i * slots : (i + 1) * slots].astype(BF16)
        for r in range(8):
            mine = (lane // WINDOW == r).astype(F32).astype(BF16)
            stack[i, r * levels : (r + 1) * levels, :] = value * mine
        start = pl.multiple_of(8 * b * levels, 8 * levels)
        both = dot(wide_ref[:, pl.ds(start, 8 * levels)], stack[i])
        parts.append(both[:levels] + both[levels:])
    mass = jnp.concatenate([layer_mass] * len(blocks), axis=1)
    done = convect(
        jnp.concatenate(parts, axis=1), top.astype(I32), (high + mid) + low, mass
    )
    turned = [done[:, start : start + LANES].T for start in range(0, done.shape[1], LANES)]
    high, low = halves(jnp.concatenate(turned, axis=0))
    return high, low, column


def expand(high, low, column, square, out_ref, add):
    levels = high.shape[1]
    flat = out_ref.reshape(REACH * 8, LANES)
    hot = (iota((REACH, 8 * WINDOW), 0) == column).astype(F32).astype(BF16)
    for group in range(2):
        for r in range(4):
            source = slice((4 * group + r) * WINDOW, (4 * group + r + 1) * WINDOW)
            target = slice(r * levels, (r + 1) * levels)
            square[group, r * WINDOW : (r + 1) * WINDOW, target] = high[source]
            square[group, (4 + r) * WINDOW : (5 + r) * WINDOW, target] = low[source]
        left = hot[:, 4 * group * WINDOW : 4 * (group + 1) * WINDOW]
        forced = dot(jnp.concatenate([left, left], axis=1), square[group])
        for r in range(4):
            rows = pl.ds(4 * group + r, REACH, stride=8)
            part = forced[:, r * levels : (r + 1) * levels]
            flat[rows, :] = flat[rows, :] + part if add else part


def force_rows(
    block, rounds, high_ref, low_ref, column_ref,
    key_ref, table_ref, wide_ref, layer_mass, stack, square, out_ref,
):
    slots = 8 * WINDOW
    here = pl.ds(pl.multiple_of(block * slots, slots), slots)
    expand(high_ref[here, :], low_ref[here, :], column_ref[0:1, here], square, out_ref, False)

    def more(index, carry):
        mixed = mix_slots([block], index, key_ref, table_ref, wide_ref, layer_mass, stack)
        expand(*mixed, square, out_ref, True)
        return carry

    lax.fori_loop(1, rounds, more, 0)


def soundings_kernel(
    got_ref, wide_ref, top_hbm, frac_hbm, lines_ref, mass_hbm,
    row_ref, courant_ref, shift_hbm, weight_hbm,
    key_ref, table_ref, high_ref, low_ref, column_ref, shift_ref, weight_ref,
    mass_ref, edge_out, rounds_ref, first_ref,
    forced, stack, square, row_scr, courant_scr, top_ref, frac_ref, mass_scr, sem,
):
    devices = got_ref.shape[0]
    levels = mass_ref.shape[0]
    n = devices * CAP
    row_count = top_ref.shape[0]
    width = 2 * LANES
    mass_in = pltpu.make_async_copy(mass_hbm, mass_scr, sem.at[6])
    late = [
        pltpu.make_async_copy(row_ref, row_scr, sem.at[0]),
        pltpu.make_async_copy(courant_ref.at[:, 0, :], courant_scr, sem.at[1]),
        pltpu.make_async_copy(shift_hbm, shift_ref, sem.at[2]),
        pltpu.make_async_copy(weight_hbm, weight_ref, sem.at[3]),
    ]
    soon = [
        pltpu.make_async_copy(top_hbm, top_ref, sem.at[4]),
        pltpu.make_async_copy(frac_hbm, frac_ref, sem.at[5]),
    ]
    for copy in [mass_in] + soon + late:
        copy.start()

    def arrive():
        mass_in.wait()
        mass_ref[...] = as_column(mass_scr[...])


    got = got_ref[...].astype(F32)
    table_ref[:levels, :n] = got[:, :CAP].reshape(n, levels).T.astype(BF16)
    table_ref[:levels, n:] = got[:, CAP : 2 * CAP].reshape(n, levels).T.astype(BF16)
    info = got[:, 2 * CAP :].reshape(devices * 8, LANES).astype(BF16)
    first = iota((devices, devices * 8), 1) == 8 * iota((devices, devices * 8), 0)
    info = dot(first.astype(F32).astype(BF16), info)
    kind = iota((devices, LANES), 1) // 32
    left = [jnp.where(kind == k, info, 0.0) for k in range(4)]
    chosen = iota((LANES, n), 0) % 32 == iota((LANES, n), 1) % CAP
    spread = dot(
        jnp.concatenate(left, axis=0).astype(BF16), chosen.astype(F32).astype(BF16)
    )
    mine = iota((devices, n), 0) == iota((devices, n), 1) // CAP
    lines = [
        jnp.sum(jnp.where(mine, spread[k * devices : (k + 1) * devices], 0.0), axis=0, keepdims=True)
        for k in range(4)
    ]
    own_row, own_col, east_row, east_col = [line.astype(I32) for line in lines]
    own_row, east_row = own_row - 1, east_row - 1
    east_row = jnp.where(east_col < EDGE, east_row, -1)
    row = jnp.concatenate([own_row, east_row], axis=1)
    place, most = find_places(row, row_count)
    rounds = (most.astype(I32) + (WINDOW - 1)) // WINDOW
    rounds_ref[0] = rounds
    key_ref[...] = as_column((row * PITCH + place).astype(F32)).astype(I32)
    column = jnp.concatenate([own_col, width + east_col], axis=1)
    cells = [[(column // EDGE).astype(F32), (column % EDGE).astype(F32)]]

    mix_edge(lines_ref, wide_ref, mass_ref, arrive, edge_out)
    layer_mass = jnp.concatenate([mass_ref[...]] * 2, axis=1)
    for copy in soon:
        copy.wait()
    packed_col = (east_row // 8) * EDGE + east_col
    parts = [
        (own_col, own_row, top_ref[...].astype(F32), frac_ref[...], row_count),
        (packed_col, east_row % 8, *edge_lines(lines_ref, levels), 8),
    ]
    for col, row, top, frac, count in parts:
        hot = (iota((width, n), 0) == col).astype(F32).astype(BF16)
        table = jnp.concatenate([top.astype(BF16)] + thirds(frac), axis=0)
        found = dot(table, hot)
        here = iota((count, n), 0) == row
        cells.append([
            jnp.sum(jnp.where(here, found[i * count : (i + 1) * count], 0.0), axis=0, keepdims=True)
            for i in range(4)
        ])
    lines = cells[0] + [jnp.concatenate(pair, axis=1) for pair in zip(cells[1], cells[2])]
    lines.append(jnp.zeros((CELL_LINES - len(lines), 2 * n), F32))
    table_ref[levels:] = jnp.concatenate(lines, axis=0).astype(BF16)

    high, low, column = mix_slots(
        list(range(row_count // 8)), 0, key_ref, table_ref, wide_ref, layer_mass, stack
    )
    high_ref[...] = high
    low_ref[...] = low
    column_ref[0:1] = column
    column_ref[1:] = jnp.zeros_like(column_ref[1:])
    square[...] = jnp.zeros_like(square)
    force_rows(
        0, rounds, high_ref, low_ref, column_ref,
        key_ref, table_ref, wide_ref, layer_mass, stack, square, forced,
    )
    edge = edge_out.reshape(width * 8, LANES)[pl.ds(0, EDGE, stride=8), :]
    for copy in late:
        copy.wait()
    value = jnp.concatenate([row_scr[...], edge], axis=0)
    value = value + forced.reshape(REACH * 8, LANES)[pl.ds(0, REACH, stride=8), :]
    shift = shift_ref[0:1, :]
    weight = weight_ref[0:1, :]
    for bit in (32, 16, 8, 4, 2, 1):
        value = jnp.where((shift & bit) != 0, value[bit:], value[:-bit])
    zonal = (1.0 - weight) * value[:width] + weight * value[1 : width + 1]
    for h in range(2):
        here = slice(h * LANES, (h + 1) * LANES)
        first_ref[:, here] = courant_scr[:, here] * zonal[here].T


def take_soundings(got, wide, cloud_top, conv_frac, edge_in, layer_mass, row, courant, shift, weight):
    levels = layer_mass.shape[1]
    row_count, col_count = cloud_top.shape
    n = got.shape[0] * CAP
    width = 2 * LANES
    in_place = pl.BlockSpec(memory_space=pl.ANY)
    return pl.pallas_call(
        soundings_kernel,
        in_specs=[IN_VMEM, IN_VMEM, in_place, in_place, IN_VMEM] + [in_place] * 5,
        out_specs=[IN_VMEM] * 9 + [pl.BlockSpec(memory_space=pltpu.SMEM), IN_VMEM],
        out_shape=[
            pltpu.VMEM((2 * n, LANES), I32),
            pltpu.VMEM((levels + CELL_LINES, 2 * n), BF16),
            pltpu.VMEM((row_count * WINDOW, levels), BF16),
            pltpu.VMEM((row_count * WINDOW, levels), BF16),
            pltpu.VMEM((8, row_count * WINDOW), I32),
            pltpu.VMEM((row_count, levels), I32),
            pltpu.VMEM((row_count, levels), F32),
            pltpu.VMEM((levels, LANES), F32),
            pltpu.VMEM((width, 8, levels), F32),
            jax.ShapeDtypeStruct((1,), I32),
            jax.ShapeDtypeStruct((levels, col_count), F32),
        ],
        scratch_shapes=[
            pltpu.VMEM((REACH, 8, levels), F32),
            pltpu.VMEM((row_count // 8, 8 * levels, 8 * WINDOW), BF16),
            pltpu.VMEM((2, 8 * WINDOW, 4 * levels), BF16),
            pltpu.VMEM((col_count, levels), F32),
            pltpu.VMEM((levels, col_count), F32),
            pltpu.VMEM((row_count, col_count), I32),
            pltpu.VMEM((row_count, col_count), F32),
            pltpu.VMEM((1, levels), F32),
            pltpu.SemaphoreType.DMA((7,)),
        ],
        compiler_params=params(24 + n // 64),
        name="take_soundings",
    )(
        got, wide, cloud_top, conv_frac, edge_in, layer_mass, row, courant, shift, weight
    )


def advect_kernel(
    key_ref, table_ref, high_ref, low_ref, column_ref, shift_ref, weight_ref, edge_ref, rounds_ref,
    wide_ref, field_ref, mass_ref, courant_ref,
    out_ref, last_ref,
    forced, coarse, done, stack, square, out_scr, prev, field_scr, courant_scr, sem, in_sem,
):
    step = pl.program_id(0)
    blocks = pl.num_programs(0) - 1
    block = blocks - 1 - step
    levels = mass_ref.shape[0]
    width = 2 * LANES

    def field_in(b):
        return pltpu.make_async_copy(field_ref.at[b], field_scr.at[b], in_sem.at[b, 0])

    def courant_in(b, h):
        source = courant_ref.at[:, pl.ds(pl.multiple_of(b * 8, 8), 8), pl.ds(h * LANES, LANES)]
        return pltpu.make_async_copy(source, courant_scr.at[b, h], in_sem.at[b, 1 + h])

    @pl.when(step == 0)
    def _():
        for b in reversed(range(out_scr.shape[0])):
            field_in(b).start()
            for h in range(2):
                courant_in(b, h).start()
        prev[...] = jnp.zeros_like(prev)
        square[...] = jnp.zeros_like(square)

    layer_mass = jnp.concatenate([mass_ref[...]] * 2, axis=1)
    lines = pl.ds(pl.multiple_of(8 * jnp.maximum(block, 0), 8), 8)
    shift = shift_ref[lines, :]
    weight = weight_ref[lines, :]
    chosen = {bit: (shift & bit) != 0 for bit in (32, 16, 8, 4, 2, 1)}

    def choose(tiles, bit, step):
        return [
            jnp.where(chosen[bit], new, old) for old, new in zip(tiles[:-step], tiles[step:])
        ]

    def by_eights(start):
        tiles = [field_scr[block, start + 8 * i] + forced[start + 8 * i] for i in range(32)]
        tiles += [
            edge_ref[EDGE * block + start + 8 * i] + forced[width + start + 8 * i] for i in range(8)
        ]
        for bit in (32, 16, 8):
            tiles = choose(tiles, bit, bit // 8)
        for i, tile in enumerate(tiles):
            coarse[start + 8 * i] = tile

    def by_ones(chunk, carry):
        start = chunk * 32
        tiles = [coarse[start + i] for i in range(40)]
        for bit in (4, 2, 1):
            tiles = choose(tiles, bit, bit)
        for i in range(32):
            done[start + i] = (1.0 - weight) * tiles[i] + weight * tiles[i + 1]
        return carry

    flat = done.reshape(width * 8, LANES)

    def meridional(beside, which=(0, 1)):
        later = [prev[0], prev[1]]
        for index in range(8):
            r = 7 - index
            for h in which:
                zonal = flat[pl.ds(h * LANES * 8 + r, LANES, stride=8), :].T
                courant = level_rows(courant_scr.at[block + 1, h], r)
                place = out_scr.at[block + 1, h].reshape(levels * 8, LANES)
                leaving = courant * zonal
                place[pl.ds(r, levels, stride=8), :] = (zonal - leaving) + later[h]
                later[h] = leaving
            beside(index)
        for h in which:
            prev[h] = later[h]

    def copies(b, which=(0, 1)):
        return [
            pltpu.make_async_copy(
                out_scr.at[b, h],
                out_ref.at[:, pl.ds(b * 8, 8), pl.ds(h * LANES, LANES)],
                sem.at[b, h],
            )
            for h in which
        ]

    def shift_only(index, carry):
        by_eights(index)
        return carry

    @pl.when(step < blocks)
    def _():
        force_rows(
            block, rounds_ref[0], high_ref, low_ref, column_ref,
            key_ref, table_ref, wide_ref, layer_mass, stack, square, forced,
        )
        field_in(block).wait()

    @pl.when(step > 0)
    def _():
        for h in range(2):
            courant_in(block + 1, h).wait()

    @pl.when(step == 0)
    def _():
        lax.fori_loop(0, 8, shift_only, 0)

    @pl.when((step > 0) & (step < blocks))
    def _():
        meridional(by_eights)

    @pl.when(step < blocks)
    def _():
        lax.fori_loop(0, width // 32, by_ones, 0)

    @pl.when(step == blocks)
    def _():
        for h in range(2):
            meridional(lambda index: None, (h,))
            copies(0, (h,))[0].start()

    @pl.when(step == 1)
    def _():
        for h in range(2):
            place = out_scr.at[blocks - 1, h].reshape(levels * 8, LANES)
            last_ref[:, h * LANES : (h + 1) * LANES] = place[pl.ds(7, levels, stride=8), :]

    for b in range(1, out_scr.shape[0]):

        @pl.when(block + 1 == b)
        def _():
            for copy in copies(b):
                copy.start()

    @pl.when(step == blocks)
    def _():
        for b in range(out_scr.shape[0]):
            for copy in copies(b):
                copy.wait()


def advect(soundings, edge_field, rounds, wide, field, layer_mass, courant):
    blocks, col_count, _, levels = field.shape
    n = soundings[0].shape[0] // 2
    in_place = pl.BlockSpec(memory_space=pl.ANY)
    return pl.pallas_call(
        advect_kernel,
        grid=(blocks + 1,),
        in_specs=[IN_VMEM] * 8
        + [pl.BlockSpec(memory_space=pltpu.SMEM), IN_VMEM, in_place, IN_VMEM, in_place],
        out_specs=[pl.BlockSpec(memory_space=pl.ANY), IN_VMEM],
        out_shape=[
            jax.ShapeDtypeStruct(courant.shape, F32),
            pltpu.VMEM((levels, col_count), F32),
        ],
        scratch_shapes=[
            pltpu.VMEM((REACH, 8, levels), F32),
            pltpu.VMEM((col_count + 8, 8, levels), F32),
            pltpu.VMEM((col_count, 8, levels), F32),
            pltpu.VMEM((1, 8 * levels, 8 * WINDOW), BF16),
            pltpu.VMEM((2, 8 * WINDOW, 4 * levels), BF16),
            pltpu.VMEM((blocks, 2, levels, 8, LANES), F32),
            pltpu.VMEM((2, levels, LANES), F32),
            pltpu.VMEM((blocks, col_count, 8, levels), F32),
            pltpu.VMEM((blocks, 2, levels, 8, LANES), F32),
            pltpu.SemaphoreType.DMA((blocks, 2)),
            pltpu.SemaphoreType.DMA((blocks, 3)),
        ],
        compiler_params=params(24 + n // 128),
        cost_estimate=pl.CostEstimate(
            flops=2 * levels * 8 * blocks * n * col_count,
            bytes_accessed=12 * levels * 8 * blocks * col_count,
            transcendentals=0,
        ),
        name="advect",
    )(
        *soundings, edge_field, rounds, wide, field, layer_mass, courant
    )


def close_kernel(last_ref, north_ref, _, out_ref, row, sem):
    row[...] = last_ref[...] + north_ref[...]
    copy = pltpu.make_async_copy(row, out_ref.at[:, out_ref.shape[1] - 1, :], sem)
    copy.start()
    copy.wait()


def close(out, last, north):
    in_place = pl.BlockSpec(memory_space=pl.ANY)
    return pl.pallas_call(
        close_kernel,
        in_specs=[IN_VMEM, IN_VMEM, in_place],
        out_specs=in_place,
        out_shape=jax.ShapeDtypeStruct(out.shape, F32),
        scratch_shapes=[pltpu.VMEM(last.shape, F32), pltpu.SemaphoreType.DMA],
        input_output_aliases={2: 0},
        compiler_params=params(4),
        name="close_last_row",
    )(last, north, out)


def shards(
    adjoint_field,
    mixing_inverse,
    cloud_top,
    conv_frac,
    thickness,
    zonal_shift,
    zonal_frac,
    merid_courant,
    obs_kernel,
    obs_depart,
    obs_dest,
    obs_col,
    obs_count,
):
    adjoint_field, mixing_inverse, cloud_top, conv_frac, merid_courant, obs_kernel = [
        in_hbm(array)
        for array in (
            adjoint_field, mixing_inverse, cloud_top, conv_frac, merid_courant, obs_kernel
        )
    ]
    levels, row_count, col_count = adjoint_field.shape
    lat_count, lon_count = lax.axis_size("lat"), lax.axis_size("lon")
    devices = lat_count * lon_count
    sent = prepare(devices, lon_count, obs_count, obs_dest, obs_col, obs_depart, obs_kernel)
    sent, field_after = lax.optimization_barrier((sent, adjoint_field))
    got = lax.all_to_all(
        sent.reshape(devices, SLOTS, levels), ("lat", "lon"), split_axis=0, concat_axis=0, tiled=True
    )
    westward = [((i + 1) % lon_count, i) for i in range(lon_count)]
    layer_mass = in_hbm(thickness.reshape(1, levels))
    field_after = in_hbm(field_after)
    edge = edge_columns(field_after, cloud_top, conv_frac).astype(jnp.float16)
    field, wide, row = mix(field_after, mixing_inverse, cloud_top, conv_frac, layer_mass)
    edge_in = in_vmem(lax.ppermute(edge, "lon", westward).astype(F32))
    shift, weight = in_hbm(zonal_shift.T), in_hbm(zonal_frac.T)
    *soundings, column, edge_field, rounds, first = take_soundings(
        got, wide, cloud_top, conv_frac, edge_in, layer_mass, row, merid_courant, shift, weight
    )
    southward = [(i + 1, i) for i in range(lat_count - 1)]
    north = lax.ppermute(first, "lat", southward)
    out, last = advect(
        [in_vmem(part) for part in soundings], in_vmem(edge_field), rounds, wide, field, in_vmem(column),
        merid_courant,
    )
    return close(out, last, north)


def solution(mesh):
    in_specs = (
        P(None, "lat", "lon"),
        P("lat", None, None),
        P("lat", "lon"),
        P("lat", "lon"),
        P(),
        P(None, "lat"),
        P(None, "lat"),
        P(None, "lat", "lon"),
        P(("lat", "lon"), None),
        P(("lat", "lon")),
        P(("lat", "lon")),
        P(("lat", "lon")),
        P(("lat", "lon")),
    )
    out_specs = P(None, "lat", "lon")
    return jax.shard_map(shards, mesh=mesh, in_specs=in_specs, out_specs=out_specs, check_vma=False)
```

```python
import functools

import jax
import jax.numpy as jnp
from jax import lax
from jax.experimental import pallas as pl
from jax.experimental.pallas import tpu as pltpu
from jax.sharding import PartitionSpec as P

F32, BF16, I32 = jnp.float32, jnp.bfloat16, jnp.int32
CAP = 16
SLOTS = 40
EDGE = 64
LANES = 128
GROUP = 32
EDGE_LINES = 4
SCALE = 4096.0
WINDOW = 32
REACH = 2 * LANES + EDGE
PITCH = 4096
CELL_LINES = 16
MIB = 1024 * 1024


IN_VMEM = pl.BlockSpec(memory_space=pltpu.VMEM)


def iota(shape, dim):
    return lax.broadcasted_iota(I32, shape, dim)


def params(mib):
    return pltpu.CompilerParams(vmem_limit_bytes=mib * MIB)


def in_hbm(array):
    return pltpu.with_memory_space_constraint(array, pltpu.HBM)


def in_vmem(array):
    return pltpu.with_memory_space_constraint(array, pltpu.VMEM)


def dot(left, right):
    return jnp.dot(left, right, preferred_element_type=F32)


def dot_nt(left, right):
    return lax.dot_general(left, right, (((1,), (1,)), ((), ())), preferred_element_type=F32)


def halves(value):
    high = value.astype(BF16)
    return high, (value - high.astype(F32)).astype(BF16)


def thirds(value):
    high = value.astype(BF16)
    rest = value - high.astype(F32)
    mid = rest.astype(BF16)
    return [high, mid, (rest - mid.astype(F32)).astype(BF16)]


def as_column(line):
    return jnp.broadcast_to(line, (LANES, line.shape[1])).T


def as_wide_column(line):
    column = as_column(line)
    return jnp.concatenate([column, column], axis=1)


def convect(mixed, top, frac, layer_mass):
    inside = iota(mixed.shape, 0) < top
    total = jnp.sum(jnp.where(inside, mixed, 0.0), axis=0, keepdims=True)
    mass = jnp.sum(jnp.where(inside, layer_mass, 0.0), axis=0, keepdims=True)
    mean = total / jnp.where(mass > 0.0, mass, 1.0)
    return mixed + jnp.where(inside, frac * (layer_mass * mean - mixed), 0.0)


def prep_kernel(lon_count, count_ref, dest_ref, col_ref, depart_ref, obs_ref, out_ref):
    n, levels = obs_ref.shape
    lane = iota((1, n), 1)
    live = lane < count_ref[0]
    first = pl.program_id(0) * GROUP
    dest = jnp.where(live, dest_ref[...] - first, -GROUP * SLOTS)
    lon = (dest + first) % lon_count
    west = jnp.where(lon == 0, dest + (lon_count - 1), dest - 1)
    cell = col_ref[...]
    cell_row = (cell // 256 + 1).astype(F32)
    cell_col = (cell % 256).astype(F32)
    contribution = (obs_ref[...].astype(F32) * as_column(depart_ref[...])).astype(BF16)
    local = iota((GROUP, n), 0)
    hit = dest == local
    before = jnp.sum((live & (dest < local)).astype(I32), axis=1, keepdims=True)
    place = jnp.sum(jnp.where(hit, lane - before, 0), axis=0, keepdims=True)
    parts, left = [], []
    for owner in (dest, west):
        pick = iota((GROUP * CAP, n), 0) == owner * CAP + place
        found = dot(pick.astype(F32).astype(BF16), contribution)
        parts.append(found.reshape(GROUP, CAP, levels))
        hit = owner == local
        left += [jnp.where(hit, cell_row, 0.0), jnp.where(hit, cell_col, 0.0)]
    spot = (iota((LANES, n), 0) % 32 == place).astype(F32).astype(BF16)
    every = dot_nt(jnp.concatenate(left, axis=0).astype(BF16), spot)
    kind = iota((GROUP, LANES), 1) // 32
    cells = [jnp.where(kind == k, every[k * GROUP : (k + 1) * GROUP], 0.0) for k in range(4)]
    cells = ((cells[0] + cells[1]) + (cells[2] + cells[3])).astype(BF16)
    spread = iota((GROUP * 8, GROUP), 0) == 8 * iota((GROUP * 8, GROUP), 1)
    parts.append(dot(spread.astype(F32).astype(BF16), cells).reshape(GROUP, 8, levels))
    whole = jnp.concatenate(parts, axis=1).reshape(GROUP * SLOTS, levels)
    out_ref[...] = whole.astype(BF16)


def prepare(devices, lon_count, obs_count, obs_dest, obs_col, obs_depart, obs_kernel):
    n, levels = obs_kernel.shape
    steps = devices // GROUP
    whole = lambda shape: pl.BlockSpec(shape, lambda g: (0, 0))
    return pl.pallas_call(
        functools.partial(prep_kernel, lon_count),
        grid=(steps,),
        in_specs=[
            pl.BlockSpec(memory_space=pltpu.SMEM),
            whole((1, n)),
            whole((1, n)),
            whole((1, n)),
            whole((n, levels)),
        ],
        out_specs=pl.BlockSpec((GROUP * SLOTS, levels), lambda g: (g, 0)),
        out_shape=pltpu.VMEM((devices * SLOTS, levels), BF16),
        compiler_params=params(16 + devices // 4),
        name="soundings_out",
    )(
        obs_count,
        in_hbm(obs_dest.reshape(1, n)),
        in_hbm(obs_col.reshape(1, n)),
        in_hbm(obs_depart.reshape(1, n)),
        obs_kernel,
    )


def level_rows(ref, row, count=None):
    levels = ref.shape[0]
    count = levels if count is None else count
    return ref.reshape(levels * 8, LANES)[pl.ds(row, count, stride=8), :]


def pack_edge(block):
    parts = [block[:, 8 * q : 8 * q + 8, :] for q in range(4)]
    low = iota(parts[0].shape, 2) < EDGE
    return [jnp.where(low, parts[2 * h], pltpu.roll(parts[2 * h + 1], EDGE, 2)) for h in range(2)]


EDGE_STEPS = 4


def edge_kernel(field_hbm, top_hbm, frac_hbm, out_ref, field, top, frac, sem):
    count = field.shape[1]
    here = [pl.ds(i * count, count) for i in range(EDGE_STEPS)]
    near = pl.ds(0, LANES)
    copies = [
        pltpu.make_async_copy(field_hbm.at[here[i], :, near], field.at[i], sem.at[i])
        for i in range(EDGE_STEPS)
    ]
    copies.append(pltpu.make_async_copy(top_hbm.at[:, near], top, sem.at[EDGE_STEPS]))
    copies.append(pltpu.make_async_copy(frac_hbm.at[:, near], frac, sem.at[EDGE_STEPS + 1]))
    for copy in copies:
        copy.start()
    for i in range(EDGE_STEPS):
        copies[i].wait()
        for h, part in enumerate(pack_edge(field[i])):
            out_ref[h, here[i]] = part * SCALE
    for copy in copies[EDGE_STEPS:]:
        copy.wait()
    pieces = thirds(frac[...])
    lines = [top[...].astype(F32)] + [piece.astype(F32) for piece in pieces]
    lines[2:] = [line * SCALE for line in lines[2:]]
    first = out_ref.shape[1] - EDGE_LINES
    for i, line in enumerate(lines):
        for h, part in enumerate(pack_edge(line[None])):
            out_ref[h, first + i : first + i + 1] = part


def edge_columns(adjoint_field, cloud_top, conv_frac):
    levels, row_count, _ = adjoint_field.shape
    in_place = pl.BlockSpec(memory_space=pl.ANY)
    return pl.pallas_call(
        edge_kernel,
        in_specs=[in_place] * 3,
        out_specs=IN_VMEM,
        out_shape=pltpu.VMEM((2, levels + EDGE_LINES, 8, LANES), F32),
        scratch_shapes=[
            pltpu.VMEM((EDGE_STEPS, levels // EDGE_STEPS, row_count, LANES), F32),
            pltpu.VMEM((row_count, LANES), I32),
            pltpu.VMEM((row_count, LANES), F32),
            pltpu.SemaphoreType.DMA((EDGE_STEPS + 2,)),
        ],
        compiler_params=params(16),
        cost_estimate=pl.CostEstimate(
            flops=levels * levels * 4 * row_count * LANES,
            bytes_accessed=12 * levels * row_count * LANES,
            transcendentals=0,
        ),
        name="edge_columns",
    )(adjoint_field, cloud_top, conv_frac)


def put_columns(ref, row, value):
    count = ref.shape[0]
    flat = ref.reshape(count * 8, LANES)
    for h in range(count // LANES):
        part = value[:, h * LANES : (h + 1) * LANES].T
        flat[pl.ds(h * LANES * 8 + row, LANES, stride=8), :] = part


def mix_rows(field_refs, mixing_ref, top, frac, layer_mass, block, out_ref, wide_ref):
    levels = mixing_ref.shape[1]
    for row in range(8):
        value = jnp.concatenate([level_rows(ref, row) for ref in field_refs], axis=1)
        high, low = halves(value)
        mix_high, mix_low = halves(mixing_ref[row])
        here = pl.ds(pl.multiple_of((8 * block + row) * levels, levels), levels)
        wide_ref[:levels, here] = mix_high
        wide_ref[levels:, here] = mix_low
        four = jnp.concatenate([mix_high, mix_low], axis=0)
        both = dot(jnp.concatenate([four, four], axis=1), jnp.concatenate([high, low], axis=0))
        mixed = both[:levels] + both[levels:]
        done = convect(mixed, top[row : row + 1, :], frac[row : row + 1, :], layer_mass)
        put_columns(out_ref.at[0], row, done)


def mix_kernel(
    west_ref, east_ref, mixing_ref, top_ref, frac_ref, mass_ref, out_ref, wide_ref, row_ref
):
    layer_mass = as_wide_column(mass_ref[...])
    block = pl.program_id(0)
    mix_rows(
        (west_ref, east_ref), mixing_ref, top_ref[...], frac_ref[...], layer_mass, block,
        out_ref, wide_ref,
    )

    @pl.when(block == 0)
    def _():
        flat = out_ref.at[0].reshape(row_ref.shape[0] * 8, LANES)
        row_ref[...] = flat[pl.ds(0, row_ref.shape[0], stride=8), :]


def mix(adjoint_field, mixing_inverse, cloud_top, conv_frac, layer_mass):
    levels, row_count, col_count = adjoint_field.shape
    blocks = row_count // 8
    half = lambda h: pl.BlockSpec((levels, 8, LANES), lambda b: (0, b, h))
    flat = pl.BlockSpec((8, col_count), lambda b: (b, 0))
    field, wide, row = pl.pallas_call(
        mix_kernel,
        grid=(blocks,),
        in_specs=[
            half(0),
            half(1),
            pl.BlockSpec((8, levels, levels), lambda b: (b, 0, 0)),
            flat,
            flat,
            pl.BlockSpec((1, levels), lambda b: (0, 0)),
        ],
        out_specs=[
            pl.BlockSpec((1, col_count, 8, levels), lambda b: (b, 0, 0, 0)),
            IN_VMEM,
            pl.BlockSpec((col_count, levels), lambda b: (0, 0)),
        ],
        out_shape=[
            pltpu.HBM((blocks, col_count, 8, levels), F32),
            pltpu.VMEM((2 * levels, row_count * levels), BF16),
            pltpu.HBM((col_count, levels), F32),
        ],
        compiler_params=params(20),
        cost_estimate=pl.CostEstimate(
            flops=2 * levels * levels * 4 * row_count * col_count,
            bytes_accessed=12 * levels * row_count * col_count,
            transcendentals=0,
        ),
        name="mix_own",
    )(adjoint_field, adjoint_field, mixing_inverse, cloud_top, conv_frac, layer_mass)
    return in_hbm(field), in_vmem(wide), in_hbm(row)


def mix_edge(edge_ref, wide_ref, mass_ref, arrive, out_ref):
    levels = mass_ref.shape[0]
    group = iota((levels, 2 * LANES), 1) // EDGE
    top, frac = edge_lines(edge_ref, levels)
    for row in range(8):
        value = jnp.concatenate([level_rows(edge_ref.at[h], row, levels) for h in range(2)], axis=1)
        value = value * (1.0 / SCALE)
        mix_high, mix_low, highs, lows = [], [], [], []
        for q in range(4):
            cols = slice((8 * q + row) * levels, (8 * q + row + 1) * levels)
            mix_high.append(wide_ref[:levels, cols])
            mix_low.append(wide_ref[levels:, cols])
            high, low = halves(jnp.where(group == q, value, 0.0))
            highs.append(high)
            lows.append(low)
        highs = jnp.concatenate(highs, axis=0)
        mixed = dot(
            jnp.concatenate(mix_high * 2, axis=1),
            jnp.concatenate([highs] + lows, axis=0),
        ) + dot(jnp.concatenate(mix_low, axis=1), highs)
        if row == 0:
            arrive()
            layer_mass = jnp.concatenate([mass_ref[...]] * 2, axis=1)
        done = convect(mixed, top[row : row + 1].astype(I32), frac[row : row + 1], layer_mass)
        put_columns(out_ref, row, done)


def edge_lines(ref, levels):
    top, high, mid, low = [
        jnp.concatenate([ref[0, levels + i], ref[1, levels + i]], axis=1)
        for i in range(EDGE_LINES)
    ]
    return top, high + (mid + low) * (1.0 / SCALE)


def find_places(row, row_count):
    count = row.shape[1]
    upto = (iota((LANES, LANES), 0) <= iota((LANES, LANES), 1)).astype(F32).astype(BF16)
    before = jnp.zeros((row_count, 1), F32)
    places = []
    for start in range(0, count, LANES):
        mine = iota((row_count, LANES), 0) == row[:, start : start + LANES]
        running = dot(mine.astype(F32).astype(BF16), upto)
        place = jnp.sum(jnp.where(mine, running + before, 0.0), axis=0, keepdims=True) - 1.0
        places.append(place.astype(I32))
        before = before + running[:, LANES - 1 :]
    return jnp.concatenate(places, axis=1), jnp.max(before)


def mix_slots(blocks, index, key_ref, table_ref, wide_ref, layer_mass, stack):
    levels = layer_mass.shape[0]
    slots = 8 * WINDOW
    lane = iota((1, slots), 1)
    target = [(8 * b + lane // WINDOW) * PITCH + index * WINDOW + lane % WINDOW for b in blocks]
    target = jnp.concatenate(target, axis=1)
    pick = [
        (key_ref[...] == target[:, start : start + LANES]).astype(F32).astype(BF16)
        for start in range(0, target.shape[1], LANES)
    ]
    found = dot(table_ref[...], jnp.concatenate(pick, axis=1))
    split_high, split_low, top, high, mid, low = [
        found[levels + i : levels + i + 1] for i in range(6)
    ]
    column = (split_high * EDGE + split_low).astype(I32)
    parts = []
    for i, b in enumerate(blocks):
        value = found[:levels, i * slots : (i + 1) * slots].astype(BF16)
        for r in range(8):
            mine = (lane // WINDOW == r).astype(F32).astype(BF16)
            stack[i, r * levels : (r + 1) * levels, :] = value * mine
        start = pl.multiple_of(8 * b * levels, 8 * levels)
        both = dot(wide_ref[:, pl.ds(start, 8 * levels)], stack[i])
        parts.append(both[:levels] + both[levels:])
    mass = jnp.concatenate([layer_mass] * len(blocks), axis=1)
    done = convect(
        jnp.concatenate(parts, axis=1), top.astype(I32), (high + mid) + low, mass
    )
    turned = [done[:, start : start + LANES].T for start in range(0, done.shape[1], LANES)]
    high, low = halves(jnp.concatenate(turned, axis=0))
    return high, low, column


def expand(high, low, column, square, out_ref, add):
    levels = high.shape[1]
    flat = out_ref.reshape(REACH * 8, LANES)
    hot = (iota((REACH, 8 * WINDOW), 0) == column).astype(F32).astype(BF16)
    for group in range(2):
        for r in range(4):
            source = slice((4 * group + r) * WINDOW, (4 * group + r + 1) * WINDOW)
            target = slice(r * levels, (r + 1) * levels)
            square[group, r * WINDOW : (r + 1) * WINDOW, target] = high[source]
            square[group, (4 + r) * WINDOW : (5 + r) * WINDOW, target] = low[source]
        left = hot[:, 4 * group * WINDOW : 4 * (group + 1) * WINDOW]
        forced = dot(jnp.concatenate([left, left], axis=1), square[group])
        for r in range(4):
            rows = pl.ds(4 * group + r, REACH, stride=8)
            part = forced[:, r * levels : (r + 1) * levels]
            flat[rows, :] = flat[rows, :] + part if add else part


def force_rows(
    block, rounds, high_ref, low_ref, column_ref,
    key_ref, table_ref, wide_ref, layer_mass, stack, square, out_ref,
):
    slots = 8 * WINDOW
    here = pl.ds(pl.multiple_of(block * slots, slots), slots)
    expand(high_ref[here, :], low_ref[here, :], column_ref[0:1, here], square, out_ref, False)

    def more(index, carry):
        mixed = mix_slots([block], index, key_ref, table_ref, wide_ref, layer_mass, stack)
        expand(*mixed, square, out_ref, True)
        return carry

    lax.fori_loop(1, rounds, more, 0)


def soundings_kernel(
    got_ref, wide_ref, top_hbm, frac_hbm, lines_ref, mass_hbm,
    row_ref, courant_ref, shift_hbm, weight_hbm,
    key_ref, table_ref, high_ref, low_ref, column_ref, shift_ref, weight_ref,
    mass_ref, edge_out, rounds_ref, first_ref,
    forced, stack, square, row_scr, courant_scr, top_ref, frac_ref, mass_scr, sem,
):
    devices = got_ref.shape[0]
    levels = mass_ref.shape[0]
    n = devices * CAP
    row_count = top_ref.shape[0]
    width = 2 * LANES
    mass_in = pltpu.make_async_copy(mass_hbm, mass_scr, sem.at[6])
    late = [
        pltpu.make_async_copy(row_ref, row_scr, sem.at[0]),
        pltpu.make_async_copy(courant_ref.at[:, 0, :], courant_scr, sem.at[1]),
        pltpu.make_async_copy(shift_hbm, shift_ref, sem.at[2]),
        pltpu.make_async_copy(weight_hbm, weight_ref, sem.at[3]),
    ]
    soon = [
        pltpu.make_async_copy(top_hbm, top_ref, sem.at[4]),
        pltpu.make_async_copy(frac_hbm, frac_ref, sem.at[5]),
    ]
    for copy in [mass_in] + soon + late:
        copy.start()

    def arrive():
        mass_in.wait()
        mass_ref[...] = as_column(mass_scr[...])


    got = got_ref[...].astype(F32)
    table_ref[:levels, :n] = got[:, :CAP].reshape(n, levels).T.astype(BF16)
    table_ref[:levels, n:] = got[:, CAP : 2 * CAP].reshape(n, levels).T.astype(BF16)
    info = got[:, 2 * CAP :].reshape(devices * 8, LANES).astype(BF16)
    first = iota((devices, devices * 8), 1) == 8 * iota((devices, devices * 8), 0)
    info = dot(first.astype(F32).astype(BF16), info)
    kind = iota((devices, LANES), 1) // 32
    left = [jnp.where(kind == k, info, 0.0) for k in range(4)]
    chosen = iota((LANES, n), 0) % 32 == iota((LANES, n), 1) % CAP
    spread = dot(
        jnp.concatenate(left, axis=0).astype(BF16), chosen.astype(F32).astype(BF16)
    )
    mine = iota((devices, n), 0) == iota((devices, n), 1) // CAP
    lines = [
        jnp.sum(jnp.where(mine, spread[k * devices : (k + 1) * devices], 0.0), axis=0, keepdims=True)
        for k in range(4)
    ]
    own_row, own_col, east_row, east_col = [line.astype(I32) for line in lines]
    own_row, east_row = own_row - 1, east_row - 1
    east_row = jnp.where(east_col < EDGE, east_row, -1)
    row = jnp.concatenate([own_row, east_row], axis=1)
    place, most = find_places(row, row_count)
    rounds = (most.astype(I32) + (WINDOW - 1)) // WINDOW
    rounds_ref[0] = rounds
    key_ref[...] = as_column((row * PITCH + place).astype(F32)).astype(I32)
    column = jnp.concatenate([own_col, width + east_col], axis=1)
    cells = [[(column // EDGE).astype(F32), (column % EDGE).astype(F32)]]

    mix_edge(lines_ref, wide_ref, mass_ref, arrive, edge_out)
    layer_mass = jnp.concatenate([mass_ref[...]] * 2, axis=1)
    for copy in soon:
        copy.wait()
    packed_col = (east_row // 8) * EDGE + east_col
    parts = [
        (own_col, own_row, top_ref[...].astype(F32), frac_ref[...], row_count),
        (packed_col, east_row % 8, *edge_lines(lines_ref, levels), 8),
    ]
    for col, row, top, frac, count in parts:
        hot = (iota((width, n), 0) == col).astype(F32).astype(BF16)
        table = jnp.concatenate([top.astype(BF16)] + thirds(frac), axis=0)
        found = dot(table, hot)
        here = iota((count, n), 0) == row
        cells.append([
            jnp.sum(jnp.where(here, found[i * count : (i + 1) * count], 0.0), axis=0, keepdims=True)
            for i in range(4)
        ])
    lines = cells[0] + [jnp.concatenate(pair, axis=1) for pair in zip(cells[1], cells[2])]
    lines.append(jnp.zeros((CELL_LINES - len(lines), 2 * n), F32))
    table_ref[levels:] = jnp.concatenate(lines, axis=0).astype(BF16)

    high, low, column = mix_slots(
        list(range(row_count // 8)), 0, key_ref, table_ref, wide_ref, layer_mass, stack
    )
    high_ref[...] = high
    low_ref[...] = low
    column_ref[0:1] = column
    column_ref[1:] = jnp.zeros_like(column_ref[1:])
    square[...] = jnp.zeros_like(square)
    force_rows(
        0, rounds, high_ref, low_ref, column_ref,
        key_ref, table_ref, wide_ref, layer_mass, stack, square, forced,
    )
    edge = edge_out.reshape(width * 8, LANES)[pl.ds(0, EDGE, stride=8), :]
    for copy in late:
        copy.wait()
    value = jnp.concatenate([row_scr[...], edge], axis=0)
    value = value + forced.reshape(REACH * 8, LANES)[pl.ds(0, REACH, stride=8), :]
    shift = shift_ref[0:1, :]
    weight = weight_ref[0:1, :]
    for bit in (32, 16, 8, 4, 2, 1):
        value = jnp.where((shift & bit) != 0, value[bit:], value[:-bit])
    zonal = (1.0 - weight) * value[:width] + weight * value[1 : width + 1]
    for h in range(2):
        here = slice(h * LANES, (h + 1) * LANES)
        first_ref[:, here] = courant_scr[:, here] * zonal[here].T


def take_soundings(got, wide, cloud_top, conv_frac, edge_in, layer_mass, row, courant, shift, weight):
    levels = layer_mass.shape[1]
    row_count, col_count = cloud_top.shape
    n = got.shape[0] * CAP
    width = 2 * LANES
    in_place = pl.BlockSpec(memory_space=pl.ANY)
    return pl.pallas_call(
        soundings_kernel,
        in_specs=[IN_VMEM, IN_VMEM, in_place, in_place, IN_VMEM] + [in_place] * 5,
        out_specs=[IN_VMEM] * 9 + [pl.BlockSpec(memory_space=pltpu.SMEM), IN_VMEM],
        out_shape=[
            pltpu.VMEM((2 * n, LANES), I32),
            pltpu.VMEM((levels + CELL_LINES, 2 * n), BF16),
            pltpu.VMEM((row_count * WINDOW, levels), BF16),
            pltpu.VMEM((row_count * WINDOW, levels), BF16),
            pltpu.VMEM((8, row_count * WINDOW), I32),
            pltpu.VMEM((row_count, levels), I32),
            pltpu.VMEM((row_count, levels), F32),
            pltpu.VMEM((levels, LANES), F32),
            pltpu.VMEM((width, 8, levels), F32),
            jax.ShapeDtypeStruct((1,), I32),
            jax.ShapeDtypeStruct((levels, col_count), F32),
        ],
        scratch_shapes=[
            pltpu.VMEM((REACH, 8, levels), F32),
            pltpu.VMEM((row_count // 8, 8 * levels, 8 * WINDOW), BF16),
            pltpu.VMEM((2, 8 * WINDOW, 4 * levels), BF16),
            pltpu.VMEM((col_count, levels), F32),
            pltpu.VMEM((levels, col_count), F32),
            pltpu.VMEM((row_count, col_count), I32),
            pltpu.VMEM((row_count, col_count), F32),
            pltpu.VMEM((1, levels), F32),
            pltpu.SemaphoreType.DMA((7,)),
        ],
        compiler_params=params(24 + n // 64),
        name="take_soundings",
    )(
        got, wide, cloud_top, conv_frac, edge_in, layer_mass, row, courant, shift, weight
    )


def advect_kernel(
    key_ref, table_ref, high_ref, low_ref, column_ref, shift_ref, weight_ref, edge_ref, rounds_ref,
    wide_ref, field_ref, mass_ref, courant_ref,
    out_ref, last_ref,
    forced, coarse, done, stack, square, out_scr, prev, field_scr, courant_scr, sem, in_sem,
):
    step = pl.program_id(0)
    blocks = pl.num_programs(0) - 1
    block = blocks - 1 - step
    levels = mass_ref.shape[0]
    width = 2 * LANES

    def field_in(b):
        return pltpu.make_async_copy(field_ref.at[b], field_scr.at[b], in_sem.at[b, 0])

    def courant_in(b, h):
        source = courant_ref.at[:, pl.ds(pl.multiple_of(b * 8, 8), 8), pl.ds(h * LANES, LANES)]
        return pltpu.make_async_copy(source, courant_scr.at[b, h], in_sem.at[b, 1 + h])

    @pl.when(step == 0)
    def _():
        for b in reversed(range(out_scr.shape[0])):
            field_in(b).start()
            for h in range(2):
                courant_in(b, h).start()
        prev[...] = jnp.zeros_like(prev)
        square[...] = jnp.zeros_like(square)

    layer_mass = jnp.concatenate([mass_ref[...]] * 2, axis=1)
    lines = pl.ds(pl.multiple_of(8 * jnp.maximum(block, 0), 8), 8)
    shift = shift_ref[lines, :]
    weight = weight_ref[lines, :]
    chosen = {bit: (shift & bit) != 0 for bit in (32, 16, 8, 4, 2, 1)}

    def choose(tiles, bit, step):
        return [
            jnp.where(chosen[bit], new, old) for old, new in zip(tiles[:-step], tiles[step:])
        ]

    def by_eights(start):
        tiles = [field_scr[block, start + 8 * i] + forced[start + 8 * i] for i in range(32)]
        tiles += [
            edge_ref[EDGE * block + start + 8 * i] + forced[width + start + 8 * i] for i in range(8)
        ]
        for bit in (32, 16, 8):
            tiles = choose(tiles, bit, bit // 8)
        for i, tile in enumerate(tiles):
            coarse[start + 8 * i] = tile

    def by_ones(chunk, carry):
        start = chunk * 32
        tiles = [coarse[start + i] for i in range(40)]
        for bit in (4, 2, 1):
            tiles = choose(tiles, bit, bit)
        for i in range(32):
            done[start + i] = (1.0 - weight) * tiles[i] + weight * tiles[i + 1]
        return carry

    flat = done.reshape(width * 8, LANES)

    def meridional(beside, which=(0, 1)):
        later = [prev[0], prev[1]]
        for index in range(8):
            r = 7 - index
            for h in which:
                zonal = flat[pl.ds(h * LANES * 8 + r, LANES, stride=8), :].T
                courant = level_rows(courant_scr.at[block + 1, h], r)
                place = out_scr.at[block + 1, h].reshape(levels * 8, LANES)
                leaving = courant * zonal
                place[pl.ds(r, levels, stride=8), :] = (zonal - leaving) + later[h]
                later[h] = leaving
            beside(index)
        for h in which:
            prev[h] = later[h]

    def copies(b, which=(0, 1)):
        return [
            pltpu.make_async_copy(
                out_scr.at[b, h],
                out_ref.at[:, pl.ds(b * 8, 8), pl.ds(h * LANES, LANES)],
                sem.at[b, h],
            )
            for h in which
        ]

    def shift_only(index, carry):
        by_eights(index)
        return carry

    @pl.when(step < blocks)
    def _():
        force_rows(
            block, rounds_ref[0], high_ref, low_ref, column_ref,
            key_ref, table_ref, wide_ref, layer_mass, stack, square, forced,
        )
        field_in(block).wait()

    @pl.when(step > 0)
    def _():
        for h in range(2):
            courant_in(block + 1, h).wait()

    @pl.when(step == 0)
    def _():
        lax.fori_loop(0, 8, shift_only, 0)

    @pl.when((step > 0) & (step < blocks))
    def _():
        meridional(by_eights)

    @pl.when(step < blocks)
    def _():
        for chunk in range(width // 32):
            by_ones(chunk, 0)

    @pl.when(step == blocks)
    def _():
        for h in range(2):
            meridional(lambda index: None, (h,))
            copies(0, (h,))[0].start()

    @pl.when(step == 1)
    def _():
        for h in range(2):
            place = out_scr.at[blocks - 1, h].reshape(levels * 8, LANES)
            last_ref[:, h * LANES : (h + 1) * LANES] = place[pl.ds(7, levels, stride=8), :]

    for b in range(1, out_scr.shape[0]):

        @pl.when(block + 1 == b)
        def _():
            for copy in copies(b):
                copy.start()

    @pl.when(step == blocks)
    def _():
        for b in range(out_scr.shape[0]):
            for copy in copies(b):
                copy.wait()


def advect(soundings, edge_field, rounds, wide, field, layer_mass, courant):
    blocks, col_count, _, levels = field.shape
    n = soundings[0].shape[0] // 2
    in_place = pl.BlockSpec(memory_space=pl.ANY)
    return pl.pallas_call(
        advect_kernel,
        grid=(blocks + 1,),
        in_specs=[IN_VMEM] * 8
        + [pl.BlockSpec(memory_space=pltpu.SMEM), IN_VMEM, in_place, IN_VMEM, in_place],
        out_specs=[pl.BlockSpec(memory_space=pl.ANY), IN_VMEM],
        out_shape=[
            jax.ShapeDtypeStruct(courant.shape, F32),
            pltpu.VMEM((levels, col_count), F32),
        ],
        scratch_shapes=[
            pltpu.VMEM((REACH, 8, levels), F32),
            pltpu.VMEM((col_count + 8, 8, levels), F32),
            pltpu.VMEM((col_count, 8, levels), F32),
            pltpu.VMEM((1, 8 * levels, 8 * WINDOW), BF16),
            pltpu.VMEM((2, 8 * WINDOW, 4 * levels), BF16),
            pltpu.VMEM((blocks, 2, levels, 8, LANES), F32),
            pltpu.VMEM((2, levels, LANES), F32),
            pltpu.VMEM((blocks, col_count, 8, levels), F32),
            pltpu.VMEM((blocks, 2, levels, 8, LANES), F32),
            pltpu.SemaphoreType.DMA((blocks, 2)),
            pltpu.SemaphoreType.DMA((blocks, 3)),
        ],
        compiler_params=params(24 + n // 128),
        cost_estimate=pl.CostEstimate(
            flops=2 * levels * 8 * blocks * n * col_count,
            bytes_accessed=12 * levels * 8 * blocks * col_count,
            transcendentals=0,
        ),
        name="advect",
    )(
        *soundings, edge_field, rounds, wide, field, layer_mass, courant
    )


def close_kernel(last_ref, north_ref, _, out_ref, row, sem):
    row[...] = last_ref[...] + north_ref[...]
    copy = pltpu.make_async_copy(row, out_ref.at[:, out_ref.shape[1] - 1, :], sem)
    copy.start()
    copy.wait()


def close(out, last, north):
    in_place = pl.BlockSpec(memory_space=pl.ANY)
    return pl.pallas_call(
        close_kernel,
        in_specs=[IN_VMEM, IN_VMEM, in_place],
        out_specs=in_place,
        out_shape=jax.ShapeDtypeStruct(out.shape, F32),
        scratch_shapes=[pltpu.VMEM(last.shape, F32), pltpu.SemaphoreType.DMA],
        input_output_aliases={2: 0},
        compiler_params=params(4),
        name="close_last_row",
    )(last, north, out)


def shards(
    adjoint_field,
    mixing_inverse,
    cloud_top,
    conv_frac,
    thickness,
    zonal_shift,
    zonal_frac,
    merid_courant,
    obs_kernel,
    obs_depart,
    obs_dest,
    obs_col,
    obs_count,
):
    adjoint_field, mixing_inverse, cloud_top, conv_frac, merid_courant, obs_kernel = [
        in_hbm(array)
        for array in (
            adjoint_field, mixing_inverse, cloud_top, conv_frac, merid_courant, obs_kernel
        )
    ]
    levels, row_count, col_count = adjoint_field.shape
    lat_count, lon_count = lax.axis_size("lat"), lax.axis_size("lon")
    devices = lat_count * lon_count
    sent = prepare(devices, lon_count, obs_count, obs_dest, obs_col, obs_depart, obs_kernel)
    sent, field_after = lax.optimization_barrier((sent, adjoint_field))
    got = lax.all_to_all(
        sent.reshape(devices, SLOTS, levels), ("lat", "lon"), split_axis=0, concat_axis=0, tiled=True
    )
    westward = [((i + 1) % lon_count, i) for i in range(lon_count)]
    layer_mass = in_hbm(thickness.reshape(1, levels))
    field_after = in_hbm(field_after)
    edge = edge_columns(field_after, cloud_top, conv_frac).astype(jnp.float16)
    field, wide, row = mix(field_after, mixing_inverse, cloud_top, conv_frac, layer_mass)
    edge_in = in_vmem(lax.ppermute(edge, "lon", westward).astype(F32))
    shift, weight = in_hbm(zonal_shift.T), in_hbm(zonal_frac.T)
    *soundings, column, edge_field, rounds, first = take_soundings(
        got, wide, cloud_top, conv_frac, edge_in, layer_mass, row, merid_courant, shift, weight
    )
    southward = [(i + 1, i) for i in range(lat_count - 1)]
    north = lax.ppermute(first, "lat", southward)
    out, last = advect(
        [in_vmem(part) for part in soundings], in_vmem(edge_field), rounds, wide, field, in_vmem(column),
        merid_courant,
    )
    return close(out, last, north)


def solution(mesh):
    in_specs = (
        P(None, "lat", "lon"),
        P("lat", None, None),
        P("lat", "lon"),
        P("lat", "lon"),
        P(),
        P(None, "lat"),
        P(None, "lat"),
        P(None, "lat", "lon"),
        P(("lat", "lon"), None),
        P(("lat", "lon")),
        P(("lat", "lon")),
        P(("lat", "lon")),
        P(("lat", "lon")),
    )
    out_specs = P(None, "lat", "lon")
    return jax.shard_map(shards, mesh=mesh, in_specs=in_specs, out_specs=out_specs, check_vma=False)
```
